32 devices in a mesh: gx: 4 (over y, core), gy: 2 (over x), gz: 4 (over z).
Axes of the slice: x: 2, y: 2, z: 4, core: 2. Of those that a mesh axis runs over, the one named last changes fastest.
Arguments:
- charges: float32 [128, 64, 512], P('gx', 'gy', 'gz'), may hold values from -4 to 4
Outputs:
- potential: float32 [128, 64, 512], P('gx', 'gy', 'gz')
The draws below stay inside these ranges and needn't reach their ends.
All inputs are finite; a program needn't handle non-finite values.
Results may differ from the reference program's by a relative error of at most 0.00014.
Values sent between devices are 32-bit elements; how exact they have to be, the bound alone decides.
No kernel may reach another device: no remote copies, remote signals or barrier semaphores. Data moves between devices by JAX's collectives and lax.ppermute only.
A program may use at most 64 MiB of HBM per device.

```python
import jax
import jax.numpy as jnp
from jax import lax

REACH = 8
NX = 128
NY = 64
NZ = 512


def draw_charges(key, part):
    key = jax.random.fold_in(key, 11)
    base = jax.random.normal(jax.random.fold_in(key, 1), (NX, NY, NZ), jnp.float32)
    return jnp.clip(base, -3.5, 3.5)


def setup_inputs(seed: int = 0) -> dict:
    splits = jax.random.split(jax.random.key(seed), 2)
    charges = draw_charges(jax.random.fold_in(splits[1], 71), 0)
    return dict(charges=charges)


STENCIL_SIGMAS = (1.0, 2.0, 3.5)
STENCIL_WEIGHTS = (0.4, 0.1, 0.03)
TOP_SIGMAS = (1.5, 4.0)
TOP_WEIGHTS = (0.03, 0.006)
SPLINE_TAPS = (-0.0625, 0.0, 0.5625, 1.0, 0.5625, 0.0, -0.0625)


def band_matrix(row_count, col_count, offset, width_sigma, reach_cells):
    row_index = lax.broadcasted_iota(jnp.int32, (row_count, col_count), 0)
    col_index = lax.broadcasted_iota(jnp.int32, (row_count, col_count), 1)
    distance = col_index - row_index - offset
    spread = distance.astype(jnp.float32)
    kernel = jnp.exp(-spread * spread / (width_sigma * width_sigma))
    return jnp.where(jnp.abs(distance) <= reach_cells, kernel, jnp.zeros_like(kernel))


def tap_matrix(row_count, col_count, row_step, col_step, offset):
    row_index = lax.broadcasted_iota(jnp.int32, (row_count, col_count), 0)
    col_index = lax.broadcasted_iota(jnp.int32, (row_count, col_count), 1)
    position = row_step * row_index + col_step * col_index + offset
    matrix = jnp.zeros((row_count, col_count), jnp.float32)
    for number, tap_value in enumerate(SPLINE_TAPS):
        matrix = matrix + jnp.where(position == number, jnp.float32(tap_value), jnp.float32(0.0))
    return matrix


def separable(mat_x, mat_y, mat_z, values):
    first = jnp.einsum("ai,ijk->ajk", mat_x, values, precision=lax.Precision.HIGHEST)
    second = jnp.einsum("bj,ajk->abk", mat_y, first, precision=lax.Precision.HIGHEST)
    return jnp.einsum("ck,abk->abc", mat_z, second, precision=lax.Precision.HIGHEST)


def smoothed(values, factor):
    size_x, size_y, size_z = values.shape
    summed = jnp.zeros(values.shape, jnp.float32)
    for width_sigma, weight in zip(STENCIL_SIGMAS, STENCIL_WEIGHTS):
        summed = summed + (factor * weight) * separable(
            band_matrix(size_x, size_x, 0, width_sigma, REACH),
            band_matrix(size_y, size_y, 0, width_sigma, REACH),
            band_matrix(size_z, size_z, 0, width_sigma, REACH), values)
    return summed


def reference(charges):
    grids = [charges]
    for level_index in range(3):
        fine_grid = grids[-1]
        size_x, size_y, size_z = fine_grid.shape
        grids.append(separable(tap_matrix(size_x // 2, size_x, -2, 1, 3),
                               tap_matrix(size_y // 2, size_y, -2, 1, 3),
                               tap_matrix(size_z // 2, size_z, -2, 1, 3), fine_grid))
    coarse = grids[3]
    size_x, size_y, size_z = coarse.shape
    potential = jnp.zeros(coarse.shape, jnp.float32)
    for width_sigma, weight in zip(TOP_SIGMAS, TOP_WEIGHTS):
        potential = potential + weight * separable(
            band_matrix(size_x, size_x, 0, width_sigma, size_x),
            band_matrix(size_y, size_y, 0, width_sigma, size_y),
            band_matrix(size_z, size_z, 0, width_sigma, size_z), coarse)
    for level_index in (2, 1, 0):
        coarse_x, coarse_y, coarse_z = potential.shape
        potential = smoothed(grids[level_index], 0.5 ** level_index) + separable(
            tap_matrix(2 * coarse_x, coarse_x, 1, -2, 3),
            tap_matrix(2 * coarse_y, coarse_y, 1, -2, 3),
            tap_matrix(2 * coarse_z, coarse_z, 1, -2, 3), potential)
    return potential
```

```python
import functools

import jax
import jax.numpy as jnp
import numpy as np
from jax import lax
from jax.experimental import pallas as pl
from jax.experimental.pallas import tpu as pltpu
from jax.sharding import PartitionSpec as P

REACH = 8
STENCIL_SIGMAS = (1.0, 2.0, 3.5)
STENCIL_WEIGHTS = (0.4, 0.1, 0.03)
TOP_SIGMAS = (1.5, 4.0)
TOP_WEIGHTS = (0.03, 0.006)
SPLINE_TAPS = np.array((-1.0, 0.0, 9.0, 16.0, 9.0, 0.0, -1.0)) / 16.0

LOW = (0, -1, -2, -2)
EXTRA = (0, 3, 5, 5)
FACE = 11
LANES = 128
BF = jnp.bfloat16
F32 = jnp.float32


def up(value, unit):
    return -(-value // unit) * unit


def band(rows, cols, sigma, reach):
    distance = cols[None, :] - rows[:, None]
    return np.where(abs(distance) <= reach, np.exp(-((distance / sigma) ** 2)), 0.0)


def restriction(size):
    position = np.arange(size)[None, :] - 2 * np.arange(size // 2)[:, None] + 3
    inside = (position >= 0) & (position <= 6)
    return np.where(inside, SPLINE_TAPS[np.clip(position, 0, 6)], 0.0)


class Axis:
    def __init__(self, count, length):
        self.count, self.length = count, length
        self.width = [(length >> level) + EXTRA[level] for level in range(4)]

    def window(self, level, brick):
        size = self.length >> level
        cells = brick * size + LOW[level] + np.arange(self.width[level])
        return cells, ((cells >= 0) & (cells < self.count * size)).astype(float)

    def partial(self, level, brick):
        matrix = np.eye(self.count * self.length)
        for _ in range(level):
            matrix = restriction(matrix.shape[0]) @ matrix
        cells, inside = self.window(level, brick)
        rows = matrix[np.clip(cells, 0, len(matrix) - 1)] * inside[:, None]
        return rows[:, brick * self.length : (brick + 1) * self.length]

    def prolong(self, level, brick):
        matrix = restriction((self.count * self.length) >> (level - 1)).T
        rows, row_inside = self.window(level - 1, brick)
        cols, col_inside = self.window(level, brick)
        taken = matrix[np.clip(rows, 0, len(matrix) - 1)][:, np.clip(cols, 0, matrix.shape[1] - 1)]
        return taken * row_inside[:, None] * col_inside[None, :]

    def mix(self, level, sigma, target, source):
        rows, row_inside = self.window(level, target)
        cols, col_inside = self.window(level, source)
        reach = REACH if level < 3 else self.count * self.length
        return band(rows, cols, sigma, reach) * row_inside[:, None] * col_inside[None, :]


def place(shape, *pieces):
    whole = np.zeros(shape)
    for row, col, block in pieces:
        whole[row : row + block.shape[0], col : col + block.shape[1]] += block
    return whole


def halves(matrix):
    high = matrix.astype(jnp.bfloat16)
    low = (matrix - high.astype(np.float64)).astype(jnp.bfloat16)
    return high, low


def left3(matrix):
    high, low = halves(matrix)
    return np.concatenate([high, low, high], axis=-1)


def left3t(matrix):
    high, low = halves(matrix)
    return np.concatenate([high, high, low], axis=-1)


def right3(matrix):
    high, low = halves(matrix)
    return np.concatenate([high, high, low], axis=-2)


def split(value):
    high = value.astype(BF)
    return high, (value - high.astype(F32)).astype(BF)


def dot(left, right, dims=((1,), (0,))):
    return lax.dot_general(left, right, (dims, ((), ())), preferred_element_type=F32)


class Plan:
    def __init__(self, counts, lengths):
        self.x, self.y, self.z = (Axis(n, length) for n, length in zip(counts, lengths))
        x, y, z = self.x, self.y, self.z
        assert x.count >= 3 and z.count >= 3
        self.lane = [0, 0, z.width[1], z.width[1] + z.width[2]]
        self.lane_end = self.lane[3] + z.width[3]
        assert self.lane_end <= LANES and z.length == LANES
        self.rows1, self.rows2, self.rows3 = up(y.width[1], 8), up(y.width[2], 16), up(y.width[3], 16)
        assert self.rows2 <= 16 and self.rows3 <= 16 and FACE <= 14 and self.rows1 == 24
        self.row = [0, 0, self.rows1, self.rows1 + self.rows2]
        self.row_face = self.rows1 + self.rows2 + self.rows3
        self.kinds = 1 if y.count == 2 else 2
        self.rows_restricted = self.row_face + 16 * self.kinds
        self.overlay = y.count == 2 and y.width[1] + 3 <= self.rows1
        self.coarse_rows = up(24 + 16 * (y.count - 1), 16) if not self.overlay else 32
        self.fine_halos = 1 if y.count == 2 else 2
        self.fine_rows = y.length + 8 * self.fine_halos
        self.planes = max(FACE, x.width[2], x.width[3])
        assert self.planes <= x.width[1]
        self.group = [0, 0, 3 * self.rows1, 3 * self.rows1 + 3 * self.rows2]
        self.rows_mixed = self.group[3] + 2 * self.rows3
        self.tall = [0, up(z.width[1], 8), up(z.width[2], 8), up(z.width[3], 8)]
        assert self.tall[1] - 16 == z.width[1] - FACE and self.tall[2] - 16 == z.width[2] - 13
        self.flat = [0, x.width[1] * self.rows1, x.width[2] * self.rows2, x.width[3] * self.rows3]
        assert self.flat[1] <= 512 and self.flat[2] <= 256 and self.flat[3] <= 256

    def face_kind(self, axis, offset, source):
        if axis.count == 2:
            return 1 - source
        return 1 if offset == 1 else 0

    def face_row(self, j):
        return j if j < 8 or not self.overlay else j + 3

    def restrict_z(self):
        z = self.z
        return np.stack(
            [
                right3(place((z.length, LANES), *[(0, self.lane[l], z.partial(l, b).T) for l in (1, 2, 3)]))
                for b in range(z.count)
            ]
        )

    def restrict_y(self):
        y, tables = self.y, []
        for b in range(y.count):
            pieces = [(self.row[l], 0, y.partial(l, b)) for l in (1, 2, 3)]
            first = y.partial(1, b)
            for k in range(self.kinds):
                kind = self.face_kind(y, 1, b) if self.kinds == 1 else 1 - k
                start = (y.width[1] - FACE) * kind
                for j in range(FACE):
                    pieces.append((self.row_face + 16 * k + self.face_row(j), 0, first[start + j][None]))
            tables.append(left3(place((self.rows_restricted, y.length), *pieces)))
        return np.stack(tables)

    def fine_y(self):
        y, tables = self.y, []
        for b in range(y.count):
            pieces = []
            for s, sigma in enumerate(STENCIL_SIGMAS):
                row = s * y.length
                pieces.append((row, 0, y.mix(0, sigma, b, b)))
                for h in range(self.fine_halos):
                    offset = 1 if h == 0 else y.count - 1
                    source = (b - offset) % y.count
                    start = (y.length - REACH) * self.face_kind(y, offset, source)
                    block = y.mix(0, sigma, b, source)[:, start : start + REACH]
                    pieces.append((row, y.length + 8 * h, block))
            tables.append(left3(place((3 * y.length, up(self.fine_rows, 16)), *pieces)))
        return np.stack(tables)

    def coarse_y(self):
        y, tables = self.y, []
        for b in range(y.count):
            whole = np.zeros((self.rows_mixed, self.coarse_rows))
            for level in (1, 2, 3):
                sigmas = STENCIL_SIGMAS if level < 3 else TOP_SIGMAS
                rows = (0, self.rows1, self.rows2, self.rows3)[level]
                for s, sigma in enumerate(sigmas):
                    top = self.group[level] + s * rows
                    for offset in range(y.count):
                        source = (b - offset) % y.count
                        block = y.mix(level, sigma, b, source)
                        if level == 1 and offset:
                            start = (y.width[1] - FACE) * self.face_kind(y, offset, source)
                            block = block[:, start : start + FACE]
                        for j in range(block.shape[1]):
                            slot = self.face_row(j) if level == 1 and offset else j
                            if self.overlay and offset:
                                slot = 24 + slot if slot < 8 else 8 + slot
                            elif offset:
                                slot = 24 + 16 * (offset - 1) + slot
                            whole[top : top + y.width[level], slot] += block[:, j]
            tables.append(left3(whole))
        return np.stack(tables)

    def top_x(self):
        x = self.x
        return np.stack(
            [
                np.stack(
                    [
                        np.stack([x.mix(3, sigma, b, (b - r) % x.count) for r in range(x.count)], axis=1)
                        for sigma in TOP_SIGMAS
                    ]
                ).reshape(-1)
                for b in range(x.count)
            ]
        ).astype(np.float32)

    def fine_z(self):
        z, own, pushed = self.z, [], []
        for b in range(z.count):
            mixes = lambda target: [
                w * z.mix(0, sigma, target, b) for sigma, w in zip(STENCIL_SIGMAS, STENCIL_WEIGHTS)
            ]
            own.append(right3(np.concatenate([m.T for m in mixes(b)], axis=0)))
            rows = [np.concatenate([m[:8] for m in mixes((b + 1) % z.count)], axis=1)]
            rows.append(np.concatenate([m[-8:] for m in mixes((b - 1) % z.count)], axis=1))
            pushed.append(left3t(np.concatenate(rows, axis=0)))
        return np.stack(own), np.stack(pushed)

    def coarse_z(self, level):
        z, tables = self.z, []
        sigmas, weights = (STENCIL_SIGMAS, STENCIL_WEIGHTS) if level < 3 else (TOP_SIGMAS, TOP_WEIGHTS)
        factor = 0.5**level if level < 3 else 1.0
        for b in range(z.count):

            def mixed(target):
                blocks = [
                    place((z.width[level], LANES), (0, self.lane[level], factor * w * z.mix(level, sigma, target, b)))
                    for sigma, w in zip(sigmas, weights)
                ]
                return np.concatenate(blocks, axis=1)

            cols = LANES * len(sigmas)
            tall = self.tall[level]
            pieces = [place((tall, cols), (0, 0, mixed(b)))]
            for offset in range(1, z.count):
                block = mixed((b + offset) % z.count)
                near = offset in (1, z.count - 1)
                if level < 3 and near:
                    layers = FACE if level == 1 else 13
                    block = block[:layers] if offset == 1 else block[-layers:]
                    pieces.append(place((16, cols), (0, 0, block)))
                elif level == 3 and near:
                    pieces.append(block[:16])
                    pieces.append(place((16, cols), (FACE, 0, block[16:])))
                elif level == 3:
                    pieces.append(place((tall, cols), (0, 0, block)))
            tables.append(left3t(np.concatenate(pieces, axis=0)))
        return np.stack(tables)

    def finish(self):
        x, y, z = self.x, self.y, self.z
        rows = (y.length, self.rows1, self.rows2, self.rows3)
        exact = lambda m: np.asarray(m, dtype=jnp.bfloat16)

        def free(axis, level):
            inner = Axis(5, axis.length)
            return inner.prolong(level, 2)

        flat = []
        for level in (3, 2, 1):
            q = place((rows[level], rows[level - 1]), (0, 0, free(y, level).T))
            flat.append(exact(np.kron(free(x, level).T, q))[None])
        masks = []
        for level in (2, 1):
            table = np.zeros((x.count * y.count, 1, self.flat[level]), np.float32)
            for bx in range(x.count):
                for by in range(y.count):
                    inside = np.zeros(rows[level])
                    inside[: y.width[level]] = y.window(level, by)[1]
                    table[bx * y.count + by, 0] = np.kron(x.window(level, bx)[1], inside)
            masks.append(table)
        tall = []
        for level in (3, 2):
            tall.append(
                np.stack(
                    [place((self.tall[level - 1], self.tall[level]), (0, 0, z.prolong(level, b))) for b in range(z.count)]
                )
            )
        pieces = [(0, 0, free(z, 1).T), (self.tall[1], 0, np.eye(8)), (self.tall[1] + 8, z.length - 8, np.eye(8))]
        last = place((up(self.tall[1] + 16, 16), z.length), *pieces)
        return flat, masks, [exact(m) for m in tall], exact(last)[None]


def restrict_kernel(plan, place_ref, q_ref, z_ref, y_ref, own_ref, *rest):
    faces, mixed = rest[: plan.kinds], rest[plan.kinds]
    nx, ny, nz = plan.x.length, plan.y.length, plan.z.length
    high, low = split(q_ref[...].reshape(nx * ny, nz))
    along_z = dot(jnp.concatenate([high, low, high], axis=1), z_ref[0])
    high, low = split(along_z)
    high, low = high.reshape(nx, ny, LANES), low.reshape(nx, ny, LANES)
    for i in range(0, nx, 2):
        pair = [jnp.concatenate([high[j], high[j], low[j]], axis=0) for j in (i, i + 1)]
        both = dot(y_ref[0], jnp.concatenate(pair, axis=1))
        mixed[i] = both[:, :LANES]
        mixed[i + 1] = both[:, LANES:]

    brick = place_ref[0]
    keep_low = jnp.where(brick > 0, 1.0, 0.0).astype(F32)
    keep_high = jnp.where(brick < plan.x.count - 1, 1.0, 0.0).astype(F32)

    def coarsen(planes, level):
        size = nx >> level
        result = {}
        for i in range(LOW[level], LOW[level] + plan.x.width[level]):
            get = lambda j: planes.get(2 * i + j)
            total = None
            for offsets, weight in (((-3, 3), -0.0625), ((-1, 1), 0.5625), ((0,), 1.0)):
                terms = [get(j) for j in offsets if get(j) is not None]
                if terms:
                    term = functools.reduce(jnp.add, terms)
                    term = term * weight if weight != 1.0 else term
                    total = term if total is None else total + term
            if i < 0:
                total = total * keep_low
            elif i >= size:
                total = total * keep_high
            result[i] = total
        return result

    lanes = lax.broadcasted_iota(jnp.int32, (8, LANES), 1)
    in1, in2 = lanes < plan.lane[2], lanes < plan.lane[3]

    def tile(planes, level, k, row):
        index = LOW[level] + k
        return planes[row][index] if k < plan.x.width[level] else None

    def rows_of(start, count, depth):
        levels = [{i: mixed[i, start : start + count, :] for i in range(nx)}]
        for level in range(1, depth + 1):
            levels.append(coarsen(levels[-1], level))
        return levels[-1]

    zero = jnp.zeros((8, LANES), F32)
    first = {r: rows_of(r, 8, 1) for r in range(0, plan.rows1, 8)}
    second = {r: rows_of(plan.row[2] + r, 8, 2) for r in (0, 8)}
    third = {r: rows_of(plan.row[3] + r, 8, 3) for r in (0, 8)}
    face = [{r: rows_of(plan.row_face + 16 * f + r, 8, 1) for r in (0, 8)} for f in range(plan.kinds)]
    for k in range(plan.x.width[1]):
        for r in range(0, plan.rows1, 8):
            one = first[r][LOW[1] + k]
            two = second[r][LOW[2] + k] if r < 16 and k < plan.x.width[2] else zero
            three = third[r][LOW[3] + k] if r < 16 and k < plan.x.width[3] else zero
            rest_ = jnp.where(in2, two, three)
            own_ref[k, r : r + 8, :] = jnp.where(in1, one, rest_)
            if r < 16:
                for f in range(plan.kinds):
                    faces[f][k, r : r + 8, :] = jnp.where(in1, face[f][r][LOW[1] + k], rest_)


def extend_kernel(plan, own_ref, *refs):
    count = plan.y.count - 1
    halos, (ext_ref, high_ref, low_ref) = refs[:count], refs[count:]
    lanes = lax.broadcasted_iota(jnp.int32, (1, 1, LANES), 2)
    own = own_ref[...]
    if plan.overlay:
        halo = halos[0][...]
        ext = jnp.concatenate([own[:, :16], own[:, 16:24] + halo[:, 8:], halo[:, :8]], axis=1)
    else:
        parts = [own] + [h[...] for h in halos]
        pad = plan.coarse_rows - 24 - 16 * count
        if pad:
            parts.append(jnp.zeros((own.shape[0], pad, LANES), F32))
        ext = jnp.concatenate(parts, axis=1)
    ext_ref[...] = ext
    low_ref[...] = ext[: plan.planes]
    start = plan.x.width[1] - FACE
    for p in range(plan.planes):
        first = ext[start + min(p, FACE - 1)]
        high_ref[p] = jnp.where(lanes[0] < plan.lane[2], first, ext[p])


def mix_planes(get, put, count, matrix, rows):
    for i in range(0, count, 2):
        pair = [i, min(i + 1, count - 1)]
        stacked = []
        for j in pair:
            high, low = split(get(j))
            stacked.append(jnp.concatenate([high, high, low], axis=0))
        both = dot(matrix, jnp.concatenate(stacked, axis=1))
        put(i, both[:, :LANES])
        if pair[1] != i:
            put(pair[1], both[:, LANES:])


def stencil(planes, start, count, sigma):
    weights = [float(np.exp(-((k / sigma) ** 2))) for k in range(REACH + 1)]
    result = []
    for i in range(start, start + count):
        total = planes[i]
        for k in range(1, REACH + 1):
            total = total + (planes[i - k] + planes[i + k]) * weights[k]
        result.append(total)
    return result


def mix_kernel(plan, place_ref, q_ref, *refs):
    x, y, z = plan.x, plan.y, plan.z
    refs = list(refs)
    take = lambda n: [refs.pop(0) for _ in range(n)]
    halos = take(plan.fine_halos)
    before_ref, after_ref, ext_ref = take(3)
    coarse = take(x.count - 1)
    fine_y, coarse_y, top_x, fine_own, fine_push, z1, z2, z3 = take(8)
    main_ref, near_next, near_prev = take(3)
    far = take(z.count - 3)
    e1_ref, e2_ref, e3_ref = take(3)
    fine_mixed, fine_ready, coarse_mixed, ready1, ready2, ready3 = take(6)

    brick = place_ref[0]
    mask = lambda condition: jnp.where(condition, 1.0, 0.0).astype(F32)
    keep_before, keep_after = mask(brick > 0), mask(brick < x.count - 1)

    pad = up(plan.fine_rows, 16) - plan.fine_rows
    padding = [jnp.zeros((pad, LANES), F32)] if pad else []

    def fine_plane(i):
        if i < REACH:
            return jnp.concatenate([before_ref[i] * keep_before] + padding, axis=0)
        if i < REACH + x.length:
            j = i - REACH
            return jnp.concatenate([q_ref[j]] + [h[j] for h in halos] + padding, axis=0)
        return jnp.concatenate([after_ref[i - REACH - x.length] * keep_after] + padding, axis=0)

    def fine_put(i, value):
        fine_mixed[i] = value

    mix_planes(fine_plane, fine_put, x.length + 2 * REACH, fine_y[0], None)

    def put_ready(ready, sigmas, s, row, value):
        high, low = split(value)
        rows = slice(row, row + value.shape[0])
        step = LANES * sigmas
        ready[rows, s * LANES : (s + 1) * LANES] = high
        ready[rows, step + s * LANES : step + (s + 1) * LANES] = low
        ready[rows, 2 * step + s * LANES : 2 * step + (s + 1) * LANES] = high

    for s, sigma in enumerate(STENCIL_SIGMAS):
        for r in range(0, y.length, 16):
            row = s * y.length + r
            planes = [fine_mixed[i, row : row + 16, :] for i in range(x.length + 2 * REACH)]
            for i, value in enumerate(stencil(planes, REACH, x.length, sigma)):
                put_ready(fine_ready, 3, s, i * y.length + r, value)

    own_planes = x.width[1]

    def coarse_plane(i):
        if i < own_planes:
            return ext_ref[i]
        return coarse[(i - own_planes) // plan.planes][(i - own_planes) % plan.planes]

    def coarse_put(i, value):
        coarse_mixed[i] = value

    mix_planes(coarse_plane, coarse_put, own_planes + plan.planes * (x.count - 1), coarse_y[0], None)

    for level, ready in ((1, ready1), (2, ready2)):
        size = x.length >> level
        rows = plan.rows1 if level == 1 else plan.rows2
        width = x.width[level]
        for s, sigma in enumerate(STENCIL_SIGMAS):
            for r in range(0, rows, 8):
                row = plan.group[level] + s * rows + r
                at = lambda i: coarse_mixed[i, row : row + 8, :]
                cells = {LOW[level] + k: at(k) for k in range(width)}
                for offset in range(1, x.count):
                    base = own_planes + plan.planes * (offset - 1)
                    for shift, here in ((-offset, brick >= offset), (x.count - offset, brick < offset)):
                        kind = plan.face_kind(x, offset, 0)
                        if abs(shift) > level:
                            continue
                        first = (width - FACE) * kind if level == 1 else 0
                        layers = FACE if level == 1 else width
                        keep = mask(here)
                        for k in range(layers):
                            cell = shift * size + LOW[level] + first + k
                            if LOW[level] - REACH <= cell < LOW[level] + width + REACH:
                                value = at(base + k) * keep
                                cells[cell] = cells[cell] + value if cell in cells else value
                planes = [cells[LOW[level] - REACH + k] for k in range(width + 2 * REACH)]
                for i, value in enumerate(stencil(planes, REACH, width, sigma)):
                    put_ready(ready, 3, s, i * rows + r, value)

    width = x.width[3]
    for s in range(len(TOP_SIGMAS)):
        row = plan.group[3] + s * plan.rows3
        totals = [None] * width
        for offset in range(x.count):
            base = 0 if offset == 0 else own_planes + plan.planes * (offset - 1)
            for k in range(width):
                value = coarse_mixed[base + k, row : row + plan.rows3, :]
                for i in range(width):
                    weight = top_x[brick, ((s * width + i) * x.count + offset) * width + k]
                    term = value * weight
                    totals[i] = term if totals[i] is None else totals[i] + term
        for i in range(width):
            put_ready(ready3, 2, s, i * plan.rows3, totals[i])

    pushed = dot(fine_push[0], fine_ready[...], ((1,), (1,)))
    near = (near_next, near_prev)
    for n, ref in enumerate(near):
        ref[8:24, :] = jnp.zeros((16, ref.shape[1]), F32)
        ref[:8, :] = pushed[8 * n : 8 * n + 8]
    one = dot(z1[0], ready1[...], ((1,), (1,)))
    two = dot(z2[0], ready2[...], ((1,), (1,)))
    three = dot(z3[0], ready3[...], ((1,), (1,)))
    e1_ref[...] = one[: plan.tall[1]]
    e2_ref[...] = two[: plan.tall[2]]
    e3_ref[...] = three[: plan.tall[3]]
    top = plan.tall[3]
    far_index = 0
    for offset in range(1, z.count):
        if offset in (1, z.count - 1):
            n = 0 if offset == 1 else 1
            ref = near[n]
            start = plan.tall[1] + 16 * n
            ref[8:24, : plan.flat[1]] = one[start : start + 16]
            ref[8:24, : plan.flat[3]] += three[top + 16 : top + 32]
            start = plan.tall[2] + 16 * n
            ref[8:24, 512 : 512 + plan.flat[2]] = two[start : start + 16]
            ref[8:24, 768 : 768 + plan.flat[3]] = three[top : top + 16]
            top += 32
        else:
            far[far_index][...] = three[top : top + plan.tall[3]]
            far_index += 1
            top += plan.tall[3]
    main_ref[...] = dot(fine_ready[...], fine_own[0])


def finish_kernel(plan, place_ref, main_ref, e1_ref, e2_ref, e3_ref, prev_ref, next_ref, *refs):
    z = plan.z
    refs = list(refs)
    far = [refs.pop(0) for _ in range(z.count - 3)]
    flat3, flat2, flat1, mask2, mask1, tall3, tall2, last, out_ref, e1, e2, e3 = refs
    e1[...], e2[...], e3[...] = e1_ref[...], e2_ref[...], e3_ref[...]
    for f in far:
        e3[...] += f[...]
    for n, ref in enumerate((prev_ref, next_ref)):
        e3[:16, :] += ref[8:24, 768 : 768 + plan.flat[3]]
        e3[16 : z.width[3], :] += ref[8 + FACE : 8 + FACE + z.width[3] - 16, : plan.flat[3]]
        start = 0 if n == 0 else plan.tall[2] - 16
        e2[start : start + 16, :] += ref[8:24, 512 : 512 + plan.flat[2]]
        start = 0 if n == 0 else z.width[1] - FACE
        e1[start : start + FACE, :] += ref[8 : 8 + FACE, : plan.flat[1]]

    def across(value, matrix):
        high, low = split(value)
        both = dot(jnp.concatenate([high, low], axis=0), matrix)
        return both[: value.shape[0]] + both[value.shape[0] :]

    def along(matrix, value):
        high, low = split(value)
        return dot(matrix, high) + dot(matrix, low)

    two = (e2[...] + along(tall3[0], across(e3[...], flat3[0]))) * mask2[0]
    one = (e1[...] + along(tall2[0], across(two, flat2[0]))) * mask1[0]
    spread = across(one, flat1[0])
    rows = jnp.concatenate([spread, prev_ref[:8, :], next_ref[:8, :]], axis=0)
    pad = last.shape[1] - rows.shape[0]
    if pad:
        rows = jnp.concatenate([rows, jnp.zeros((pad, rows.shape[1]), F32)], axis=0)
    high, low = split(rows)
    stacked = jnp.concatenate([high, low], axis=0)
    matrix = jnp.concatenate([last[0], last[0]], axis=0)
    out_ref[...] = main_ref[...] + dot(stacked, matrix, ((0,), (0,)))


def call(kernel, plan, place_at, operands, tables, outs, scratch=(), smem=()):
    whole = lambda a: pl.BlockSpec(a.shape, lambda i, at, n=a.ndim: (0,) * n)
    specs = [whole(a) for a in operands]
    arrays = list(operands)
    for table, index in tables:
        arrays.append(jnp.asarray(table))
        if index is None:
            specs.append(pl.BlockSpec(memory_space=pltpu.SMEM))
        elif index < 0:
            specs.append(whole(table))
        else:
            specs.append(
                pl.BlockSpec((1,) + table.shape[1:], lambda i, at, k=index, n=table.ndim: (at[k],) + (0,) * (n - 1))
            )
    return pl.pallas_call(
        functools.partial(kernel, plan),
        grid_spec=pltpu.PrefetchScalarGridSpec(
            num_scalar_prefetch=1,
            grid=(1,),
            in_specs=specs,
            out_specs=[whole(o) for o in outs],
            scratch_shapes=list(scratch),
        ),
        out_shape=list(outs),
        compiler_params=pltpu.CompilerParams(vmem_limit_bytes=48 * 2**20),
    )(place_at, *arrays)


def shift(value, axis, offset):
    count = lax.axis_size(axis)
    return lax.ppermute(value, axis, [(i, (i + offset) % count) for i in range(count)])


def shards(plan, charges):
    x, y, z = plan.x, plan.y, plan.z
    array = lambda *shape: jax.ShapeDtypeStruct(shape, F32)
    at = [lax.axis_index(name) for name in ("gx", "gy", "gz")]
    place_at = jnp.stack(at + [at[0] * y.count + at[1]]).astype(jnp.int32)

    faces = charges[:, : REACH], charges[:, y.length - REACH :]
    if y.count == 2:
        fine_y = [shift(jnp.where(at[1] == 0, faces[1], faces[0]), "gy", 1)]
    else:
        fine_y = [shift(faces[1], "gy", 1), shift(faces[0], "gy", y.count - 1)]
    own, *coarse_faces = call(
        restrict_kernel,
        plan,
        place_at,
        [charges],
        [(plan.restrict_z(), 2), (plan.restrict_y(), 1)],
        [array(x.width[1], plan.rows1, LANES)] + [array(x.width[1], 16, LANES)] * plan.kinds,
        [pltpu.VMEM((x.length, plan.rows_restricted, LANES), F32)],
    )
    coarse_halos = [shift(coarse_faces[0 if r == 1 else -1], "gy", r) for r in range(1, y.count)]

    fine_x = [
        shift(jnp.concatenate([charges[-REACH:]] + [f[-REACH:] for f in fine_y], axis=1), "gx", 1),
        shift(jnp.concatenate([charges[:REACH]] + [f[:REACH] for f in fine_y], axis=1), "gx", x.count - 1),
    ]
    extended = [array(n, plan.coarse_rows, LANES) for n in (x.width[1], plan.planes, plan.planes)]
    ext, high, low = pl.pallas_call(functools.partial(extend_kernel, plan), out_shape=extended)(own, *coarse_halos)
    coarse_x = [shift(high if r == 1 else low, "gx", r) for r in range(1, x.count)]

    fine_own, fine_push = plan.fine_z()
    zs = [plan.coarse_z(level) for level in (1, 2, 3)]
    cells = x.length * y.length
    ready = lambda rows, sigmas: pltpu.VMEM((rows, 3 * sigmas * LANES), BF)
    results = call(
        mix_kernel,
        plan,
        place_at,
        [charges] + fine_y + fine_x + [ext] + coarse_x,
        [
            (plan.fine_y(), 1),
            (plan.coarse_y(), 1),
            (plan.top_x(), None),
            (fine_own, 2),
            (fine_push, 2),
            (zs[0], 2),
            (zs[1], 2),
            (zs[2], 2),
        ],
        [array(cells, LANES), array(24, cells), array(24, cells)]
        + [array(plan.tall[3], plan.flat[3])] * (z.count - 3)
        + [array(plan.tall[l], plan.flat[l]) for l in (1, 2, 3)],
        [
            pltpu.VMEM((x.length + 2 * REACH, 3 * y.length, LANES), F32),
            ready(cells, 3),
            pltpu.VMEM((x.width[1] + plan.planes * (x.count - 1), plan.rows_mixed, LANES), F32),
            ready(plan.flat[1], 3),
            ready(plan.flat[2], 3),
            ready(plan.flat[3], 2),
        ],
    )
    main, near_next, near_prev = results[:3]
    far, windows = results[3 : z.count], results[z.count :]
    from_prev = shift(near_next, "gz", 1)
    from_next = shift(near_prev, "gz", z.count - 1)
    from_far = [shift(f, "gz", r) for f, r in zip(far, range(2, z.count - 1))]
    flat, masks, tall, last = plan.finish()
    (potential,) = call(
        finish_kernel,
        plan,
        place_at,
        [main, *windows, from_prev, from_next, *from_far],
        [(m, -1) for m in flat] + [(m, 3) for m in masks] + [(m, 2) for m in tall] + [(last, -1)],
        [array(cells, LANES)],
        [pltpu.VMEM((plan.tall[l], plan.flat[l]), F32) for l in (1, 2, 3)],
    )
    return potential.reshape(charges.shape)


def solution(mesh):
    counts = [mesh.shape[name] for name in ("gx", "gy", "gz")]

    def run(charges):
        plan = Plan(counts, [size // n for size, n in zip(charges.shape, counts)])
        placed = P("gx", "gy", "gz")
        return jax.shard_map(
            functools.partial(shards, plan), mesh=mesh, in_specs=(placed,), out_specs=placed, check_vma=False
        )(charges)

    return run
```

```python
import functools

import jax
import jax.numpy as jnp
import numpy as np
from jax import lax
from jax.experimental import pallas as pl
from jax.experimental.pallas import tpu as pltpu
from jax.sharding import PartitionSpec as P

REACH = 8
STENCIL_SIGMAS = (1.0, 2.0, 3.5)
STENCIL_WEIGHTS = (0.4, 0.1, 0.03)
TOP_SIGMAS = (1.5, 4.0)
TOP_WEIGHTS = (0.03, 0.006)
SPLINE_TAPS = np.array((-1.0, 0.0, 9.0, 16.0, 9.0, 0.0, -1.0)) / 16.0

LOW = (0, -1, -2, -2)
EXTRA = (0, 3, 5, 5)
FACE = 11
LANES = 128
BF = jnp.bfloat16
F32 = jnp.float32


def up(value, unit):
    return -(-value // unit) * unit


def band(rows, cols, sigma, reach):
    distance = cols[None, :] - rows[:, None]
    return np.where(abs(distance) <= reach, np.exp(-((distance / sigma) ** 2)), 0.0)


def restriction(size):
    position = np.arange(size)[None, :] - 2 * np.arange(size // 2)[:, None] + 3
    inside = (position >= 0) & (position <= 6)
    return np.where(inside, SPLINE_TAPS[np.clip(position, 0, 6)], 0.0)


class Axis:
    def __init__(self, count, length):
        self.count, self.length = count, length
        self.width = [(length >> level) + EXTRA[level] for level in range(4)]

    def window(self, level, brick):
        size = self.length >> level
        cells = brick * size + LOW[level] + np.arange(self.width[level])
        return cells, ((cells >= 0) & (cells < self.count * size)).astype(float)

    def partial(self, level, brick):
        matrix = np.eye(self.count * self.length)
        for _ in range(level):
            matrix = restriction(matrix.shape[0]) @ matrix
        cells, inside = self.window(level, brick)
        rows = matrix[np.clip(cells, 0, len(matrix) - 1)] * inside[:, None]
        return rows[:, brick * self.length : (brick + 1) * self.length]

    def prolong(self, level, brick):
        matrix = restriction((self.count * self.length) >> (level - 1)).T
        rows, row_inside = self.window(level - 1, brick)
        cols, col_inside = self.window(level, brick)
        taken = matrix[np.clip(rows, 0, len(matrix) - 1)][:, np.clip(cols, 0, matrix.shape[1] - 1)]
        return taken * row_inside[:, None] * col_inside[None, :]

    def mix(self, level, sigma, target, source):
        rows, row_inside = self.window(level, target)
        cols, col_inside = self.window(level, source)
        reach = REACH if level < 3 else self.count * self.length
        return band(rows, cols, sigma, reach) * row_inside[:, None] * col_inside[None, :]


def place(shape, *pieces):
    whole = np.zeros(shape)
    for row, col, block in pieces:
        whole[row : row + block.shape[0], col : col + block.shape[1]] += block
    return whole


def halves(matrix):
    high = matrix.astype(jnp.bfloat16)
    low = (matrix - high.astype(np.float64)).astype(jnp.bfloat16)
    return high, low


def left3(matrix):
    high, low = halves(matrix)
    return np.concatenate([high, low, high], axis=-1)


def left3t(matrix):
    high, low = halves(matrix)
    return np.concatenate([high, high, low], axis=-1)


def right3(matrix):
    high, low = halves(matrix)
    return np.concatenate([high, high, low], axis=-2)


def split(value):
    high = value.astype(BF)
    return high, (value - high.astype(F32)).astype(BF)


def dot(left, right, dims=((1,), (0,))):
    return lax.dot_general(left, right, (dims, ((), ())), preferred_element_type=F32)


class Plan:
    def __init__(self, counts, lengths):
        self.x, self.y, self.z = (Axis(n, length) for n, length in zip(counts, lengths))
        x, y, z = self.x, self.y, self.z
        assert x.count >= 3 and z.count >= 3
        self.lane = [0, 0, z.width[1], z.width[1] + z.width[2]]
        self.lane_end = self.lane[3] + z.width[3]
        assert self.lane_end <= LANES and z.length == LANES
        self.rows1, self.rows2, self.rows3 = up(y.width[1], 8), up(y.width[2], 16), up(y.width[3], 16)
        assert self.rows2 <= 16 and self.rows3 <= 16 and FACE <= 14 and self.rows1 == 24
        self.row = [0, 0, self.rows1, self.rows1 + self.rows2]
        self.row_face = self.rows1 + self.rows2 + self.rows3
        self.kinds = 1 if y.count == 2 else 2
        self.rows_restricted = self.row_face + 16 * self.kinds
        self.overlay = y.count == 2 and y.width[1] + 3 <= self.rows1
        self.coarse_rows = up(24 + 16 * (y.count - 1), 16) if not self.overlay else 32
        self.fine_halos = 1 if y.count == 2 else 2
        self.fine_rows = y.length + 8 * self.fine_halos
        self.planes = max(FACE, x.width[2], x.width[3])
        assert self.planes <= x.width[1]
        self.group = [0, 0, 3 * self.rows1, 3 * self.rows1 + 3 * self.rows2]
        self.rows_mixed = self.group[3] + 2 * self.rows3
        self.tall = [0, up(z.width[1], 8), up(z.width[2], 8), up(z.width[3], 8)]
        assert self.tall[1] - 16 == z.width[1] - FACE and self.tall[2] - 16 == z.width[2] - 13
        self.flat = [0, x.width[1] * self.rows1, x.width[2] * self.rows2, x.width[3] * self.rows3]
        assert self.flat[1] <= 512 and self.flat[2] <= 256 and self.flat[3] <= 256

    def face_kind(self, axis, offset, source):
        if axis.count == 2:
            return 1 - source
        return 1 if offset == 1 else 0

    def face_row(self, j):
        return j if j < 8 or not self.overlay else j + 3

    def restrict_z(self):
        z = self.z
        return np.stack(
            [
                right3(place((z.length, LANES), *[(0, self.lane[l], z.partial(l, b).T) for l in (1, 2, 3)]))
                for b in range(z.count)
            ]
        )

    def restrict_y(self):
        y, tables = self.y, []
        for b in range(y.count):
            pieces = [(self.row[l], 0, y.partial(l, b)) for l in (1, 2, 3)]
            first = y.partial(1, b)
            for k in range(self.kinds):
                kind = self.face_kind(y, 1, b) if self.kinds == 1 else 1 - k
                start = (y.width[1] - FACE) * kind
                for j in range(FACE):
                    pieces.append((self.row_face + 16 * k + self.face_row(j), 0, first[start + j][None]))
            tables.append(left3(place((self.rows_restricted, y.length), *pieces)))
        return np.stack(tables)

    def fine_y(self):
        y, tables = self.y, []
        for b in range(y.count):
            pieces = []
            for s, sigma in enumerate(STENCIL_SIGMAS):
                row = s * y.length
                pieces.append((row, 0, y.mix(0, sigma, b, b)))
                for h in range(self.fine_halos):
                    offset = 1 if h == 0 else y.count - 1
                    source = (b - offset) % y.count
                    start = (y.length - REACH) * self.face_kind(y, offset, source)
                    block = y.mix(0, sigma, b, source)[:, start : start + REACH]
                    pieces.append((row, y.length + 8 * h, block))
            tables.append(left3(place((3 * y.length, up(self.fine_rows, 16)), *pieces)))
        return np.stack(tables)

    def coarse_y(self):
        y, tables = self.y, []
        for b in range(y.count):
            whole = np.zeros((self.rows_mixed, self.coarse_rows))
            for level in (1, 2, 3):
                sigmas = STENCIL_SIGMAS if level < 3 else TOP_SIGMAS
                rows = (0, self.rows1, self.rows2, self.rows3)[level]
                for s, sigma in enumerate(sigmas):
                    top = self.group[level] + s * rows
                    for offset in range(y.count):
                        source = (b - offset) % y.count
                        block = y.mix(level, sigma, b, source)
                        if level == 1 and offset:
                            start = (y.width[1] - FACE) * self.face_kind(y, offset, source)
                            block = block[:, start : start + FACE]
                        for j in range(block.shape[1]):
                            slot = self.face_row(j) if level == 1 and offset else j
                            if self.overlay and offset:
                                slot = 24 + slot if slot < 8 else 8 + slot
                            elif offset:
                                slot = 24 + 16 * (offset - 1) + slot
                            whole[top : top + y.width[level], slot] += block[:, j]
            tables.append(left3(whole))
        return np.stack(tables)

    def fine_z(self):
        z, own, pushed = self.z, [], []
        for b in range(z.count):
            mixes = lambda target: [
                w * z.mix(0, sigma, target, b) for sigma, w in zip(STENCIL_SIGMAS, STENCIL_WEIGHTS)
            ]
            own.append(right3(np.concatenate([m.T for m in mixes(b)], axis=0)))
            rows = [np.concatenate([m[:8] for m in mixes((b + 1) % z.count)], axis=1)]
            rows.append(np.concatenate([m[-8:] for m in mixes((b - 1) % z.count)], axis=1))
            pushed.append(left3t(np.concatenate(rows, axis=0)))
        return np.stack(own), np.stack(pushed)

    def coarse_z(self, level):
        z, tables = self.z, []
        sigmas, weights = (STENCIL_SIGMAS, STENCIL_WEIGHTS) if level < 3 else (TOP_SIGMAS, TOP_WEIGHTS)
        factor = 0.5**level if level < 3 else 1.0
        for b in range(z.count):

            def mixed(target):
                blocks = [
                    place((z.width[level], LANES), (0, self.lane[level], factor * w * z.mix(level, sigma, target, b)))
                    for sigma, w in zip(sigmas, weights)
                ]
                return np.concatenate(blocks, axis=1)

            cols = LANES * len(sigmas)
            tall = self.tall[level]
            pieces = [place((tall, cols), (0, 0, mixed(b)))]
            for offset in range(1, z.count):
                block = mixed((b + offset) % z.count)
                near = offset in (1, z.count - 1)
                if level < 3 and near:
                    layers = FACE if level == 1 else 13
                    block = block[:layers] if offset == 1 else block[-layers:]
                    pieces.append(place((16, cols), (0, 0, block)))
                elif level == 3 and near:
                    pieces.append(block[:16])
                    pieces.append(place((16, cols), (FACE, 0, block[16:])))
                elif level == 3:
                    pieces.append(place((tall, cols), (0, 0, block)))
            tables.append(left3t(np.concatenate(pieces, axis=0)))
        return np.stack(tables)

    def finish(self):
        x, y, z = self.x, self.y, self.z
        rows = (y.length, self.rows1, self.rows2, self.rows3)
        exact = lambda m: np.asarray(m, dtype=jnp.bfloat16)

        def free(axis, level):
            inner = Axis(5, axis.length)
            return inner.prolong(level, 2)

        flat = []
        for level in (3, 2, 1):
            q = place((rows[level], rows[level - 1]), (0, 0, free(y, level).T))
            flat.append(exact(np.kron(free(x, level).T, q)))
        masks = []
        for level in (3, 2, 1):
            table = np.zeros((x.count * y.count, 1, self.flat[level]), np.float32)
            for bx in range(x.count):
                for by in range(y.count):
                    inside = np.zeros(rows[level])
                    inside[: y.width[level]] = y.window(level, by)[1]
                    table[bx * y.count + by, 0] = np.kron(x.window(level, bx)[1], inside)
            masks.append(table)
        tall = []
        for level in (3, 2):
            tall.append(
                np.stack(
                    [place((self.tall[level - 1], self.tall[level]), (0, 0, z.prolong(level, b))) for b in range(z.count)]
                )
            )
        pieces = [(0, 0, free(z, 1).T), (self.tall[1], 0, np.eye(8)), (self.tall[1] + 8, z.length - 8, np.eye(8))]
        last = place((up(self.tall[1] + 16, 16), z.length), *pieces)
        return flat, masks, [exact(m) for m in tall], exact(last)


def restrict_kernel(plan, q_ref, z_ref, y_ref, own_ref, *rest):
    faces, mixed = rest[: plan.kinds], rest[plan.kinds]
    nx, ny, nz = plan.x.length, plan.y.length, plan.z.length
    high, low = split(q_ref[...].reshape(nx * ny, nz))
    along_z = dot(jnp.concatenate([high, low, high], axis=1), z_ref[lax.axis_index("gz")])
    high, low = split(along_z)
    high, low = high.reshape(nx, ny, LANES), low.reshape(nx, ny, LANES)
    matrix_y = y_ref[lax.axis_index("gy")]
    for i in range(0, nx, 2):
        pair = [jnp.concatenate([high[j], high[j], low[j]], axis=0) for j in (i, i + 1)]
        both = dot(matrix_y, jnp.concatenate(pair, axis=1))
        mixed[i] = both[:, :LANES]
        mixed[i + 1] = both[:, LANES:]

    brick = lax.axis_index("gx")
    keep_low = jnp.where(brick > 0, 1.0, 0.0).astype(F32)
    keep_high = jnp.where(brick < plan.x.count - 1, 1.0, 0.0).astype(F32)

    def coarsen(planes, level):
        size = nx >> level
        result = {}
        for i in range(LOW[level], LOW[level] + plan.x.width[level]):
            get = lambda j: planes.get(2 * i + j)
            total = None
            for offsets, weight in (((-3, 3), -0.0625), ((-1, 1), 0.5625), ((0,), 1.0)):
                terms = [get(j) for j in offsets if get(j) is not None]
                if terms:
                    term = functools.reduce(jnp.add, terms)
                    term = term * weight if weight != 1.0 else term
                    total = term if total is None else total + term
            if i < 0:
                total = total * keep_low
            elif i >= size:
                total = total * keep_high
            result[i] = total
        return result

    lanes = lax.broadcasted_iota(jnp.int32, (8, LANES), 1)
    in1, in2 = lanes < plan.lane[2], lanes < plan.lane[3]

    def tile(planes, level, k, row):
        index = LOW[level] + k
        return planes[row][index] if k < plan.x.width[level] else None

    def rows_of(start, count, depth):
        levels = [{i: mixed[i, start : start + count, :] for i in range(nx)}]
        for level in range(1, depth + 1):
            levels.append(coarsen(levels[-1], level))
        return levels[-1]

    zero = jnp.zeros((8, LANES), F32)
    first = {r: rows_of(r, 8, 1) for r in range(0, plan.rows1, 8)}
    second = {r: rows_of(plan.row[2] + r, 8, 2) for r in (0, 8)}
    third = {r: rows_of(plan.row[3] + r, 8, 3) for r in (0, 8)}
    face = [{r: rows_of(plan.row_face + 16 * f + r, 8, 1) for r in (0, 8)} for f in range(plan.kinds)]
    for k in range(plan.x.width[1]):
        for r in range(0, plan.rows1, 8):
            one = first[r][LOW[1] + k]
            two = second[r][LOW[2] + k] if r < 16 and k < plan.x.width[2] else zero
            three = third[r][LOW[3] + k] if r < 16 and k < plan.x.width[3] else zero
            rest_ = jnp.where(in2, two, three)
            own_ref[k, r : r + 8, :] = jnp.where(in1, one, rest_)
            if r < 16:
                for f in range(plan.kinds):
                    faces[f][k, r : r + 8, :] = jnp.where(in1, face[f][r][LOW[1] + k], rest_)


def extend_kernel(plan, own_ref, *refs):
    count = plan.y.count - 1
    halos, (ext_ref, high_ref, low_ref) = refs[:count], refs[count:]
    lanes = lax.broadcasted_iota(jnp.int32, (1, 1, LANES), 2)
    own = own_ref[...]
    if plan.overlay:
        halo = halos[0][...]
        ext = jnp.concatenate([own[:, :16], own[:, 16:24] + halo[:, 8:], halo[:, :8]], axis=1)
    else:
        parts = [own] + [h[...] for h in halos]
        pad = plan.coarse_rows - 24 - 16 * count
        if pad:
            parts.append(jnp.zeros((own.shape[0], pad, LANES), F32))
        ext = jnp.concatenate(parts, axis=1)
    ext_ref[...] = ext
    low_ref[...] = ext[: plan.planes]
    start = plan.x.width[1] - FACE
    for p in range(plan.planes):
        first = ext[start + min(p, FACE - 1)]
        high_ref[p] = jnp.where(lanes[0] < plan.lane[2], first, ext[p])


def mix_planes(get, put, count, matrix):
    for i in range(0, count, 2):
        pair = [i, min(i + 1, count - 1)]
        stacked = []
        for j in pair:
            high, low = split(get(j))
            stacked.append(jnp.concatenate([high, high, low], axis=0))
        both = dot(matrix, jnp.concatenate(stacked, axis=1))
        put(i, both[:, :LANES])
        if pair[1] != i:
            put(pair[1], both[:, LANES:])


def stencil(planes, start, count, sigma):
    weights = [float(np.exp(-((k / sigma) ** 2))) for k in range(REACH + 1)]
    result = []
    for i in range(start, start + count):
        total = planes[i]
        for k in range(1, REACH + 1):
            total = total + (planes[i - k] + planes[i + k]) * weights[k]
        result.append(total)
    return result


def mix_kernel(plan, q_ref, *refs):
    x, y, z = plan.x, plan.y, plan.z
    refs = list(refs)
    take = lambda n: [refs.pop(0) for _ in range(n)]
    halos = take(plan.fine_halos)
    before_ref, after_ref, ext_ref = take(3)
    coarse = take(x.count - 1)
    fine_y, coarse_y, fine_own, fine_push, z1, z2, z3 = take(7)
    main_ref, near_next, near_prev = take(3)
    far = take(z.count - 3)
    e1_ref, e2_ref, e3_ref = take(3)
    fine_mixed, fine_ready, coarse_mixed, ready1, ready2, ready3 = take(6)

    brick = lax.axis_index("gx")
    by, bz = lax.axis_index("gy"), lax.axis_index("gz")
    mask = lambda condition: jnp.where(condition, 1.0, 0.0).astype(F32)
    keep_before, keep_after = mask(brick > 0), mask(brick < x.count - 1)

    pad = up(plan.fine_rows, 16) - plan.fine_rows
    padding = [jnp.zeros((pad, LANES), F32)] if pad else []

    def fine_plane(i):
        if i < REACH:
            return jnp.concatenate([before_ref[i] * keep_before] + padding, axis=0)
        if i < REACH + x.length:
            j = i - REACH
            return jnp.concatenate([q_ref[j]] + [h[j] for h in halos] + padding, axis=0)
        return jnp.concatenate([after_ref[i - REACH - x.length] * keep_after] + padding, axis=0)

    def fine_put(i, value):
        fine_mixed[i] = value

    mix_planes(fine_plane, fine_put, x.length + 2 * REACH, fine_y[by])

    def put_ready(ready, sigmas, s, row, value):
        high, low = split(value)
        rows = slice(row, row + value.shape[0])
        step = LANES * sigmas
        ready[rows, s * LANES : (s + 1) * LANES] = high
        ready[rows, step + s * LANES : step + (s + 1) * LANES] = low
        ready[rows, 2 * step + s * LANES : 2 * step + (s + 1) * LANES] = high

    for s, sigma in enumerate(STENCIL_SIGMAS):
        for r in range(0, y.length, 16):
            row = s * y.length + r
            planes = [fine_mixed[i, row : row + 16, :] for i in range(x.length + 2 * REACH)]
            for i, value in enumerate(stencil(planes, REACH, x.length, sigma)):
                put_ready(fine_ready, 3, s, i * y.length + r, value)

    own_planes = x.width[1]

    def coarse_plane(i):
        if i < own_planes:
            return ext_ref[i]
        return coarse[(i - own_planes) // plan.planes][(i - own_planes) % plan.planes]

    def coarse_put(i, value):
        coarse_mixed[i] = value

    mix_planes(coarse_plane, coarse_put, own_planes + plan.planes * (x.count - 1), coarse_y[by])

    for level, ready in ((1, ready1), (2, ready2)):
        size = x.length >> level
        rows = plan.rows1 if level == 1 else plan.rows2
        width = x.width[level]
        for s, sigma in enumerate(STENCIL_SIGMAS):
            for r in range(0, rows, 8):
                row = plan.group[level] + s * rows + r
                at = lambda i: coarse_mixed[i, row : row + 8, :]
                cells = {LOW[level] + k: at(k) for k in range(width)}
                for offset in range(1, x.count):
                    base = own_planes + plan.planes * (offset - 1)
                    for shift, here in ((-offset, brick >= offset), (x.count - offset, brick < offset)):
                        kind = plan.face_kind(x, offset, 0)
                        if abs(shift) > level:
                            continue
                        first = (width - FACE) * kind if level == 1 else 0
                        layers = FACE if level == 1 else width
                        keep = mask(here)
                        for k in range(layers):
                            cell = shift * size + LOW[level] + first + k
                            if LOW[level] - REACH <= cell < LOW[level] + width + REACH:
                                value = at(base + k) * keep
                                cells[cell] = cells[cell] + value if cell in cells else value
                planes = [cells[LOW[level] - REACH + k] for k in range(width + 2 * REACH)]
                for i, value in enumerate(stencil(planes, REACH, width, sigma)):
                    put_ready(ready, 3, s, i * rows + r, value)

    width, size = x.width[3], x.length >> 3
    for s, sigma in enumerate(TOP_SIGMAS):
        row = plan.group[3] + s * plan.rows3
        at = lambda i: coarse_mixed[i, row : row + plan.rows3, :]
        cells = {LOW[3] + k: at(k) for k in range(width)}
        for offset in range(1, x.count):
            base = own_planes + plan.planes * (offset - 1)
            for shift, here in ((-offset, brick >= offset), (x.count - offset, brick < offset)):
                keep = mask(here)
                for k in range(width):
                    cell, value = shift * size + LOW[3] + k, at(base + k) * keep
                    cells[cell] = cells[cell] + value if cell in cells else value
        for i in range(width):
            terms = [v * float(np.exp(-(((c - LOW[3] - i) / sigma) ** 2))) for c, v in cells.items()]
            put_ready(ready3, 2, s, i * plan.rows3, functools.reduce(jnp.add, terms))

    pushed = dot(fine_push[bz], fine_ready[...], ((1,), (1,)))
    near = (near_next, near_prev)
    for n, ref in enumerate(near):
        ref[8:24, :] = jnp.zeros((16, ref.shape[1]), F32)
        ref[:8, :] = pushed[8 * n : 8 * n + 8]
    one = dot(z1[bz], ready1[...], ((1,), (1,)))
    two = dot(z2[bz], ready2[...], ((1,), (1,)))
    three = dot(z3[bz], ready3[...], ((1,), (1,)))
    e1_ref[...] = one[: plan.tall[1]]
    e2_ref[...] = two[: plan.tall[2]]
    e3_ref[...] = three[: plan.tall[3]]
    top = plan.tall[3]
    far_index = 0
    for offset in range(1, z.count):
        if offset in (1, z.count - 1):
            n = 0 if offset == 1 else 1
            ref = near[n]
            start = plan.tall[1] + 16 * n
            ref[8:24, : plan.flat[1]] = one[start : start + 16]
            ref[8:24, : plan.flat[3]] += three[top + 16 : top + 32]
            start = plan.tall[2] + 16 * n
            ref[8:24, 512 : 512 + plan.flat[2]] = two[start : start + 16]
            ref[8:24, 768 : 768 + plan.flat[3]] = three[top : top + 16]
            top += 32
        else:
            far[far_index][...] = three[top : top + plan.tall[3]]
            far_index += 1
            top += plan.tall[3]
    main_ref[...] = dot(fine_ready[...], fine_own[bz])


def finish_kernel(plan, main_ref, e1_ref, e2_ref, e3_ref, prev_ref, next_ref, *refs):
    z = plan.z
    refs = list(refs)
    far = [refs.pop(0) for _ in range(z.count - 3)]
    flat3, flat2, flat1, mask3, mask2, mask1, tall3, tall2, last, out_ref, e1, e2, e3 = refs
    bz = lax.axis_index("gz")
    column = lax.axis_index("gx") * plan.y.count + lax.axis_index("gy")
    e1[...], e2[...], e3[...] = e1_ref[...], e2_ref[...], e3_ref[...]
    for f in far:
        e3[...] += f[...]
    for n, ref in enumerate((prev_ref, next_ref)):
        e3[:16, :] += ref[8:24, 768 : 768 + plan.flat[3]]
        e3[16 : z.width[3], :] += ref[8 + FACE : 8 + FACE + z.width[3] - 16, : plan.flat[3]]
        start = 0 if n == 0 else plan.tall[2] - 16
        e2[start : start + 16, :] += ref[8:24, 512 : 512 + plan.flat[2]]
        start = 0 if n == 0 else z.width[1] - FACE
        e1[start : start + FACE, :] += ref[8 : 8 + FACE, : plan.flat[1]]

    def across(value, matrix):
        high, low = split(value)
        both = dot(jnp.concatenate([high, low], axis=0), matrix)
        return both[: value.shape[0]] + both[value.shape[0] :]

    def along(matrix, value):
        high, low = split(value)
        return dot(matrix, high) + dot(matrix, low)

    three = e3[...] * mask3[column]
    two = (e2[...] + along(tall3[bz], across(three, flat3[...]))) * mask2[column]
    one = (e1[...] + along(tall2[bz], across(two, flat2[...]))) * mask1[column]
    spread = across(one, flat1[...])
    rows = jnp.concatenate([spread, prev_ref[:8, :], next_ref[:8, :]], axis=0)
    pad = last.shape[0] - rows.shape[0]
    if pad:
        rows = jnp.concatenate([rows, jnp.zeros((pad, rows.shape[1]), F32)], axis=0)
    high, low = split(rows)
    stacked = jnp.concatenate([high, low], axis=0)
    matrix = jnp.concatenate([last[...], last[...]], axis=0)
    out_ref[...] = main_ref[...] + dot(stacked, matrix, ((0,), (0,)))


def call(kernel, plan, operands, outs, scratch=()):
    whole = pl.BlockSpec(memory_space=pltpu.VMEM)
    return pl.pallas_call(
        functools.partial(kernel, plan),
        in_specs=[whole] * len(operands),
        out_specs=[whole] * len(outs),
        scratch_shapes=list(scratch),
        out_shape=list(outs),
        compiler_params=pltpu.CompilerParams(vmem_limit_bytes=48 * 2**20),
    )(*[jnp.asarray(o) for o in operands])


def shift(value, axis, offset):
    count = lax.axis_size(axis)
    return lax.ppermute(value, axis, [(i, (i + offset) % count) for i in range(count)])


def shards(plan, charges):
    x, y, z = plan.x, plan.y, plan.z
    array = lambda *shape: jax.ShapeDtypeStruct(shape, F32)
    at_y = lax.axis_index("gy")

    faces = charges[:, : REACH], charges[:, y.length - REACH :]
    if y.count == 2:
        fine_y = [shift(jnp.where(at_y == 0, faces[1], faces[0]), "gy", 1)]
    else:
        fine_y = [shift(faces[1], "gy", 1), shift(faces[0], "gy", y.count - 1)]
    own, *coarse_faces = call(
        restrict_kernel,
        plan,
        [charges, plan.restrict_z(), plan.restrict_y()],
        [array(x.width[1], plan.rows1, LANES)] + [array(x.width[1], 16, LANES)] * plan.kinds,
        [pltpu.VMEM((x.length, plan.rows_restricted, LANES), F32)],
    )
    coarse_halos = [shift(coarse_faces[0 if r == 1 else -1], "gy", r) for r in range(1, y.count)]

    fine_x = [
        shift(jnp.concatenate([charges[-REACH:]] + [f[-REACH:] for f in fine_y], axis=1), "gx", 1),
        shift(jnp.concatenate([charges[:REACH]] + [f[:REACH] for f in fine_y], axis=1), "gx", x.count - 1),
    ]
    extended = [array(n, plan.coarse_rows, LANES) for n in (x.width[1], plan.planes, plan.planes)]
    ext, high, low = call(extend_kernel, plan, [own, *coarse_halos], extended)
    coarse_x = [shift(high if r == 1 else low, "gx", r) for r in range(1, x.count)]

    fine_own, fine_push = plan.fine_z()
    zs = [plan.coarse_z(level) for level in (1, 2, 3)]
    cells = x.length * y.length
    ready = lambda rows, sigmas: pltpu.VMEM((rows, 3 * sigmas * LANES), BF)
    results = call(
        mix_kernel,
        plan,
        [charges] + fine_y + fine_x + [ext] + coarse_x + [plan.fine_y(), plan.coarse_y(), fine_own, fine_push] + zs,
        [array(cells, LANES), array(24, cells), array(24, cells)]
        + [array(plan.tall[3], plan.flat[3])] * (z.count - 3)
        + [array(plan.tall[l], plan.flat[l]) for l in (1, 2, 3)],
        [
            pltpu.VMEM((x.length + 2 * REACH, 3 * y.length, LANES), F32),
            ready(cells, 3),
            pltpu.VMEM((x.width[1] + plan.planes * (x.count - 1), plan.rows_mixed, LANES), F32),
            ready(plan.flat[1], 3),
            ready(plan.flat[2], 3),
            ready(plan.flat[3], 2),
        ],
    )
    main, near_next, near_prev = results[:3]
    far, windows = results[3 : z.count], results[z.count :]
    from_prev = shift(near_next, "gz", 1)
    from_next = shift(near_prev, "gz", z.count - 1)
    from_far = [shift(f, "gz", r) for f, r in zip(far, range(2, z.count - 1))]
    flat, masks, tall, last = plan.finish()
    (potential,) = call(
        finish_kernel,
        plan,
        [main, *windows, from_prev, from_next, *from_far, *flat, *masks, *tall, last],
        [array(cells, LANES)],
        [pltpu.VMEM((plan.tall[l], plan.flat[l]), F32) for l in (1, 2, 3)],
    )
    return potential.reshape(charges.shape)


def solution(mesh):
    counts = [mesh.shape[name] for name in ("gx", "gy", "gz")]

    def run(charges):
        plan = Plan(counts, [size // n for size, n in zip(charges.shape, counts)])
        placed = P("gx", "gy", "gz")
        return jax.shard_map(
            functools.partial(shards, plan), mesh=mesh, in_specs=(placed,), out_specs=placed, check_vma=False
        )(charges)

    return run
```

```python
import functools

import jax
import jax.numpy as jnp
import numpy as np
from jax import lax
from jax.experimental import pallas as pl
from jax.experimental.pallas import tpu as pltpu
from jax.sharding import PartitionSpec as P

REACH = 8
STENCIL_SIGMAS = (1.0, 2.0, 3.5)
STENCIL_WEIGHTS = (0.4, 0.1, 0.03)
TOP_SIGMAS = (1.5, 4.0)
TOP_WEIGHTS = (0.03, 0.006)
SPLINE_TAPS = np.array((-1.0, 0.0, 9.0, 16.0, 9.0, 0.0, -1.0)) / 16.0

LOW = (0, -1, -2, -2)
EXTRA = (0, 3, 5, 5)
FACE = 11
LANES = 128
BF = jnp.bfloat16
F32 = jnp.float32


def up(value, unit):
    return -(-value // unit) * unit


def band(rows, cols, sigma, reach):
    distance = cols[None, :] - rows[:, None]
    return np.where(abs(distance) <= reach, np.exp(-((distance / sigma) ** 2)), 0.0)


def restriction(size):
    position = np.arange(size)[None, :] - 2 * np.arange(size // 2)[:, None] + 3
    inside = (position >= 0) & (position <= 6)
    return np.where(inside, SPLINE_TAPS[np.clip(position, 0, 6)], 0.0)


class Axis:
    def __init__(self, count, length):
        self.count, self.length = count, length
        self.width = [(length >> level) + EXTRA[level] for level in range(4)]

    def window(self, level, brick):
        size = self.length >> level
        cells = brick * size + LOW[level] + np.arange(self.width[level])
        return cells, ((cells >= 0) & (cells < self.count * size)).astype(float)

    def partial(self, level, brick):
        matrix = np.eye(self.count * self.length)
        for _ in range(level):
            matrix = restriction(matrix.shape[0]) @ matrix
        cells, inside = self.window(level, brick)
        rows = matrix[np.clip(cells, 0, len(matrix) - 1)] * inside[:, None]
        return rows[:, brick * self.length : (brick + 1) * self.length]

    def prolong(self, level, brick):
        matrix = restriction((self.count * self.length) >> (level - 1)).T
        rows, row_inside = self.window(level - 1, brick)
        cols, col_inside = self.window(level, brick)
        taken = matrix[np.clip(rows, 0, len(matrix) - 1)][:, np.clip(cols, 0, matrix.shape[1] - 1)]
        return taken * row_inside[:, None] * col_inside[None, :]

    def mix(self, level, sigma, target, source):
        rows, row_inside = self.window(level, target)
        cols, col_inside = self.window(level, source)
        reach = REACH if level < 3 else self.count * self.length
        return band(rows, cols, sigma, reach) * row_inside[:, None] * col_inside[None, :]


def place(shape, *pieces):
    whole = np.zeros(shape)
    for row, col, block in pieces:
        whole[row : row + block.shape[0], col : col + block.shape[1]] += block
    return whole


def halves(matrix):
    high = matrix.astype(jnp.bfloat16)
    low = (matrix - high.astype(np.float64)).astype(jnp.bfloat16)
    return high, low


def left3(matrix):
    high, low = halves(matrix)
    return np.concatenate([high, low, high], axis=-1)


def left3t(matrix):
    high, low = halves(matrix)
    return np.concatenate([high, high, low], axis=-1)


def right3(matrix):
    high, low = halves(matrix)
    return np.concatenate([high, high, low], axis=-2)


def split(value):
    high = value.astype(BF)
    return high, (value - high.astype(F32)).astype(BF)


def dot(left, right, dims=((1,), (0,))):
    return lax.dot_general(left, right, (dims, ((), ())), preferred_element_type=F32)


class Plan:
    def __init__(self, counts, lengths):
        self.x, self.y, self.z = (Axis(n, length) for n, length in zip(counts, lengths))
        x, y, z = self.x, self.y, self.z
        assert x.count % 2 == 0 and x.count >= 4 and y.count % 2 == 0
        assert z.count >= 4 and z.count & (z.count - 1) == 0
        self.lane = [0, 0, z.width[1], z.width[1] + z.width[2]]
        self.lane_end = self.lane[3] + z.width[3]
        assert self.lane_end <= LANES and z.length == LANES
        self.rows1, self.rows2, self.rows3 = up(y.width[1], 8), up(y.width[2], 16), up(y.width[3], 16)
        assert self.rows2 <= 16 and self.rows3 <= 16 and FACE <= 14 and self.rows1 == 24
        self.row = [0, 0, self.rows1, self.rows1 + self.rows2]
        self.row_face = self.rows1 + self.rows2 + self.rows3
        self.kinds = 1 if y.count == 2 else 2
        self.rows_restricted = self.row_face + 16 * self.kinds
        self.overlay = y.count == 2 and y.width[1] + 3 <= self.rows1
        self.coarse_rows = up(24 + 16 * (y.count - 1), 16) if not self.overlay else 32
        self.fine_halos = 1 if y.count == 2 else 2
        self.fine_rows = y.length + 8 * self.fine_halos
        self.pair_width = [w + (x.length >> l) for l, w in enumerate(x.width)]
        self.planes = max(FACE, x.width[2], self.pair_width[3])
        assert self.planes <= x.width[1]
        self.group = [0, 0, 3 * self.rows1, 3 * self.rows1 + 3 * self.rows2]
        self.rows_mixed = up(self.group[3] + 2 * self.rows3, 16)
        self.tall = [0, up(z.width[1], 8), up(z.width[2], 8), up(z.width[3], 8)]
        assert self.tall[1] - 16 == z.width[1] - FACE and self.tall[2] - 16 == z.width[2] - 13
        self.flat = [0, x.width[1] * self.rows1, x.width[2] * self.rows2, x.width[3] * self.rows3]
        assert self.flat[1] <= 512 and self.flat[2] <= 256 and self.flat[3] <= 256

    def face_kind(self, axis, offset, source):
        if axis.count == 2:
            return 1 - source
        return 1 if offset == 1 else 0

    def near_y(self, halos):
        return [halos[0]] if self.y.count == 2 else [halos[0], halos[-1]]

    def pair_plane(self, ref, index):
        return plane(ref, self.fine_rows * REACH, self.coarse_rows, index)

    def face_row(self, j):
        return j if j < 8 or not self.overlay else j + 3

    def restrict_tables(self):
        rows = up(self.rows_restricted, 16)
        along_y = [place((rows, LANES), (0, 0, m)) for m in self.restrict_y().astype(np.float32)]
        along_z = list(self.restrict_z().astype(np.float32))
        return np.concatenate(along_z + along_y).astype(jnp.bfloat16).reshape(-1, 16, LANES)

    def y_tables(self):
        fine, coarse = self.fine_y(), self.coarse_y()
        cols = up(max(fine.shape[2], coarse.shape[2]), LANES)
        widen = lambda t: np.pad(t, ((0, 0), (0, 0), (0, cols - t.shape[2])))
        self.fine_cols, self.coarse_cols = fine.shape[2], coarse.shape[2]
        return np.concatenate([widen(fine), widen(coarse)], axis=1)

    def z_tables(self):
        tables = [*self.fine_z(), *[self.coarse_z(level) for level in (1, 2, 3)]]
        cols = 9 * LANES
        self.z_rows = np.cumsum([0] + [t.shape[1] for t in tables])
        return np.concatenate([np.pad(t, ((0, 0), (0, 0), (0, cols - t.shape[2]))) for t in tables], axis=1)

    def fine_matrix(self, ref):
        return ref[lax.axis_index("gy"), : 3 * self.y.length, :][:, : self.fine_cols]

    def coarse_matrix(self, ref):
        return ref[lax.axis_index("gy"), 3 * self.y.length :, :][:, : self.coarse_cols]

    def z_matrix(self, ref, number):
        cols = LANES * (6 if number == 4 else 9)
        return ref[lax.axis_index("gz"), int(self.z_rows[number]) : int(self.z_rows[number + 1]), :][:, :cols]

    def restrict_z(self):
        z = self.z
        return np.stack(
            [
                right3(place((z.length, LANES), *[(0, self.lane[l], z.partial(l, b).T) for l in (1, 2, 3)]))
                for b in range(z.count)
            ]
        )

    def restrict_y(self):
        y, tables = self.y, []
        for b in range(y.count):
            pieces = [(self.row[l], 0, y.partial(l, b)) for l in (1, 2, 3)]
            first = y.partial(1, b)
            for k in range(self.kinds):
                kind = self.face_kind(y, 1, b) if self.kinds == 1 else 1 - k
                start = (y.width[1] - FACE) * kind
                for j in range(FACE):
                    pieces.append((self.row_face + 16 * k + self.face_row(j), 0, first[start + j][None]))
            tables.append(left3(place((self.rows_restricted, y.length), *pieces)))
        return np.stack(tables)

    def fine_y(self):
        y, tables = self.y, []
        for b in range(y.count):
            pieces = []
            for s, sigma in enumerate(STENCIL_SIGMAS):
                row = s * y.length
                pieces.append((row, 0, y.mix(0, sigma, b, b)))
                for h in range(self.fine_halos):
                    offset = 1 if h == 0 else y.count - 1
                    source = (b - offset) % y.count
                    start = (y.length - REACH) * self.face_kind(y, offset, source)
                    block = y.mix(0, sigma, b, source)[:, start : start + REACH]
                    pieces.append((row, y.length + 8 * h, block))
            tables.append(left3(place((3 * y.length, up(self.fine_rows, 16)), *pieces)))
        return np.stack(tables)

    def coarse_y(self):
        y, tables = self.y, []
        for b in range(y.count):
            whole = np.zeros((self.rows_mixed, self.coarse_rows))
            for level in (1, 2, 3):
                sigmas = STENCIL_SIGMAS if level < 3 else TOP_SIGMAS
                rows = (0, self.rows1, self.rows2, self.rows3)[level]
                for s, sigma in enumerate(sigmas):
                    top = self.group[level] + s * rows
                    for offset in range(y.count):
                        source = (b - offset) % y.count
                        block = y.mix(level, sigma, b, source)
                        if level == 1 and offset:
                            start = (y.width[1] - FACE) * self.face_kind(y, offset, source)
                            block = block[:, start : start + FACE]
                        for j in range(block.shape[1]):
                            slot = self.face_row(j) if level == 1 and offset else j
                            if self.overlay and offset:
                                slot = 24 + slot if slot < 8 else 8 + slot
                            elif offset:
                                slot = 24 + 16 * (offset - 1) + slot
                            whole[top : top + y.width[level], slot] += block[:, j]
            tables.append(left3(whole))
        return np.stack(tables)

    def near_z(self, b, step):
        side = 1 if (b % 2 == 0) == (step == 0) else -1
        return side, b + side if 0 <= b + side < self.z.count else None

    def fine_z(self):
        z, own, pushed = self.z, [], []
        for b in range(z.count):
            mixes = lambda target: [
                w * z.mix(0, sigma, target, b) for sigma, w in zip(STENCIL_SIGMAS, STENCIL_WEIGHTS)
            ]
            own.append(left3t(np.concatenate(mixes(b), axis=1)))
            rows = []
            for step in (0, 1):
                side, target = self.near_z(b, step)
                if target is None:
                    rows.append(np.zeros((8, 3 * z.length)))
                else:
                    rows.append(np.concatenate([m[:8] if side > 0 else m[-8:] for m in mixes(target)], axis=1))
            pushed.append(left3t(np.concatenate(rows, axis=0)))
        return np.stack(own), np.stack(pushed)

    def coarse_z(self, level):
        z, tables = self.z, []
        sigmas, weights = (STENCIL_SIGMAS, STENCIL_WEIGHTS) if level < 3 else (TOP_SIGMAS, TOP_WEIGHTS)
        factor = 0.5**level if level < 3 else 1.0
        cols, tall = LANES * len(sigmas), self.tall[level]
        for b in range(z.count):

            def mixed(target):
                blocks = [
                    place((z.width[level], LANES), (0, self.lane[level], factor * w * z.mix(level, sigma, target, b)))
                    for sigma, w in zip(sigmas, weights)
                ]
                return np.concatenate(blocks, axis=1)

            pieces = [place((tall, cols), (0, 0, mixed(b)))]
            if level < 3:
                layers = FACE if level == 1 else 13
                for step in (0, 1):
                    side, target = self.near_z(b, step)
                    if target is None:
                        pieces.append(np.zeros((16, cols)))
                    else:
                        block = mixed(target)
                        pieces.append(place((16, cols), (0, 0, block[:layers] if side > 0 else block[-layers:])))
            else:
                block = mixed(b ^ 1)
                pieces.append(block[:16])
                pieces.append(place((16, cols), (FACE, 0, block[16:])))
                for m in range(2, z.count):
                    pieces.append(place((tall, cols), (0, 0, mixed(b ^ m))))
            whole = np.concatenate(pieces, axis=0)
            tables.append(left3t(place((up(len(whole), 16), cols), (0, 0, whole))))
        return np.stack(tables)

    def finish(self):
        x, y, z = self.x, self.y, self.z
        rows = (y.length, self.rows1, self.rows2, self.rows3)
        exact = lambda m: np.asarray(m, dtype=jnp.bfloat16)

        def free(axis, level):
            inner = Axis(5, axis.length)
            return inner.prolong(level, 2)

        flat = []
        for level in (3, 2, 1):
            q = place((rows[level], rows[level - 1]), (0, 0, free(y, level).T))
            flat.append(exact(np.kron(free(x, level).T, q)))
        joined = np.concatenate([np.pad(m, ((0, -len(m) % 16), (0, 1024 - m.shape[1]))) for m in flat])
        self.flat_rows = np.cumsum([0] + [up(len(m), 16) for m in flat])
        masks = np.zeros((x.count * y.count, 8, 512), np.float32)
        for level in (3, 2, 1):
            for bx in range(x.count):
                for by in range(y.count):
                    inside = np.zeros(rows[level])
                    inside[: y.width[level]] = y.window(level, by)[1]
                    line = np.kron(x.window(level, bx)[1], inside)
                    masks[bx * y.count + by, level, : len(line)] = line
        tall = []
        for b in range(z.count):
            ends = (0, z.length - 8) if b % 2 else (z.length - 8, 0)
            pieces = [(0, 0, free(z, 1).T)] + [(self.tall[1] + 8 * k, end, np.eye(8)) for k, end in enumerate(ends)]
            last = place((up(self.tall[1] + 16, 16), LANES), *pieces)
            parts = [place((up(self.tall[l - 1], 16), LANES), (0, 0, z.prolong(l, b))) for l in (3, 2)]
            tall.append(np.concatenate([last, *parts]))
        return joined, masks, exact(np.stack(tall))


def plane(ref, base, rows, index):
    return ref[pl.ds(base // 8 + rows // 8 * index, rows // 8)].reshape(rows, LANES)


def put_plane(ref, row, value):
    ref[row // 8 : (row + value.shape[0]) // 8] = value.reshape(value.shape[0] // 8, 8, LANES)


def restrict_kernel(plan, q_ref, table_ref, own_ref, *rest):
    targets, mixed = rest[: plan.kinds], rest[plan.kinds]
    nx, ny, nz = plan.x.length, plan.y.length, plan.z.length
    by, bz = lax.axis_index("gy"), lax.axis_index("gz")
    matrix_z = table_ref[pl.ds(3 * nz // 16 * bz, 3 * nz // 16)].reshape(3 * nz, LANES)
    rows = up(plan.rows_restricted, 16)
    matrix_y = table_ref[pl.ds(3 * nz // 16 * plan.z.count + rows // 16 * by, rows // 16)].reshape(rows, LANES)
    matrix_y = matrix_y[:, : 3 * ny]
    for i in range(nx):
        faces = [q_ref[i, ny - REACH :, :], q_ref[i, :REACH, :]]
        if plan.kinds == 1:
            faces = [jnp.where(by == 0, *faces)]
        for face, ref in zip(faces, targets):
            ref[i] = face
    high, low = split(q_ref[...].reshape(nx * ny, nz))
    along_z = dot(jnp.concatenate([high, low, high], axis=1), matrix_z)
    high, low = split(along_z)
    high, low = high.reshape(nx, ny, LANES), low.reshape(nx, ny, LANES)
    for i in range(0, nx, 2):
        pair = [jnp.concatenate([high[j], high[j], low[j]], axis=0) for j in (i, i + 1)]
        both = dot(matrix_y, jnp.concatenate(pair, axis=1))[: plan.rows_restricted]
        mixed[i] = both[:, :LANES]
        mixed[i + 1] = both[:, LANES:]

    brick = lax.axis_index("gx")
    keep_low = jnp.where(brick > 0, 1.0, 0.0).astype(F32)
    keep_high = jnp.where(brick < plan.x.count - 1, 1.0, 0.0).astype(F32)

    def coarsen(planes, level):
        size = nx >> level
        result = {}
        for i in range(LOW[level], LOW[level] + plan.x.width[level]):
            get = lambda j: planes.get(2 * i + j)
            total = None
            for offsets, weight in (((-3, 3), -0.0625), ((-1, 1), 0.5625), ((0,), 1.0)):
                terms = [get(j) for j in offsets if get(j) is not None]
                if terms:
                    term = functools.reduce(jnp.add, terms)
                    term = term * weight if weight != 1.0 else term
                    total = term if total is None else total + term
            if i < 0:
                total = total * keep_low
            elif i >= size:
                total = total * keep_high
            result[i] = total
        return result

    lanes = lax.broadcasted_iota(jnp.int32, (8, LANES), 1)
    in1, in2 = lanes < plan.lane[2], lanes < plan.lane[3]

    def tile(planes, level, k, row):
        index = LOW[level] + k
        return planes[row][index] if k < plan.x.width[level] else None

    def rows_of(start, count, depth):
        levels = [{i: mixed[i, start : start + count, :] for i in range(nx)}]
        for level in range(1, depth + 1):
            levels.append(coarsen(levels[-1], level))
        return levels[-1]

    zero = jnp.zeros((8, LANES), F32)
    first = {r: rows_of(r, 8, 1) for r in range(0, plan.rows1, 8)}
    second = {r: rows_of(plan.row[2] + r, 8, 2) for r in (0, 8)}
    third = {r: rows_of(plan.row[3] + r, 8, 3) for r in (0, 8)}
    face = [{r: rows_of(plan.row_face + 16 * f + r, 8, 1) for r in (0, 8)} for f in range(plan.kinds)]
    for k in range(plan.x.width[1]):
        for r in range(0, plan.rows1, 8):
            one = first[r][LOW[1] + k]
            two = second[r][LOW[2] + k] if r < 16 and k < plan.x.width[2] else zero
            three = third[r][LOW[3] + k] if r < 16 and k < plan.x.width[3] else zero
            rest_ = jnp.where(in2, two, three)
            own_ref[k, r : r + 8, :] = jnp.where(in1, one, rest_)
            if r < 16:
                for f in range(plan.kinds):
                    targets[f][nx + 2 * k + r // 8] = jnp.where(in1, face[f][r][LOW[1] + k], rest_)


def mask(condition):
    return jnp.where(condition, 1.0, 0.0).astype(F32)


def extend_kernel(plan, q_ref, own_ref, *refs):
    count = plan.y.count - 1
    halos, (ext_ref, partner_ref, side_ref) = refs[:count], refs[count:]
    x, y = plan.x, plan.y
    odd = lax.axis_index("gx") % 2
    end = x.length - REACH
    near = plan.near_y(halos)
    for start, ref in ((end * odd, side_ref), (end * (1 - odd), partner_ref)):
        for i in range(REACH):
            row = plan.fine_rows * i
            put_plane(ref, row, q_ref[start + i])
            for h, halo in enumerate(near):
                ref[(row + y.length) // 8 + h] = halo[start + i]

    base = [0 if halo.shape[0] == 2 * x.width[1] else 8 * x.length for halo in halos]
    for i in range(x.width[1]):
        own = own_ref[i]
        parts = [plane(halo, at, 16, i) for halo, at in zip(halos, base)]
        if plan.overlay:
            halo = parts[0]
            parts = [own[:16], own[16:] + halo[8:], halo[:8]]
        else:
            pad = plan.coarse_rows - 24 - 16 * count
            parts = [own] + parts + ([jnp.zeros((pad, LANES), F32)] if pad else [])
        ext_ref[i] = jnp.concatenate(parts, axis=0)
    lanes = lax.broadcasted_iota(jnp.int32, (1, LANES), 1)
    start = (x.width[1] - FACE) * (1 - odd)
    for p in range(plan.planes):
        row = plan.fine_rows * REACH + plan.coarse_rows * p
        value = jnp.where(lanes < plan.lane[2], ext_ref[start + min(p, FACE - 1)], ext_ref[p])
        put_plane(partner_ref, row, value)


def chip_kernel(plan, ext_ref, pair_ref, *targets):
    x, gx = plan.x, lax.axis_index("gx")
    odd, chip = gx % 2, gx // 2
    lanes = lax.broadcasted_iota(jnp.int32, (1, LANES), 1)
    in1, in2 = lanes < plan.lane[2], lanes < plan.lane[3]
    keep_even, keep_odd = mask(odd == 0), mask(odd == 1)

    def merged(level, cell):
        size, total = x.length >> level, None
        for where_own, where_partner, at in ((keep_even, keep_odd, cell), (keep_odd, keep_even, cell - size)):
            if 0 <= at < x.width[level]:
                value = ext_ref[at] * where_own + plan.pair_plane(pair_ref, at) * where_partner
                total = value if total is None else total + value
        return total

    second = [merged(2, c) for c in range(plan.pair_width[2])]
    third = [merged(3, c) for c in range(plan.pair_width[3])]
    start = (x.width[1] - FACE) * odd
    chips = x.count // 2
    for k, ref in zip(range(1, chips), targets):
        high = x.length >> 2
        for p in range(plan.planes):
            if chips == 2:
                two = jnp.where(chip == 0, second[high + p], second[p])
            else:
                two = second[high + p] if k == 1 else second[p]
            first = ext_ref[start + min(p, FACE - 1)]
            ref[p] = jnp.where(in1, first, jnp.where(in2, two, third[p]))


def mix_planes(get, put, count, matrix):
    for i in range(0, count, 2):
        pair = [i, min(i + 1, count - 1)]
        stacked = []
        for j in pair:
            high, low = split(get(j))
            stacked.append(jnp.concatenate([high, high, low], axis=0))
        both = dot(matrix, jnp.concatenate(stacked, axis=1))
        put(i, both[:, :LANES])
        if pair[1] != i:
            put(pair[1], both[:, LANES:])


def stencil(cells, wanted, sigma, reach=REACH):
    result = []
    for i in wanted:
        total = cells.get(i)
        for k in range(1, reach + 1):
            terms = [cells[j] for j in (i - k, i + k) if j in cells]
            if terms:
                term = functools.reduce(jnp.add, terms) * float(np.exp(-((k / sigma) ** 2)))
                total = term if total is None else total + term
        result.append(total)
    return result


def put_ready(ready, sigmas, s, row, value):
    high, low = split(value)
    rows = slice(row, row + value.shape[0])
    step = LANES * sigmas
    ready[rows, s * LANES : (s + 1) * LANES] = high
    ready[rows, step + s * LANES : step + (s + 1) * LANES] = low
    ready[rows, 2 * step + s * LANES : 2 * step + (s + 1) * LANES] = high


def fine_padding(plan):
    pad = up(plan.fine_rows, 16) - plan.fine_rows
    return [jnp.zeros((pad, LANES), F32)] if pad else []


def fine_inner_kernel(plan, q_ref, y_table, z_table, *refs):
    refs = list(refs)
    take = lambda n: [refs.pop(0) for _ in range(n)]
    halos = take(plan.y.count - 1)
    main_ref, push_ref, edge_ref = take(3)
    mixed, ready = refs
    x, y = plan.x, plan.y
    padding = fine_padding(plan)

    def get(i):
        return jnp.concatenate([q_ref[i]] + [plane(h, 0, 8, i) for h in plan.near_y(halos)] + padding, axis=0)

    def put(i, value):
        mixed[i] = value

    mix_planes(get, put, x.length, plan.fine_matrix(y_table))
    inner = range(REACH, x.length - REACH)
    edge = [*range(REACH), *range(x.length - REACH, x.length)]
    for s, sigma in enumerate(STENCIL_SIGMAS):
        for r in range(0, y.length, 16):
            row = s * y.length + r
            planes = {i: mixed[i, row : row + 16, :] for i in range(x.length)}
            for i, value in zip(inner, stencil(planes, inner, sigma)):
                put_ready(ready, 3, s, (i - REACH) * y.length + r, value)
            for i, value in enumerate(stencil(planes, edge, sigma)):
                edge_ref[i, row : row + 16, :] = value
    main_ref[...] = dot(ready[...], plan.z_matrix(z_table, 0), ((1,), (1,)))
    push_ref[...] = dot(plan.z_matrix(z_table, 1), ready[...], ((1,), (1,)))


def fine_edge_kernel(plan, partner_ref, side_ref, edge_ref, inner_ref, y_table, z_table, *refs):
    main_ref, push_ref, mixed, ready = refs
    x, y = plan.x, plan.y
    gx = lax.axis_index("gx")
    odd = gx % 2 == 1
    from_partner = mask(odd), mask(~odd)
    from_side = mask(~odd & (gx > 0)), mask(odd & (gx < x.count - 1))
    padding = fine_padding(plan)

    def get(i):
        blocks = []
        for k in range(plan.fine_rows // 8):
            at = plan.fine_rows // 8 * (i % REACH) + k
            blocks.append(partner_ref[at] * from_partner[i // REACH] + side_ref[at] * from_side[i // REACH])
        return jnp.concatenate(blocks + padding, axis=0)

    def put(i, value):
        mixed[i] = value

    mix_planes(get, put, 2 * REACH, plan.fine_matrix(y_table))
    for s, sigma in enumerate(STENCIL_SIGMAS):
        for r in range(0, y.length, 16):
            row = s * y.length + r
            at = lambda i: mixed[i, row : row + 16, :]
            before = {k - REACH: at(k) for k in range(REACH)}
            after = {x.length + k: at(REACH + k) for k in range(REACH)}
            added = stencil(before, range(REACH), sigma)
            added += stencil(after, range(x.length - REACH, x.length), sigma)
            for i, value in enumerate(added):
                put_ready(ready, 3, s, i * y.length + r, edge_ref[i, row : row + 16, :] + value)
    main_ref[...] = dot(ready[...], plan.z_matrix(z_table, 0), ((1,), (1,)))
    pushed = dot(plan.z_matrix(z_table, 1), ready[...], ((1,), (1,)))
    half = pushed.shape[1] // 2
    push_ref[...] = jnp.concatenate([pushed[:, :half], inner_ref[...], pushed[:, half:]], axis=1)


def coarse_inner_kernel(plan, ext_ref, pair_ref, y_table, mixed):
    own = plan.x.width[1]

    def put(i, value):
        mixed[i] = value

    mix_planes(lambda i: ext_ref[i] if i < own else plan.pair_plane(pair_ref, i - own), put, own + plan.planes, plan.coarse_matrix(y_table))


def collect(plan, level, inner, outer, row, rows):
    x, gx = plan.x, lax.axis_index("gx")
    odd, chip, chips = gx % 2, gx // 2, plan.x.count // 2
    size, width = x.length >> level, x.width[level]
    start = LOW[level]
    reach = REACH if level < 3 else x.count * x.length
    cells = {start + k: inner[k, row : row + rows, :] for k in range(width)}

    def add(cell, value, keep):
        if start - reach <= cell < start + width + reach:
            value = value * keep
            cells[cell] = cells[cell] + value if cell in cells else value

    own = x.width[1]
    layers = FACE if level == 1 else width
    for k in range(layers):
        value = inner[own + k, row : row + rows, :]
        add(size + start + k, value, mask(odd == 0))
        add(-size + start + width - layers + k, value, mask(odd == 1))
    for offset in range(1, chips):
        base = plan.planes * (offset - 1)
        at = lambda k: outer[base + k, row : row + rows, :]
        for shift, here in ((-offset, chip >= offset), (chips - offset, chip < offset)):
            if level < 3 and abs(shift) != 1:
                continue
            if level == 1:
                keep = mask(here & (odd == (0 if shift < 0 else 1)))
                first = -size + start + width - FACE if shift < 0 else size + start
                for k in range(FACE):
                    add(first + k, at(k), keep)
                continue
            for core in (0, 1):
                keep = mask(here & (odd == core))
                first = 2 * size * shift - size * core + start
                if level == 2 and shift < 0:
                    first += size
                for k in range(plan.planes if level == 2 else plan.pair_width[3]):
                    add(first + k, at(k), keep)
    return cells


def top_kernel(plan, inner, *refs):
    refs = list(refs)
    take = lambda n: [refs.pop(0) for _ in range(n)]
    chips, (y_table, z_table) = take(plan.x.count // 2 - 1), take(2)
    outer, own_ref, partner_ref = take(3)
    far, ready = take(plan.z.count - 2), refs[0]

    def put(i, value):
        outer[i] = value

    mix_planes(lambda i: chips[i // plan.planes][i % plan.planes], put, plan.planes * len(chips), plan.coarse_matrix(y_table))
    start, width, rows = LOW[3], plan.x.width[3], plan.rows3
    for s, sigma in enumerate(TOP_SIGMAS):
        for r in range(0, rows, 8):
            cells = collect(plan, 3, inner, outer, plan.group[3] + s * rows + r, 8)
            reach = max(cells) - min(cells)
            for i, value in enumerate(stencil(cells, range(start, start + width), sigma, reach)):
                put_ready(ready, 2, s, i * rows + r, value)
    three = dot(plan.z_matrix(z_table, 4), ready[...], ((1,), (1,)))
    tall = plan.tall[3]
    own_ref[...] = three[:tall]
    partner_ref[...] = three[tall : tall + 32]
    for m, ref in enumerate(far):
        ref[...] = three[tall * (m + 1) + 32 : tall * (m + 2) + 32]


def coarse_kernel(plan, inner, outer, top_ref, push_ref, z_table, *refs):
    partner_ref, side_ref, e1_ref, e2_ref, *ready = refs
    x = plan.x
    results = []
    for level in (1, 2):
        rows = plan.rows1 if level == 1 else plan.rows2
        wanted = range(LOW[level], LOW[level] + x.width[level])
        for s, sigma in enumerate(STENCIL_SIGMAS):
            for r in range(0, rows, 8):
                cells = collect(plan, level, inner, outer, plan.group[level] + s * rows + r, 8)
                for i, value in enumerate(stencil(cells, wanted, sigma)):
                    put_ready(ready[level - 1], 3, s, i * rows + r, value)
        results.append(dot(plan.z_matrix(z_table, level + 1), ready[level - 1][...], ((1,), (1,))))
    one, two = results
    e1_ref[...] = one[: plan.tall[1]]
    e2_ref[...] = two[: plan.tall[2]]
    for n, ref in enumerate((partner_ref, side_ref)):
        ref[:8, :] = push_ref[8 * n : 8 * n + 8, :]
        ref[8:, :] = jnp.zeros((16, ref.shape[1]), F32)
        start = plan.tall[1] + 16 * n
        ref[8:, : plan.flat[1]] = one[start : start + 16]
        start = plan.tall[2] + 16 * n
        ref[8:, 512 : 512 + plan.flat[2]] = two[start : start + 16]
    partner_ref[8:, : plan.flat[3]] += top_ref[16:]
    partner_ref[8:, 768 : 768 + plan.flat[3]] = top_ref[:16]


def finish_kernel(plan, inner_ref, edge_ref, e1_ref, e2_ref, e3_ref, *refs):
    z = plan.z
    refs = list(refs)
    partner_ref, side_ref, *far = [refs.pop(0) for _ in range(z.count)]
    flat, masks, tall, out_ref, e1, e2, e3 = refs
    bz = lax.axis_index("gz")
    column = lax.axis_index("gx") * plan.y.count + lax.axis_index("gy")
    odd = bz % 2
    spread_cols = plan.x.length * plan.y.length
    keep = lambda level: masks[column, level : level + 1, : plan.flat[level]]
    bounds = [int(r) for r in plan.flat_rows]
    flat3, flat2, flat1 = (
        flat[bounds[k] : bounds[k + 1], :][: plan.flat[3 - k], :cols]
        for k, cols in enumerate((plan.flat[2], plan.flat[1], spread_cols))
    )
    e1[...], e2[...], e3[...] = e1_ref[...], e2_ref[...], e3_ref[...]
    for f in far:
        e3[...] += f[...]
    e3[:16, :] += partner_ref[8:24, 768 : 768 + plan.flat[3]]
    e3[16 : z.width[3], :] += partner_ref[8 + FACE : 8 + FACE + z.width[3] - 16, : plan.flat[3]]
    kept = lax.broadcasted_iota(jnp.int32, (16, 1), 0) < FACE
    for ref, high in ((partner_ref, odd == 0), (side_ref, odd == 1)):
        one = jnp.where(kept, ref[8:, : plan.flat[1]], 0.0)
        two = ref[8:, 512 : 512 + plan.flat[2]]
        for window, value, tall_ in ((e1, one, plan.tall[1]), (e2, two, plan.tall[2])):
            window[:16, :] += value * mask(~high)
            window[tall_ - 16 :, :] += value * mask(high)

    def across(value, matrix):
        high, low = split(value)
        both = dot(jnp.concatenate([high, low], axis=0), matrix)
        return both[: value.shape[0]] + both[value.shape[0] :]

    def along(matrix, value):
        high, low = split(value)
        return dot(matrix, high) + dot(matrix, low)

    top = up(plan.tall[1] + 16, 16)
    middle = top + up(plan.tall[2], 16)
    tall3 = tall[bz, top:middle, :][: plan.tall[2], : plan.tall[3]]
    tall2 = tall[bz, middle:, :][: plan.tall[1], : plan.tall[2]]
    last = tall[bz, :top, :]
    three = e3[...] * keep(3)
    two = (e2[...] + along(tall3, across(three, flat3))) * keep(2)
    one = (e1[...] + along(tall2, across(two, flat2))) * keep(1)
    spread = across(one, flat1)
    rows = jnp.concatenate([spread, partner_ref[:8], side_ref[:8]], axis=0)
    pad = last.shape[0] - rows.shape[0]
    if pad:
        rows = jnp.concatenate([rows, jnp.zeros((pad, rows.shape[1]), F32)], axis=0)
    high, low = split(rows)
    stacked = jnp.concatenate([high, low], axis=0)
    matrix = jnp.concatenate([last, last], axis=0)
    coarse = dot(stacked, matrix, ((0,), (0,)))
    edge = REACH * plan.y.length
    end = coarse.shape[0] - edge
    out_ref[:edge] = coarse[:edge] + edge_ref[:edge]
    out_ref[edge:end] = coarse[edge:end] + inner_ref[...]
    out_ref[end:] = coarse[end:] + edge_ref[edge:]


def call(kernel, plan, operands, outs, scratch=()):
    whole = pl.BlockSpec(memory_space=pltpu.VMEM)
    return pl.pallas_call(
        functools.partial(kernel, plan),
        in_specs=[whole] * len(operands),
        out_specs=[whole] * len(outs),
        scratch_shapes=list(scratch),
        out_shape=list(outs),
        compiler_params=pltpu.CompilerParams(vmem_limit_bytes=32 * 2**20),
    )(*[jnp.asarray(o) for o in operands])


def shift(value, axis, offset):
    count = lax.axis_size(axis)
    return lax.ppermute(value, axis, [(i, (i + offset) % count) for i in range(count)])


def swap(value, axes, partner):
    first, second = (lax.axis_size(a) for a in axes)
    pairs = []
    for i in range(first):
        for j in range(second):
            k, m = partner(i, j)
            pairs.append((i * second + j, k * second + m))
    return lax.ppermute(value, axes, pairs)


def side_of(count):
    return lambda i: None if i in (0, count - 1) else i + (1 if i % 2 else -1)


def shards(plan, charges):
    x, y, z = plan.x, plan.y, plan.z
    array = lambda *shape: jax.ShapeDtypeStruct(shape, F32)
    vmem = lambda *shape: pltpu.VMEM(shape, F32)
    ready = lambda rows, sigmas: pltpu.VMEM((rows, 3 * sigmas * LANES), BF)
    side_x, side_z = side_of(x.count), side_of(z.count)
    partner_x = lambda v: swap(v, ("gx", "gy"), lambda i, j: (i ^ 1, j))
    across_x = lambda v: swap(v, ("gx", "gy"), lambda i, j: (i, j ^ 1) if side_x(i) is None else (side_x(i), j))
    partner_z = lambda v: swap(v, ("gx", "gz"), lambda i, j: (i, j ^ 1))
    across_z = lambda v: swap(v, ("gx", "gz"), lambda i, j: (i ^ 1, j) if side_z(j) is None else (i, side_z(j)))

    rows_y = 8 * x.length + 16 * x.width[1]
    own, *to_y = call(
        restrict_kernel,
        plan,
        [charges, plan.restrict_tables()],
        [array(x.width[1], plan.rows1, LANES)] + [array(rows_y // 8, 8, LANES)] * plan.kinds,
        [vmem(x.length, plan.rows_restricted, LANES)],
    )
    from_y = []
    for offset in range(1, y.count):
        value = to_y[0 if offset == 1 else -1]
        value = value if offset in (1, y.count - 1) else value[x.length :]
        from_y.append(shift(value, "gy", offset))

    ext, to_partner, to_side = call(
        extend_kernel,
        plan,
        [charges, own, *from_y],
        [
            array(x.width[1], plan.coarse_rows, LANES),
            array((REACH * plan.fine_rows + plan.planes * plan.coarse_rows) // 8, 8, LANES),
            array(REACH * plan.fine_rows // 8, 8, LANES),
        ],
    )
    from_side, pair = across_x(to_side), partner_x(to_partner)

    y_table, z_table = plan.y_tables(), plan.z_tables()
    inner_cells = (x.length - 2 * REACH) * y.length
    edge_cells = 2 * REACH * y.length
    main_inner, push_inner, edge = call(
        fine_inner_kernel,
        plan,
        [charges, y_table, z_table, *from_y],
        [array(inner_cells, z.length), array(16, inner_cells), array(2 * REACH, 3 * y.length, LANES)],
        [vmem(x.length, 3 * y.length, LANES), ready(inner_cells, 3)],
    )

    chips = x.count // 2
    to_chips = call(chip_kernel, plan, [ext, pair], [array(plan.planes, plan.coarse_rows, LANES)] * (chips - 1))
    from_chips = [
        swap(v, ("gx", "gy"), lambda i, j, k=k: ((i + 2 * k) % x.count ^ 1, j))
        for k, v in zip(range(1, chips), to_chips)
    ]
    planes_inner = x.width[1] + plan.planes
    (mixed_inner,) = call(
        coarse_inner_kernel, plan, [ext, pair, y_table], [array(planes_inner, plan.rows_mixed, LANES)]
    )

    main_edge, push = call(
        fine_edge_kernel,
        plan,
        [pair, from_side, edge, push_inner, y_table, z_table],
        [array(edge_cells, z.length), array(16, x.length * y.length)],
        [vmem(2 * REACH, 3 * y.length, LANES), ready(edge_cells, 3)],
    )
    planes_outer = plan.planes * (chips - 1)
    window = lambda level: array(plan.tall[level], plan.flat[level])
    mixed_outer, e3, top_partner, *far = call(
        top_kernel,
        plan,
        [mixed_inner, *from_chips, y_table, z_table],
        [array(planes_outer, plan.rows_mixed, LANES), window(3), array(32, plan.flat[3])]
        + [window(3)] * (z.count - 2),
        [ready(plan.flat[3], 2)],
    )
    from_far = [swap(f, ("gx", "gz"), lambda i, j, m=m: (i, j ^ m)) for m, f in zip(range(2, z.count), far)]
    to_partner, to_side, e1, e2 = call(
        coarse_kernel,
        plan,
        [mixed_inner, mixed_outer, top_partner, push, z_table],
        [array(24, 1024), array(24, 1024), window(1), window(2)],
        [ready(plan.flat[1], 3), ready(plan.flat[2], 3)],
    )
    from_near = [partner_z(to_partner), across_z(to_side)]

    (potential,) = call(
        finish_kernel,
        plan,
        [main_inner, main_edge, e1, e2, e3, *from_near, *from_far, *plan.finish()],
        [array(x.length * y.length, z.length)],
        [vmem(plan.tall[level], plan.flat[level]) for level in (1, 2, 3)],
    )
    return potential.reshape(charges.shape)


def solution(mesh):
    counts = [mesh.shape[name] for name in ("gx", "gy", "gz")]

    def run(charges):
        plan = Plan(counts, [size // n for size, n in zip(charges.shape, counts)])
        placed = P("gx", "gy", "gz")
        return jax.shard_map(
            functools.partial(shards, plan), mesh=mesh, in_specs=(placed,), out_specs=placed, check_vma=False
        )(charges)

    return run
```

```python
import functools

import jax
import jax.numpy as jnp
import numpy as np
from jax import lax
from jax.experimental import pallas as pl
from jax.experimental.pallas import tpu as pltpu
from jax.sharding import PartitionSpec as P

REACH = 8
STENCIL_SIGMAS = (1.0, 2.0, 3.5)
STENCIL_WEIGHTS = (0.4, 0.1, 0.03)
TOP_SIGMAS = (1.5, 4.0)
TOP_WEIGHTS = (0.03, 0.006)
SPLINE_TAPS = np.array((-1.0, 0.0, 9.0, 16.0, 9.0, 0.0, -1.0)) / 16.0

LOW = (0, -1, -2, -2)
EXTRA = (0, 3, 5, 5)
FACE = 11
LANES = 128
BF = jnp.bfloat16
F32 = jnp.float32


def up(value, unit):
    return -(-value // unit) * unit


def band(rows, cols, sigma, reach):
    distance = cols[None, :] - rows[:, None]
    return np.where(abs(distance) <= reach, np.exp(-((distance / sigma) ** 2)), 0.0)


def restriction(size):
    position = np.arange(size)[None, :] - 2 * np.arange(size // 2)[:, None] + 3
    inside = (position >= 0) & (position <= 6)
    return np.where(inside, SPLINE_TAPS[np.clip(position, 0, 6)], 0.0)


class Axis:
    def __init__(self, count, length):
        self.count, self.length = count, length
        self.width = [(length >> level) + EXTRA[level] for level in range(4)]

    def window(self, level, brick):
        size = self.length >> level
        cells = brick * size + LOW[level] + np.arange(self.width[level])
        return cells, ((cells >= 0) & (cells < self.count * size)).astype(float)

    def partial(self, level, brick):
        matrix = np.eye(self.count * self.length)
        for _ in range(level):
            matrix = restriction(matrix.shape[0]) @ matrix
        cells, inside = self.window(level, brick)
        rows = matrix[np.clip(cells, 0, len(matrix) - 1)] * inside[:, None]
        return rows[:, brick * self.length : (brick + 1) * self.length]

    def prolong(self, level, brick):
        matrix = restriction((self.count * self.length) >> (level - 1)).T
        rows, row_inside = self.window(level - 1, brick)
        cols, col_inside = self.window(level, brick)
        taken = matrix[np.clip(rows, 0, len(matrix) - 1)][:, np.clip(cols, 0, matrix.shape[1] - 1)]
        return taken * row_inside[:, None] * col_inside[None, :]

    def mix(self, level, sigma, target, source):
        rows, row_inside = self.window(level, target)
        cols, col_inside = self.window(level, source)
        reach = REACH if level < 3 else self.count * self.length
        return band(rows, cols, sigma, reach) * row_inside[:, None] * col_inside[None, :]


def place(shape, *pieces):
    whole = np.zeros(shape)
    for row, col, block in pieces:
        whole[row : row + block.shape[0], col : col + block.shape[1]] += block
    return whole


def halves(matrix):
    high = matrix.astype(jnp.bfloat16)
    low = (matrix - high.astype(np.float64)).astype(jnp.bfloat16)
    return high, low


def left3(matrix):
    high, low = halves(matrix)
    return np.concatenate([high, low, high], axis=-1)


def left3t(matrix):
    high, low = halves(matrix)
    return np.concatenate([high, high, low], axis=-1)


def right3(matrix):
    high, low = halves(matrix)
    return np.concatenate([high, high, low], axis=-2)


def split(value):
    high = value.astype(BF)
    return high, (value - high.astype(F32)).astype(BF)


def dot(left, right, dims=((1,), (0,))):
    return lax.dot_general(left, right, (dims, ((), ())), preferred_element_type=F32)


class Plan:
    def __init__(self, counts, lengths):
        self.x, self.y, self.z = (Axis(n, length) for n, length in zip(counts, lengths))
        x, y, z = self.x, self.y, self.z
        assert x.count % 2 == 0 and x.count >= 4 and y.count % 2 == 0
        assert z.count >= 4 and z.count & (z.count - 1) == 0
        self.lane = [0, 0, z.width[1], z.width[1] + z.width[2]]
        self.lane_end = self.lane[3] + z.width[3]
        assert self.lane_end <= LANES and z.length == LANES
        self.rows1, self.rows2 = up(y.width[1], 8), up(y.width[2], 16)
        self.rows3, self.whole3 = up(y.width[3], 16), up(y.count * y.length >> 3, 8)
        assert self.rows2 <= 16 and self.rows3 <= 16 and FACE <= 14 and self.rows1 == 24
        self.row = [0, 0, self.rows1, self.rows1 + self.rows2]
        self.row_face = self.rows1 + self.rows2 + self.whole3
        self.kinds = 1 if y.count == 2 else 2
        self.rows_restricted = self.row_face + 16 * self.kinds
        self.overlay = y.count == 2 and y.width[1] + 3 <= self.rows1
        self.coarse_rows = up(24 + 16 * (y.count - 1), 16) if not self.overlay else 32
        self.fine_halos = 1 if y.count == 2 else 2
        self.fine_rows = y.length + 8 * self.fine_halos
        self.pair_width = [w + (x.length >> l) for l, w in enumerate(x.width)]
        self.planes = max(FACE, x.width[2])
        self.flat_top = up((x.count * x.length >> 3) * self.whole3, LANES)
        self.top_shape = up(z.width[3], 8), self.flat_top
        self.top_rows = self.top_shape[0] * self.flat_top // LANES
        self.top_row = REACH * self.fine_rows + self.planes * self.coarse_rows
        assert self.planes <= x.width[1]
        self.group = [0, 0, 3 * self.rows1]
        self.rows_mixed = up(3 * self.rows1 + 3 * self.rows2, 16)
        self.tall = [0, up(z.width[1], 8), up(z.width[2], 8), up(z.width[3], 8)]
        assert self.tall[1] - 16 == z.width[1] - FACE and self.tall[2] - 16 == z.width[2] - 13
        self.flat = [0, x.width[1] * self.rows1, x.width[2] * self.rows2, x.width[3] * self.rows3]
        assert self.flat[1] <= 512 and self.flat[2] <= 256 and self.flat[3] <= 256

    def face_kind(self, axis, offset, source):
        if axis.count == 2:
            return 1 - source
        return 1 if offset == 1 else 0

    def near_y(self, halos):
        return [halos[0]] if self.y.count == 2 else [halos[0], halos[-1]]

    def tiles(self):
        nx, nt = self.x.length, self.y.length // 8
        inner = range(REACH, nx - REACH)
        edge = [*range(REACH), *range(nx - REACH, nx)]
        order = [(x, t) for x in inner for t in range(1, nt - 1)]
        order += [(x, t) for x in inner for t in (0, nt - 1)]
        return order + [(x, t) for x in edge for t in range(nt)]

    def pair_plane(self, ref, index):
        return plane(ref, self.fine_rows * REACH, self.coarse_rows, index)

    def face_row(self, j):
        return j if j < 8 or not self.overlay else j + 3

    def restrict_tables(self):
        rows = up(self.rows_restricted, 16)
        along_y = np.stack([place((rows, LANES), (0, 0, m)) for m in self.restrict_y().astype(np.float32)])
        parts = [self.restrict_z(), along_y, self.y_tables(), self.top_z()]
        parts = [p.astype(np.float32) for p in parts]
        blocks = []
        for p in parts:
            columns = [p[:, :, c : c + LANES] for c in range(0, p.shape[2], LANES)]
            blocks.append(np.concatenate(columns, axis=1).reshape(len(p), -1, 16, LANES))
        self.blocks = [b.shape[1] for b in blocks]
        table = np.concatenate([b.reshape(-1, 16, LANES) for b in blocks] + [self.top_select().reshape(-1, 2, LANES)
            .transpose(1, 0, 2).reshape(-1, 16, LANES).astype(np.float32)])
        return table.astype(jnp.bfloat16)

    def y_tables(self):
        fine, halo, coarse = self.fine_y(), self.halo_y(), self.coarse_y()
        cols = up(max(fine.shape[2], coarse.shape[2]), LANES)
        self.halo_rows, self.halo_cols = halo.shape[1:]
        widen = lambda t: np.pad(t, ((0, 0), (0, 0), (0, cols - t.shape[2])))
        self.fine_cols, self.coarse_cols = fine.shape[2], coarse.shape[2]
        self.y_cols = cols
        return np.concatenate([widen(fine), widen(coarse), widen(halo)], axis=1)

    def z_tables(self):
        tables = [*self.fine_z(), *[self.coarse_z(level) for level in (1, 2)]]
        cols = 9 * LANES
        self.z_rows = np.cumsum([0] + [t.shape[1] for t in tables])
        return np.concatenate([np.pad(t, ((0, 0), (0, 0), (0, cols - t.shape[2]))) for t in tables], axis=1)

    def fine_matrix(self, ref):
        return ref[: 3 * self.y.length, :][:, : self.fine_cols]

    def coarse_matrix(self, ref):
        start = 3 * self.y.length
        return ref[start : start + self.rows_mixed, :][:, : self.coarse_cols]

    def halo_matrix(self, ref):
        return ref[3 * self.y.length + self.rows_mixed :, :][:, : self.halo_cols]

    def z_matrix(self, ref, number):
        return ref[lax.axis_index("gz"), int(self.z_rows[number]) : int(self.z_rows[number + 1]), :]

    def restrict_z(self):
        z = self.z
        return np.stack(
            [
                right3(place((z.length, LANES), *[(0, self.lane[l], z.partial(l, b).T) for l in (1, 2, 3)]))
                for b in range(z.count)
            ]
        )

    def restrict_y(self):
        y, tables = self.y, []
        for b in range(y.count):
            pieces = [(self.row[l], 0, y.partial(l, b)) for l in (1, 2)]
            cells, inside = y.window(3, b)
            for cell, line in zip(cells[inside > 0], y.partial(3, b)[inside > 0]):
                pieces.append((self.row[3] + cell, 0, line[None]))
            first = y.partial(1, b)
            for k in range(self.kinds):
                kind = self.face_kind(y, 1, b) if self.kinds == 1 else 1 - k
                start = (y.width[1] - FACE) * kind
                for j in range(FACE):
                    pieces.append((self.row_face + 16 * k + self.face_row(j), 0, first[start + j][None]))
            tables.append(left3(place((self.rows_restricted, y.length), *pieces)))
        return np.stack(tables)

    def fine_y(self):
        y, tables = self.y, []
        for b in range(y.count):
            pieces = []
            for s, sigma in enumerate(STENCIL_SIGMAS):
                row = s * y.length
                pieces.append((row, 0, y.mix(0, sigma, b, b)))
                for h in range(self.fine_halos):
                    offset = 1 if h == 0 else y.count - 1
                    source = (b - offset) % y.count
                    start = (y.length - REACH) * self.face_kind(y, offset, source)
                    block = y.mix(0, sigma, b, source)[:, start : start + REACH]
                    pieces.append((row, y.length + 8 * h, block))
            tables.append(left3(place((3 * y.length, up(self.fine_rows, 16)), *pieces)))
        return np.stack(tables)

    def halo_y(self):
        n, cols = self.y.length, up(self.fine_rows, 16)
        rows = [s * n + r for s in range(3) for r in (*range(8), *range(n - 8, n))]
        columns = [c * cols + n + k for c in range(3) for k in range(cols - n)]
        return self.fine_y()[:, rows][:, :, columns]

    def coarse_y(self):
        y, tables = self.y, []
        for b in range(y.count):
            whole = np.zeros((self.rows_mixed, self.coarse_rows))
            for level in (1, 2):
                rows = self.rows1 if level == 1 else self.rows2
                for s, sigma in enumerate(STENCIL_SIGMAS):
                    top = self.group[level] + s * rows
                    for offset in range(y.count):
                        source = (b - offset) % y.count
                        block = y.mix(level, sigma, b, source)
                        if level == 1 and offset:
                            start = (y.width[1] - FACE) * self.face_kind(y, offset, source)
                            block = block[:, start : start + FACE]
                        for j in range(block.shape[1]):
                            slot = self.face_row(j) if level == 1 and offset else j
                            if self.overlay and offset:
                                slot = 24 + slot if slot < 8 else 8 + slot
                            elif offset:
                                slot = 24 + 16 * (offset - 1) + slot
                            whole[top : top + y.width[level], slot] += block[:, j]
            tables.append(left3(whole))
        return np.stack(tables)

    def near_z(self, b, step):
        side = 1 if (b % 2 == 0) == (step == 0) else -1
        return side, b + side if 0 <= b + side < self.z.count else None

    def fine_z(self):
        z, own, pushed = self.z, [], []
        for b in range(z.count):
            mixes = lambda target: [
                w * z.mix(0, sigma, target, b) for sigma, w in zip(STENCIL_SIGMAS, STENCIL_WEIGHTS)
            ]
            own.append(left3t(np.concatenate(mixes(b), axis=1)))
            rows = []
            for step in (0, 1):
                side, target = self.near_z(b, step)
                if target is None:
                    rows.append(np.zeros((8, 3 * z.length)))
                else:
                    rows.append(np.concatenate([m[:8] if side > 0 else m[-8:] for m in mixes(target)], axis=1))
            pushed.append(left3t(np.concatenate(rows, axis=0)))
        return np.stack(own), np.stack(pushed)

    def coarse_z(self, level):
        z, tables = self.z, []
        cols, tall = LANES * len(STENCIL_SIGMAS), self.tall[level]
        for b in range(z.count):

            def mixed(target):
                blocks = [z.mix(level, sigma, target, b) * w * 0.5**level for sigma, w in zip(STENCIL_SIGMAS, STENCIL_WEIGHTS)]
                blocks = [place((z.width[level], LANES), (0, self.lane[level], block)) for block in blocks]
                return np.concatenate(blocks, axis=1)

            pieces = [place((tall, cols), (0, 0, mixed(b)))]
            layers = FACE if level == 1 else 13
            for step in (0, 1):
                side, target = self.near_z(b, step)
                if target is None:
                    pieces.append(np.zeros((16, cols)))
                else:
                    block = mixed(target)
                    pieces.append(place((16, cols), (0, 0, block[:layers] if side > 0 else block[-layers:])))
            whole = np.concatenate(pieces, axis=0)
            tables.append(left3t(place((up(len(whole), 16), cols), (0, 0, whole))))
        return np.stack(tables)

    def top_z(self):
        z, tall, tables = self.z, self.tall[3], []
        for b in range(z.count):
            pieces = []
            for s, (sigma, w) in enumerate(zip(TOP_SIGMAS, TOP_WEIGHTS)):
                for m in range(z.count):
                    pieces.append((tall * s, tall * m, w * z.mix(3, sigma, b, b ^ m)))
            tables.append(left3(place((2 * tall, z.count * tall), *pieces)))
        self.top_cols = tables[0].shape[1]
        widen = up(self.top_cols, LANES) - self.top_cols
        return np.pad(np.stack(tables), ((0, 0), (0, 0), (0, widen)))

    def top_select(self):
        matrix = place((up(self.tall[3], 16), LANES), (0, self.lane[3], np.eye(self.z.width[3])))
        return np.concatenate([matrix, matrix], axis=1).astype(jnp.bfloat16)

    def finish(self):
        x, y, z = self.x, self.y, self.z
        rows = (y.length, self.rows1, self.rows2, self.rows3)
        exact = lambda m: np.asarray(m, dtype=jnp.bfloat16)

        def free(axis, level):
            inner = Axis(5, axis.length)
            return inner.prolong(level, 2)

        flat = []
        for level in (3, 2, 1):
            q = place((rows[level], rows[level - 1]), (0, 0, free(y, level).T))
            matrix = np.kron(free(x, level).T, q)
            if level == 1:
                cells = [x_ * y.length + 8 * t + k for x_, t in self.tiles() for k in range(8)]
                matrix = matrix[:, cells]
            flat.append(exact(matrix))
        joined = np.concatenate([np.pad(m, ((0, -len(m) % 16), (0, 1024 - m.shape[1]))) for m in flat])
        self.flat_rows = np.cumsum([0] + [up(len(m), 16) for m in flat])
        masks = np.zeros((x.count * y.count, 8, 512), np.float32)
        for level in (3, 2, 1):
            for bx in range(x.count):
                for by in range(y.count):
                    inside = np.zeros(rows[level])
                    inside[: y.width[level]] = y.window(level, by)[1]
                    line = np.kron(x.window(level, bx)[1], inside)
                    masks[bx * y.count + by, level, : len(line)] = line
        tall = []
        for b in range(z.count):
            ends = (0, z.length - 8) if b % 2 else (z.length - 8, 0)
            pieces = [(0, 0, free(z, 1).T)] + [(self.tall[1] + 8 * k, end, np.eye(8)) for k, end in enumerate(ends)]
            last = place((up(self.tall[1] + 16, 16), LANES), *pieces)
            parts = [place((up(self.tall[l - 1], 16), LANES), (0, 0, z.prolong(l, b))) for l in (3, 2)]
            tall.append(np.concatenate([last, *parts]))
        return joined, masks, exact(np.stack(tall))


def plane(ref, base, rows, index):
    return ref[pl.ds(base // 8 + rows // 8 * index, rows // 8)].reshape(rows, LANES)


def put_plane(ref, row, value):
    ref[row // 8 : (row + value.shape[0]) // 8] = value.reshape(value.shape[0] // 8, 8, LANES)


def put_flat(ref, row, value):
    for c in range(value.shape[1] // LANES):
        put_plane(ref, row + c * value.shape[0], value[:, c * LANES : (c + 1) * LANES])


def get_flat(ref, row, shape):
    parts = [plane(ref, row, shape[0], c) for c in range(shape[1] // LANES)]
    return jnp.concatenate(parts, axis=1)


def restrict_kernel(plan, q_ref, table_ref, own_ref, top_ref, q_out, y_table_ref, z_table_ref, *rest):
    targets, (mixed, top) = rest[: plan.kinds], rest[plan.kinds :]
    nx, ny, nz = plan.x.length, plan.y.length, plan.z.length
    by, bz = lax.axis_index("gy"), lax.axis_index("gz")
    blocks_z, blocks_y, blocks_table, blocks_top = plan.blocks
    at_y = plan.z.count * blocks_z
    at_table = at_y + plan.y.count * blocks_y
    at_top = at_table + plan.y.count * blocks_table
    at_select = at_top + plan.z.count * blocks_top
    matrix_z = table_ref[pl.ds(blocks_z * bz, blocks_z)].reshape(3 * nz, LANES)
    matrix_y = table_ref[pl.ds(at_y + blocks_y * by, blocks_y)].reshape(16 * blocks_y, LANES)
    matrix_y = matrix_y[:, : 3 * ny]
    q_out[...] = q_ref[...]
    for ref, at in ((y_table_ref, at_table + blocks_table * by), (z_table_ref, at_top + blocks_top * bz)):
        rows = ref.shape[0]
        for c in range(ref.shape[1] // LANES):
            part = table_ref[pl.ds(at + rows // 16 * c, rows // 16)]
            ref[:, c * LANES : (c + 1) * LANES] = part.reshape(rows, LANES)
    for i in range(nx):
        faces = [q_ref[i, ny - REACH :, :], q_ref[i, :REACH, :]]
        if plan.kinds == 1:
            faces = [jnp.where(by == 0, *faces)]
        for face, ref in zip(faces, targets):
            ref[i] = face
    high, low = split(q_ref[...].reshape(nx * ny, nz))
    along_z = dot(jnp.concatenate([high, low, high], axis=1), matrix_z)
    high, low = split(along_z)
    high, low = high.reshape(nx, ny, LANES), low.reshape(nx, ny, LANES)
    for i in range(0, nx, 2):
        pair = [jnp.concatenate([high[j], high[j], low[j]], axis=0) for j in (i, i + 1)]
        both = dot(matrix_y, jnp.concatenate(pair, axis=1))[: plan.rows_restricted]
        mixed[i] = both[:, :LANES]
        mixed[i + 1] = both[:, LANES:]

    brick = lax.axis_index("gx")
    keep_low = jnp.where(brick > 0, 1.0, 0.0).astype(F32)
    keep_high = jnp.where(brick < plan.x.count - 1, 1.0, 0.0).astype(F32)

    def coarsen(planes, level):
        size = nx >> level
        result = {}
        for i in range(LOW[level], LOW[level] + plan.x.width[level]):
            get = lambda j: planes.get(2 * i + j)
            total = None
            for offsets, weight in (((-3, 3), -0.0625), ((-1, 1), 0.5625), ((0,), 1.0)):
                terms = [get(j) for j in offsets if get(j) is not None]
                if terms:
                    term = functools.reduce(jnp.add, terms)
                    term = term * weight if weight != 1.0 else term
                    total = term if total is None else total + term
            if i < 0:
                total = total * keep_low
            elif i >= size:
                total = total * keep_high
            result[i] = total
        return result

    lanes = lax.broadcasted_iota(jnp.int32, (8, LANES), 1)
    in1, in2 = lanes < plan.lane[2], lanes < plan.lane[3]

    def rows_of(start, count, depth):
        levels = [{i: mixed[i, start : start + count, :] for i in range(nx)}]
        for level in range(1, depth + 1):
            levels.append(coarsen(levels[-1], level))
        return levels[-1]

    zero = jnp.zeros((8, LANES), F32)
    first = {r: rows_of(r, 8, 1) for r in range(0, plan.rows1, 8)}
    second = {r: rows_of(plan.row[2] + r, 8, 2) for r in (0, 8)}
    face = [{r: rows_of(plan.row_face + 16 * f + r, 8, 1) for r in (0, 8)} for f in range(plan.kinds)]
    for r in range(0, plan.whole3, 8):
        third = rows_of(plan.row[3] + r, 8, 3)
        for k in range(plan.x.width[3]):
            top[k, r : r + 8, :] = third[LOW[3] + k]
    high, low = split(top[...].reshape(plan.x.width[3] * plan.whole3, LANES))
    select = table_ref[at_select:].reshape(2, -1, LANES)
    select = jnp.concatenate([select[0], select[1]], axis=1)
    flat = dot(select, jnp.concatenate([high, low], axis=1), ((1,), (1,)))[: plan.tall[3]]
    flat = jnp.concatenate([flat, jnp.zeros((plan.tall[3], plan.flat_top - flat.shape[1]), F32)], axis=1)
    start = ((plan.x.length >> 3) * brick + LOW[3]) * plan.whole3
    flat = pltpu.roll(flat, lax.rem(start + plan.flat_top, plan.flat_top), 1)
    top_ref[...] = flat
    for ref in targets:
        put_flat(ref, 8 * nx + 16 * plan.x.width[1], flat)
    for k in range(plan.x.width[1]):
        for r in range(0, plan.rows1, 8):
            one = first[r][LOW[1] + k]
            two = second[r][LOW[2] + k] if r < 16 and k < plan.x.width[2] else zero
            rest_ = jnp.where(in2, two, 0.0)
            own_ref[k, r : r + 8, :] = jnp.where(in1, one, rest_)
            if r < 16:
                for f in range(plan.kinds):
                    targets[f][nx + 2 * k + r // 8] = jnp.where(in1, face[f][r][LOW[1] + k], rest_)


def mask(condition):
    return jnp.where(condition, 1.0, 0.0).astype(F32)


def top_z_kernel(plan, own_ref, *refs):
    others, (table_ref, out_ref) = refs[: plan.z.count - 1], refs[plan.z.count - 1 :]
    value = jnp.concatenate([ref[...] for ref in (own_ref, *others)], axis=0)
    high, low = split(value)
    stacked = jnp.concatenate([high, high, low], axis=0)
    out_ref[...] = dot(table_ref[...][:, : plan.top_cols], stacked)


def extend_kernel(plan, q_ref, own_ref, top_ref, *refs):
    count = plan.y.count - 1
    halos, (ext_ref, top_out, partner_ref, side_ref) = refs[:count], refs[count:]
    x, y = plan.x, plan.y
    odd = lax.axis_index("gx") % 2
    end = x.length - REACH
    near = plan.near_y(halos)
    top = top_ref[...]
    for halo in halos:
        top = top + get_flat(halo, 8 * halo.shape[0] - plan.top_rows, plan.top_shape)
    top_out[...] = top
    put_flat(partner_ref, plan.top_row, top)
    for start, ref in ((end * odd, side_ref), (end * (1 - odd), partner_ref)):
        for i in range(REACH):
            row = plan.fine_rows * i
            put_plane(ref, row, q_ref[start + i])
            for h, halo in enumerate(near):
                ref[(row + y.length) // 8 + h] = halo[start + i]

    base = [8 * halo.shape[0] - plan.top_rows - 16 * x.width[1] for halo in halos]
    for i in range(x.width[1]):
        own = own_ref[i]
        parts = [plane(halo, at, 16, i) for halo, at in zip(halos, base)]
        if plan.overlay:
            halo = parts[0]
            parts = [own[:16], own[16:] + halo[8:], halo[:8]]
        else:
            pad = plan.coarse_rows - 24 - 16 * count
            parts = [own] + parts + ([jnp.zeros((pad, LANES), F32)] if pad else [])
        ext_ref[i] = jnp.concatenate(parts, axis=0)
    lanes = lax.broadcasted_iota(jnp.int32, (1, LANES), 1)
    start = (x.width[1] - FACE) * (1 - odd)
    for p in range(plan.planes):
        row = plan.fine_rows * REACH + plan.coarse_rows * p
        value = jnp.where(lanes < plan.lane[2], ext_ref[start + min(p, FACE - 1)], ext_ref[p])
        put_plane(partner_ref, row, value)


def chip_kernel(plan, ext_ref, pair_ref, top_ref, top_out, *targets):
    x, gx = plan.x, lax.axis_index("gx")
    odd, chip = gx % 2, gx // 2
    lanes = lax.broadcasted_iota(jnp.int32, (1, LANES), 1)
    in1 = lanes < plan.lane[2]
    keep_even, keep_odd = mask(odd == 0), mask(odd == 1)
    top = top_ref[...] + get_flat(pair_ref, plan.top_row, plan.top_shape)
    top_out[...] = top

    def merged(level, cell):
        size, total = x.length >> level, None
        for where_own, where_partner, at in ((keep_even, keep_odd, cell), (keep_odd, keep_even, cell - size)):
            if 0 <= at < x.width[level]:
                value = ext_ref[at] * where_own + plan.pair_plane(pair_ref, at) * where_partner
                total = value if total is None else total + value
        return total

    second = [merged(2, c) for c in range(plan.pair_width[2])]
    start = (x.width[1] - FACE) * odd
    chips = x.count // 2
    for k, ref in zip(range(1, chips), targets):
        high = x.length >> 2
        for p in range(plan.planes):
            if chips == 2:
                two = jnp.where(chip == 0, second[high + p], second[p])
            else:
                two = second[high + p] if k == 1 else second[p]
            first = ext_ref[start + min(p, FACE - 1)]
            put_plane(ref, plan.coarse_rows * p, jnp.where(in1, first, two))


def mix_planes(get, put, count, matrix):
    for i in range(0, count, 2):
        pair = [i, min(i + 1, count - 1)]
        stacked = []
        for j in pair:
            high, low = split(get(j))
            stacked.append(jnp.concatenate([high, high, low], axis=0))
        both = dot(matrix, jnp.concatenate(stacked, axis=1))
        put(i, both[:, :LANES])
        if pair[1] != i:
            put(pair[1], both[:, LANES:])


def stencil(cells, wanted, sigma, reach=REACH):
    result = []
    for i in wanted:
        total = cells.get(i)
        for k in range(1, reach + 1):
            terms = [cells[j] for j in (i - k, i + k) if j in cells]
            if terms:
                term = functools.reduce(jnp.add, terms) * float(np.exp(-((k / sigma) ** 2)))
                total = term if total is None else total + term
        result.append(total)
    return result


def put_ready(ready, sigmas, s, row, value):
    high, low = split(value)
    rows = slice(row, row + value.shape[0])
    step = LANES * sigmas
    ready[rows, s * LANES : (s + 1) * LANES] = high
    ready[rows, step + s * LANES : step + (s + 1) * LANES] = low
    ready[rows, 2 * step + s * LANES : 2 * step + (s + 1) * LANES] = high


def fine_padding(plan):
    pad = up(plan.fine_rows, 16) - plan.fine_rows
    return [jnp.zeros((pad, LANES), F32)] if pad else []


def fine_inner_kernel(plan, q_ref, y_table, z_table, main_ref, push_ref, edge_ref, mixed, ready):
    x, y = plan.x, plan.y
    halo = jnp.zeros((up(plan.fine_rows, 16) - y.length, LANES), F32)

    def put(i, value):
        mixed[i] = value

    mix_planes(lambda i: jnp.concatenate([q_ref[i], halo], axis=0), put, x.length, plan.fine_matrix(y_table))
    inner = range(REACH, x.length - REACH)
    edge = [*range(REACH), *range(x.length - REACH, x.length)]
    half = len(inner) * (y.length - 16)
    for s, sigma in enumerate(STENCIL_SIGMAS):
        row, end = s * y.length, (s + 1) * y.length
        planes = {i: mixed[i, row + 8 : end - 8, :] for i in range(x.length)}
        for i, value in enumerate(stencil(planes, inner, sigma)):
            put_ready(ready, 3, s, i * (y.length - 16), value)
        for i, value in enumerate(stencil(planes, edge, sigma)):
            edge_ref[i, row + 8 : end - 8, :] = value
        ends = lambda i: jnp.concatenate([mixed[i, row : row + 8, :], mixed[i, end - 8 : end, :]], axis=0)
        planes = {i: ends(i) for i in range(x.length)}
        for i, value in enumerate(stencil(planes, inner, sigma)):
            put_ready(ready, 3, s, half + i * 16, value)
        for i, value in enumerate(stencil(planes, edge, sigma)):
            edge_ref[i, row : row + 8, :] = value[:8]
            edge_ref[i, end - 8 : end, :] = value[8:]
    main_ref[...] = dot(ready[...], plan.z_matrix(z_table, 0), ((1,), (1,)))
    push_ref[...] = dot(plan.z_matrix(z_table, 1), ready[...], ((1,), (1,)))


def fine_halo_kernel(plan, edge_ref, y_table, z_table, *refs):
    halos, (main_ref, push_ref, out_ref, mixed, ready) = refs[: plan.y.count - 1], refs[plan.y.count - 1 :]
    x, y = plan.x, plan.y
    near = plan.near_y(halos)
    padding = [jnp.zeros((8, LANES), F32)] * (plan.halo_cols // 24 - len(near))

    def get(i):
        return jnp.concatenate([plane(h, 0, 8, i) for h in near] + padding, axis=0)

    def put(i, value):
        mixed[i] = value

    mix_planes(get, put, x.length, plan.halo_matrix(y_table))
    inner = range(REACH, x.length - REACH)
    edge = [*range(REACH), *range(x.length - REACH, x.length)]
    out_ref[...] = edge_ref[...]
    for s, sigma in enumerate(STENCIL_SIGMAS):
        row, end = s * y.length, (s + 1) * y.length
        planes = {i: mixed[i, 16 * s : 16 * s + 16, :] for i in range(x.length)}
        for i, value in enumerate(stencil(planes, inner, sigma)):
            put_ready(ready, 3, s, i * 16, value)
        for i, value in enumerate(stencil(planes, edge, sigma)):
            out_ref[i, row : row + 8, :] += value[:8]
            out_ref[i, end - 8 : end, :] += value[8:]
    main_ref[...] = dot(ready[...], plan.z_matrix(z_table, 0), ((1,), (1,)))
    push_ref[...] = dot(plan.z_matrix(z_table, 1), ready[...], ((1,), (1,)))


def fine_edge_kernel(plan, partner_ref, side_ref, edge_ref, inner_ref, halo_ref, y_table, z_table, *refs):
    main_ref, push_ref, mixed, ready = refs
    x, y = plan.x, plan.y
    gx = lax.axis_index("gx")
    odd = gx % 2 == 1
    from_partner = mask(odd), mask(~odd)
    from_side = mask(~odd & (gx > 0)), mask(odd & (gx < x.count - 1))
    padding = fine_padding(plan)

    def get(i):
        blocks = []
        for k in range(plan.fine_rows // 8):
            at = plan.fine_rows // 8 * (i % REACH) + k
            blocks.append(partner_ref[at] * from_partner[i // REACH] + side_ref[at] * from_side[i // REACH])
        return jnp.concatenate(blocks + padding, axis=0)

    def put(i, value):
        mixed[i] = value

    mix_planes(get, put, 2 * REACH, plan.fine_matrix(y_table))
    for s, sigma in enumerate(STENCIL_SIGMAS):
        for r in range(0, y.length, 16):
            row = s * y.length + r
            at = lambda i: mixed[i, row : row + 16, :]
            before = {k - REACH: at(k) for k in range(REACH)}
            after = {x.length + k: at(REACH + k) for k in range(REACH)}
            added = stencil(before, range(REACH), sigma)
            added += stencil(after, range(x.length - REACH, x.length), sigma)
            for i, value in enumerate(added):
                put_ready(ready, 3, s, i * y.length + r, edge_ref[i, row : row + 16, :] + value)
    main_ref[...] = dot(ready[...], plan.z_matrix(z_table, 0), ((1,), (1,)))
    pushed = dot(plan.z_matrix(z_table, 1), ready[...], ((1,), (1,)))
    inner = inner_ref[...]
    half = inner.shape[1] - halo_ref.shape[1]
    push_ref[...] = jnp.concatenate([inner[:, :half], inner[:, half:] + halo_ref[...], pushed], axis=1)


def coarse_inner_kernel(plan, ext_ref, pair_ref, y_table, mixed):
    own = plan.x.width[1]

    def put(i, value):
        mixed[i] = value

    mix_planes(lambda i: ext_ref[i] if i < own else plan.pair_plane(pair_ref, i - own), put, own + plan.planes, plan.coarse_matrix(y_table))


def collect(plan, level, inner, outer, row, rows):
    x, gx = plan.x, lax.axis_index("gx")
    odd, chip, chips = gx % 2, gx // 2, plan.x.count // 2
    size, width = x.length >> level, x.width[level]
    start = LOW[level]
    reach = REACH
    cells = {start + k: inner[k, row : row + rows, :] for k in range(width)}

    def add(cell, value, keep):
        if start - reach <= cell < start + width + reach:
            value = value * keep
            cells[cell] = cells[cell] + value if cell in cells else value

    own = x.width[1]
    layers = FACE if level == 1 else width
    for k in range(layers):
        value = inner[own + k, row : row + rows, :]
        add(size + start + k, value, mask(odd == 0))
        add(-size + start + width - layers + k, value, mask(odd == 1))
    for offset in range(1, chips):
        base = plan.planes * (offset - 1)
        at = lambda k: outer[base + k, row : row + rows, :]
        for shift, here in ((-offset, chip >= offset), (chips - offset, chip < offset)):
            if abs(shift) != 1:
                continue
            if level == 1:
                keep = mask(here & (odd == (0 if shift < 0 else 1)))
                first = -size + start + width - FACE if shift < 0 else size + start
                for k in range(FACE):
                    add(first + k, at(k), keep)
                continue
            for core in (0, 1):
                keep = mask(here & (odd == core))
                first = 2 * size * shift - size * core + start
                if level == 2 and shift < 0:
                    first += size
                for k in range(plan.planes):
                    add(first + k, at(k), keep)
    return cells


def coarse_kernel(plan, inner, *refs):
    chips = plan.x.count // 2 - 1
    others, refs = refs[:chips], refs[chips:]
    push_ref, y_table, z_table, partner_ref, side_ref, e1_ref, e2_ref, outer, *ready = refs

    def put(i, value):
        outer[i] = value

    count = plan.planes * chips
    get = lambda i: plane(others[i // plan.planes], 0, plan.coarse_rows, i % plan.planes)
    mix_planes(get, put, count, plan.coarse_matrix(y_table))
    x = plan.x
    results = []
    for level in (1, 2):
        rows = plan.rows1 if level == 1 else plan.rows2
        wanted = range(LOW[level], LOW[level] + x.width[level])
        for s, sigma in enumerate(STENCIL_SIGMAS):
            for r in range(0, rows, 8):
                cells = collect(plan, level, inner, outer, plan.group[level] + s * rows + r, 8)
                for i, value in enumerate(stencil(cells, wanted, sigma)):
                    put_ready(ready[level - 1], 3, s, i * rows + r, value)
        results.append(dot(plan.z_matrix(z_table, level + 1), ready[level - 1][...], ((1,), (1,))))
    one, two = results
    e1_ref[...] = one[: plan.tall[1]]
    e2_ref[...] = two[: plan.tall[2]]
    for n, ref in enumerate((partner_ref, side_ref)):
        ref[:8, :] = push_ref[8 * n : 8 * n + 8, :]
        ref[8:, :] = jnp.zeros((16, ref.shape[1]), F32)
        start = plan.tall[1] + 16 * n
        ref[8:, : plan.flat[1]] = one[start : start + 16]
        start = plan.tall[2] + 16 * n
        ref[8:, 512 : 512 + plan.flat[2]] = two[start : start + 16]


def top_kernel(plan, *refs):
    *values, out_ref = refs
    total = functools.reduce(jnp.add, [v[...] for v in values])
    shape = (plan.flat_top, plan.flat[3])
    source, target = (lax.broadcasted_iota(jnp.int32, shape, d) for d in (0, 1))
    first_x = (plan.x.length >> 3) * lax.axis_index("gx") + LOW[3]
    first_y = (plan.y.length >> 3) * lax.axis_index("gy") + LOW[3]
    apart_x = source // plan.whole3 - target // plan.rows3 - first_x
    apart_y = source % plan.whole3 - target % plan.rows3 - first_y
    square = (apart_x * apart_x + apart_y * apart_y).astype(F32)
    result, tall = None, plan.tall[3]
    for s, sigma in enumerate(TOP_SIGMAS):
        matrix = jnp.exp(square * (-1.0 / sigma**2))
        matrix_high, matrix_low = split(matrix)
        high, low = split(total[s * tall : (s + 1) * tall])
        left = jnp.concatenate([high, low, high], axis=1)
        term = dot(left, jnp.concatenate([matrix_high, matrix_high, matrix_low], axis=0))
        result = term if result is None else result + term
    out_ref[...] = result


def finish_kernel(plan, inner_ref, halo_ref, edge_ref, e1_ref, e2_ref, *refs):
    z = plan.z
    refs = list(refs)
    partner_ref, side_ref, e3_ref, flat, masks, tall, out_ref, e1, e2 = refs
    bz = lax.axis_index("gz")
    column = lax.axis_index("gx") * plan.y.count + lax.axis_index("gy")
    odd = bz % 2
    spread_cols = plan.x.length * plan.y.length
    keep = lambda level: masks[column, level : level + 1, : plan.flat[level]]
    bounds = [int(r) for r in plan.flat_rows]
    flat3, flat2, flat1 = (
        flat[bounds[k] : bounds[k + 1], :][: plan.flat[3 - k], :cols]
        for k, cols in enumerate((plan.flat[2], plan.flat[1], spread_cols))
    )
    e1[...], e2[...] = e1_ref[...], e2_ref[...]
    kept = lax.broadcasted_iota(jnp.int32, (16, 1), 0) < FACE
    for ref, high in ((partner_ref, odd == 0), (side_ref, odd == 1)):
        one = jnp.where(kept, ref[8:, : plan.flat[1]], 0.0)
        two = ref[8:, 512 : 512 + plan.flat[2]]
        for window, value, tall_ in ((e1, one, plan.tall[1]), (e2, two, plan.tall[2])):
            window[:16, :] += value * mask(~high)
            window[tall_ - 16 :, :] += value * mask(high)

    def across(value, matrix):
        high, low = split(value)
        both = dot(jnp.concatenate([high, low], axis=0), matrix)
        return both[: value.shape[0]] + both[value.shape[0] :]

    def along(matrix, value):
        high, low = split(value)
        return dot(matrix, high) + dot(matrix, low)

    start = up(plan.tall[1] + 16, 16)
    middle = start + up(plan.tall[2], 16)
    tall3 = tall[bz, start:middle, :][: plan.tall[2], : plan.tall[3]]
    tall2 = tall[bz, middle:, :][: plan.tall[1], : plan.tall[2]]
    last = tall[bz, :start, :]
    three = e3_ref[...] * keep(3)
    two = (e2[...] + along(tall3, across(three, flat3))) * keep(2)
    one = (e1[...] + along(tall2, across(two, flat2))) * keep(1)
    spread = across(one, flat1)
    rows = jnp.concatenate([spread, partner_ref[:8], side_ref[:8]], axis=0)
    pad = last.shape[0] - rows.shape[0]
    if pad:
        rows = jnp.concatenate([rows, jnp.zeros((pad, rows.shape[1]), F32)], axis=0)
    high, low = split(rows)
    stacked = jnp.concatenate([high, low], axis=0)
    matrix = jnp.concatenate([last, last], axis=0)
    coarse = dot(stacked, matrix, ((0,), (0,)))
    inner = inner_ref.shape[0]
    half = inner - halo_ref.shape[0]
    tiles = plan.y.length // 8
    for k, (x, t) in enumerate(plan.tiles()):
        row = 8 * k
        value = coarse[row : row + 8]
        if row < inner:
            value = value + inner_ref[row : row + 8]
            if row >= half:
                value = value + halo_ref[row - half : row - half + 8]
        else:
            value = value + edge_ref[row - inner : row - inner + 8]
        out_ref[8 * (tiles * x + t) : 8 * (tiles * x + t) + 8] = value


def call(kernel, plan, operands, outs, scratch=()):
    whole = pl.BlockSpec(memory_space=pltpu.VMEM)
    return pl.pallas_call(
        functools.partial(kernel, plan),
        in_specs=[whole] * len(operands),
        out_specs=[whole] * len(outs),
        scratch_shapes=list(scratch),
        out_shape=list(outs),
        compiler_params=pltpu.CompilerParams(vmem_limit_bytes=32 * 2**20),
    )(*[jnp.asarray(o) for o in operands])


def shift(value, axis, offset):
    count = lax.axis_size(axis)
    return lax.ppermute(value, axis, [(i, (i + offset) % count) for i in range(count)])


def swap(value, axes, partner):
    first, second = (lax.axis_size(a) for a in axes)
    pairs = []
    for i in range(first):
        for j in range(second):
            k, m = partner(i, j)
            pairs.append((i * second + j, k * second + m))
    return lax.ppermute(value, axes, pairs)


def side_of(count):
    return lambda i: None if i in (0, count - 1) else i + (1 if i % 2 else -1)


def shards(plan, charges):
    x, y, z = plan.x, plan.y, plan.z
    array = lambda *shape: jax.ShapeDtypeStruct(shape, F32)
    vmem = lambda *shape: pltpu.VMEM(shape, F32)
    ready = lambda rows, sigmas: pltpu.VMEM((rows, 3 * sigmas * LANES), BF)
    side_x, side_z = side_of(x.count), side_of(z.count)
    partner_x = lambda v: swap(v, ("gx", "gy"), lambda i, j: (i ^ 1, j))
    across_x = lambda v: swap(v, ("gx", "gy"), lambda i, j: (i, j ^ 1) if side_x(i) is None else (side_x(i), j))
    partner_z = lambda v: swap(v, ("gx", "gz"), lambda i, j: (i, j ^ 1))
    across_z = lambda v: swap(v, ("gx", "gz"), lambda i, j: (i ^ 1, j) if side_z(j) is None else (i, side_z(j)))

    rows_y = 8 * x.length + 16 * x.width[1] + plan.top_rows
    table = plan.restrict_tables()
    own, top, charges, y_table, top_table, *to_y = call(
        restrict_kernel,
        plan,
        [charges, table],
        [
            array(x.width[1], plan.rows1, LANES),
            array(plan.tall[3], plan.flat_top),
            array(*charges.shape),
            jax.ShapeDtypeStruct((3 * y.length + plan.rows_mixed + plan.halo_rows, plan.y_cols), BF),
            jax.ShapeDtypeStruct((2 * plan.tall[3], up(plan.top_cols, LANES)), BF),
        ]
        + [array(rows_y // 8, 8, LANES)] * plan.kinds,
        [vmem(x.length, plan.rows_restricted, LANES), vmem(x.width[3], plan.whole3, LANES)],
    )
    from_y = []
    for offset in range(1, y.count):
        value = to_y[0 if offset == 1 else -1]
        value = value if offset in (1, y.count - 1) else value[x.length :]
        from_y.append(shift(value, "gy", offset))

    z_table = plan.z_tables()
    inner_cells = (x.length - 2 * REACH) * y.length
    edge_cells = 2 * REACH * y.length
    main_inner, push_inner, edge = call(
        fine_inner_kernel,
        plan,
        [charges, y_table, z_table],
        [array(inner_cells, z.length), array(16, inner_cells), array(2 * REACH, 3 * y.length, LANES)],
        [vmem(x.length, 3 * y.length, LANES), ready(inner_cells, 3)],
    )
    edge, *from_y = lax.optimization_barrier((edge, *from_y))

    ext, top, to_partner, to_side = call(
        extend_kernel,
        plan,
        [charges, own, top, *from_y],
        [
            array(x.width[1], plan.coarse_rows, LANES),
            array(*plan.top_shape),
            array((plan.top_row + plan.top_rows) // 8, 8, LANES),
            array(REACH * plan.fine_rows // 8, 8, LANES),
        ],
    )
    from_side, pair = across_x(to_side), partner_x(to_partner)

    halo_cells = (x.length - 2 * REACH) * 16
    main_halo, push_halo, edge = call(
        fine_halo_kernel,
        plan,
        [edge, y_table, z_table, *from_y],
        [array(halo_cells, z.length), array(16, halo_cells), array(2 * REACH, 3 * y.length, LANES)],
        [vmem(x.length, plan.halo_rows, LANES), ready(halo_cells, 3)],
    )

    chips = x.count // 2
    rows_x = plan.planes * plan.coarse_rows
    top, *to_chips = call(
        chip_kernel,
        plan,
        [ext, pair, top],
        [array(*plan.top_shape)] + [array(rows_x // 8, 8, LANES)] * (chips - 1),
    )
    from_chips = [
        swap(v, ("gx", "gy"), lambda i, j, k=k: ((i + 2 * k) % x.count ^ 1, j))
        for k, v in zip(range(1, chips), to_chips)
    ]
    planes_inner = x.width[1] + plan.planes
    (mixed_inner,) = call(
        coarse_inner_kernel, plan, [ext, pair, y_table], [array(planes_inner, plan.rows_mixed, LANES)]
    )

    tops = [swap(top, ("gx", "gz"), lambda i, j, m=m: (i, j ^ m)) for m in range(1, z.count)]
    (top,) = call(top_z_kernel, plan, [top, *tops, top_table], [array(2 * plan.tall[3], plan.flat_top)])

    main_edge, push = call(
        fine_edge_kernel,
        plan,
        [pair, from_side, edge, push_inner, push_halo, y_table, z_table],
        [array(edge_cells, z.length), array(16, x.length * y.length)],
        [vmem(2 * REACH, 3 * y.length, LANES), ready(edge_cells, 3)],
    )
    push, top = lax.optimization_barrier((push, top))
    window = lambda level: array(plan.tall[level], plan.flat[level])
    to_partner, to_side, e1, e2 = call(
        coarse_kernel,
        plan,
        [mixed_inner, *from_chips, push, y_table, z_table],
        [array(24, 1024), array(24, 1024), window(1), window(2)],
        [vmem(plan.planes * (chips - 1), plan.rows_mixed, LANES), ready(plan.flat[1], 3), ready(plan.flat[2], 3)],
    )
    from_near = [partner_z(to_partner), across_z(to_side)]

    chip_swap = lambda k: lambda i, j: ((i + 2 * k) % x.count ^ 1, j)
    tops = [top] + [swap(top, ("gx", "gy"), chip_swap(k)) for k in range(1, chips)]
    (e3,) = call(top_kernel, plan, tops, [window(3)])

    (potential,) = call(
        finish_kernel,
        plan,
        [main_inner, main_halo, main_edge, e1, e2, *from_near, e3, *plan.finish()],
        [array(x.length * y.length, z.length)],
        [vmem(plan.tall[level], plan.flat[level]) for level in (1, 2)],
    )
    return potential.reshape(charges.shape)


def solution(mesh):
    counts = [mesh.shape[name] for name in ("gx", "gy", "gz")]

    def run(charges):
        plan = Plan(counts, [size // n for size, n in zip(charges.shape, counts)])
        placed = P("gx", "gy", "gz")
        return jax.shard_map(
            functools.partial(shards, plan), mesh=mesh, in_specs=(placed,), out_specs=placed, check_vma=False
        )(charges)

    return run
```

```python
import functools

import jax
import jax.numpy as jnp
import numpy as np
from jax import lax
from jax.experimental import pallas as pl
from jax.experimental.pallas import tpu as pltpu
from jax.sharding import PartitionSpec as P

REACH = 8
STENCIL_SIGMAS = (1.0, 2.0, 3.5)
STENCIL_WEIGHTS = (0.4, 0.1, 0.03)
TOP_SIGMAS = (1.5, 4.0)
TOP_WEIGHTS = (0.03, 0.006)
SPLINE_TAPS = np.array((-1.0, 0.0, 9.0, 16.0, 9.0, 0.0, -1.0)) / 16.0

LOW = (0, -1, -2, -2)
EXTRA = (0, 3, 5, 5)
SLOT = 40
FACE = 11
LANES = 128
BF = jnp.bfloat16
F32 = jnp.float32


def up(value, unit):
    return -(-value // unit) * unit


def band(rows, cols, sigma, reach):
    distance = cols[None, :] - rows[:, None]
    return np.where(abs(distance) <= reach, np.exp(-((distance / sigma) ** 2)), 0.0)


def restriction(size):
    position = np.arange(size)[None, :] - 2 * np.arange(size // 2)[:, None] + 3
    inside = (position >= 0) & (position <= 6)
    return np.where(inside, SPLINE_TAPS[np.clip(position, 0, 6)], 0.0)


class Axis:
    def __init__(self, count, length):
        self.count, self.length = count, length
        self.width = [(length >> level) + EXTRA[level] for level in range(4)]

    def window(self, level, brick):
        size = self.length >> level
        cells = brick * size + LOW[level] + np.arange(self.width[level])
        return cells, ((cells >= 0) & (cells < self.count * size)).astype(float)

    def partial(self, level, brick):
        matrix = np.eye(self.count * self.length)
        for _ in range(level):
            matrix = restriction(matrix.shape[0]) @ matrix
        cells, inside = self.window(level, brick)
        rows = matrix[np.clip(cells, 0, len(matrix) - 1)] * inside[:, None]
        return rows[:, brick * self.length : (brick + 1) * self.length]

    def prolong(self, level, brick):
        matrix = restriction((self.count * self.length) >> (level - 1)).T
        rows, row_inside = self.window(level - 1, brick)
        cols, col_inside = self.window(level, brick)
        taken = matrix[np.clip(rows, 0, len(matrix) - 1)][:, np.clip(cols, 0, matrix.shape[1] - 1)]
        return taken * row_inside[:, None] * col_inside[None, :]

    def mix(self, level, sigma, target, source):
        rows, row_inside = self.window(level, target)
        cols, col_inside = self.window(level, source)
        reach = REACH if level < 3 else self.count * self.length
        return band(rows, cols, sigma, reach) * row_inside[:, None] * col_inside[None, :]


def place(shape, *pieces):
    whole = np.zeros(shape)
    for row, col, block in pieces:
        whole[row : row + block.shape[0], col : col + block.shape[1]] += block
    return whole


def halves(matrix):
    high = matrix.astype(jnp.bfloat16)
    low = (matrix - high.astype(np.float64)).astype(jnp.bfloat16)
    return high, low


def left3(matrix):
    high, low = halves(matrix)
    return np.concatenate([high, low, high], axis=-1)


def left3t(matrix):
    high, low = halves(matrix)
    return np.concatenate([high, high, low], axis=-1)


def right3(matrix):
    high, low = halves(matrix)
    return np.concatenate([high, high, low], axis=-2)


def split(value):
    high = value.astype(BF)
    return high, (value - high.astype(F32)).astype(BF)


def dot(left, right, dims=((1,), (0,))):
    return lax.dot_general(left, right, (dims, ((), ())), preferred_element_type=F32)


class Plan:
    def __init__(self, counts, lengths):
        self.x, self.y, self.z = (Axis(n, length) for n, length in zip(counts, lengths))
        x, y, z = self.x, self.y, self.z
        assert x.count % 2 == 0 and x.count >= 4 and y.count % 2 == 0
        assert z.count >= 4 and z.count & (z.count - 1) == 0
        self.lane = [0, 0, z.width[1], z.width[1] + z.width[2]]
        self.lane_end = self.lane[3] + z.width[3]
        assert self.lane_end <= LANES and z.length == LANES
        self.rows1, self.rows2 = up(y.width[1], 8), up(y.width[2], 16)
        self.rows3, self.whole3 = up(y.width[3], 16), up(y.count * y.length >> 3, 8)
        assert self.rows2 <= 16 and self.rows3 <= 16 and FACE <= 14 and self.rows1 == 24
        self.row = [0, 0, self.rows1, self.rows1 + self.rows2]
        self.row_face = self.rows1 + self.rows2 + self.whole3
        self.kinds = 1 if y.count == 2 else 2
        self.rows_restricted = self.row_face + 16 * self.kinds
        self.overlay = y.count == 2 and y.width[1] + 3 <= self.rows1
        self.coarse_rows = up(24 + 16 * (y.count - 1), 16) if not self.overlay else 32
        self.fine_halos = 1 if y.count == 2 else 2
        self.fine_rows = y.length + 8 * self.fine_halos
        self.pair_width = [w + (x.length >> l) for l, w in enumerate(x.width)]
        self.planes = max(FACE, x.width[2])
        self.half, self.left = LANES // 2, z.width[1] - LANES // 2
        self.face_groups = up(FACE, 2) // 2
        assert 0 < self.left and self.left * FACE <= LANES and z.width[2] <= SLOT
        chips = x.count // 2
        self.near_chips = [1] if chips == 2 else [1, chips - 1]
        self.pair_groups = up(self.planes, 3) // 3
        self.side_rows = REACH * self.fine_rows + (self.face_groups + 1) * self.coarse_rows
        self.flat_top = up((x.count * x.length >> 3) * self.whole3, LANES)
        self.top_shape = 2 * up(z.width[3], 8), self.flat_top
        self.top_rows = self.top_shape[0] * self.flat_top // LANES
        self.top_row = REACH * self.fine_rows + self.planes * self.coarse_rows
        assert self.planes <= x.width[1]
        self.group = [0, 0, 3 * self.rows1]
        self.rows_mixed = up(3 * self.rows1 + 3 * self.rows2, 16)
        self.tall = [0, up(z.width[1], 8), up(z.width[2], 8), up(z.width[3], 8)]
        assert self.tall[1] - 16 == z.width[1] - FACE and self.tall[2] - 16 == z.width[2] - 13
        self.flat = [0, x.width[1] * self.rows1, x.width[2] * self.rows2, x.width[3] * self.rows3]
        assert self.flat[1] <= 512 and self.flat[2] <= 256 and self.flat[3] <= 256

    def face_kind(self, axis, offset, source):
        if axis.count == 2:
            return 1 - source
        return 1 if offset == 1 else 0

    def near_y(self, halos):
        return [halos[0]] if self.y.count == 2 else [halos[0], halos[-1]]

    def tiles(self):
        nx, nt = self.x.length, self.y.length // 8
        inner = range(REACH, nx - REACH)
        edge = [*range(REACH), *range(nx - REACH, nx)]
        order = [(x, t) for x in inner for t in range(1, nt - 1)]
        order += [(x, t) for x in inner for t in (0, nt - 1)]
        return order + [(x, t) for x in edge for t in range(nt)]

    def pair_plane(self, ref, index):
        return plane(ref, self.fine_rows * REACH, self.coarse_rows, index)

    def face_row(self, j):
        return j if j < 8 or not self.overlay else j + 3

    def restrict_tables(self):
        rows = up(self.rows_restricted, 16)
        along_y = np.stack([place((rows, LANES), (0, 0, m)) for m in self.restrict_y().astype(np.float32)])
        parts = [self.restrict_z(), along_y, self.y_tables(), self.top_z()]
        parts = [p.astype(np.float32) for p in parts]
        blocks = []
        for p in parts:
            columns = [p[:, :, c : c + LANES] for c in range(0, p.shape[2], LANES)]
            blocks.append(np.concatenate(columns, axis=1).reshape(len(p), -1, 16, LANES))
        self.blocks = [b.shape[1] for b in blocks]
        table = np.concatenate([b.reshape(-1, 16, LANES) for b in blocks] + [self.top_select().reshape(-1, 2, LANES)
            .transpose(1, 0, 2).reshape(-1, 16, LANES).astype(np.float32)])
        return table.astype(jnp.bfloat16)

    def y_tables(self):
        fine, halo, coarse = self.fine_y(), self.halo_y(), self.coarse_y()
        cols = up(max(fine.shape[2], coarse.shape[2]), LANES)
        self.halo_rows, self.halo_cols = halo.shape[1:]
        widen = lambda t: np.pad(t, ((0, 0), (0, 0), (0, cols - t.shape[2])))
        self.fine_cols, self.coarse_cols = fine.shape[2], coarse.shape[2]
        self.y_cols = cols
        return np.concatenate([widen(fine), widen(coarse), widen(halo)], axis=1)

    def z_tables(self):
        tables = [*self.fine_z(), *[self.coarse_z(level) for level in (1, 2)]]
        cols = 9 * LANES
        self.z_rows = np.cumsum([0] + [t.shape[1] for t in tables])
        return np.concatenate([np.pad(t, ((0, 0), (0, 0), (0, cols - t.shape[2]))) for t in tables], axis=1)

    def fine_matrix(self, ref):
        return ref[: 3 * self.y.length, :][:, : self.fine_cols]

    def coarse_matrix(self, ref):
        start = 3 * self.y.length
        return ref[start : start + self.rows_mixed, :][:, : self.coarse_cols]

    def halo_matrix(self, ref):
        return ref[3 * self.y.length + self.rows_mixed :, :][:, : self.halo_cols]

    def z_matrix(self, ref, number):
        return ref[lax.axis_index("gz"), int(self.z_rows[number]) : int(self.z_rows[number + 1]), :]

    def restrict_z(self):
        z = self.z
        return np.stack(
            [
                right3(place((z.length, LANES), *[(0, self.lane[l], z.partial(l, b).T) for l in (1, 2, 3)]))
                for b in range(z.count)
            ]
        )

    def restrict_y(self):
        y, tables = self.y, []
        for b in range(y.count):
            pieces = [(self.row[l], 0, y.partial(l, b)) for l in (1, 2)]
            cells, inside = y.window(3, b)
            for cell, line in zip(cells[inside > 0], y.partial(3, b)[inside > 0]):
                pieces.append((self.row[3] + cell, 0, line[None]))
            first = y.partial(1, b)
            for k in range(self.kinds):
                kind = self.face_kind(y, 1, b) if self.kinds == 1 else 1 - k
                start = (y.width[1] - FACE) * kind
                for j in range(FACE):
                    pieces.append((self.row_face + 16 * k + self.face_row(j), 0, first[start + j][None]))
            tables.append(left3(place((self.rows_restricted, y.length), *pieces)))
        return np.stack(tables)

    def fine_y(self):
        y, tables = self.y, []
        for b in range(y.count):
            pieces = []
            for s, sigma in enumerate(STENCIL_SIGMAS):
                row = s * y.length
                pieces.append((row, 0, y.mix(0, sigma, b, b)))
                for h in range(self.fine_halos):
                    offset = 1 if h == 0 else y.count - 1
                    source = (b - offset) % y.count
                    start = (y.length - REACH) * self.face_kind(y, offset, source)
                    block = y.mix(0, sigma, b, source)[:, start : start + REACH]
                    pieces.append((row, y.length + 8 * h, block))
            tables.append(left3(place((3 * y.length, up(self.fine_rows, 16)), *pieces)))
        return np.stack(tables)

    def halo_y(self):
        n, cols = self.y.length, up(self.fine_rows, 16)
        rows = [s * n + r for s in range(3) for r in (*range(8), *range(n - 8, n))]
        columns = [c * cols + n + k for c in range(3) for k in range(cols - n)]
        return self.fine_y()[:, rows][:, :, columns]

    def coarse_y(self):
        y, tables = self.y, []
        for b in range(y.count):
            whole = np.zeros((self.rows_mixed, self.coarse_rows))
            for level in (1, 2):
                rows = self.rows1 if level == 1 else self.rows2
                for s, sigma in enumerate(STENCIL_SIGMAS):
                    top = self.group[level] + s * rows
                    for offset in range(y.count):
                        source = (b - offset) % y.count
                        block = y.mix(level, sigma, b, source)
                        if level == 1 and offset:
                            start = (y.width[1] - FACE) * self.face_kind(y, offset, source)
                            block = block[:, start : start + FACE]
                        for j in range(block.shape[1]):
                            slot = self.face_row(j) if level == 1 and offset else j
                            if self.overlay and offset:
                                slot = 24 + slot if slot < 8 else 8 + slot
                            elif offset:
                                slot = 24 + 16 * (offset - 1) + slot
                            whole[top : top + y.width[level], slot] += block[:, j]
            tables.append(left3(whole))
        return np.stack(tables)

    def near_z(self, b, step):
        side = 1 if (b % 2 == 0) == (step == 0) else -1
        return side, b + side if 0 <= b + side < self.z.count else None

    def fine_z(self):
        z, own, pushed = self.z, [], []
        for b in range(z.count):
            mixes = lambda target: [
                w * z.mix(0, sigma, target, b) for sigma, w in zip(STENCIL_SIGMAS, STENCIL_WEIGHTS)
            ]
            own.append(left3t(np.concatenate(mixes(b), axis=1)))
            rows = []
            for step in (0, 1):
                side, target = self.near_z(b, step)
                if target is None:
                    rows.append(np.zeros((8, 3 * z.length)))
                else:
                    rows.append(np.concatenate([m[:8] if side > 0 else m[-8:] for m in mixes(target)], axis=1))
            pushed.append(left3t(np.concatenate(rows, axis=0)))
        return np.stack(own), np.stack(pushed)

    def coarse_z(self, level):
        z, tables = self.z, []
        cols, tall = LANES * len(STENCIL_SIGMAS), self.tall[level]
        for b in range(z.count):

            def mixed(target):
                blocks = [z.mix(level, sigma, target, b) * w * 0.5**level for sigma, w in zip(STENCIL_SIGMAS, STENCIL_WEIGHTS)]
                blocks = [place((z.width[level], LANES), (0, self.lane[level], block)) for block in blocks]
                return np.concatenate(blocks, axis=1)

            pieces = [place((tall, cols), (0, 0, mixed(b)))]
            layers = FACE if level == 1 else 13
            for step in (0, 1):
                side, target = self.near_z(b, step)
                if target is None:
                    pieces.append(np.zeros((16, cols)))
                else:
                    block = mixed(target)
                    pieces.append(place((16, cols), (0, 0, block[:layers] if side > 0 else block[-layers:])))
            whole = np.concatenate(pieces, axis=0)
            tables.append(left3t(place((up(len(whole), 16), cols), (0, 0, whole))))
        return np.stack(tables)

    def top_z(self):
        z, tall, tables = self.z, self.tall[3], []
        for b in range(z.count):
            pieces = []
            for s, (sigma, w) in enumerate(zip(TOP_SIGMAS, TOP_WEIGHTS)):
                for m in range(z.count):
                    pieces.append((tall * s, tall * m, w * z.mix(3, sigma, b, b ^ m)))
            tables.append(left3(place((2 * tall, z.count * tall), *pieces)))
        self.top_cols = tables[0].shape[1]
        widen = up(self.top_cols, LANES) - self.top_cols
        return np.pad(np.stack(tables), ((0, 0), (0, 0), (0, widen)))

    def top_select(self):
        matrix = place((up(self.tall[3], 16), LANES), (0, self.lane[3], np.eye(self.z.width[3])))
        return np.concatenate([matrix, matrix], axis=1).astype(jnp.bfloat16)

    def finish(self):
        x, y, z = self.x, self.y, self.z
        rows = (y.length, self.rows1, self.rows2, self.rows3)
        exact = lambda m: np.asarray(m, dtype=jnp.bfloat16)

        def free(axis, level):
            inner = Axis(5, axis.length)
            return inner.prolong(level, 2)

        flat = []
        for level in (3, 2, 1):
            q = place((rows[level], rows[level - 1]), (0, 0, free(y, level).T))
            matrix = np.kron(free(x, level).T, q)
            if level == 1:
                cells = [x_ * y.length + 8 * t + k for x_, t in self.tiles() for k in range(8)]
                matrix = matrix[:, cells]
            flat.append(exact(matrix))
        joined = np.concatenate([np.pad(m, ((0, -len(m) % 16), (0, 1024 - m.shape[1]))) for m in flat])
        self.flat_rows = np.cumsum([0] + [up(len(m), 16) for m in flat])
        masks = np.zeros((x.count * y.count, 8, 512), np.float32)
        for level in (3, 2, 1):
            for bx in range(x.count):
                for by in range(y.count):
                    inside = np.zeros(rows[level])
                    inside[: y.width[level]] = y.window(level, by)[1]
                    line = np.kron(x.window(level, bx)[1], inside)
                    masks[bx * y.count + by, level, : len(line)] = line
        tall = []
        for b in range(z.count):
            ends = (0, z.length - 8) if b % 2 else (z.length - 8, 0)
            pieces = [(0, 0, free(z, 1).T)] + [(self.tall[1] + 8 * k, end, np.eye(8)) for k, end in enumerate(ends)]
            last = place((up(self.tall[1] + 16, 16), LANES), *pieces)
            parts = [place((up(self.tall[l - 1], 16), LANES), (0, 0, z.prolong(l, b))) for l in (3, 2)]
            tall.append(np.concatenate([last, *parts]))
        return joined, masks, exact(np.stack(tall))


def plane(ref, base, rows, index):
    return ref[pl.ds(base // 8 + rows // 8 * index, rows // 8)].reshape(rows, LANES)


def put_plane(ref, row, value):
    ref[row // 8 : (row + value.shape[0]) // 8] = value.reshape(value.shape[0] // 8, 8, LANES)


def put_flat(ref, row, value):
    for c in range(value.shape[1] // LANES):
        put_plane(ref, row + c * value.shape[0], value[:, c * LANES : (c + 1) * LANES])


def get_flat(ref, row, shape):
    parts = [plane(ref, row, shape[0], c) for c in range(shape[1] // LANES)]
    return jnp.concatenate(parts, axis=1)


def restrict_kernel(plan, q_ref, table_ref, own_ref, top_ref, q_out, y_table_ref, z_table_ref, *rest):
    targets, (mixed, top) = rest[: plan.kinds], rest[plan.kinds :]
    nx, ny, nz = plan.x.length, plan.y.length, plan.z.length
    by, bz = lax.axis_index("gy"), lax.axis_index("gz")
    blocks_z, blocks_y, blocks_table, blocks_top = plan.blocks
    at_y = plan.z.count * blocks_z
    at_table = at_y + plan.y.count * blocks_y
    at_top = at_table + plan.y.count * blocks_table
    at_select = at_top + plan.z.count * blocks_top
    matrix_z = table_ref[pl.ds(blocks_z * bz, blocks_z)].reshape(3 * nz, LANES)
    matrix_y = table_ref[pl.ds(at_y + blocks_y * by, blocks_y)].reshape(16 * blocks_y, LANES)
    matrix_y = matrix_y[:, : 3 * ny]
    q_out[...] = q_ref[...]
    for ref, at in ((y_table_ref, at_table + blocks_table * by), (z_table_ref, at_top + blocks_top * bz)):
        rows = ref.shape[0]
        for c in range(ref.shape[1] // LANES):
            part = table_ref[pl.ds(at + rows // 16 * c, rows // 16)]
            ref[:, c * LANES : (c + 1) * LANES] = part.reshape(rows, LANES)
    for i in range(nx):
        faces = [q_ref[i, ny - REACH :, :], q_ref[i, :REACH, :]]
        if plan.kinds == 1:
            faces = [jnp.where(by == 0, *faces)]
        for face, ref in zip(faces, targets):
            ref[i] = face
    high, low = split(q_ref[...].reshape(nx * ny, nz))
    along_z = dot(jnp.concatenate([high, low, high], axis=1), matrix_z)
    high, low = split(along_z)
    high, low = high.reshape(nx, ny, LANES), low.reshape(nx, ny, LANES)
    for i in range(0, nx, 2):
        pair = [jnp.concatenate([high[j], high[j], low[j]], axis=0) for j in (i, i + 1)]
        both = dot(matrix_y, jnp.concatenate(pair, axis=1))[: plan.rows_restricted]
        mixed[i] = both[:, :LANES]
        mixed[i + 1] = both[:, LANES:]

    brick = lax.axis_index("gx")
    keep_low = jnp.where(brick > 0, 1.0, 0.0).astype(F32)
    keep_high = jnp.where(brick < plan.x.count - 1, 1.0, 0.0).astype(F32)

    def coarsen(planes, level):
        size = nx >> level
        result = {}
        for i in range(LOW[level], LOW[level] + plan.x.width[level]):
            get = lambda j: planes.get(2 * i + j)
            total = None
            for offsets, weight in (((-3, 3), -0.0625), ((-1, 1), 0.5625), ((0,), 1.0)):
                terms = [get(j) for j in offsets if get(j) is not None]
                if terms:
                    term = functools.reduce(jnp.add, terms)
                    term = term * weight if weight != 1.0 else term
                    total = term if total is None else total + term
            if i < 0:
                total = total * keep_low
            elif i >= size:
                total = total * keep_high
            result[i] = total
        return result

    lanes = lax.broadcasted_iota(jnp.int32, (8, LANES), 1)
    in1, in2 = lanes < plan.lane[2], lanes < plan.lane[3]

    def rows_of(start, count, depth):
        levels = [{i: mixed[i, start : start + count, :] for i in range(nx)}]
        for level in range(1, depth + 1):
            levels.append(coarsen(levels[-1], level))
        return levels[-1]

    zero = jnp.zeros((8, LANES), F32)
    first = {r: rows_of(r, 8, 1) for r in range(0, plan.rows1, 8)}
    second = {r: rows_of(plan.row[2] + r, 8, 2) for r in (0, 8)}
    face = [{r: rows_of(plan.row_face + 16 * f + r, 8, 1) for r in (0, 8)} for f in range(plan.kinds)]
    for r in range(0, plan.whole3, 8):
        third = rows_of(plan.row[3] + r, 8, 3)
        for k in range(plan.x.width[3]):
            top[k, r : r + 8, :] = third[LOW[3] + k]
    high, low = split(top[...].reshape(plan.x.width[3] * plan.whole3, LANES))
    select = table_ref[at_select:].reshape(2, -1, LANES)
    select = jnp.concatenate([select[0], select[1]], axis=1)
    flat = dot(select, jnp.concatenate([high, low], axis=1), ((1,), (1,)))[: plan.tall[3]]
    flat = jnp.concatenate([flat, jnp.zeros((plan.tall[3], plan.flat_top - flat.shape[1]), F32)], axis=1)
    start = ((plan.x.length >> 3) * brick + LOW[3]) * plan.whole3
    top_ref[...] = pltpu.roll(flat, lax.rem(start + plan.flat_top, plan.flat_top), 1)
    for k in range(plan.x.width[1]):
        for r in range(0, plan.rows1, 8):
            one = first[r][LOW[1] + k]
            two = second[r][LOW[2] + k] if r < 16 and k < plan.x.width[2] else zero
            rest_ = jnp.where(in2, two, 0.0)
            own_ref[k, r : r + 8, :] = jnp.where(in1, one, rest_)
            if r < 16:
                for f in range(plan.kinds):
                    targets[f][nx + 2 * k + r // 8] = jnp.where(in1, face[f][r][LOW[1] + k], rest_)


def mask(condition):
    return jnp.where(condition, 1.0, 0.0).astype(F32)


def top_z_kernel(plan, own_ref, *refs):
    others, (table_ref, out_ref) = refs[: plan.z.count - 1], refs[plan.z.count - 1 :]
    value = jnp.concatenate([ref[...] for ref in (own_ref, *others)], axis=0)
    high, low = split(value)
    stacked = jnp.concatenate([high, high, low], axis=0)
    out_ref[...] = dot(table_ref[...][:, : plan.top_cols], stacked)


def roll_lanes(value, amount):
    return pltpu.roll(value, amount % LANES, 1)


def pack_faces(plan, faces):
    lanes = lax.broadcasted_iota(jnp.int32, (1, LANES), 1)
    groups = []
    for g in range(plan.face_groups):
        value = faces[g]
        if g + plan.face_groups < FACE:
            value = jnp.where(lanes < plan.half, value, roll_lanes(faces[g + plan.face_groups], plan.half))
        groups.append(value)
    rest = jnp.zeros(faces[0].shape, F32)
    for p, face in enumerate(faces):
        start = plan.left * p
        inside = (lanes >= start) & (lanes < start + plan.left)
        rest = jnp.where(inside, roll_lanes(face, start - plan.half), rest)
    return groups + [rest]


def unpack_face(plan, groups, p):
    lanes = lax.broadcasted_iota(jnp.int32, (1, LANES), 1)
    value = groups[p] if p < plan.face_groups else roll_lanes(groups[p - plan.face_groups], plan.half)
    return jnp.where(lanes < plan.half, value, roll_lanes(groups[-1], plan.half - plan.left * p))


def extend_kernel(plan, q_ref, own_ref, top_ref, *refs):
    count = plan.y.count - 1
    halos, (ext_ref, partner_ref, side_ref) = refs[:count], refs[count:]
    x, y = plan.x, plan.y
    odd = lax.axis_index("gx") % 2
    end = x.length - REACH
    near = plan.near_y(halos)
    put_flat(partner_ref, plan.top_row, top_ref[...])
    for start, ref in ((end * odd, side_ref), (end * (1 - odd), partner_ref)):
        for i in range(REACH):
            row = plan.fine_rows * i
            put_plane(ref, row, q_ref[start + i])
            for h, halo in enumerate(near):
                ref[(row + y.length) // 8 + h] = halo[start + i]

    base = [8 * halo.shape[0] - 16 * x.width[1] for halo in halos]
    for i in range(x.width[1]):
        own = own_ref[i]
        parts = [plane(halo, at, 16, i) for halo, at in zip(halos, base)]
        if plan.overlay:
            halo = parts[0]
            parts = [own[:16], own[16:] + halo[8:], halo[:8]]
        else:
            pad = plan.coarse_rows - 24 - 16 * count
            parts = [own] + parts + ([jnp.zeros((pad, LANES), F32)] if pad else [])
        ext_ref[i] = jnp.concatenate(parts, axis=0)
    lanes = lax.broadcasted_iota(jnp.int32, (1, LANES), 1)
    start = (x.width[1] - FACE) * (1 - odd)
    for p in range(plan.planes):
        row = plan.fine_rows * REACH + plan.coarse_rows * p
        value = jnp.where(lanes < plan.lane[2], ext_ref[start + min(p, FACE - 1)], ext_ref[p])
        put_plane(partner_ref, row, value)
    start = (x.width[1] - FACE) * odd
    for g, value in enumerate(pack_faces(plan, [ext_ref[start + p] for p in range(FACE)])):
        put_plane(side_ref, plan.fine_rows * REACH + plan.coarse_rows * g, value)


def chip_kernel(plan, ext_ref, pair_ref, top_ref, top_out, *targets):
    x, gx = plan.x, lax.axis_index("gx")
    odd, chip = gx % 2, gx // 2
    lanes = lax.broadcasted_iota(jnp.int32, (1, LANES), 1)
    keep_even, keep_odd = mask(odd == 0), mask(odd == 1)
    top = top_ref[...] + get_flat(pair_ref, plan.top_row, plan.top_shape)
    top_out[...] = top

    def merged(level, cell):
        size, total = x.length >> level, None
        for where_own, where_partner, at in ((keep_even, keep_odd, cell), (keep_odd, keep_even, cell - size)):
            if 0 <= at < x.width[level]:
                value = ext_ref[at] * where_own + plan.pair_plane(pair_ref, at) * where_partner
                total = value if total is None else total + value
        return total

    second = [merged(2, c) for c in range(plan.pair_width[2])]
    chips = x.count // 2
    high = x.length >> 2
    for k, ref in zip(range(1, chips), targets):
        for g in range(plan.pair_groups):
            total = None
            for slot, p in enumerate(range(3 * g, min(3 * g + 3, plan.planes))):
                if chips == 2:
                    two = jnp.where(chip == 0, second[high + p], second[p])
                else:
                    two = second[high + p] if k == 1 else second[p]
                two = roll_lanes(two, SLOT * slot - plan.lane[2])
                total = two if slot == 0 else jnp.where(lanes < SLOT * slot, total, two)
            put_plane(ref, plan.coarse_rows * g, total)
        put_flat(ref, plan.coarse_rows * plan.pair_groups, top)


def mix_planes(get, put, count, matrix):
    for i in range(0, count, 2):
        pair = [i, min(i + 1, count - 1)]
        stacked = []
        for j in pair:
            high, low = split(get(j))
            stacked.append(jnp.concatenate([high, high, low], axis=0))
        both = dot(matrix, jnp.concatenate(stacked, axis=1))
        put(i, both[:, :LANES])
        if pair[1] != i:
            put(pair[1], both[:, LANES:])


def stencil(cells, wanted, sigma, reach=REACH):
    result = []
    for i in wanted:
        total = cells.get(i)
        for k in range(1, reach + 1):
            terms = [cells[j] for j in (i - k, i + k) if j in cells]
            if terms:
                term = functools.reduce(jnp.add, terms) * float(np.exp(-((k / sigma) ** 2)))
                total = term if total is None else total + term
        result.append(total)
    return result


def put_ready(ready, sigmas, s, row, value):
    high, low = split(value)
    rows = slice(row, row + value.shape[0])
    step = LANES * sigmas
    ready[rows, s * LANES : (s + 1) * LANES] = high
    ready[rows, step + s * LANES : step + (s + 1) * LANES] = low
    ready[rows, 2 * step + s * LANES : 2 * step + (s + 1) * LANES] = high


def fine_padding(plan):
    pad = up(plan.fine_rows, 16) - plan.fine_rows
    return [jnp.zeros((pad, LANES), F32)] if pad else []


def fine_inner_kernel(plan, q_ref, y_table, inner_ref, edge_ref, mixed):
    x, y = plan.x, plan.y
    halo = jnp.zeros((up(plan.fine_rows, 16) - y.length, LANES), F32)

    def put(i, value):
        mixed[i] = value

    mix_planes(lambda i: jnp.concatenate([q_ref[i], halo], axis=0), put, x.length, plan.fine_matrix(y_table))
    inner = range(REACH, x.length - REACH)
    edge = [*range(REACH), *range(x.length - REACH, x.length)]
    half = len(inner) * (y.length - 16)
    for s, sigma in enumerate(STENCIL_SIGMAS):
        row, end = s * y.length, (s + 1) * y.length
        planes = {i: mixed[i, row + 8 : end - 8, :] for i in range(x.length)}
        step = y.length - 16
        for i, value in enumerate(stencil(planes, inner, sigma)):
            inner_ref[s, i * step : (i + 1) * step, :] = value
        for i, value in enumerate(stencil(planes, edge, sigma)):
            edge_ref[i, row + 8 : end - 8, :] = value
        ends = lambda i: jnp.concatenate([mixed[i, row : row + 8, :], mixed[i, end - 8 : end, :]], axis=0)
        planes = {i: ends(i) for i in range(x.length)}
        for i, value in enumerate(stencil(planes, inner, sigma)):
            inner_ref[s, half + i * 16 : half + i * 16 + 16, :] = value
        for i, value in enumerate(stencil(planes, edge, sigma)):
            edge_ref[i, row : row + 8, :] = value[:8]
            edge_ref[i, end - 8 : end, :] = value[8:]


def fine_halo_kernel(plan, inner_ref, edge_ref, y_table, z_table, *refs):
    halos, (main_ref, push_ref, out_ref, mixed, ready) = refs[: plan.y.count - 1], refs[plan.y.count - 1 :]
    x, y = plan.x, plan.y
    near = plan.near_y(halos)
    padding = [jnp.zeros((8, LANES), F32)] * (plan.halo_cols // 24 - len(near))

    def get(i):
        return jnp.concatenate([plane(h, 0, 8, i) for h in near] + padding, axis=0)

    def put(i, value):
        mixed[i] = value

    mix_planes(get, put, x.length, plan.halo_matrix(y_table))
    inner = range(REACH, x.length - REACH)
    edge = [*range(REACH), *range(x.length - REACH, x.length)]
    out_ref[...] = edge_ref[...]
    half = len(inner) * (y.length - 16)
    for s, sigma in enumerate(STENCIL_SIGMAS):
        row, end = s * y.length, (s + 1) * y.length
        planes = {i: mixed[i, 16 * s : 16 * s + 16, :] for i in range(x.length)}
        for start in range(0, half, 64):
            put_ready(ready, 3, s, start, inner_ref[s, start : start + 64, :])
        for i, value in enumerate(stencil(planes, inner, sigma)):
            start = half + 16 * i
            put_ready(ready, 3, s, start, inner_ref[s, start : start + 16, :] + value)
        for i, value in enumerate(stencil(planes, edge, sigma)):
            out_ref[i, row : row + 8, :] += value[:8]
            out_ref[i, end - 8 : end, :] += value[8:]
    main_ref[...] = dot(ready[...], plan.z_matrix(z_table, 0), ((1,), (1,)))
    push_ref[...] = dot(plan.z_matrix(z_table, 1), ready[...], ((1,), (1,)))


def fine_edge_kernel(plan, partner_ref, side_ref, edge_ref, inner_ref, y_table, z_table, *refs):
    main_ref, push_ref, mixed, ready = refs
    x, y = plan.x, plan.y
    gx = lax.axis_index("gx")
    odd = gx % 2 == 1
    from_partner = mask(odd), mask(~odd)
    from_side = mask(~odd & (gx > 0)), mask(odd & (gx < x.count - 1))
    padding = fine_padding(plan)

    def get(i):
        blocks = []
        for k in range(plan.fine_rows // 8):
            at = plan.fine_rows // 8 * (i % REACH) + k
            blocks.append(partner_ref[at] * from_partner[i // REACH] + side_ref[at] * from_side[i // REACH])
        return jnp.concatenate(blocks + padding, axis=0)

    def put(i, value):
        mixed[i] = value

    mix_planes(get, put, 2 * REACH, plan.fine_matrix(y_table))
    for s, sigma in enumerate(STENCIL_SIGMAS):
        for r in range(0, y.length, 16):
            row = s * y.length + r
            at = lambda i: mixed[i, row : row + 16, :]
            before = {k - REACH: at(k) for k in range(REACH)}
            after = {x.length + k: at(REACH + k) for k in range(REACH)}
            added = stencil(before, range(REACH), sigma)
            added += stencil(after, range(x.length - REACH, x.length), sigma)
            for i, value in enumerate(added):
                put_ready(ready, 3, s, i * y.length + r, edge_ref[i, row : row + 16, :] + value)
    main_ref[...] = dot(ready[...], plan.z_matrix(z_table, 0), ((1,), (1,)))
    pushed = dot(plan.z_matrix(z_table, 1), ready[...], ((1,), (1,)))
    push_ref[...] = jnp.concatenate([inner_ref[...], pushed], axis=1)


def coarse_inner_kernel(plan, ext_ref, pair_ref, y_table, mixed):
    own = plan.x.width[1]

    def put(i, value):
        mixed[i] = value

    mix_planes(lambda i: ext_ref[i] if i < own else plan.pair_plane(pair_ref, i - own), put, own + plan.planes, plan.coarse_matrix(y_table))


def collect(plan, level, inner, outer, row, rows):
    x, gx = plan.x, lax.axis_index("gx")
    odd, chip, chips = gx % 2, gx // 2, plan.x.count // 2
    size, width = x.length >> level, x.width[level]
    start = LOW[level]
    reach = REACH
    cells = {start + k: inner[k, row : row + rows, :] for k in range(width)}

    def add(cell, value, keep):
        if start - reach <= cell < start + width + reach:
            value = value * keep
            cells[cell] = cells[cell] + value if cell in cells else value

    own = x.width[1]
    layers = FACE if level == 1 else width
    for k in range(layers):
        value = inner[own + k, row : row + rows, :]
        add(size + start + k, value, mask(odd == 0))
        add(-size + start + width - layers + k, value, mask(odd == 1))
    if level == 1:
        for k in range(FACE):
            value = outer[k, row : row + rows, :]
            add(-size + start + width - FACE + k, value, mask((chip > 0) & (odd == 0)))
            add(size + start + k, value, mask((chip < chips - 1) & (odd == 1)))
        return cells
    for n, offset in enumerate(plan.near_chips):
        for shift, here in ((-offset, chip >= offset), (chips - offset, chip < offset)):
            if abs(shift) != 1:
                continue
            for core in (0, 1):
                keep = mask(here & (odd == core))
                first = 2 * size * shift - size * core + start + (size if shift < 0 else 0)
                for k in range(plan.planes):
                    add(first + k, outer[plan.planes * n + k, row : row + rows, :], keep)
    return cells


def coarse_kernel(plan, inner, *refs):
    chips = plan.x.count // 2 - 1
    others, refs = refs[:chips], refs[chips:]
    side_in, push_ref, y_table, z_table, partner_ref, side_ref, e1_ref, e2_ref, outer, *ready = refs

    def put(i, value):
        outer[i] = value

    lanes = lax.broadcasted_iota(jnp.int32, (1, LANES), 1)
    groups = [plane(side_in, plan.fine_rows * REACH, plan.coarse_rows, g) for g in range(plan.face_groups + 1)]

    def get(i):
        n, p = i // plan.planes, i % plan.planes
        two = plane(others[plan.near_chips[n] - 1], 0, plan.coarse_rows, p // 3)
        value = roll_lanes(two, plan.lane[2] - SLOT * (p % 3))
        if n == 0 and p < FACE:
            value = jnp.where(lanes < plan.lane[2], unpack_face(plan, groups, p), value)
        return value

    mix_planes(get, put, plan.planes * len(plan.near_chips), plan.coarse_matrix(y_table))
    x = plan.x
    results = []
    for level in (1, 2):
        rows = plan.rows1 if level == 1 else plan.rows2
        wanted = range(LOW[level], LOW[level] + x.width[level])
        for s, sigma in enumerate(STENCIL_SIGMAS):
            for r in range(0, rows, 8):
                cells = collect(plan, level, inner, outer, plan.group[level] + s * rows + r, 8)
                for i, value in enumerate(stencil(cells, wanted, sigma)):
                    put_ready(ready[level - 1], 3, s, i * rows + r, value)
        results.append(dot(plan.z_matrix(z_table, level + 1), ready[level - 1][...], ((1,), (1,))))
    one, two = results
    e1_ref[...] = one[: plan.tall[1]]
    e2_ref[...] = two[: plan.tall[2]]
    for n, ref in enumerate((partner_ref, side_ref)):
        ref[:8, :] = push_ref[8 * n : 8 * n + 8, :]
        ref[8:, :] = jnp.zeros((16, ref.shape[1]), F32)
        start = plan.tall[1] + 16 * n
        ref[8:, : plan.flat[1]] = one[start : start + 16]
        start = plan.tall[2] + 16 * n
        ref[8:, 512 : 512 + plan.flat[2]] = two[start : start + 16]


def top_chips_kernel(plan, top_ref, *refs):
    *others, out_ref = refs
    total = top_ref[...]
    for ref in others:
        total = total + get_flat(ref, plan.coarse_rows * plan.pair_groups, plan.top_shape)
    out_ref[...] = total


def top_kernel(plan, *refs):
    *values, out_ref = refs
    total = functools.reduce(jnp.add, [v[...] for v in values])
    shape = (plan.flat_top, plan.flat[3])
    source, target = (lax.broadcasted_iota(jnp.int32, shape, d) for d in (0, 1))
    first_x = (plan.x.length >> 3) * lax.axis_index("gx") + LOW[3]
    first_y = (plan.y.length >> 3) * lax.axis_index("gy") + LOW[3]
    apart_x = source // plan.whole3 - target // plan.rows3 - first_x
    apart_y = source % plan.whole3 - target % plan.rows3 - first_y
    square = (apart_x * apart_x + apart_y * apart_y).astype(F32)
    result, tall = None, plan.tall[3]
    for s, sigma in enumerate(TOP_SIGMAS):
        matrix = jnp.exp(square * (-1.0 / sigma**2))
        matrix_high, matrix_low = split(matrix)
        high, low = split(total[s * tall : (s + 1) * tall])
        left = jnp.concatenate([high, low, high], axis=1)
        term = dot(left, jnp.concatenate([matrix_high, matrix_high, matrix_low], axis=0))
        result = term if result is None else result + term
    out_ref[...] = result


def finish_kernel(plan, inner_ref, edge_ref, e1_ref, e2_ref, *refs):
    z = plan.z
    refs = list(refs)
    partner_ref, side_ref, e3_ref, flat, masks, tall, out_ref, e1, e2 = refs
    bz = lax.axis_index("gz")
    column = lax.axis_index("gx") * plan.y.count + lax.axis_index("gy")
    odd = bz % 2
    spread_cols = plan.x.length * plan.y.length
    keep = lambda level: masks[column, level : level + 1, : plan.flat[level]]
    bounds = [int(r) for r in plan.flat_rows]
    flat3, flat2, flat1 = (
        flat[bounds[k] : bounds[k + 1], :][: plan.flat[3 - k], :cols]
        for k, cols in enumerate((plan.flat[2], plan.flat[1], spread_cols))
    )
    e1[...], e2[...] = e1_ref[...], e2_ref[...]
    kept = lax.broadcasted_iota(jnp.int32, (16, 1), 0) < FACE
    for ref, high in ((partner_ref, odd == 0), (side_ref, odd == 1)):
        one = jnp.where(kept, ref[8:, : plan.flat[1]], 0.0)
        two = ref[8:, 512 : 512 + plan.flat[2]]
        for window, value, tall_ in ((e1, one, plan.tall[1]), (e2, two, plan.tall[2])):
            window[:16, :] += value * mask(~high)
            window[tall_ - 16 :, :] += value * mask(high)

    def across(value, matrix):
        high, low = split(value)
        both = dot(jnp.concatenate([high, low], axis=0), matrix)
        return both[: value.shape[0]] + both[value.shape[0] :]

    def along(matrix, value):
        high, low = split(value)
        return dot(matrix, high) + dot(matrix, low)

    start = up(plan.tall[1] + 16, 16)
    middle = start + up(plan.tall[2], 16)
    tall3 = tall[bz, start:middle, :][: plan.tall[2], : plan.tall[3]]
    tall2 = tall[bz, middle:, :][: plan.tall[1], : plan.tall[2]]
    last = tall[bz, :start, :]
    three = e3_ref[...] * keep(3)
    two = (e2[...] + along(tall3, across(three, flat3))) * keep(2)
    one = (e1[...] + along(tall2, across(two, flat2))) * keep(1)
    spread = across(one, flat1)
    rows = jnp.concatenate([spread, partner_ref[:8], side_ref[:8]], axis=0)
    pad = last.shape[0] - rows.shape[0]
    if pad:
        rows = jnp.concatenate([rows, jnp.zeros((pad, rows.shape[1]), F32)], axis=0)
    high, low = split(rows)
    stacked = jnp.concatenate([high, low], axis=0)
    matrix = jnp.concatenate([last, last], axis=0)
    coarse = dot(stacked, matrix, ((0,), (0,)))
    inner = inner_ref.shape[0]
    tiles = plan.y.length // 8
    for k, (x, t) in enumerate(plan.tiles()):
        row = 8 * k
        value = coarse[row : row + 8]
        if row < inner:
            value = value + inner_ref[row : row + 8]
        else:
            value = value + edge_ref[row - inner : row - inner + 8]
        out_ref[8 * (tiles * x + t) : 8 * (tiles * x + t) + 8] = value


def call(kernel, plan, operands, outs, scratch=()):
    whole = pl.BlockSpec(memory_space=pltpu.VMEM)
    return pl.pallas_call(
        functools.partial(kernel, plan),
        in_specs=[whole] * len(operands),
        out_specs=[whole] * len(outs),
        scratch_shapes=list(scratch),
        out_shape=list(outs),
        compiler_params=pltpu.CompilerParams(vmem_limit_bytes=32 * 2**20),
    )(*[jnp.asarray(o) for o in operands])


def shift(value, axis, offset):
    count = lax.axis_size(axis)
    return lax.ppermute(value, axis, [(i, (i + offset) % count) for i in range(count)])


def swap(value, axes, partner):
    first, second = (lax.axis_size(a) for a in axes)
    pairs = []
    for i in range(first):
        for j in range(second):
            k, m = partner(i, j)
            pairs.append((i * second + j, k * second + m))
    return lax.ppermute(value, axes, pairs)


def side_of(count):
    return lambda i: None if i in (0, count - 1) else i + (1 if i % 2 else -1)


def shards(plan, charges):
    x, y, z = plan.x, plan.y, plan.z
    array = lambda *shape: jax.ShapeDtypeStruct(shape, F32)
    vmem = lambda *shape: pltpu.VMEM(shape, F32)
    ready = lambda rows, sigmas: pltpu.VMEM((rows, 3 * sigmas * LANES), BF)
    side_x, side_z = side_of(x.count), side_of(z.count)
    partner_x = lambda v: swap(v, ("gx", "gy"), lambda i, j: (i ^ 1, j))
    across_x = lambda v: swap(v, ("gx", "gy"), lambda i, j: (i, j ^ 1) if side_x(i) is None else (side_x(i), j))
    partner_z = lambda v: swap(v, ("gx", "gz"), lambda i, j: (i, j ^ 1))
    across_z = lambda v: swap(v, ("gx", "gz"), lambda i, j: (i ^ 1, j) if side_z(j) is None else (i, side_z(j)))

    rows_y = 8 * x.length + 16 * x.width[1]
    table = plan.restrict_tables()
    own, top, charges, y_table, top_table, *to_y = call(
        restrict_kernel,
        plan,
        [charges, table],
        [
            array(x.width[1], plan.rows1, LANES),
            array(plan.tall[3], plan.flat_top),
            array(*charges.shape),
            jax.ShapeDtypeStruct((3 * y.length + plan.rows_mixed + plan.halo_rows, plan.y_cols), BF),
            jax.ShapeDtypeStruct((2 * plan.tall[3], up(plan.top_cols, LANES)), BF),
        ]
        + [array(rows_y // 8, 8, LANES)] * plan.kinds,
        [vmem(x.length, plan.rows_restricted, LANES), vmem(x.width[3], plan.whole3, LANES)],
    )
    from_y = []
    for offset in range(1, y.count):
        value = to_y[0 if offset == 1 else -1]
        value = value if offset in (1, y.count - 1) else value[x.length :]
        from_y.append(shift(value, "gy", offset))

    tops = [swap(top, ("gx", "gz"), lambda i, j, m=m: (i, j ^ m)) for m in range(1, z.count)]
    (top,) = call(top_z_kernel, plan, [top, *tops, top_table], [array(*plan.top_shape)])

    z_table = plan.z_tables()
    inner_cells = (x.length - 2 * REACH) * y.length
    edge_cells = 2 * REACH * y.length
    inner, edge = call(
        fine_inner_kernel,
        plan,
        [charges, y_table],
        [array(3, inner_cells, LANES), array(2 * REACH, 3 * y.length, LANES)],
        [vmem(x.length, 3 * y.length, LANES)],
    )
    edge, *from_y = lax.optimization_barrier((edge, *from_y))

    ext, to_partner, to_side = call(
        extend_kernel,
        plan,
        [charges, own, top, *from_y],
        [
            array(x.width[1], plan.coarse_rows, LANES),
            array((plan.top_row + plan.top_rows) // 8, 8, LANES),
            array(plan.side_rows // 8, 8, LANES),
        ],
    )
    from_side, pair = across_x(to_side), partner_x(to_partner)

    main_inner, push_inner, edge = call(
        fine_halo_kernel,
        plan,
        [inner, edge, y_table, z_table, *from_y],
        [array(inner_cells, z.length), array(16, inner_cells), array(2 * REACH, 3 * y.length, LANES)],
        [vmem(x.length, plan.halo_rows, LANES), ready(inner_cells, 3)],
    )

    chips = x.count // 2
    rows_x = plan.pair_groups * plan.coarse_rows + plan.top_rows
    top, *to_chips = call(
        chip_kernel,
        plan,
        [ext, pair, top],
        [array(*plan.top_shape)] + [array(rows_x // 8, 8, LANES)] * (chips - 1),
    )
    from_chips = [
        swap(v, ("gx", "gy"), lambda i, j, k=k: ((i + 2 * k) % x.count ^ 1, j))
        for k, v in zip(range(1, chips), to_chips)
    ]
    planes_inner = x.width[1] + plan.planes
    (mixed_inner,) = call(
        coarse_inner_kernel, plan, [ext, pair, y_table], [array(planes_inner, plan.rows_mixed, LANES)]
    )

    main_edge, push = call(
        fine_edge_kernel,
        plan,
        [pair, from_side, edge, push_inner, y_table, z_table],
        [array(edge_cells, z.length), array(16, x.length * y.length)],
        [vmem(2 * REACH, 3 * y.length, LANES), ready(edge_cells, 3)],
    )
    window = lambda level: array(plan.tall[level], plan.flat[level])
    to_partner, to_side, e1, e2 = call(
        coarse_kernel,
        plan,
        [mixed_inner, *from_chips, from_side, push, y_table, z_table],
        [array(24, 1024), array(24, 1024), window(1), window(2)],
        [vmem(plan.planes * len(plan.near_chips), plan.rows_mixed, LANES), ready(plan.flat[1], 3), ready(plan.flat[2], 3)],
    )
    from_near = [partner_z(to_partner), across_z(to_side)]

    (top,) = call(top_chips_kernel, plan, [top, *from_chips], [array(*top.shape)])
    tops = [top] + [shift(top, "gy", offset) for offset in range(1, y.count)]
    (e3,) = call(top_kernel, plan, tops, [window(3)])

    (potential,) = call(
        finish_kernel,
        plan,
        [main_inner, main_edge, e1, e2, *from_near, e3, *plan.finish()],
        [array(x.length * y.length, z.length)],
        [vmem(plan.tall[level], plan.flat[level]) for level in (1, 2)],
    )
    return potential.reshape(charges.shape)


def solution(mesh):
    counts = [mesh.shape[name] for name in ("gx", "gy", "gz")]

    def run(charges):
        plan = Plan(counts, [size // n for size, n in zip(charges.shape, counts)])
        placed = P("gx", "gy", "gz")
        return jax.shard_map(
            functools.partial(shards, plan), mesh=mesh, in_specs=(placed,), out_specs=placed, check_vma=False
        )(charges)

    return run
```

```python
import functools

import jax
import jax.numpy as jnp
import numpy as np
from jax import lax
from jax.experimental import pallas as pl
from jax.experimental.pallas import tpu as pltpu
from jax.sharding import PartitionSpec as P

REACH = 8
STENCIL_SIGMAS = (1.0, 2.0, 3.5)
STENCIL_WEIGHTS = (0.4, 0.1, 0.03)
TOP_SIGMAS = (1.5, 4.0)
TOP_WEIGHTS = (0.03, 0.006)
SPLINE_TAPS = np.array((-1.0, 0.0, 9.0, 16.0, 9.0, 0.0, -1.0)) / 16.0

LOW = (0, -1, -2, -2)
EXTRA = (0, 3, 5, 5)
SLOT = 40
FACE = 11
LANES = 128
BF = jnp.bfloat16
F32 = jnp.float32


def up(value, unit):
    return -(-value // unit) * unit


def band(rows, cols, sigma, reach):
    distance = cols[None, :] - rows[:, None]
    return np.where(abs(distance) <= reach, np.exp(-((distance / sigma) ** 2)), 0.0)


def restriction(size):
    position = np.arange(size)[None, :] - 2 * np.arange(size // 2)[:, None] + 3
    inside = (position >= 0) & (position <= 6)
    return np.where(inside, SPLINE_TAPS[np.clip(position, 0, 6)], 0.0)


class Axis:
    def __init__(self, count, length):
        self.count, self.length = count, length
        self.width = [(length >> level) + EXTRA[level] for level in range(4)]

    def window(self, level, brick):
        size = self.length >> level
        cells = brick * size + LOW[level] + np.arange(self.width[level])
        return cells, ((cells >= 0) & (cells < self.count * size)).astype(float)

    def partial(self, level, brick):
        matrix = np.eye(self.count * self.length)
        for _ in range(level):
            matrix = restriction(matrix.shape[0]) @ matrix
        cells, inside = self.window(level, brick)
        rows = matrix[np.clip(cells, 0, len(matrix) - 1)] * inside[:, None]
        return rows[:, brick * self.length : (brick + 1) * self.length]

    def prolong(self, level, brick):
        matrix = restriction((self.count * self.length) >> (level - 1)).T
        rows, row_inside = self.window(level - 1, brick)
        cols, col_inside = self.window(level, brick)
        taken = matrix[np.clip(rows, 0, len(matrix) - 1)][:, np.clip(cols, 0, matrix.shape[1] - 1)]
        return taken * row_inside[:, None] * col_inside[None, :]

    def mix(self, level, sigma, target, source):
        rows, row_inside = self.window(level, target)
        cols, col_inside = self.window(level, source)
        reach = REACH if level < 3 else self.count * self.length
        return band(rows, cols, sigma, reach) * row_inside[:, None] * col_inside[None, :]


def place(shape, *pieces):
    whole = np.zeros(shape)
    for row, col, block in pieces:
        whole[row : row + block.shape[0], col : col + block.shape[1]] += block
    return whole


def halves(matrix):
    high = matrix.astype(jnp.bfloat16)
    low = (matrix - high.astype(np.float64)).astype(jnp.bfloat16)
    return high, low


def left3(matrix):
    high, low = halves(matrix)
    return np.concatenate([high, low, high], axis=-1)


def left3t(matrix):
    high, low = halves(matrix)
    return np.concatenate([high, high, low], axis=-1)


def right3(matrix):
    high, low = halves(matrix)
    return np.concatenate([high, high, low], axis=-2)


def split(value):
    high = value.astype(BF)
    return high, (value - high.astype(F32)).astype(BF)


def dot(left, right, dims=((1,), (0,))):
    return lax.dot_general(left, right, (dims, ((), ())), preferred_element_type=F32)


class Plan:
    def __init__(self, counts, lengths):
        self.x, self.y, self.z = (Axis(n, length) for n, length in zip(counts, lengths))
        x, y, z = self.x, self.y, self.z
        assert x.count % 2 == 0 and x.count >= 4 and y.count % 2 == 0
        assert z.count >= 4 and z.count & (z.count - 1) == 0
        self.lane = [0, 0, z.width[1], z.width[1] + z.width[2]]
        self.lane_end = self.lane[3] + z.width[3]
        assert self.lane_end <= LANES and z.length == LANES
        self.rows1, self.rows2 = up(y.width[1], 8), up(y.width[2], 16)
        self.rows3, self.whole3 = up(y.width[3], 16), up(y.count * y.length >> 3, 8)
        assert self.rows2 <= 16 and self.rows3 <= 16 and FACE <= 14 and self.rows1 == 24
        self.row = [0, 0, self.rows1, self.rows1 + self.rows2]
        self.row_face = self.rows1 + self.rows2 + self.whole3
        self.kinds = 1 if y.count == 2 else 2
        self.rows_restricted = self.row_face + 16 * self.kinds
        self.overlay = y.count == 2 and y.width[1] + 3 <= self.rows1
        self.coarse_rows = up(24 + 16 * (y.count - 1), 16) if not self.overlay else 32
        self.fine_halos = 1 if y.count == 2 else 2
        self.fine_rows = y.length + 8 * self.fine_halos
        self.pair_width = [w + (x.length >> l) for l, w in enumerate(x.width)]
        self.planes = max(FACE, x.width[2])
        self.half, self.left = LANES // 2, z.width[1] - LANES // 2
        self.face_groups = up(FACE, 2) // 2
        assert 0 < self.left and self.left * FACE <= LANES and z.width[2] <= SLOT
        chips = x.count // 2
        self.near_chips = [1] if chips == 2 else [1, chips - 1]
        self.pair_groups = up(self.planes, 3) // 3
        self.side_rows = REACH * self.fine_rows + (self.face_groups + 1) * self.coarse_rows
        self.flat_top = up((x.count * x.length >> 3) * self.whole3, LANES)
        self.top_shape = 2 * up(z.width[3], 8), self.flat_top
        self.top_rows = self.top_shape[0] * self.flat_top // LANES
        self.top_row = REACH * self.fine_rows + self.planes * self.coarse_rows
        assert self.planes <= x.width[1]
        self.group = [0, 0, 3 * self.rows1]
        self.rows_mixed = up(3 * self.rows1 + 3 * self.rows2, 16)
        self.tall = [0, up(z.width[1], 8), up(z.width[2], 8), up(z.width[3], 8)]
        assert self.tall[1] - 16 == z.width[1] - FACE and self.tall[2] - 16 == z.width[2] - 13
        self.flat = [0, x.width[1] * self.rows1, x.width[2] * self.rows2, x.width[3] * self.rows3]
        assert self.flat[1] <= 512 and self.flat[2] <= 256 and self.flat[3] <= 256

    def face_kind(self, axis, offset, source):
        if axis.count == 2:
            return 1 - source
        return 1 if offset == 1 else 0

    def near_y(self, halos):
        return [halos[0]] if self.y.count == 2 else [halos[0], halos[-1]]

    def tiles(self):
        nx, nt = self.x.length, self.y.length // 8
        inner = range(REACH, nx - REACH)
        edge = [*range(REACH), *range(nx - REACH, nx)]
        order = [(x, t) for x in inner for t in range(1, nt - 1)]
        order += [(x, t) for x in inner for t in (0, nt - 1)]
        return order + [(x, t) for x in edge for t in range(nt)]

    def pair_plane(self, ref, index):
        return plane(ref, self.fine_rows * REACH, self.coarse_rows, index)

    def face_row(self, j):
        return j if j < 8 or not self.overlay else j + 3

    def restrict_tables(self):
        rows = up(self.rows_restricted, 16)
        along_y = np.stack([place((rows, LANES), (0, 0, m)) for m in self.restrict_y().astype(np.float32)])
        parts = [self.restrict_z(), along_y, self.y_tables(), self.top_z()]
        parts = [p.astype(np.float32) for p in parts]
        blocks = []
        for p in parts:
            columns = [p[:, :, c : c + LANES] for c in range(0, p.shape[2], LANES)]
            blocks.append(np.concatenate(columns, axis=1).reshape(len(p), -1, 16, LANES))
        self.blocks = [b.shape[1] for b in blocks]
        table = np.concatenate([b.reshape(-1, 16, LANES) for b in blocks] + [self.top_select().reshape(-1, 2, LANES)
            .transpose(1, 0, 2).reshape(-1, 16, LANES).astype(np.float32)])
        return table.astype(jnp.bfloat16)

    def y_tables(self):
        fine, halo, coarse = self.fine_y(), self.halo_y(), self.coarse_y()
        cols = up(max(fine.shape[2], coarse.shape[2]), LANES)
        self.halo_rows, self.halo_cols = halo.shape[1:]
        widen = lambda t: np.pad(t, ((0, 0), (0, 0), (0, cols - t.shape[2])))
        self.fine_cols, self.coarse_cols = fine.shape[2], coarse.shape[2]
        self.y_cols = cols
        return np.concatenate([widen(fine), widen(coarse), widen(halo)], axis=1)

    def z_tables(self):
        tables = [*self.fine_z(), *[self.coarse_z(level) for level in (1, 2)]]
        cols = 9 * LANES
        self.z_rows = np.cumsum([0] + [t.shape[1] for t in tables])
        return np.concatenate([np.pad(t, ((0, 0), (0, 0), (0, cols - t.shape[2]))) for t in tables], axis=1)

    def fine_matrix(self, ref):
        return ref[: 3 * self.y.length, :][:, : self.fine_cols]

    def coarse_matrix(self, ref):
        start = 3 * self.y.length
        return ref[start : start + self.rows_mixed, :][:, : self.coarse_cols]

    def halo_matrix(self, ref):
        return ref[3 * self.y.length + self.rows_mixed :, :][:, : self.halo_cols]

    def z_matrix(self, ref, number):
        return ref[lax.axis_index("gz"), int(self.z_rows[number]) : int(self.z_rows[number + 1]), :]

    def restrict_z(self):
        z = self.z
        return np.stack(
            [
                right3(place((z.length, LANES), *[(0, self.lane[l], z.partial(l, b).T) for l in (1, 2, 3)]))
                for b in range(z.count)
            ]
        )

    def restrict_y(self):
        y, tables = self.y, []
        for b in range(y.count):
            pieces = [(self.row[l], 0, y.partial(l, b)) for l in (1, 2)]
            cells, inside = y.window(3, b)
            for cell, line in zip(cells[inside > 0], y.partial(3, b)[inside > 0]):
                pieces.append((self.row[3] + cell, 0, line[None]))
            first = y.partial(1, b)
            for k in range(self.kinds):
                kind = self.face_kind(y, 1, b) if self.kinds == 1 else 1 - k
                start = (y.width[1] - FACE) * kind
                for j in range(FACE):
                    pieces.append((self.row_face + 16 * k + self.face_row(j), 0, first[start + j][None]))
            tables.append(left3(place((self.rows_restricted, y.length), *pieces)))
        return np.stack(tables)

    def fine_y(self):
        y, tables = self.y, []
        for b in range(y.count):
            pieces = []
            for s, sigma in enumerate(STENCIL_SIGMAS):
                row = s * y.length
                pieces.append((row, 0, y.mix(0, sigma, b, b)))
                for h in range(self.fine_halos):
                    offset = 1 if h == 0 else y.count - 1
                    source = (b - offset) % y.count
                    start = (y.length - REACH) * self.face_kind(y, offset, source)
                    block = y.mix(0, sigma, b, source)[:, start : start + REACH]
                    pieces.append((row, y.length + 8 * h, block))
            tables.append(left3(place((3 * y.length, up(self.fine_rows, 16)), *pieces)))
        return np.stack(tables)

    def halo_y(self):
        n, cols = self.y.length, up(self.fine_rows, 16)
        rows = [s * n + r for s in range(3) for r in (*range(8), *range(n - 8, n))]
        columns = [c * cols + n + k for c in range(3) for k in range(cols - n)]
        return self.fine_y()[:, rows][:, :, columns]

    def coarse_y(self):
        y, tables = self.y, []
        for b in range(y.count):
            whole = np.zeros((self.rows_mixed, self.coarse_rows))
            for level in (1, 2):
                rows = self.rows1 if level == 1 else self.rows2
                for s, sigma in enumerate(STENCIL_SIGMAS):
                    top = self.group[level] + s * rows
                    for offset in range(y.count):
                        source = (b - offset) % y.count
                        block = y.mix(level, sigma, b, source)
                        if level == 1 and offset:
                            start = (y.width[1] - FACE) * self.face_kind(y, offset, source)
                            block = block[:, start : start + FACE]
                        for j in range(block.shape[1]):
                            slot = self.face_row(j) if level == 1 and offset else j
                            if self.overlay and offset:
                                slot = 24 + slot if slot < 8 else 8 + slot
                            elif offset:
                                slot = 24 + 16 * (offset - 1) + slot
                            whole[top : top + y.width[level], slot] += block[:, j]
            tables.append(left3(whole))
        return np.stack(tables)

    def near_z(self, b, step):
        side = 1 if (b % 2 == 0) == (step == 0) else -1
        return side, b + side if 0 <= b + side < self.z.count else None

    def fine_z(self):
        z, own, pushed = self.z, [], []
        for b in range(z.count):
            mixes = lambda target: [
                w * z.mix(0, sigma, target, b) for sigma, w in zip(STENCIL_SIGMAS, STENCIL_WEIGHTS)
            ]
            own.append(left3t(np.concatenate(mixes(b), axis=1)))
            rows = []
            for step in (0, 1):
                side, target = self.near_z(b, step)
                if target is None:
                    rows.append(np.zeros((8, 3 * z.length)))
                else:
                    rows.append(np.concatenate([m[:8] if side > 0 else m[-8:] for m in mixes(target)], axis=1))
            pushed.append(left3t(np.concatenate(rows, axis=0)))
        return np.stack(own), np.stack(pushed)

    def coarse_z(self, level):
        z, tables = self.z, []
        cols, tall = LANES * len(STENCIL_SIGMAS), self.tall[level]
        for b in range(z.count):

            def mixed(target):
                blocks = [z.mix(level, sigma, target, b) * w * 0.5**level for sigma, w in zip(STENCIL_SIGMAS, STENCIL_WEIGHTS)]
                blocks = [place((z.width[level], LANES), (0, self.lane[level], block)) for block in blocks]
                return np.concatenate(blocks, axis=1)

            pieces = [place((tall, cols), (0, 0, mixed(b)))]
            layers = FACE if level == 1 else 13
            for step in (0, 1):
                side, target = self.near_z(b, step)
                if target is None:
                    pieces.append(np.zeros((16, cols)))
                else:
                    block = mixed(target)
                    pieces.append(place((16, cols), (0, 0, block[:layers] if side > 0 else block[-layers:])))
            whole = np.concatenate(pieces, axis=0)
            tables.append(left3t(place((up(len(whole), 16), cols), (0, 0, whole))))
        return np.stack(tables)

    def top_z(self):
        z, tall, tables = self.z, self.tall[3], []
        for b in range(z.count):
            pieces = []
            for s, (sigma, w) in enumerate(zip(TOP_SIGMAS, TOP_WEIGHTS)):
                for m in range(z.count):
                    pieces.append((tall * s, tall * m, w * z.mix(3, sigma, b, b ^ m)))
            tables.append(left3(place((2 * tall, z.count * tall), *pieces)))
        self.top_cols = tables[0].shape[1]
        widen = up(self.top_cols, LANES) - self.top_cols
        return np.pad(np.stack(tables), ((0, 0), (0, 0), (0, widen)))

    def top_select(self):
        matrix = place((up(self.tall[3], 16), LANES), (0, self.lane[3], np.eye(self.z.width[3])))
        return np.concatenate([matrix, matrix], axis=1).astype(jnp.bfloat16)

    def finish(self):
        x, y, z = self.x, self.y, self.z
        rows = (y.length, self.rows1, self.rows2, self.rows3)
        exact = lambda m: np.asarray(m, dtype=jnp.bfloat16)

        def free(axis, level):
            inner = Axis(5, axis.length)
            return inner.prolong(level, 2)

        flat = []
        for level in (3, 2, 1):
            q = place((rows[level], rows[level - 1]), (0, 0, free(y, level).T))
            matrix = np.kron(free(x, level).T, q)
            if level == 1:
                cells = [x_ * y.length + 8 * t + k for x_, t in self.tiles() for k in range(8)]
                matrix = matrix[:, cells]
            flat.append(exact(matrix))
        joined = np.concatenate([np.pad(m, ((0, -len(m) % 16), (0, 1024 - m.shape[1]))) for m in flat])
        self.flat_rows = np.cumsum([0] + [up(len(m), 16) for m in flat])
        masks = np.zeros((x.count * y.count, 8, 512), np.float32)
        for level in (3, 2, 1):
            for bx in range(x.count):
                for by in range(y.count):
                    inside = np.zeros(rows[level])
                    inside[: y.width[level]] = y.window(level, by)[1]
                    line = np.kron(x.window(level, bx)[1], inside)
                    masks[bx * y.count + by, level, : len(line)] = line
        tall = []
        for b in range(z.count):
            ends = (0, z.length - 8) if b % 2 else (z.length - 8, 0)
            pieces = [(0, 0, free(z, 1).T)] + [(self.tall[1] + 8 * k, end, np.eye(8)) for k, end in enumerate(ends)]
            last = place((up(self.tall[1] + 16, 16), LANES), *pieces)
            parts = [place((up(self.tall[l - 1], 16), LANES), (0, 0, z.prolong(l, b))) for l in (3, 2)]
            tall.append(np.concatenate([last, *parts]))
        return joined, masks, exact(np.stack(tall))


def plane(ref, base, rows, index):
    return ref[pl.ds(base // 8 + rows // 8 * index, rows // 8)].reshape(rows, LANES)


def put_plane(ref, row, value):
    ref[row // 8 : (row + value.shape[0]) // 8] = value.reshape(value.shape[0] // 8, 8, LANES)


def put_flat(ref, row, value):
    for c in range(value.shape[1] // LANES):
        put_plane(ref, row + c * value.shape[0], value[:, c * LANES : (c + 1) * LANES])


def get_flat(ref, row, shape):
    parts = [plane(ref, row, shape[0], c) for c in range(shape[1] // LANES)]
    return jnp.concatenate(parts, axis=1)


def restrict_kernel(plan, q_ref, table_ref, own_ref, top_ref, q_out, y_table_ref, z_table_ref, *rest):
    targets, (mixed, top) = rest[: plan.kinds], rest[plan.kinds :]
    nx, ny, nz = plan.x.length, plan.y.length, plan.z.length
    by, bz = lax.axis_index("gy"), lax.axis_index("gz")
    blocks_z, blocks_y, blocks_table, blocks_top = plan.blocks
    at_y = plan.z.count * blocks_z
    at_table = at_y + plan.y.count * blocks_y
    at_top = at_table + plan.y.count * blocks_table
    at_select = at_top + plan.z.count * blocks_top
    matrix_z = table_ref[pl.ds(blocks_z * bz, blocks_z)].reshape(3 * nz, LANES)
    matrix_y = table_ref[pl.ds(at_y + blocks_y * by, blocks_y)].reshape(16 * blocks_y, LANES)
    matrix_y = matrix_y[:, : 3 * ny]
    q_out[...] = q_ref[...]
    for ref, at in ((y_table_ref, at_table + blocks_table * by), (z_table_ref, at_top + blocks_top * bz)):
        rows = ref.shape[0]
        for c in range(ref.shape[1] // LANES):
            part = table_ref[pl.ds(at + rows // 16 * c, rows // 16)]
            ref[:, c * LANES : (c + 1) * LANES] = part.reshape(rows, LANES)
    for i in range(nx):
        faces = [q_ref[i, ny - REACH :, :], q_ref[i, :REACH, :]]
        if plan.kinds == 1:
            faces = [jnp.where(by == 0, *faces)]
        for face, ref in zip(faces, targets):
            ref[i] = face
    high, low = split(q_ref[...].reshape(nx * ny, nz))
    along_z = dot(jnp.concatenate([high, low, high], axis=1), matrix_z)
    high, low = split(along_z)
    high, low = high.reshape(nx, ny, LANES), low.reshape(nx, ny, LANES)
    for i in range(0, nx, 2):
        pair = [jnp.concatenate([high[j], high[j], low[j]], axis=0) for j in (i, i + 1)]
        both = dot(matrix_y, jnp.concatenate(pair, axis=1))[: plan.rows_restricted]
        mixed[i] = both[:, :LANES]
        mixed[i + 1] = both[:, LANES:]

    brick = lax.axis_index("gx")
    keep_low = jnp.where(brick > 0, 1.0, 0.0).astype(F32)
    keep_high = jnp.where(brick < plan.x.count - 1, 1.0, 0.0).astype(F32)

    def coarsen(planes, level):
        size = nx >> level
        result = {}
        for i in range(LOW[level], LOW[level] + plan.x.width[level]):
            get = lambda j: planes.get(2 * i + j)
            total = None
            for offsets, weight in (((-3, 3), -0.0625), ((-1, 1), 0.5625), ((0,), 1.0)):
                terms = [get(j) for j in offsets if get(j) is not None]
                if terms:
                    term = functools.reduce(jnp.add, terms)
                    term = term * weight if weight != 1.0 else term
                    total = term if total is None else total + term
            if i < 0:
                total = total * keep_low
            elif i >= size:
                total = total * keep_high
            result[i] = total
        return result

    lanes = lax.broadcasted_iota(jnp.int32, (8, LANES), 1)
    in1, in2 = lanes < plan.lane[2], lanes < plan.lane[3]

    def rows_of(start, count, depth):
        levels = [{i: mixed[i, start : start + count, :] for i in range(nx)}]
        for level in range(1, depth + 1):
            levels.append(coarsen(levels[-1], level))
        return levels[-1]

    zero = jnp.zeros((8, LANES), F32)
    first = {r: rows_of(r, 8, 1) for r in range(0, plan.rows1, 8)}
    second = {r: rows_of(plan.row[2] + r, 8, 2) for r in (0, 8)}
    face = [{r: rows_of(plan.row_face + 16 * f + r, 8, 1) for r in (0, 8)} for f in range(plan.kinds)]
    for r in range(0, plan.whole3, 8):
        third = rows_of(plan.row[3] + r, 8, 3)
        for k in range(plan.x.width[3]):
            top[k, r : r + 8, :] = third[LOW[3] + k]
    high, low = split(top[...].reshape(plan.x.width[3] * plan.whole3, LANES))
    select = table_ref[at_select:].reshape(2, -1, LANES)
    select = jnp.concatenate([select[0], select[1]], axis=1)
    flat = dot(select, jnp.concatenate([high, low], axis=1), ((1,), (1,)))[: plan.tall[3]]
    flat = jnp.concatenate([flat, jnp.zeros((plan.tall[3], plan.flat_top - flat.shape[1]), F32)], axis=1)
    start = ((plan.x.length >> 3) * brick + LOW[3]) * plan.whole3
    top_ref[...] = pltpu.roll(flat, lax.rem(start + plan.flat_top, plan.flat_top), 1)
    for k in range(plan.x.width[1]):
        for r in range(0, plan.rows1, 8):
            one = first[r][LOW[1] + k]
            two = second[r][LOW[2] + k] if r < 16 and k < plan.x.width[2] else zero
            rest_ = jnp.where(in2, two, 0.0)
            own_ref[k, r : r + 8, :] = jnp.where(in1, one, rest_)
            if r < 16:
                for f in range(plan.kinds):
                    targets[f][nx + 2 * k + r // 8] = jnp.where(in1, face[f][r][LOW[1] + k], rest_)


def mask(condition):
    return jnp.where(condition, 1.0, 0.0).astype(F32)


def top_z_kernel(plan, own_ref, *refs):
    others, (table_ref, out_ref) = refs[: plan.z.count - 1], refs[plan.z.count - 1 :]
    value = jnp.concatenate([ref[...] for ref in (own_ref, *others)], axis=0)
    high, low = split(value)
    stacked = jnp.concatenate([high, high, low], axis=0)
    out_ref[...] = dot(table_ref[...][:, : plan.top_cols], stacked)


def roll_lanes(value, amount):
    return pltpu.roll(value, amount % LANES, 1)


def pack_faces(plan, faces):
    lanes = lax.broadcasted_iota(jnp.int32, (1, LANES), 1)
    groups = []
    for g in range(plan.face_groups):
        value = faces[g]
        if g + plan.face_groups < FACE:
            value = jnp.where(lanes < plan.half, value, roll_lanes(faces[g + plan.face_groups], plan.half))
        groups.append(value)
    rest = jnp.zeros(faces[0].shape, F32)
    for p, face in enumerate(faces):
        start = plan.left * p
        inside = (lanes >= start) & (lanes < start + plan.left)
        rest = jnp.where(inside, roll_lanes(face, start - plan.half), rest)
    return groups + [rest]


def unpack_face(plan, groups, p):
    lanes = lax.broadcasted_iota(jnp.int32, (1, LANES), 1)
    value = groups[p] if p < plan.face_groups else roll_lanes(groups[p - plan.face_groups], plan.half)
    return jnp.where(lanes < plan.half, value, roll_lanes(groups[-1], plan.half - plan.left * p))


def extend_kernel(plan, q_ref, own_ref, top_ref, *refs):
    count = plan.y.count - 1
    halos, (ext_ref, partner_ref, side_ref) = refs[:count], refs[count:]
    x, y = plan.x, plan.y
    odd = lax.axis_index("gx") % 2
    end = x.length - REACH
    near = plan.near_y(halos)
    put_flat(partner_ref, plan.top_row, top_ref[...])
    for start, ref in ((end * odd, side_ref), (end * (1 - odd), partner_ref)):
        for i in range(REACH):
            row = plan.fine_rows * i
            put_plane(ref, row, q_ref[start + i])
            for h, halo in enumerate(near):
                ref[(row + y.length) // 8 + h] = halo[start + i]

    base = [8 * halo.shape[0] - 16 * x.width[1] for halo in halos]
    for i in range(x.width[1]):
        own = own_ref[i]
        parts = [plane(halo, at, 16, i) for halo, at in zip(halos, base)]
        if plan.overlay:
            halo = parts[0]
            parts = [own[:16], own[16:] + halo[8:], halo[:8]]
        else:
            pad = plan.coarse_rows - 24 - 16 * count
            parts = [own] + parts + ([jnp.zeros((pad, LANES), F32)] if pad else [])
        ext_ref[i] = jnp.concatenate(parts, axis=0)
    lanes = lax.broadcasted_iota(jnp.int32, (1, LANES), 1)
    start = (x.width[1] - FACE) * (1 - odd)
    for p in range(plan.planes):
        row = plan.fine_rows * REACH + plan.coarse_rows * p
        value = jnp.where(lanes < plan.lane[2], ext_ref[start + min(p, FACE - 1)], ext_ref[p])
        put_plane(partner_ref, row, value)
    start = (x.width[1] - FACE) * odd
    for g, value in enumerate(pack_faces(plan, [ext_ref[start + p] for p in range(FACE)])):
        put_plane(side_ref, plan.fine_rows * REACH + plan.coarse_rows * g, value)


def chip_kernel(plan, ext_ref, pair_ref, top_ref, top_out, *targets):
    x, gx = plan.x, lax.axis_index("gx")
    odd, chip = gx % 2, gx // 2
    lanes = lax.broadcasted_iota(jnp.int32, (1, LANES), 1)
    keep_even, keep_odd = mask(odd == 0), mask(odd == 1)
    top = top_ref[...] + get_flat(pair_ref, plan.top_row, plan.top_shape)
    top_out[...] = top

    def merged(level, cell):
        size, total = x.length >> level, None
        for where_own, where_partner, at in ((keep_even, keep_odd, cell), (keep_odd, keep_even, cell - size)):
            if 0 <= at < x.width[level]:
                value = ext_ref[at] * where_own + plan.pair_plane(pair_ref, at) * where_partner
                total = value if total is None else total + value
        return total

    second = [merged(2, c) for c in range(plan.pair_width[2])]
    chips = x.count // 2
    high = x.length >> 2
    for k, ref in zip(range(1, chips), targets):
        for g in range(plan.pair_groups):
            total = None
            for slot, p in enumerate(range(3 * g, min(3 * g + 3, plan.planes))):
                if chips == 2:
                    two = jnp.where(chip == 0, second[high + p], second[p])
                else:
                    two = second[high + p] if k == 1 else second[p]
                two = roll_lanes(two, SLOT * slot - plan.lane[2])
                total = two if slot == 0 else jnp.where(lanes < SLOT * slot, total, two)
            put_plane(ref, plan.coarse_rows * g, total)
        put_flat(ref, plan.coarse_rows * plan.pair_groups, top)


def mix_planes(get, put, count, matrix):
    for i in range(0, count, 2):
        pair = [i, min(i + 1, count - 1)]
        stacked = []
        for j in pair:
            high, low = split(get(j))
            stacked.append(jnp.concatenate([high, high, low], axis=0))
        both = dot(matrix, jnp.concatenate(stacked, axis=1))
        put(i, both[:, :LANES])
        if pair[1] != i:
            put(pair[1], both[:, LANES:])


def stencil(cells, wanted, sigma, reach=REACH):
    result = []
    for i in wanted:
        total = cells.get(i)
        for k in range(1, reach + 1):
            terms = [cells[j] for j in (i - k, i + k) if j in cells]
            if terms:
                term = functools.reduce(jnp.add, terms) * float(np.exp(-((k / sigma) ** 2)))
                total = term if total is None else total + term
        result.append(total)
    return result


def put_ready(ready, sigmas, s, row, value):
    high, low = split(value)
    rows = slice(row, row + value.shape[0])
    step = LANES * sigmas
    ready[rows, s * LANES : (s + 1) * LANES] = high
    ready[rows, step + s * LANES : step + (s + 1) * LANES] = low
    ready[rows, 2 * step + s * LANES : 2 * step + (s + 1) * LANES] = high


def fine_padding(plan):
    pad = up(plan.fine_rows, 16) - plan.fine_rows
    return [jnp.zeros((pad, LANES), F32)] if pad else []


def fine_inner_kernel(plan, q_ref, y_table, inner_ref, edge_ref, mixed):
    x, y = plan.x, plan.y
    halo = jnp.zeros((up(plan.fine_rows, 16) - y.length, LANES), F32)

    def put(i, value):
        mixed[i] = value

    mix_planes(lambda i: jnp.concatenate([q_ref[i], halo], axis=0), put, x.length, plan.fine_matrix(y_table))
    inner = range(REACH, x.length - REACH)
    edge = [*range(REACH), *range(x.length - REACH, x.length)]
    half = len(inner) * (y.length - 16)
    for s, sigma in enumerate(STENCIL_SIGMAS):
        row, end = s * y.length, (s + 1) * y.length
        planes = {i: mixed[i, row + 8 : end - 8, :] for i in range(x.length)}
        step = y.length - 16
        for i, value in enumerate(stencil(planes, inner, sigma)):
            inner_ref[s, i * step : (i + 1) * step, :] = value
        for i, value in enumerate(stencil(planes, edge, sigma)):
            edge_ref[i, row + 8 : end - 8, :] = value
        ends = lambda i: jnp.concatenate([mixed[i, row : row + 8, :], mixed[i, end - 8 : end, :]], axis=0)
        planes = {i: ends(i) for i in range(x.length)}
        for i, value in enumerate(stencil(planes, inner, sigma)):
            inner_ref[s, half + i * 16 : half + i * 16 + 16, :] = value
        for i, value in enumerate(stencil(planes, edge, sigma)):
            edge_ref[i, row : row + 8, :] = value[:8]
            edge_ref[i, end - 8 : end, :] = value[8:]


def fine_halo_kernel(plan, inner_ref, edge_ref, y_table, z_table, *refs):
    halos, (main_ref, push_ref, out_ref, mixed, ready) = refs[: plan.y.count - 1], refs[plan.y.count - 1 :]
    x, y = plan.x, plan.y
    near = plan.near_y(halos)
    padding = [jnp.zeros((8, LANES), F32)] * (plan.halo_cols // 24 - len(near))

    def get(i):
        return jnp.concatenate([plane(h, 0, 8, i) for h in near] + padding, axis=0)

    def put(i, value):
        mixed[i] = value

    mix_planes(get, put, x.length, plan.halo_matrix(y_table))
    inner = range(REACH, x.length - REACH)
    edge = [*range(REACH), *range(x.length - REACH, x.length)]
    out_ref[...] = edge_ref[...]
    half = len(inner) * (y.length - 16)
    for s, sigma in enumerate(STENCIL_SIGMAS):
        row, end = s * y.length, (s + 1) * y.length
        planes = {i: mixed[i, 16 * s : 16 * s + 16, :] for i in range(x.length)}
        for start in range(0, half, 64):
            put_ready(ready, 3, s, start, inner_ref[s, start : start + 64, :])
        for i, value in enumerate(stencil(planes, inner, sigma)):
            start = half + 16 * i
            put_ready(ready, 3, s, start, inner_ref[s, start : start + 16, :] + value)
        for i, value in enumerate(stencil(planes, edge, sigma)):
            out_ref[i, row : row + 8, :] += value[:8]
            out_ref[i, end - 8 : end, :] += value[8:]
    main_ref[...] = dot(ready[...], plan.z_matrix(z_table, 0), ((1,), (1,)))
    push_ref[...] = dot(plan.z_matrix(z_table, 1), ready[...], ((1,), (1,)))


def fine_edge_kernel(plan, halo_ref, edge_ref, y_table, z_table, push_ref, ready_ref, mixed, *, partner):
    x, y = plan.x, plan.y
    gx = lax.axis_index("gx")
    odd = gx % 2
    high = 1 - odd if partner else odd
    keep = mask(True) if partner else mask(jnp.where(high == 1, gx < x.count - 1, gx > 0))
    padding = fine_padding(plan)
    away = lambda k: jnp.where(high == 1, k, REACH - 1 - k)

    def get(k):
        return jnp.concatenate([plane(halo_ref, 0, plan.fine_rows, away(k)) * keep] + padding, axis=0)

    def put(k, value):
        mixed[k] = value

    mix_planes(get, put, REACH, plan.fine_matrix(y_table))
    for s, sigma in enumerate(STENCIL_SIGMAS):
        for r in range(0, y.length, 16):
            row = s * y.length + r
            after = {REACH + k: mixed[k, row : row + 16, :] for k in range(REACH)}
            for i, added in enumerate(stencil(after, range(REACH), sigma)):
                value = edge_ref[away(i) + REACH * high, row : row + 16, :] + added
                top, low = split(value)
                at = away(i) * (y.length // 16) + r // 16
                for c, part in enumerate((top, low, top)):
                    start = (3 * c + s) * LANES
                    ready_ref[at, :, start : start + LANES] = part
    whole = ready_ref[...].reshape(REACH * y.length, 9 * LANES)
    push_ref[...] = dot(plan.z_matrix(z_table, 1), whole, ((1,), (1,)))


def fine_main_kernel(plan, partner_ref, side_ref, z_table, out_ref):
    odd = lax.axis_index("gx") % 2
    for ref, at in ((partner_ref, 1 - odd), (side_ref, odd)):
        whole = ref[...].reshape(REACH * plan.y.length, 9 * LANES)
        out_ref[at] = dot(whole, plan.z_matrix(z_table, 0), ((1,), (1,)))


def coarse_inner_kernel(plan, ext_ref, pair_ref, y_table, *refs):
    *parts, mixed = refs
    own = plan.x.width[1]

    def put(i, value):
        mixed[i] = value

    get = lambda i: ext_ref[i] if i < own else plan.pair_plane(pair_ref, i - own)
    mix_planes(get, put, own + plan.planes, plan.coarse_matrix(y_table))
    for level, part in zip((1, 2), parts):
        rows, width = (plan.rows1, plan.rows2)[level - 1], plan.x.width[level]
        wanted = range(LOW[level], LOW[level] + width)
        for s, sigma in enumerate(STENCIL_SIGMAS):
            for r in range(0, rows, 8):
                cells = collect_inner(plan, level, mixed, plan.group[level] + s * rows + r, 8)
                for i, value in enumerate(stencil(cells, wanted, sigma)):
                    part[s * width + i, r : r + 8, :] = value


def adder(plan, level, cells):
    start, width = LOW[level], plan.x.width[level]

    def add(cell, value, keep):
        if start - REACH <= cell < start + width + REACH:
            value = value * keep
            cells[cell] = cells[cell] + value if cell in cells else value

    return add


def collect_inner(plan, level, inner, row, rows):
    x, odd = plan.x, lax.axis_index("gx") % 2
    size, width, start, own = x.length >> level, x.width[level], LOW[level], x.width[1]
    cells = {start + k: inner[k, row : row + rows, :] for k in range(width)}
    add = adder(plan, level, cells)
    layers = FACE if level == 1 else width
    for k in range(layers):
        value = inner[own + k, row : row + rows, :]
        add(size + start + k, value, mask(odd == 0))
        add(-size + start + width - layers + k, value, mask(odd == 1))
    return cells


def collect_outer(plan, level, outer, row, rows):
    x, gx = plan.x, lax.axis_index("gx")
    odd, chip, chips = gx % 2, gx // 2, plan.x.count // 2
    size, width, start = x.length >> level, x.width[level], LOW[level]
    cells = {}
    add = adder(plan, level, cells)
    if level == 1:
        for k in range(FACE):
            value = outer[k, row : row + rows, :]
            add(-size + start + width - FACE + k, value, mask((chip > 0) & (odd == 0)))
            add(size + start + k, value, mask((chip < chips - 1) & (odd == 1)))
        return cells
    for n, offset in enumerate(plan.near_chips):
        for shift, here in ((-offset, chip >= offset), (chips - offset, chip < offset)):
            if abs(shift) != 1:
                continue
            for core in (0, 1):
                keep = mask(here & (odd == core))
                first = 2 * size * shift - size * core + start + (size if shift < 0 else 0)
                for k in range(plan.planes):
                    add(first + k, outer[plan.planes * n + k, row : row + rows, :], keep)
    return cells


def coarse_kernel(plan, part1, part2, *refs):
    chips = plan.x.count // 2 - 1
    others, refs = refs[:chips], refs[chips:]
    side_in, *pushes = refs[:4]
    y_table, z_table, partner_ref, side_ref, e1_ref, e2_ref, outer, *ready = refs[4:]

    def put(i, value):
        outer[i] = value

    lanes = lax.broadcasted_iota(jnp.int32, (1, LANES), 1)
    groups = [plane(side_in, plan.fine_rows * REACH, plan.coarse_rows, g) for g in range(plan.face_groups + 1)]

    def get(i):
        n, p = i // plan.planes, i % plan.planes
        two = plane(others[plan.near_chips[n] - 1], 0, plan.coarse_rows, p // 3)
        value = roll_lanes(two, plan.lane[2] - SLOT * (p % 3))
        if n == 0 and p < FACE:
            value = jnp.where(lanes < plan.lane[2], unpack_face(plan, groups, p), value)
        return value

    mix_planes(get, put, plan.planes * len(plan.near_chips), plan.coarse_matrix(y_table))
    x = plan.x
    results = []
    for level in (1, 2):
        rows = plan.rows1 if level == 1 else plan.rows2
        wanted = range(LOW[level], LOW[level] + x.width[level])
        for s, sigma in enumerate(STENCIL_SIGMAS):
            for r in range(0, rows, 8):
                cells = collect_outer(plan, level, outer, plan.group[level] + s * rows + r, 8)
                for i, added in enumerate(stencil(cells, wanted, sigma)):
                    value = (part1, part2)[level - 1][s * x.width[level] + i, r : r + 8, :]
                    put_ready(ready[level - 1], 3, s, i * rows + r, value if added is None else value + added)
        results.append(dot(plan.z_matrix(z_table, level + 1), ready[level - 1][...], ((1,), (1,))))
    one, two = results
    e1_ref[...] = one[: plan.tall[1]]
    e2_ref[...] = two[: plan.tall[2]]
    inner, partner, side = (p[...] for p in pushes)
    odd = lax.axis_index("gx") % 2 == 1
    pushed = jnp.concatenate([inner, jnp.where(odd, partner, side), jnp.where(odd, side, partner)], axis=1)
    for n, ref in enumerate((partner_ref, side_ref)):
        ref[:8, :] = pushed[8 * n : 8 * n + 8, :]
        ref[8:, :] = jnp.zeros((16, ref.shape[1]), F32)
        start = plan.tall[1] + 16 * n
        ref[8:, : plan.flat[1]] = one[start : start + 16]
        start = plan.tall[2] + 16 * n
        ref[8:, 512 : 512 + plan.flat[2]] = two[start : start + 16]


def top_chips_kernel(plan, top_ref, *refs):
    *others, out_ref = refs
    total = top_ref[...]
    for ref in others:
        total = total + get_flat(ref, plan.coarse_rows * plan.pair_groups, plan.top_shape)
    out_ref[...] = total


def top_kernel(plan, *refs):
    *values, out_ref = refs
    total = functools.reduce(jnp.add, [v[...] for v in values])
    shape = (plan.flat_top, plan.flat[3])
    source, target = (lax.broadcasted_iota(jnp.int32, shape, d) for d in (0, 1))
    first_x = (plan.x.length >> 3) * lax.axis_index("gx") + LOW[3]
    first_y = (plan.y.length >> 3) * lax.axis_index("gy") + LOW[3]
    apart_x = source // plan.whole3 - target // plan.rows3 - first_x
    apart_y = source % plan.whole3 - target % plan.rows3 - first_y
    square = (apart_x * apart_x + apart_y * apart_y).astype(F32)
    result, tall = None, plan.tall[3]
    for s, sigma in enumerate(TOP_SIGMAS):
        matrix = jnp.exp(square * (-1.0 / sigma**2))
        matrix_high, matrix_low = split(matrix)
        high, low = split(total[s * tall : (s + 1) * tall])
        left = jnp.concatenate([high, low, high], axis=1)
        term = dot(left, jnp.concatenate([matrix_high, matrix_high, matrix_low], axis=0))
        result = term if result is None else result + term
    out_ref[...] = result


def finish_kernel(plan, inner_ref, edge_ref, e1_ref, e2_ref, *refs):
    z = plan.z
    refs = list(refs)
    partner_ref, side_ref, e3_ref, flat, masks, tall, out_ref, e1, e2 = refs
    bz = lax.axis_index("gz")
    column = lax.axis_index("gx") * plan.y.count + lax.axis_index("gy")
    odd = bz % 2
    spread_cols = plan.x.length * plan.y.length
    keep = lambda level: masks[column, level : level + 1, : plan.flat[level]]
    bounds = [int(r) for r in plan.flat_rows]
    flat3, flat2, flat1 = (
        flat[bounds[k] : bounds[k + 1], :][: plan.flat[3 - k], :cols]
        for k, cols in enumerate((plan.flat[2], plan.flat[1], spread_cols))
    )
    e1[...], e2[...] = e1_ref[...], e2_ref[...]
    kept = lax.broadcasted_iota(jnp.int32, (16, 1), 0) < FACE
    for ref, high in ((partner_ref, odd == 0), (side_ref, odd == 1)):
        one = jnp.where(kept, ref[8:, : plan.flat[1]], 0.0)
        two = ref[8:, 512 : 512 + plan.flat[2]]
        for window, value, tall_ in ((e1, one, plan.tall[1]), (e2, two, plan.tall[2])):
            window[:16, :] += value * mask(~high)
            window[tall_ - 16 :, :] += value * mask(high)

    def across(value, matrix):
        high, low = split(value)
        both = dot(jnp.concatenate([high, low], axis=0), matrix)
        return both[: value.shape[0]] + both[value.shape[0] :]

    def along(matrix, value):
        high, low = split(value)
        return dot(matrix, high) + dot(matrix, low)

    start = up(plan.tall[1] + 16, 16)
    middle = start + up(plan.tall[2], 16)
    tall3 = tall[bz, start:middle, :][: plan.tall[2], : plan.tall[3]]
    tall2 = tall[bz, middle:, :][: plan.tall[1], : plan.tall[2]]
    last = tall[bz, :start, :]
    three = e3_ref[...] * keep(3)
    two = (e2[...] + along(tall3, across(three, flat3))) * keep(2)
    one = (e1[...] + along(tall2, across(two, flat2))) * keep(1)
    spread = across(one, flat1)
    rows = jnp.concatenate([spread, partner_ref[:8], side_ref[:8]], axis=0)
    pad = last.shape[0] - rows.shape[0]
    if pad:
        rows = jnp.concatenate([rows, jnp.zeros((pad, rows.shape[1]), F32)], axis=0)
    high, low = split(rows)
    stacked = jnp.concatenate([high, low], axis=0)
    matrix = jnp.concatenate([last, last], axis=0)
    coarse = dot(stacked, matrix, ((0,), (0,)))
    inner = inner_ref.shape[0]
    tiles = plan.y.length // 8
    for k, (x, t) in enumerate(plan.tiles()):
        row = 8 * k
        value = coarse[row : row + 8]
        if row < inner:
            value = value + inner_ref[row : row + 8]
        else:
            end, row = divmod(row - inner, edge_ref.shape[1])
            value = value + edge_ref[end, row : row + 8]
        out_ref[8 * (tiles * x + t) : 8 * (tiles * x + t) + 8] = value


def call(kernel, plan, operands, outs, scratch=()):
    whole = pl.BlockSpec(memory_space=pltpu.VMEM)
    return pl.pallas_call(
        functools.partial(kernel, plan),
        in_specs=[whole] * len(operands),
        out_specs=[whole] * len(outs),
        scratch_shapes=list(scratch),
        out_shape=list(outs),
        compiler_params=pltpu.CompilerParams(vmem_limit_bytes=32 * 2**20),
    )(*[jnp.asarray(o) for o in operands])


def shift(value, axis, offset):
    count = lax.axis_size(axis)
    return lax.ppermute(value, axis, [(i, (i + offset) % count) for i in range(count)])


def swap(value, axes, partner):
    first, second = (lax.axis_size(a) for a in axes)
    pairs = []
    for i in range(first):
        for j in range(second):
            k, m = partner(i, j)
            pairs.append((i * second + j, k * second + m))
    return lax.ppermute(value, axes, pairs)


def side_of(count):
    return lambda i: None if i in (0, count - 1) else i + (1 if i % 2 else -1)


def shards(plan, charges):
    x, y, z = plan.x, plan.y, plan.z
    array = lambda *shape: jax.ShapeDtypeStruct(shape, F32)
    vmem = lambda *shape: pltpu.VMEM(shape, F32)
    ready = lambda rows, sigmas: pltpu.VMEM((rows, 3 * sigmas * LANES), BF)
    side_x, side_z = side_of(x.count), side_of(z.count)
    partner_x = lambda v: swap(v, ("gx", "gy"), lambda i, j: (i ^ 1, j))
    across_x = lambda v: swap(v, ("gx", "gy"), lambda i, j: (i, j ^ 1) if side_x(i) is None else (side_x(i), j))
    partner_z = lambda v: swap(v, ("gx", "gz"), lambda i, j: (i, j ^ 1))
    across_z = lambda v: swap(v, ("gx", "gz"), lambda i, j: (i ^ 1, j) if side_z(j) is None else (i, side_z(j)))

    rows_y = 8 * x.length + 16 * x.width[1]
    table = plan.restrict_tables()
    own, top, charges, y_table, top_table, *to_y = call(
        restrict_kernel,
        plan,
        [charges, table],
        [
            array(x.width[1], plan.rows1, LANES),
            array(plan.tall[3], plan.flat_top),
            array(*charges.shape),
            jax.ShapeDtypeStruct((3 * y.length + plan.rows_mixed + plan.halo_rows, plan.y_cols), BF),
            jax.ShapeDtypeStruct((2 * plan.tall[3], up(plan.top_cols, LANES)), BF),
        ]
        + [array(rows_y // 8, 8, LANES)] * plan.kinds,
        [vmem(x.length, plan.rows_restricted, LANES), vmem(x.width[3], plan.whole3, LANES)],
    )
    from_y = []
    for offset in range(1, y.count):
        value = to_y[0 if offset == 1 else -1]
        value = value if offset in (1, y.count - 1) else value[x.length :]
        from_y.append(shift(value, "gy", offset))

    tops = [swap(top, ("gx", "gz"), lambda i, j, m=m: (i, j ^ m)) for m in range(1, z.count)]
    (top,) = call(top_z_kernel, plan, [top, *tops, top_table], [array(*plan.top_shape)])

    z_table = plan.z_tables()
    inner_cells = (x.length - 2 * REACH) * y.length
    inner, edge = call(
        fine_inner_kernel,
        plan,
        [charges, y_table],
        [array(3, inner_cells, LANES), array(2 * REACH, 3 * y.length, LANES)],
        [vmem(x.length, 3 * y.length, LANES)],
    )
    edge, *from_y = lax.optimization_barrier((edge, *from_y))

    ext, to_partner, to_side = call(
        extend_kernel,
        plan,
        [charges, own, top, *from_y],
        [
            array(x.width[1], plan.coarse_rows, LANES),
            array((plan.top_row + plan.top_rows) // 8, 8, LANES),
            array(plan.side_rows // 8, 8, LANES),
        ],
    )
    from_side, pair = across_x(to_side), partner_x(to_partner)

    main_inner, push_inner, edge = call(
        fine_halo_kernel,
        plan,
        [inner, edge, y_table, z_table, *from_y],
        [array(inner_cells, z.length), array(16, inner_cells), array(2 * REACH, 3 * y.length, LANES)],
        [vmem(x.length, plan.halo_rows, LANES), ready(inner_cells, 3)],
    )

    chips = x.count // 2
    rows_x = plan.pair_groups * plan.coarse_rows + plan.top_rows
    top, *to_chips = call(
        chip_kernel,
        plan,
        [ext, pair, top],
        [array(*plan.top_shape)] + [array(rows_x // 8, 8, LANES)] * (chips - 1),
    )
    from_chips = [
        swap(v, ("gx", "gy"), lambda i, j, k=k: ((i + 2 * k) % x.count ^ 1, j))
        for k, v in zip(range(1, chips), to_chips)
    ]
    parts = call(
        coarse_inner_kernel,
        plan,
        [ext, pair, y_table],
        [array(3 * x.width[1], plan.rows1, LANES), array(3 * x.width[2], plan.rows2, LANES)],
        [vmem(x.width[1] + plan.planes, plan.rows_mixed, LANES)],
    )

    def fine_end(halo, is_partner):
        return call(
            functools.partial(fine_edge_kernel, partner=is_partner),
            plan,
            [halo, edge, y_table, z_table],
            [array(16, REACH * y.length), jax.ShapeDtypeStruct((REACH * y.length // 16, 16, 9 * LANES), BF)],
            [vmem(REACH, 3 * y.length, LANES)],
        )

    push_partner, ready_partner = fine_end(pair, True)
    from_side, push_partner, *parts = lax.optimization_barrier((from_side, push_partner, *parts))
    push_side, ready_side = fine_end(from_side, False)
    pushes = [push_inner, push_partner, push_side]
    window = lambda level: array(plan.tall[level], plan.flat[level])
    to_partner, to_side, e1, e2 = call(
        coarse_kernel,
        plan,
        [*parts, *from_chips, from_side, *pushes, y_table, z_table],
        [array(24, 1024), array(24, 1024), window(1), window(2)],
        [vmem(plan.planes * len(plan.near_chips), plan.rows_mixed, LANES), ready(plan.flat[1], 3), ready(plan.flat[2], 3)],
    )
    from_near = [partner_z(to_partner), across_z(to_side)]

    (top,) = call(top_chips_kernel, plan, [top, *from_chips], [array(*top.shape)])
    tops = [top] + [shift(top, "gy", offset) for offset in range(1, y.count)]
    (e3,) = call(top_kernel, plan, tops, [window(3)])

    (main_edge,) = call(
        fine_main_kernel, plan, [ready_partner, ready_side, z_table], [array(2, REACH * y.length, z.length)]
    )
    (potential,) = call(
        finish_kernel,
        plan,
        [main_inner, main_edge, e1, e2, *from_near, e3, *plan.finish()],
        [array(x.length * y.length, z.length)],
        [vmem(plan.tall[level], plan.flat[level]) for level in (1, 2)],
    )
    return potential.reshape(charges.shape)


def solution(mesh):
    counts = [mesh.shape[name] for name in ("gx", "gy", "gz")]

    def run(charges):
        plan = Plan(counts, [size // n for size, n in zip(charges.shape, counts)])
        placed = P("gx", "gy", "gz")
        return jax.shard_map(
            functools.partial(shards, plan), mesh=mesh, in_specs=(placed,), out_specs=placed, check_vma=False
        )(charges)

    return run
```

```python
import functools

import jax
import jax.numpy as jnp
import numpy as np
from jax import lax
from jax.experimental import pallas as pl
from jax.experimental.pallas import tpu as pltpu
from jax.sharding import PartitionSpec as P

REACH = 8
STENCIL_SIGMAS = (1.0, 2.0, 3.5)
STENCIL_WEIGHTS = (0.4, 0.1, 0.03)
TOP_SIGMAS = (1.5, 4.0)
TOP_WEIGHTS = (0.03, 0.006)
SPLINE_TAPS = np.array((-1.0, 0.0, 9.0, 16.0, 9.0, 0.0, -1.0)) / 16.0

LOW = (0, -1, -2, -2)
EXTRA = (0, 3, 5, 5)
SLOT = 40
FACE = 11
LANES = 128
BF = jnp.bfloat16
F32 = jnp.float32


def up(value, unit):
    return -(-value // unit) * unit


def band(rows, cols, sigma, reach):
    distance = cols[None, :] - rows[:, None]
    return np.where(abs(distance) <= reach, np.exp(-((distance / sigma) ** 2)), 0.0)


def restriction(size):
    position = np.arange(size)[None, :] - 2 * np.arange(size // 2)[:, None] + 3
    inside = (position >= 0) & (position <= 6)
    return np.where(inside, SPLINE_TAPS[np.clip(position, 0, 6)], 0.0)


class Axis:
    def __init__(self, count, length):
        self.count, self.length = count, length
        self.width = [(length >> level) + EXTRA[level] for level in range(4)]

    def window(self, level, brick):
        size = self.length >> level
        cells = brick * size + LOW[level] + np.arange(self.width[level])
        return cells, ((cells >= 0) & (cells < self.count * size)).astype(float)

    def partial(self, level, brick):
        matrix = np.eye(self.count * self.length)
        for _ in range(level):
            matrix = restriction(matrix.shape[0]) @ matrix
        cells, inside = self.window(level, brick)
        rows = matrix[np.clip(cells, 0, len(matrix) - 1)] * inside[:, None]
        return rows[:, brick * self.length : (brick + 1) * self.length]

    def prolong(self, level, brick):
        matrix = restriction((self.count * self.length) >> (level - 1)).T
        rows, row_inside = self.window(level - 1, brick)
        cols, col_inside = self.window(level, brick)
        taken = matrix[np.clip(rows, 0, len(matrix) - 1)][:, np.clip(cols, 0, matrix.shape[1] - 1)]
        return taken * row_inside[:, None] * col_inside[None, :]

    def mix(self, level, sigma, target, source):
        rows, row_inside = self.window(level, target)
        cols, col_inside = self.window(level, source)
        reach = REACH if level < 3 else self.count * self.length
        return band(rows, cols, sigma, reach) * row_inside[:, None] * col_inside[None, :]


def place(shape, *pieces):
    whole = np.zeros(shape)
    for row, col, block in pieces:
        whole[row : row + block.shape[0], col : col + block.shape[1]] += block
    return whole


def halves(matrix):
    high = matrix.astype(jnp.bfloat16)
    low = (matrix - high.astype(np.float64)).astype(jnp.bfloat16)
    return high, low


def left3(matrix):
    high, low = halves(matrix)
    return np.concatenate([high, low, high], axis=-1)


def left3t(matrix):
    high, low = halves(matrix)
    return np.concatenate([high, high, low], axis=-1)


def right3(matrix):
    high, low = halves(matrix)
    return np.concatenate([high, high, low], axis=-2)


def split(value):
    high = value.astype(BF)
    return high, (value - high.astype(F32)).astype(BF)


def dot(left, right, dims=((1,), (0,))):
    return lax.dot_general(left, right, (dims, ((), ())), preferred_element_type=F32)


class Plan:
    def __init__(self, counts, lengths):
        self.x, self.y, self.z = (Axis(n, length) for n, length in zip(counts, lengths))
        x, y, z = self.x, self.y, self.z
        assert x.count % 2 == 0 and x.count >= 4 and y.count % 2 == 0
        assert z.count >= 4 and z.count & (z.count - 1) == 0
        self.lane = [0, 0, z.width[1], z.width[1] + z.width[2]]
        self.lane_end = self.lane[3] + z.width[3]
        assert self.lane_end <= LANES and z.length == LANES
        self.rows1, self.rows2 = up(y.width[1], 8), up(y.width[2], 16)
        self.rows3, self.whole3 = up(y.width[3], 16), up(y.count * y.length >> 3, 8)
        assert self.rows2 <= 16 and self.rows3 <= 16 and FACE <= 14 and self.rows1 == 24
        self.row = [0, 0, self.rows1, self.rows1 + self.rows2]
        self.row_face = self.rows1 + self.rows2 + self.whole3
        self.kinds = 1 if y.count == 2 else 2
        self.rows_restricted = self.row_face + 16 * self.kinds
        self.overlay = y.count == 2 and y.width[1] + 3 <= self.rows1
        self.coarse_rows = up(24 + 16 * (y.count - 1), 16) if not self.overlay else 32
        self.fine_halos = 1 if y.count == 2 else 2
        self.fine_rows = y.length + 8 * self.fine_halos
        self.pair_width = [w + (x.length >> l) for l, w in enumerate(x.width)]
        self.planes = max(FACE, x.width[2])
        self.half, self.left = LANES // 2, z.width[1] - LANES // 2
        self.face_groups = up(FACE, 2) // 2
        assert 0 < self.left and self.left * FACE <= LANES and z.width[2] <= SLOT
        chips = x.count // 2
        self.near_chips = [1] if chips == 2 else [1, chips - 1]
        self.pair_groups = up(self.planes, 3) // 3
        self.side_rows = REACH * self.fine_rows + (self.face_groups + 1) * self.coarse_rows
        self.flat_top = up((x.count * x.length >> 3) * self.whole3, LANES)
        self.top_shape = 2 * up(z.width[3], 8), self.flat_top
        self.top_rows = self.top_shape[0] * self.flat_top // LANES
        self.top_row = REACH * self.fine_rows + self.planes * self.coarse_rows
        assert self.planes <= x.width[1]
        self.group = [0, 0, 3 * self.rows1]
        self.rows_mixed = up(3 * self.rows1 + 3 * self.rows2, 16)
        self.tall = [0, up(z.width[1], 8), up(z.width[2], 8), up(z.width[3], 8)]
        assert self.tall[1] - 16 == z.width[1] - FACE and self.tall[2] - 16 == z.width[2] - 13
        self.flat = [0, x.width[1] * self.rows1, x.width[2] * self.rows2, x.width[3] * self.rows3]
        assert self.flat[1] <= 512 and self.flat[2] <= 256 and self.flat[3] <= 256

    def face_kind(self, axis, offset, source):
        if axis.count == 2:
            return 1 - source
        return 1 if offset == 1 else 0

    def near_y(self, halos):
        return [halos[0]] if self.y.count == 2 else [halos[0], halos[-1]]

    def tiles(self):
        nx, nt = self.x.length, self.y.length // 8
        inner = range(REACH, nx - REACH)
        edge = [*range(REACH), *range(nx - REACH, nx)]
        order = [(x, t) for x in inner for t in range(1, nt - 1)]
        order += [(x, t) for x in inner for t in (0, nt - 1)]
        return order + [(x, t) for x in edge for t in range(nt)]

    def pair_plane(self, ref, index):
        return plane(ref, self.fine_rows * REACH, self.coarse_rows, index)

    def face_row(self, j):
        return j if j < 8 or not self.overlay else j + 3

    def restrict_tables(self):
        rows = up(self.rows_restricted, 16)
        along_y = np.stack([place((rows, LANES), (0, 0, m)) for m in self.restrict_y().astype(np.float32)])
        parts = [self.restrict_z(), along_y, self.y_tables(), self.top_z()]
        parts = [p.astype(np.float32) for p in parts]
        blocks = []
        for p in parts:
            columns = [p[:, :, c : c + LANES] for c in range(0, p.shape[2], LANES)]
            blocks.append(np.concatenate(columns, axis=1).reshape(len(p), -1, 16, LANES))
        self.blocks = [b.shape[1] for b in blocks]
        self.blocks.append(2 * up(self.tall[3], 16) // 16)
        table = np.concatenate([b.reshape(-1, 16, LANES) for b in blocks] + [self.top_select().reshape(-1, 2, LANES)
            .transpose(1, 0, 2).reshape(-1, 16, LANES).astype(np.float32)])
        return table.astype(jnp.bfloat16)

    def y_tables(self):
        fine, halo, coarse = self.fine_y(), self.halo_y(), self.coarse_y()
        cols = up(max(fine.shape[2], coarse.shape[2]), LANES)
        self.halo_rows, self.halo_cols = halo.shape[1:]
        widen = lambda t: np.pad(t, ((0, 0), (0, 0), (0, cols - t.shape[2])))
        self.fine_cols, self.coarse_cols = fine.shape[2], coarse.shape[2]
        self.y_cols = cols
        return np.concatenate([widen(fine), widen(coarse), widen(halo)], axis=1)

    def z_tables(self):
        tables = [*self.fine_z(), *[self.coarse_z(level) for level in (1, 2)]]
        cols = 9 * LANES
        self.z_rows = np.cumsum([0] + [t.shape[1] for t in tables])
        return np.concatenate([np.pad(t, ((0, 0), (0, 0), (0, cols - t.shape[2]))) for t in tables], axis=1)

    def fine_matrix(self, ref):
        return ref[: 3 * self.y.length, :][:, : self.fine_cols]

    def coarse_matrix(self, ref):
        start = 3 * self.y.length
        return ref[start : start + self.rows_mixed, :][:, : self.coarse_cols]

    def halo_matrix(self, ref):
        return ref[3 * self.y.length + self.rows_mixed :, :][:, : self.halo_cols]

    def z_matrix(self, ref, number):
        return ref[lax.axis_index("gz"), int(self.z_rows[number]) : int(self.z_rows[number + 1]), :]

    def restrict_z(self):
        z = self.z
        return np.stack(
            [
                right3(place((z.length, LANES), *[(0, self.lane[l], z.partial(l, b).T) for l in (1, 2, 3)]))
                for b in range(z.count)
            ]
        )

    def restrict_y(self):
        y, tables = self.y, []
        for b in range(y.count):
            pieces = [(self.row[l], 0, y.partial(l, b)) for l in (1, 2)]
            cells, inside = y.window(3, b)
            for cell, line in zip(cells[inside > 0], y.partial(3, b)[inside > 0]):
                pieces.append((self.row[3] + cell, 0, line[None]))
            first = y.partial(1, b)
            for k in range(self.kinds):
                kind = self.face_kind(y, 1, b) if self.kinds == 1 else 1 - k
                start = (y.width[1] - FACE) * kind
                for j in range(FACE):
                    pieces.append((self.row_face + 16 * k + self.face_row(j), 0, first[start + j][None]))
            tables.append(left3(place((self.rows_restricted, y.length), *pieces)))
        return np.stack(tables)

    def fine_y(self):
        y, tables = self.y, []
        for b in range(y.count):
            pieces = []
            for s, sigma in enumerate(STENCIL_SIGMAS):
                row = s * y.length
                pieces.append((row, 0, y.mix(0, sigma, b, b)))
                for h in range(self.fine_halos):
                    offset = 1 if h == 0 else y.count - 1
                    source = (b - offset) % y.count
                    start = (y.length - REACH) * self.face_kind(y, offset, source)
                    block = y.mix(0, sigma, b, source)[:, start : start + REACH]
                    pieces.append((row, y.length + 8 * h, block))
            tables.append(left3(place((3 * y.length, up(self.fine_rows, 16)), *pieces)))
        return np.stack(tables)

    def halo_y(self):
        n, cols = self.y.length, up(self.fine_rows, 16)
        rows = [s * n + r for s in range(3) for r in (*range(8), *range(n - 8, n))]
        columns = [c * cols + n + k for c in range(3) for k in range(cols - n)]
        return self.fine_y()[:, rows][:, :, columns]

    def coarse_y(self):
        y, tables = self.y, []
        for b in range(y.count):
            whole = np.zeros((self.rows_mixed, self.coarse_rows))
            for level in (1, 2):
                rows = self.rows1 if level == 1 else self.rows2
                for s, sigma in enumerate(STENCIL_SIGMAS):
                    top = self.group[level] + s * rows
                    for offset in range(y.count):
                        source = (b - offset) % y.count
                        block = y.mix(level, sigma, b, source)
                        if level == 1 and offset:
                            start = (y.width[1] - FACE) * self.face_kind(y, offset, source)
                            block = block[:, start : start + FACE]
                        for j in range(block.shape[1]):
                            slot = self.face_row(j) if level == 1 and offset else j
                            if self.overlay and offset:
                                slot = 24 + slot if slot < 8 else 8 + slot
                            elif offset:
                                slot = 24 + 16 * (offset - 1) + slot
                            whole[top : top + y.width[level], slot] += block[:, j]
            tables.append(left3(whole))
        return np.stack(tables)

    def near_z(self, b, step):
        side = 1 if (b % 2 == 0) == (step == 0) else -1
        return side, b + side if 0 <= b + side < self.z.count else None

    def fine_z(self):
        z, own, pushed = self.z, [], []
        for b in range(z.count):
            mixes = lambda target: [
                w * z.mix(0, sigma, target, b) for sigma, w in zip(STENCIL_SIGMAS, STENCIL_WEIGHTS)
            ]
            own.append(left3t(np.concatenate(mixes(b), axis=1)))
            rows = []
            for step in (0, 1):
                side, target = self.near_z(b, step)
                if target is None:
                    rows.append(np.zeros((8, 3 * z.length)))
                else:
                    rows.append(np.concatenate([m[:8] if side > 0 else m[-8:] for m in mixes(target)], axis=1))
            pushed.append(left3t(np.concatenate(rows, axis=0)))
        return np.stack(own), np.stack(pushed)

    def coarse_z(self, level):
        z, tables = self.z, []
        cols, tall = LANES * len(STENCIL_SIGMAS), self.tall[level]
        for b in range(z.count):

            def mixed(target):
                blocks = [z.mix(level, sigma, target, b) * w * 0.5**level for sigma, w in zip(STENCIL_SIGMAS, STENCIL_WEIGHTS)]
                blocks = [place((z.width[level], LANES), (0, self.lane[level], block)) for block in blocks]
                return np.concatenate(blocks, axis=1)

            pieces = [place((tall, cols), (0, 0, mixed(b)))]
            layers = FACE if level == 1 else 13
            for step in (0, 1):
                side, target = self.near_z(b, step)
                if target is None:
                    pieces.append(np.zeros((16, cols)))
                else:
                    block = mixed(target)
                    pieces.append(place((16, cols), (0, 0, block[:layers] if side > 0 else block[-layers:])))
            whole = np.concatenate(pieces, axis=0)
            tables.append(left3t(place((up(len(whole), 16), cols), (0, 0, whole))))
        return np.stack(tables)

    def top_z(self):
        z, tall, tables = self.z, self.tall[3], []
        for b in range(z.count):
            pieces = []
            for s, (sigma, w) in enumerate(zip(TOP_SIGMAS, TOP_WEIGHTS)):
                for m in range(z.count):
                    pieces.append((tall * s, tall * m, w * z.mix(3, sigma, b, b ^ m)))
            tables.append(left3(place((2 * tall, z.count * tall), *pieces)))
        self.top_cols = tables[0].shape[1]
        widen = up(self.top_cols, LANES) - self.top_cols
        return np.pad(np.stack(tables), ((0, 0), (0, 0), (0, widen)))

    def top_select(self):
        matrix = place((up(self.tall[3], 16), LANES), (0, self.lane[3], np.eye(self.z.width[3])))
        return np.concatenate([matrix, matrix], axis=1).astype(jnp.bfloat16)

    def finish(self):
        x, y, z = self.x, self.y, self.z
        rows = (y.length, self.rows1, self.rows2, self.rows3)
        exact = lambda m: np.asarray(m, dtype=jnp.bfloat16)
        tall = []
        for b in range(z.count):
            ends = (0, z.length - 8) if b % 2 else (z.length - 8, 0)
            one = z.prolong(1, b)
            two = one @ z.prolong(2, b)
            three = two @ z.prolong(3, b)
            deep = [place((up(self.tall[l], 16), LANES), (0, 0, m.T)) for l, m in ((1, one), (2, two), (3, three))]
            ends = place((16, LANES), *[(8 * k, 0, np.eye(8, LANES, end)) for k, end in enumerate(ends)])
            parts = [exact(deep[0]), exact(deep[0]), exact(ends), exact(ends), right3(deep[1]), right3(deep[2])]
            tall.append(np.concatenate(parts))
        self.tall_rows = np.cumsum([0] + [2 * up(self.tall[1], 16), 32, 3 * up(self.tall[2], 16), 3 * up(self.tall[3], 16)])

        flat = []
        for level in (3, 2, 1):
            p, q = (Axis(5, axis.length).prolong(level, 2) for axis in (x, y))
            matrix = np.kron(p, place((rows[level - 1], rows[level]), (0, 0, q)))
            if level == 1:
                matrix = matrix[[x_ * y.length + 8 * t + k for x_, t in self.tiles() for k in range(8)]]
            flat.append(matrix)
        self.flat_rows = np.cumsum([0] + [up(len(m), 16) for m in flat])
        cols = up(max(self.flat), LANES)
        joined = np.concatenate([np.pad(m, ((0, -len(m) % 16), (0, cols - m.shape[1]))) for m in flat])
        return exact(joined), np.stack(tall)


def plane(ref, base, rows, index):
    return ref[pl.ds(base // 8 + rows // 8 * index, rows // 8)].reshape(rows, LANES)


def put_plane(ref, row, value):
    ref[row // 8 : (row + value.shape[0]) // 8] = value.reshape(value.shape[0] // 8, 8, LANES)


def put_flat(ref, row, value):
    for c in range(value.shape[1] // LANES):
        put_plane(ref, row + c * value.shape[0], value[:, c * LANES : (c + 1) * LANES])


def get_flat(ref, row, shape):
    parts = [plane(ref, row, shape[0], c) for c in range(shape[1] // LANES)]
    return jnp.concatenate(parts, axis=1)


def restrict_kernel(plan, q_hbm, table_hbm, own_ref, top_ref, y_table_ref, z_table_ref, *rest):
    targets, (mixed, top, q_ref, table_ref, sems) = rest[: plan.kinds], rest[plan.kinds :]
    nx, ny, nz = plan.x.length, plan.y.length, plan.z.length
    by, bz = lax.axis_index("gy"), lax.axis_index("gz")
    copies, starts, source, at = [pltpu.make_async_copy(q_hbm, q_ref, sems.at[0])], [], 0, 0
    bricks = ((plan.z.count, bz), (plan.y.count, by), (plan.y.count, by), (plan.z.count, bz), (1, 0))
    for n, (blocks, (count, brick)) in enumerate(zip(plan.blocks, bricks)):
        part = table_hbm.at[pl.ds(source + blocks * brick, blocks)]
        copies.append(pltpu.make_async_copy(part, table_ref.at[pl.ds(at, blocks)], sems.at[n + 1]))
        starts.append(at)
        source, at = source + count * blocks, at + blocks
    for copy in copies:
        copy.start()
    for copy in copies:
        copy.wait()
    blocks_z, blocks_y = plan.blocks[:2]
    matrix_z = table_ref[:blocks_z].reshape(3 * nz, LANES)
    matrix_y = table_ref[blocks_z : blocks_z + blocks_y].reshape(16 * blocks_y, LANES)
    matrix_y = matrix_y[:, : 3 * ny]
    at_select = starts[4]
    for ref, at in ((y_table_ref, starts[2]), (z_table_ref, starts[3])):
        rows = ref.shape[0]
        for c in range(ref.shape[1] // LANES):
            first = at + rows // 16 * c
            ref[:, c * LANES : (c + 1) * LANES] = table_ref[first : first + rows // 16].reshape(rows, LANES)
    for i in range(nx):
        faces = [q_ref[i, ny - REACH :, :], q_ref[i, :REACH, :]]
        if plan.kinds == 1:
            faces = [jnp.where(by == 0, *faces)]
        for face, ref in zip(faces, targets):
            ref[i] = face
    high, low = split(q_ref[...].reshape(nx * ny, nz))
    along_z = dot(jnp.concatenate([high, low, high], axis=1), matrix_z)
    high, low = split(along_z)
    high, low = high.reshape(nx, ny, LANES), low.reshape(nx, ny, LANES)
    for i in range(0, nx, 2):
        pair = [jnp.concatenate([high[j], high[j], low[j]], axis=0) for j in (i, i + 1)]
        both = dot(matrix_y, jnp.concatenate(pair, axis=1))[: plan.rows_restricted]
        mixed[i] = both[:, :LANES]
        mixed[i + 1] = both[:, LANES:]

    brick = lax.axis_index("gx")
    keep_low = jnp.where(brick > 0, 1.0, 0.0).astype(F32)
    keep_high = jnp.where(brick < plan.x.count - 1, 1.0, 0.0).astype(F32)

    def coarsen(planes, level):
        size = nx >> level
        result = {}
        for i in range(LOW[level], LOW[level] + plan.x.width[level]):
            get = lambda j: planes.get(2 * i + j)
            total = None
            for offsets, weight in (((-3, 3), -0.0625), ((-1, 1), 0.5625), ((0,), 1.0)):
                terms = [get(j) for j in offsets if get(j) is not None]
                if terms:
                    term = functools.reduce(jnp.add, terms)
                    term = term * weight if weight != 1.0 else term
                    total = term if total is None else total + term
            if i < 0:
                total = total * keep_low
            elif i >= size:
                total = total * keep_high
            result[i] = total
        return result

    lanes = lax.broadcasted_iota(jnp.int32, (8, LANES), 1)
    in1, in2 = lanes < plan.lane[2], lanes < plan.lane[3]

    def rows_of(start, count, depth):
        levels = [{i: mixed[i, start : start + count, :] for i in range(nx)}]
        for level in range(1, depth + 1):
            levels.append(coarsen(levels[-1], level))
        return levels[-1]

    zero = jnp.zeros((8, LANES), F32)
    first = {r: rows_of(r, 8, 1) for r in range(0, plan.rows1, 8)}
    second = {r: rows_of(plan.row[2] + r, 8, 2) for r in (0, 8)}
    face = [{r: rows_of(plan.row_face + 16 * f + r, 8, 1) for r in (0, 8)} for f in range(plan.kinds)]
    for r in range(0, plan.whole3, 8):
        third = rows_of(plan.row[3] + r, 8, 3)
        for k in range(plan.x.width[3]):
            top[k, r : r + 8, :] = third[LOW[3] + k]
    high, low = split(top[...].reshape(plan.x.width[3] * plan.whole3, LANES))
    select = table_ref[at_select:].reshape(2, -1, LANES)
    select = jnp.concatenate([select[0], select[1]], axis=1)
    flat = dot(select, jnp.concatenate([high, low], axis=1), ((1,), (1,)))[: plan.tall[3]]
    flat = jnp.concatenate([flat, jnp.zeros((plan.tall[3], plan.flat_top - flat.shape[1]), F32)], axis=1)
    start = ((plan.x.length >> 3) * brick + LOW[3]) * plan.whole3
    top_ref[...] = pltpu.roll(flat, lax.rem(start + plan.flat_top, plan.flat_top), 1)
    for k in range(plan.x.width[1]):
        for r in range(0, plan.rows1, 8):
            one = first[r][LOW[1] + k]
            two = second[r][LOW[2] + k] if r < 16 and k < plan.x.width[2] else zero
            rest_ = jnp.where(in2, two, 0.0)
            own_ref[k, r : r + 8, :] = jnp.where(in1, one, rest_)
            if r < 16:
                for f in range(plan.kinds):
                    targets[f][nx + 2 * k + r // 8] = jnp.where(in1, face[f][r][LOW[1] + k], rest_)


def mask(condition):
    return jnp.where(condition, 1.0, 0.0).astype(F32)


def top_z_kernel(plan, own_ref, *refs):
    others, (table_ref, out_ref) = refs[: plan.z.count - 1], refs[plan.z.count - 1 :]
    value = jnp.concatenate([ref[...] for ref in (own_ref, *others)], axis=0)
    high, low = split(value)
    stacked = jnp.concatenate([high, high, low], axis=0)
    out_ref[...] = dot(table_ref[...][:, : plan.top_cols], stacked)


def roll_lanes(value, amount):
    return pltpu.roll(value, amount % LANES, 1)


def pack_faces(plan, faces):
    lanes = lax.broadcasted_iota(jnp.int32, (1, LANES), 1)
    groups = []
    for g in range(plan.face_groups):
        value = faces[g]
        if g + plan.face_groups < FACE:
            value = jnp.where(lanes < plan.half, value, roll_lanes(faces[g + plan.face_groups], plan.half))
        groups.append(value)
    rest = jnp.zeros(faces[0].shape, F32)
    for p, face in enumerate(faces):
        start = plan.left * p
        inside = (lanes >= start) & (lanes < start + plan.left)
        rest = jnp.where(inside, roll_lanes(face, start - plan.half), rest)
    return groups + [rest]


def unpack_face(plan, groups, p):
    lanes = lax.broadcasted_iota(jnp.int32, (1, LANES), 1)
    value = groups[p] if p < plan.face_groups else roll_lanes(groups[p - plan.face_groups], plan.half)
    return jnp.where(lanes < plan.half, value, roll_lanes(groups[-1], plan.half - plan.left * p))


def extend_kernel(plan, q_ref, own_ref, top_ref, *refs):
    count = plan.y.count - 1
    halos, (ext_ref, partner_ref, side_ref) = refs[:count], refs[count:]
    x, y = plan.x, plan.y
    odd = lax.axis_index("gx") % 2
    end = x.length - REACH
    near = plan.near_y(halos)
    put_flat(partner_ref, plan.top_row, top_ref[...])
    for start, ref in ((end * odd, side_ref), (end * (1 - odd), partner_ref)):
        for i in range(REACH):
            row = plan.fine_rows * i
            put_plane(ref, row, q_ref[start + i])
            for h, halo in enumerate(near):
                ref[(row + y.length) // 8 + h] = halo[start + i]

    base = [8 * halo.shape[0] - 16 * x.width[1] for halo in halos]
    for i in range(x.width[1]):
        own = own_ref[i]
        parts = [plane(halo, at, 16, i) for halo, at in zip(halos, base)]
        if plan.overlay:
            halo = parts[0]
            parts = [own[:16], own[16:] + halo[8:], halo[:8]]
        else:
            pad = plan.coarse_rows - 24 - 16 * count
            parts = [own] + parts + ([jnp.zeros((pad, LANES), F32)] if pad else [])
        ext_ref[i] = jnp.concatenate(parts, axis=0)
    lanes = lax.broadcasted_iota(jnp.int32, (1, LANES), 1)
    start = (x.width[1] - FACE) * (1 - odd)
    for p in range(plan.planes):
        row = plan.fine_rows * REACH + plan.coarse_rows * p
        value = jnp.where(lanes < plan.lane[2], ext_ref[start + min(p, FACE - 1)], ext_ref[p])
        put_plane(partner_ref, row, value)
    start = (x.width[1] - FACE) * odd
    for g, value in enumerate(pack_faces(plan, [ext_ref[start + p] for p in range(FACE)])):
        put_plane(side_ref, plan.fine_rows * REACH + plan.coarse_rows * g, value)


def chip_kernel(plan, ext_ref, pair_ref, top_ref, top_out, *targets):
    x, gx = plan.x, lax.axis_index("gx")
    odd, chip = gx % 2, gx // 2
    lanes = lax.broadcasted_iota(jnp.int32, (1, LANES), 1)
    keep_even, keep_odd = mask(odd == 0), mask(odd == 1)
    top = top_ref[...] + get_flat(pair_ref, plan.top_row, plan.top_shape)
    top_out[...] = top

    def merged(level, cell):
        size, total = x.length >> level, None
        for where_own, where_partner, at in ((keep_even, keep_odd, cell), (keep_odd, keep_even, cell - size)):
            if 0 <= at < x.width[level]:
                value = ext_ref[at] * where_own + plan.pair_plane(pair_ref, at) * where_partner
                total = value if total is None else total + value
        return total

    second = [merged(2, c) for c in range(plan.pair_width[2])]
    chips = x.count // 2
    high = x.length >> 2
    for k, ref in zip(range(1, chips), targets):
        for g in range(plan.pair_groups):
            total = None
            for slot, p in enumerate(range(3 * g, min(3 * g + 3, plan.planes))):
                if chips == 2:
                    two = jnp.where(chip == 0, second[high + p], second[p])
                else:
                    two = second[high + p] if k == 1 else second[p]
                two = roll_lanes(two, SLOT * slot - plan.lane[2])
                total = two if slot == 0 else jnp.where(lanes < SLOT * slot, total, two)
            put_plane(ref, plan.coarse_rows * g, total)
        put_flat(ref, plan.coarse_rows * plan.pair_groups, top)


def mix_planes(get, put, count, matrix):
    for i in range(0, count, 2):
        pair = [i, min(i + 1, count - 1)]
        stacked = []
        for j in pair:
            high, low = split(get(j))
            stacked.append(jnp.concatenate([high, high, low], axis=0))
        both = dot(matrix, jnp.concatenate(stacked, axis=1))
        put(i, both[:, :LANES])
        if pair[1] != i:
            put(pair[1], both[:, LANES:])


def stencil(cells, wanted, sigma, reach=REACH):
    result = []
    for i in wanted:
        total = cells.get(i)
        for k in range(1, reach + 1):
            terms = [cells[j] for j in (i - k, i + k) if j in cells]
            if terms:
                term = functools.reduce(jnp.add, terms) * float(np.exp(-((k / sigma) ** 2)))
                total = term if total is None else total + term
        result.append(total)
    return result


def put_ready(ready, sigmas, s, row, value):
    high, low = split(value)
    rows = slice(row, row + value.shape[0])
    step = LANES * sigmas
    ready[rows, s * LANES : (s + 1) * LANES] = high
    ready[rows, step + s * LANES : step + (s + 1) * LANES] = low
    ready[rows, 2 * step + s * LANES : 2 * step + (s + 1) * LANES] = high


def fine_padding(plan):
    pad = up(plan.fine_rows, 16) - plan.fine_rows
    return [jnp.zeros((pad, LANES), F32)] if pad else []


def fine_inner_kernel(plan, q_ref, y_table, inner_ref, edge_ref, q_out, mixed):
    x, y = plan.x, plan.y
    q_out[...] = q_ref[...]
    halo = jnp.zeros((up(plan.fine_rows, 16) - y.length, LANES), F32)

    def put(i, value):
        mixed[i] = value

    mix_planes(lambda i: jnp.concatenate([q_ref[i], halo], axis=0), put, x.length, plan.fine_matrix(y_table))
    inner = range(REACH, x.length - REACH)
    edge = [*range(REACH), *range(x.length - REACH, x.length)]
    half = len(inner) * (y.length - 16)
    for s, sigma in enumerate(STENCIL_SIGMAS):
        row, end = s * y.length, (s + 1) * y.length
        planes = {i: mixed[i, row + 8 : end - 8, :] for i in range(x.length)}
        step = y.length - 16
        for i, value in enumerate(stencil(planes, inner, sigma)):
            inner_ref[s, i * step : (i + 1) * step, :] = value
        for i, value in enumerate(stencil(planes, edge, sigma)):
            edge_ref[i, row + 8 : end - 8, :] = value
        ends = lambda i: jnp.concatenate([mixed[i, row : row + 8, :], mixed[i, end - 8 : end, :]], axis=0)
        planes = {i: ends(i) for i in range(x.length)}
        for i, value in enumerate(stencil(planes, inner, sigma)):
            inner_ref[s, half + i * 16 : half + i * 16 + 16, :] = value
        for i, value in enumerate(stencil(planes, edge, sigma)):
            edge_ref[i, row : row + 8, :] = value[:8]
            edge_ref[i, end - 8 : end, :] = value[8:]


def fine_halo_kernel(plan, inner_ref, edge_ref, y_table, z_table, *refs):
    halos, (main_ref, push_ref, out_ref, mixed, ready) = refs[: plan.y.count - 1], refs[plan.y.count - 1 :]
    x, y = plan.x, plan.y
    near = plan.near_y(halos)
    padding = [jnp.zeros((8, LANES), F32)] * (plan.halo_cols // 24 - len(near))

    def get(i):
        return jnp.concatenate([plane(h, 0, 8, i) for h in near] + padding, axis=0)

    def put(i, value):
        mixed[i] = value

    mix_planes(get, put, x.length, plan.halo_matrix(y_table))
    inner = range(REACH, x.length - REACH)
    edge = [*range(REACH), *range(x.length - REACH, x.length)]
    out_ref[...] = edge_ref[...]
    half = len(inner) * (y.length - 16)
    for s, sigma in enumerate(STENCIL_SIGMAS):
        row, end = s * y.length, (s + 1) * y.length
        planes = {i: mixed[i, 16 * s : 16 * s + 16, :] for i in range(x.length)}
        for start in range(0, half, 64):
            put_ready(ready, 3, s, start, inner_ref[s, start : start + 64, :])
        for i, value in enumerate(stencil(planes, inner, sigma)):
            start = half + 16 * i
            put_ready(ready, 3, s, start, inner_ref[s, start : start + 16, :] + value)
        for i, value in enumerate(stencil(planes, edge, sigma)):
            out_ref[i, row : row + 8, :] += value[:8]
            out_ref[i, end - 8 : end, :] += value[8:]
    main_ref[...] = dot(ready[...], plan.z_matrix(z_table, 0), ((1,), (1,)))
    push_ref[...] = dot(plan.z_matrix(z_table, 1), ready[...], ((1,), (1,)))


def fine_edge_kernel(plan, halo_ref, edge_ref, y_table, z_table, push_ref, ready_ref, mixed, *, partner):
    x, y = plan.x, plan.y
    gx = lax.axis_index("gx")
    odd = gx % 2
    high = 1 - odd if partner else odd
    keep = mask(True) if partner else mask(jnp.where(high == 1, gx < x.count - 1, gx > 0))
    padding = fine_padding(plan)
    away = lambda k: jnp.where(high == 1, k, REACH - 1 - k)

    def get(k):
        return jnp.concatenate([plane(halo_ref, 0, plan.fine_rows, away(k)) * keep] + padding, axis=0)

    def put(k, value):
        mixed[k] = value

    mix_planes(get, put, REACH, plan.fine_matrix(y_table))
    for s, sigma in enumerate(STENCIL_SIGMAS):
        for r in range(0, y.length, 16):
            row = s * y.length + r
            after = {REACH + k: mixed[k, row : row + 16, :] for k in range(REACH)}
            for i, added in enumerate(stencil(after, range(REACH), sigma)):
                value = edge_ref[away(i) + REACH * high, row : row + 16, :] + added
                top, low = split(value)
                at = away(i) * (y.length // 16) + r // 16
                for c, part in enumerate((top, low, top)):
                    start = (3 * c + s) * LANES
                    ready_ref[at, :, start : start + LANES] = part
    whole = ready_ref[...].reshape(REACH * y.length, 9 * LANES)
    push_ref[...] = dot(plan.z_matrix(z_table, 1), whole, ((1,), (1,)))


def fine_main_kernel(plan, partner_ref, side_ref, z_table, out_ref):
    odd = lax.axis_index("gx") % 2
    for ref, at in ((partner_ref, 1 - odd), (side_ref, odd)):
        whole = ref[...].reshape(REACH * plan.y.length, 9 * LANES)
        out_ref[at] = dot(whole, plan.z_matrix(z_table, 0), ((1,), (1,)))


def coarse_inner_kernel(plan, ext_ref, pair_ref, y_table, *refs):
    *parts, mixed = refs
    own = plan.x.width[1]

    def put(i, value):
        mixed[i] = value

    get = lambda i: ext_ref[i] if i < own else plan.pair_plane(pair_ref, i - own)
    mix_planes(get, put, own + plan.planes, plan.coarse_matrix(y_table))
    for level, part in zip((1, 2), parts):
        rows, width = (plan.rows1, plan.rows2)[level - 1], plan.x.width[level]
        wanted = range(LOW[level], LOW[level] + width)
        for s, sigma in enumerate(STENCIL_SIGMAS):
            for r in range(0, rows, 8):
                cells = collect_inner(plan, level, mixed, plan.group[level] + s * rows + r, 8)
                for i, value in enumerate(stencil(cells, wanted, sigma)):
                    part[s * width + i, r : r + 8, :] = value


def adder(plan, level, cells):
    start, width = LOW[level], plan.x.width[level]

    def add(cell, value, keep):
        if start - REACH <= cell < start + width + REACH:
            value = value * keep
            cells[cell] = cells[cell] + value if cell in cells else value

    return add


def collect_inner(plan, level, inner, row, rows):
    x, odd = plan.x, lax.axis_index("gx") % 2
    size, width, start, own = x.length >> level, x.width[level], LOW[level], x.width[1]
    cells = {start + k: inner[k, row : row + rows, :] for k in range(width)}
    add = adder(plan, level, cells)
    layers = FACE if level == 1 else width
    for k in range(layers):
        value = inner[own + k, row : row + rows, :]
        add(size + start + k, value, mask(odd == 0))
        add(-size + start + width - layers + k, value, mask(odd == 1))
    return cells


def collect_outer(plan, level, outer, row, rows):
    x, gx = plan.x, lax.axis_index("gx")
    odd, chip, chips = gx % 2, gx // 2, plan.x.count // 2
    size, width, start = x.length >> level, x.width[level], LOW[level]
    cells = {}
    add = adder(plan, level, cells)
    if level == 1:
        for k in range(FACE):
            value = outer[k, row : row + rows, :]
            add(-size + start + width - FACE + k, value, mask((chip > 0) & (odd == 0)))
            add(size + start + k, value, mask((chip < chips - 1) & (odd == 1)))
        return cells
    for n, offset in enumerate(plan.near_chips):
        for shift, here in ((-offset, chip >= offset), (chips - offset, chip < offset)):
            if abs(shift) != 1:
                continue
            for core in (0, 1):
                keep = mask(here & (odd == core))
                first = 2 * size * shift - size * core + start + (size if shift < 0 else 0)
                for k in range(plan.planes):
                    add(first + k, outer[plan.planes * n + k, row : row + rows, :], keep)
    return cells


def coarse_kernel(plan, part1, part2, *refs):
    chips = plan.x.count // 2 - 1
    others, refs = refs[:chips], refs[chips:]
    side_in, *pushes = refs[:4]
    y_table, z_table, partner_ref, side_ref, e1_ref, e2_ref, outer, *ready = refs[4:]

    def put(i, value):
        outer[i] = value

    lanes = lax.broadcasted_iota(jnp.int32, (1, LANES), 1)
    groups = [plane(side_in, plan.fine_rows * REACH, plan.coarse_rows, g) for g in range(plan.face_groups + 1)]

    def get(i):
        n, p = i // plan.planes, i % plan.planes
        two = plane(others[plan.near_chips[n] - 1], 0, plan.coarse_rows, p // 3)
        value = roll_lanes(two, plan.lane[2] - SLOT * (p % 3))
        if n == 0 and p < FACE:
            value = jnp.where(lanes < plan.lane[2], unpack_face(plan, groups, p), value)
        return value

    mix_planes(get, put, plan.planes * len(plan.near_chips), plan.coarse_matrix(y_table))
    x = plan.x
    results = []
    for level in (1, 2):
        rows = plan.rows1 if level == 1 else plan.rows2
        wanted = range(LOW[level], LOW[level] + x.width[level])
        for s, sigma in enumerate(STENCIL_SIGMAS):
            for r in range(0, rows, 8):
                cells = collect_outer(plan, level, outer, plan.group[level] + s * rows + r, 8)
                for i, added in enumerate(stencil(cells, wanted, sigma)):
                    value = (part1, part2)[level - 1][s * x.width[level] + i, r : r + 8, :]
                    put_ready(ready[level - 1], 3, s, i * rows + r, value if added is None else value + added)
        results.append(dot(plan.z_matrix(z_table, level + 1), ready[level - 1][...], ((1,), (1,))))
    one, two = results
    e1_ref[...] = one[: plan.tall[1]]
    e2_ref[...] = two[: plan.tall[2]]
    inner, partner, side = (p[...] for p in pushes)
    odd = lax.axis_index("gx") % 2 == 1
    pushed = jnp.concatenate([inner, jnp.where(odd, partner, side), jnp.where(odd, side, partner)], axis=1)
    for n, ref in enumerate((partner_ref, side_ref)):
        ref[:8, :] = pushed[8 * n : 8 * n + 8, :]
        ref[8:, :] = jnp.zeros((16, ref.shape[1]), F32)
        start = plan.tall[1] + 16 * n
        ref[8:, : plan.flat[1]] = one[start : start + 16]
        start = plan.tall[2] + 16 * n
        ref[8:, 512 : 512 + plan.flat[2]] = two[start : start + 16]


def top_chips_kernel(plan, top_ref, *refs):
    *others, out_ref = refs
    total = top_ref[...]
    for ref in others:
        total = total + get_flat(ref, plan.coarse_rows * plan.pair_groups, plan.top_shape)
    out_ref[...] = total


def top_kernel(plan, *refs):
    *values, out_ref = refs
    total = functools.reduce(jnp.add, [v[...] for v in values])
    shape = (plan.flat_top, plan.flat[3])
    source, target = (lax.broadcasted_iota(jnp.int32, shape, d) for d in (0, 1))
    first_x = (plan.x.length >> 3) * lax.axis_index("gx") + LOW[3]
    first_y = (plan.y.length >> 3) * lax.axis_index("gy") + LOW[3]
    apart_x = source // plan.whole3 - target // plan.rows3 - first_x
    apart_y = source % plan.whole3 - target % plan.rows3 - first_y
    square = (apart_x * apart_x + apart_y * apart_y).astype(F32)
    result, tall = None, plan.tall[3]
    for s, sigma in enumerate(TOP_SIGMAS):
        matrix = jnp.exp(square * (-1.0 / sigma**2))
        matrix_high, matrix_low = split(matrix)
        high, low = split(total[s * tall : (s + 1) * tall])
        left = jnp.concatenate([high, low, high], axis=1)
        term = dot(left, jnp.concatenate([matrix_high, matrix_high, matrix_low], axis=0))
        result = term if result is None else result + term
    out_ref[...] = result


def finish_kernel(plan, inner_ref, edge_ref, e1_ref, e2_ref, partner_ref, side_ref, e3_ref, flat, tall, out_ref, e1, e2):
    x, y, z = plan.x, plan.y, plan.z
    gx, gy, gz = (lax.axis_index(name) for name in ("gx", "gy", "gz"))
    odd = gz % 2
    for window, own, tall_ in ((e1, e1_ref, plan.tall[1]), (e2, e2_ref, plan.tall[2])):
        window[:tall_, :] = own[...]
        if window.shape[0] > tall_:
            window[tall_:, :] = jnp.zeros((window.shape[0] - tall_, window.shape[1]), F32)
    kept = lax.broadcasted_iota(jnp.int32, (16, 1), 0) < FACE
    for ref, high in ((partner_ref, odd == 0), (side_ref, odd == 1)):
        one = jnp.where(kept, ref[8:, : plan.flat[1]], 0.0)
        two = ref[8:, 512 : 512 + plan.flat[2]]
        for window, value, tall_ in ((e1, one, plan.tall[1]), (e2, two, plan.tall[2])):
            window[:16, :] += value * mask(~high)
            window[tall_ - 16 : tall_, :] += value * mask(high)

    bounds = [int(r) for r in plan.tall_rows]

    def along_z(value, number, parts):
        high, low = split(value)
        stacked = jnp.concatenate([high, low, high][:parts], axis=0)
        return dot(stacked, tall[gz, bounds[number] : bounds[number + 1], :], ((0,), (0,)))

    def inside(level):
        rows = (0, plan.rows1, plan.rows2, plan.rows3)[level]
        index = lax.broadcasted_iota(jnp.int32, (plan.flat[level], LANES), 0)
        cell_x = index // rows + ((x.length >> level) * gx + LOW[level])
        cell_y = index % rows + ((y.length >> level) * gy + LOW[level])
        in_x = (cell_x >= 0) & (cell_x < (x.count * x.length) >> level)
        return in_x & (cell_y >= 0) & (cell_y < (y.count * y.length) >> level)

    flat_bounds = [int(r) for r in plan.flat_rows]

    def finer(value, number):
        high, low = split(value)
        matrix = flat[flat_bounds[number] : flat_bounds[number + 1], :][:, : value.shape[0]]
        both = dot(matrix, jnp.concatenate([high, low], axis=1))
        return both[:, :LANES] + both[:, LANES:]

    pad = up(plan.tall[3], 16) - plan.tall[3]
    e3 = jnp.concatenate([e3_ref[...]] + ([jnp.zeros((pad, e3_ref.shape[1]), F32)] if pad else []), axis=0)
    ends = along_z(jnp.concatenate([partner_ref[:8], side_ref[:8]], axis=0), 1, 2)
    one, two, three = along_z(e1[...], 0, 2), along_z(e2[...], 2, 3), along_z(e3, 3, 3)
    three = jnp.where(inside(3), three, 0.0)
    two = jnp.where(inside(2), two + finer(three, 0)[: plan.flat[2]], 0.0)
    one = jnp.where(inside(1), one + finer(two, 1)[: plan.flat[1]], 0.0)
    coarse = finer(one, 2) + ends
    inner = inner_ref.shape[0]
    tiles = y.length // 8
    for k, (x_, t) in enumerate(plan.tiles()):
        row = 8 * k
        value = coarse[row : row + 8]
        if row < inner:
            value = value + inner_ref[row : row + 8]
        else:
            end, row = divmod(row - inner, edge_ref.shape[1])
            value = value + edge_ref[end, row : row + 8]
        out_ref[8 * (tiles * x_ + t) : 8 * (tiles * x_ + t) + 8] = value


def call(kernel, plan, operands, outs, scratch=(), hbm=(), vmem=32):
    whole, left = pl.BlockSpec(memory_space=pltpu.VMEM), pl.BlockSpec(memory_space=pl.ANY)
    return pl.pallas_call(
        functools.partial(kernel, plan),
        in_specs=[left if i in hbm else whole for i in range(len(operands))],
        out_specs=[whole] * len(outs),
        scratch_shapes=list(scratch),
        out_shape=list(outs),
        compiler_params=pltpu.CompilerParams(vmem_limit_bytes=int(vmem * 2**20)),
    )(*[jnp.asarray(o) for o in operands])


def shift(value, axis, offset):
    count = lax.axis_size(axis)
    return lax.ppermute(value, axis, [(i, (i + offset) % count) for i in range(count)])


def swap(value, axes, partner):
    first, second = (lax.axis_size(a) for a in axes)
    pairs = []
    for i in range(first):
        for j in range(second):
            k, m = partner(i, j)
            pairs.append((i * second + j, k * second + m))
    return lax.ppermute(value, axes, pairs)


def side_of(count):
    return lambda i: None if i in (0, count - 1) else i + (1 if i % 2 else -1)


def shards(plan, charges):
    x, y, z = plan.x, plan.y, plan.z
    array = lambda *shape: jax.ShapeDtypeStruct(shape, F32)
    vmem = lambda *shape: pltpu.VMEM(shape, F32)
    ready = lambda rows, sigmas: pltpu.VMEM((rows, 3 * sigmas * LANES), BF)
    side_x, side_z = side_of(x.count), side_of(z.count)
    partner_x = lambda v: swap(v, ("gx", "gy"), lambda i, j: (i ^ 1, j))
    across_x = lambda v: swap(v, ("gx", "gy"), lambda i, j: (i, j ^ 1) if side_x(i) is None else (side_x(i), j))
    partner_z = lambda v: swap(v, ("gx", "gz"), lambda i, j: (i, j ^ 1))
    across_z = lambda v: swap(v, ("gx", "gz"), lambda i, j: (i ^ 1, j) if side_z(j) is None else (i, side_z(j)))

    rows_y = 8 * x.length + 16 * x.width[1]
    table = plan.restrict_tables()
    own, top, y_table, top_table, *to_y = call(
        restrict_kernel,
        plan,
        [charges, table],
        [
            array(x.width[1], plan.rows1, LANES),
            array(plan.tall[3], plan.flat_top),
            jax.ShapeDtypeStruct((3 * y.length + plan.rows_mixed + plan.halo_rows, plan.y_cols), BF),
            jax.ShapeDtypeStruct((2 * plan.tall[3], up(plan.top_cols, LANES)), BF),
        ]
        + [array(rows_y // 8, 8, LANES)] * plan.kinds,
        [
            vmem(x.length, plan.rows_restricted, LANES),
            vmem(x.width[3], plan.whole3, LANES),
            vmem(*charges.shape),
            pltpu.VMEM((sum(plan.blocks), 16, LANES), BF),
            pltpu.SemaphoreType.DMA((6,)),
        ],
        hbm=(0, 1),
        vmem=53,
    )
    from_y = []
    for offset in range(1, y.count):
        value = to_y[0 if offset == 1 else -1]
        value = value if offset in (1, y.count - 1) else value[x.length :]
        from_y.append(shift(value, "gy", offset))

    tops = [swap(top, ("gx", "gz"), lambda i, j, m=m: (i, j ^ m)) for m in range(1, z.count)]
    (top,) = call(top_z_kernel, plan, [top, *tops, top_table], [array(*plan.top_shape)])

    z_table = plan.z_tables()
    inner_cells = (x.length - 2 * REACH) * y.length
    inner, edge, held = call(
        fine_inner_kernel,
        plan,
        [charges, y_table],
        [array(3, inner_cells, LANES), array(2 * REACH, 3 * y.length, LANES), array(*charges.shape)],
        [vmem(x.length, 3 * y.length, LANES)],
    )
    edge, *from_y = lax.optimization_barrier((edge, *from_y))

    ext, to_partner, to_side = call(
        extend_kernel,
        plan,
        [held, own, top, *from_y],
        [
            array(x.width[1], plan.coarse_rows, LANES),
            array((plan.top_row + plan.top_rows) // 8, 8, LANES),
            array(plan.side_rows // 8, 8, LANES),
        ],
    )
    from_side, pair = across_x(to_side), partner_x(to_partner)

    main_inner, push_inner, edge = call(
        fine_halo_kernel,
        plan,
        [inner, edge, y_table, z_table, *from_y],
        [array(inner_cells, z.length), array(16, inner_cells), array(2 * REACH, 3 * y.length, LANES)],
        [vmem(x.length, plan.halo_rows, LANES), ready(inner_cells, 3)],
    )

    chips = x.count // 2
    rows_x = plan.pair_groups * plan.coarse_rows + plan.top_rows
    top, *to_chips = call(
        chip_kernel,
        plan,
        [ext, pair, top],
        [array(*plan.top_shape)] + [array(rows_x // 8, 8, LANES)] * (chips - 1),
    )
    from_chips = [
        swap(v, ("gx", "gy"), lambda i, j, k=k: ((i + 2 * k) % x.count ^ 1, j))
        for k, v in zip(range(1, chips), to_chips)
    ]
    parts = call(
        coarse_inner_kernel,
        plan,
        [ext, pair, y_table],
        [array(3 * x.width[1], plan.rows1, LANES), array(3 * x.width[2], plan.rows2, LANES)],
        [vmem(x.width[1] + plan.planes, plan.rows_mixed, LANES)],
    )

    def fine_end(halo, is_partner):
        return call(
            functools.partial(fine_edge_kernel, partner=is_partner),
            plan,
            [halo, edge, y_table, z_table],
            [array(16, REACH * y.length), jax.ShapeDtypeStruct((REACH * y.length // 16, 16, 9 * LANES), BF)],
            [vmem(REACH, 3 * y.length, LANES)],
        )

    push_partner, ready_partner = fine_end(pair, True)
    from_side, push_partner, *parts = lax.optimization_barrier((from_side, push_partner, *parts))
    push_side, ready_side = fine_end(from_side, False)
    pushes = [push_inner, push_partner, push_side]
    window = lambda level: array(plan.tall[level], plan.flat[level])
    to_partner, to_side, e1, e2 = call(
        coarse_kernel,
        plan,
        [*parts, *from_chips, from_side, *pushes, y_table, z_table],
        [array(24, 1024), array(24, 1024), window(1), window(2)],
        [vmem(plan.planes * len(plan.near_chips), plan.rows_mixed, LANES), ready(plan.flat[1], 3), ready(plan.flat[2], 3)],
    )
    from_near = [partner_z(to_partner), across_z(to_side)]

    (top,) = call(top_chips_kernel, plan, [top, *from_chips], [array(*top.shape)])
    tops = [top] + [shift(top, "gy", offset) for offset in range(1, y.count)]
    (e3,) = call(top_kernel, plan, tops, [window(3)])

    (main_edge,) = call(
        fine_main_kernel, plan, [ready_partner, ready_side, z_table], [array(2, REACH * y.length, z.length)]
    )
    (potential,) = call(
        finish_kernel,
        plan,
        [main_inner, main_edge, e1, e2, *from_near, e3, *plan.finish()],
        [array(x.length * y.length, z.length)],
        [vmem(up(plan.tall[level], 16), plan.flat[level]) for level in (1, 2)],
    )
    return potential.reshape(charges.shape)


def solution(mesh):
    counts = [mesh.shape[name] for name in ("gx", "gy", "gz")]

    def run(charges):
        plan = Plan(counts, [size // n for size, n in zip(charges.shape, counts)])
        placed = P("gx", "gy", "gz")
        return jax.shard_map(
            functools.partial(shards, plan), mesh=mesh, in_specs=(placed,), out_specs=placed, check_vma=False
        )(charges)

    return run
```

```python
import functools

import jax
import jax.numpy as jnp
import numpy as np
from jax import lax
from jax.experimental import pallas as pl
from jax.experimental.pallas import tpu as pltpu
from jax.sharding import PartitionSpec as P

REACH = 8
STENCIL_SIGMAS = (1.0, 2.0, 3.5)
STENCIL_WEIGHTS = (0.4, 0.1, 0.03)
TOP_SIGMAS = (1.5, 4.0)
TOP_WEIGHTS = (0.03, 0.006)
SPLINE_TAPS = np.array((-1.0, 0.0, 9.0, 16.0, 9.0, 0.0, -1.0)) / 16.0

LOW = (0, -1, -2, -2)
EXTRA = (0, 3, 5, 5)
SLOT = 40
FACE = 11
LANES = 128
BF = jnp.bfloat16
F32 = jnp.float32


def up(value, unit):
    return -(-value // unit) * unit


def band(rows, cols, sigma, reach):
    distance = cols[None, :] - rows[:, None]
    return np.where(abs(distance) <= reach, np.exp(-((distance / sigma) ** 2)), 0.0)


def restriction(size):
    position = np.arange(size)[None, :] - 2 * np.arange(size // 2)[:, None] + 3
    inside = (position >= 0) & (position <= 6)
    return np.where(inside, SPLINE_TAPS[np.clip(position, 0, 6)], 0.0)


class Axis:
    def __init__(self, count, length):
        self.count, self.length = count, length
        self.width = [(length >> level) + EXTRA[level] for level in range(4)]

    def window(self, level, brick):
        size = self.length >> level
        cells = brick * size + LOW[level] + np.arange(self.width[level])
        return cells, ((cells >= 0) & (cells < self.count * size)).astype(float)

    def partial(self, level, brick):
        matrix = np.eye(self.count * self.length)
        for _ in range(level):
            matrix = restriction(matrix.shape[0]) @ matrix
        cells, inside = self.window(level, brick)
        rows = matrix[np.clip(cells, 0, len(matrix) - 1)] * inside[:, None]
        return rows[:, brick * self.length : (brick + 1) * self.length]

    def prolong(self, level, brick):
        matrix = restriction((self.count * self.length) >> (level - 1)).T
        rows, row_inside = self.window(level - 1, brick)
        cols, col_inside = self.window(level, brick)
        taken = matrix[np.clip(rows, 0, len(matrix) - 1)][:, np.clip(cols, 0, matrix.shape[1] - 1)]
        return taken * row_inside[:, None] * col_inside[None, :]

    def mix(self, level, sigma, target, source):
        rows, row_inside = self.window(level, target)
        cols, col_inside = self.window(level, source)
        reach = REACH if level < 3 else self.count * self.length
        return band(rows, cols, sigma, reach) * row_inside[:, None] * col_inside[None, :]


def place(shape, *pieces):
    whole = np.zeros(shape)
    for row, col, block in pieces:
        whole[row : row + block.shape[0], col : col + block.shape[1]] += block
    return whole


def halves(matrix):
    high = matrix.astype(jnp.bfloat16)
    low = (matrix - high.astype(np.float64)).astype(jnp.bfloat16)
    return high, low


def left3(matrix):
    high, low = halves(matrix)
    return np.concatenate([high, low, high], axis=-1)


def left3t(matrix):
    high, low = halves(matrix)
    return np.concatenate([high, high, low], axis=-1)


def right3(matrix):
    high, low = halves(matrix)
    return np.concatenate([high, high, low], axis=-2)


def split(value):
    high = value.astype(BF)
    return high, (value - high.astype(F32)).astype(BF)


def dot(left, right, dims=((1,), (0,))):
    return lax.dot_general(left, right, (dims, ((), ())), preferred_element_type=F32)


class Plan:
    def __init__(self, counts, lengths):
        self.x, self.y, self.z = (Axis(n, length) for n, length in zip(counts, lengths))
        x, y, z = self.x, self.y, self.z
        assert x.count % 2 == 0 and x.count >= 4 and y.count % 2 == 0
        assert z.count >= 4 and z.count & (z.count - 1) == 0
        self.lane = [0, 0, z.width[1], z.width[1] + z.width[2]]
        self.lane_end = self.lane[3] + z.width[3]
        assert self.lane_end <= LANES and z.length == LANES
        self.rows1, self.rows2 = up(y.width[1], 8), up(y.width[2], 16)
        self.rows3, self.whole3 = up(y.width[3], 16), up(y.count * y.length >> 3, 8)
        assert self.rows2 <= 16 and self.rows3 <= 16 and FACE <= 14 and self.rows1 == 24
        self.row = [0, 0, self.rows1, self.rows1 + self.rows2]
        self.row_face = self.rows1 + self.rows2 + self.whole3
        self.kinds = 1 if y.count == 2 else 2
        self.rows_restricted = self.row_face + 16 * self.kinds
        self.overlay = y.count == 2 and y.width[1] + 3 <= self.rows1
        self.coarse_rows = up(24 + 16 * (y.count - 1), 16) if not self.overlay else 32
        self.fine_halos = 1 if y.count == 2 else 2
        self.fine_rows = y.length + 8 * self.fine_halos
        self.pair_width = [w + (x.length >> l) for l, w in enumerate(x.width)]
        self.planes = max(FACE, x.width[2])
        self.half, self.left = LANES // 2, z.width[1] - LANES // 2
        self.face_groups = up(FACE, 2) // 2
        assert 0 < self.left and self.left * FACE <= LANES and z.width[2] <= SLOT
        chips = x.count // 2
        self.near_chips = [1] if chips == 2 else [1, chips - 1]
        self.pair_groups = up(self.planes, 3) // 3
        self.side_rows = REACH * self.fine_rows + (self.face_groups + 1) * self.coarse_rows
        self.flat_top = up((x.count * x.length >> 3) * self.whole3, LANES)
        self.top_shape = 2 * up(z.width[3], 8), self.flat_top
        self.top_rows = self.top_shape[0] * self.flat_top // LANES
        self.top_row = REACH * self.fine_rows + self.planes * self.coarse_rows
        assert self.planes <= x.width[1]
        self.group = [0, 0, 3 * self.rows1]
        self.rows_mixed = up(3 * self.rows1 + 3 * self.rows2, 16)
        self.tall = [0, up(z.width[1], 8), up(z.width[2], 8), up(z.width[3], 8)]
        assert self.tall[1] - 16 == z.width[1] - FACE and self.tall[2] - 16 == z.width[2] - 13
        self.flat = [0, x.width[1] * self.rows1, x.width[2] * self.rows2, x.width[3] * self.rows3]
        assert self.flat[1] <= 512 and self.flat[2] <= 256 and self.flat[3] <= 256

    def face_kind(self, axis, offset, source):
        if axis.count == 2:
            return 1 - source
        return 1 if offset == 1 else 0

    def near_y(self, halos):
        return [halos[0]] if self.y.count == 2 else [halos[0], halos[-1]]

    def tiles(self):
        nx, nt = self.x.length, self.y.length // 8
        inner = range(REACH, nx - REACH)
        edge = [*range(REACH), *range(nx - REACH, nx)]
        order = [(x, t) for x in inner for t in range(1, nt - 1)]
        order += [(x, t) for x in inner for t in (0, nt - 1)]
        return order + [(x, t) for x in edge for t in range(nt)]

    def pair_plane(self, ref, index):
        return plane(ref, self.fine_rows * REACH, self.coarse_rows, index)

    def face_row(self, j):
        return j if j < 8 or not self.overlay else j + 3

    def restrict_tables(self):
        rows = up(self.rows_restricted, 16)
        along_y = np.stack([place((rows, LANES), (0, 0, m)) for m in self.restrict_y().astype(np.float32)])
        parts = [self.restrict_z(), along_y, self.y_tables(), self.top_z()]
        parts = [p.astype(np.float32) for p in parts]
        blocks = []
        for p in parts:
            columns = [p[:, :, c : c + LANES] for c in range(0, p.shape[2], LANES)]
            blocks.append(np.concatenate(columns, axis=1).reshape(len(p), -1, 16, LANES))
        self.blocks = [b.shape[1] for b in blocks]
        self.blocks.append(2 * up(self.tall[3], 16) // 16)
        table = np.concatenate([b.reshape(-1, 16, LANES) for b in blocks] + [self.top_select().reshape(-1, 2, LANES)
            .transpose(1, 0, 2).reshape(-1, 16, LANES).astype(np.float32)])
        return table.astype(jnp.bfloat16)

    def y_tables(self):
        fine, halo, coarse = self.fine_y(), self.halo_y(), self.coarse_y()
        cols = up(max(fine.shape[2], coarse.shape[2]), LANES)
        self.halo_rows, self.halo_cols = halo.shape[1:]
        widen = lambda t: np.pad(t, ((0, 0), (0, 0), (0, cols - t.shape[2])))
        self.fine_cols, self.coarse_cols = fine.shape[2], coarse.shape[2]
        self.y_cols = cols
        return np.concatenate([widen(fine), widen(coarse), widen(halo)], axis=1)

    def z_tables(self):
        tables = [*self.fine_z(), *[self.coarse_z(level) for level in (1, 2)]]
        cols = 9 * LANES
        self.z_rows = np.cumsum([0] + [t.shape[1] for t in tables])
        return np.concatenate([np.pad(t, ((0, 0), (0, 0), (0, cols - t.shape[2]))) for t in tables], axis=1)

    def fine_matrix(self, ref):
        return ref[: 3 * self.y.length, :][:, : self.fine_cols]

    def coarse_matrix(self, ref):
        start = 3 * self.y.length
        return ref[start : start + self.rows_mixed, :][:, : self.coarse_cols]

    def halo_matrix(self, ref):
        return ref[3 * self.y.length + self.rows_mixed :, :][:, : self.halo_cols]

    def z_matrix(self, ref, number):
        return ref[lax.axis_index("gz"), int(self.z_rows[number]) : int(self.z_rows[number + 1]), :]

    def restrict_z(self):
        z = self.z
        return np.stack(
            [
                right3(place((z.length, LANES), *[(0, self.lane[l], z.partial(l, b).T) for l in (1, 2, 3)]))
                for b in range(z.count)
            ]
        )

    def restrict_y(self):
        y, tables = self.y, []
        for b in range(y.count):
            pieces = [(self.row[l], 0, y.partial(l, b)) for l in (1, 2)]
            cells, inside = y.window(3, b)
            for cell, line in zip(cells[inside > 0], y.partial(3, b)[inside > 0]):
                pieces.append((self.row[3] + cell, 0, line[None]))
            first = y.partial(1, b)
            for k in range(self.kinds):
                kind = self.face_kind(y, 1, b) if self.kinds == 1 else 1 - k
                start = (y.width[1] - FACE) * kind
                for j in range(FACE):
                    pieces.append((self.row_face + 16 * k + self.face_row(j), 0, first[start + j][None]))
            tables.append(left3(place((self.rows_restricted, y.length), *pieces)))
        return np.stack(tables)

    def fine_y(self):
        y, tables = self.y, []
        for b in range(y.count):
            pieces = []
            for s, sigma in enumerate(STENCIL_SIGMAS):
                row = s * y.length
                pieces.append((row, 0, y.mix(0, sigma, b, b)))
                for h in range(self.fine_halos):
                    offset = 1 if h == 0 else y.count - 1
                    source = (b - offset) % y.count
                    start = (y.length - REACH) * self.face_kind(y, offset, source)
                    block = y.mix(0, sigma, b, source)[:, start : start + REACH]
                    pieces.append((row, y.length + 8 * h, block))
            tables.append(left3(place((3 * y.length, up(self.fine_rows, 16)), *pieces)))
        return np.stack(tables)

    def halo_y(self):
        n, cols = self.y.length, up(self.fine_rows, 16)
        rows = [s * n + r for s in range(3) for r in (*range(8), *range(n - 8, n))]
        columns = [c * cols + n + k for c in range(3) for k in range(cols - n)]
        return self.fine_y()[:, rows][:, :, columns]

    def coarse_y(self):
        y, tables = self.y, []
        for b in range(y.count):
            whole = np.zeros((self.rows_mixed, self.coarse_rows))
            for level in (1, 2):
                rows = self.rows1 if level == 1 else self.rows2
                for s, sigma in enumerate(STENCIL_SIGMAS):
                    top = self.group[level] + s * rows
                    for offset in range(y.count):
                        source = (b - offset) % y.count
                        block = y.mix(level, sigma, b, source)
                        if level == 1 and offset:
                            start = (y.width[1] - FACE) * self.face_kind(y, offset, source)
                            block = block[:, start : start + FACE]
                        for j in range(block.shape[1]):
                            slot = self.face_row(j) if level == 1 and offset else j
                            if self.overlay and offset:
                                slot = 24 + slot if slot < 8 else 8 + slot
                            elif offset:
                                slot = 24 + 16 * (offset - 1) + slot
                            whole[top : top + y.width[level], slot] += block[:, j]
            tables.append(left3(whole))
        return np.stack(tables)

    def near_z(self, b, step):
        side = 1 if (b % 2 == 0) == (step == 0) else -1
        return side, b + side if 0 <= b + side < self.z.count else None

    def fine_z(self):
        z, own, pushed = self.z, [], []
        for b in range(z.count):
            mixes = lambda target: [
                w * z.mix(0, sigma, target, b) for sigma, w in zip(STENCIL_SIGMAS, STENCIL_WEIGHTS)
            ]
            own.append(left3t(np.concatenate(mixes(b), axis=1)))
            rows = []
            for step in (0, 1):
                side, target = self.near_z(b, step)
                if target is None:
                    rows.append(np.zeros((8, 3 * z.length)))
                else:
                    rows.append(np.concatenate([m[:8] if side > 0 else m[-8:] for m in mixes(target)], axis=1))
            pushed.append(left3t(np.concatenate(rows, axis=0)))
        return np.stack(own), np.stack(pushed)

    def coarse_z(self, level):
        z, tables = self.z, []
        cols, tall = LANES * len(STENCIL_SIGMAS), self.tall[level]
        for b in range(z.count):

            def mixed(target):
                blocks = [z.mix(level, sigma, target, b) * w * 0.5**level for sigma, w in zip(STENCIL_SIGMAS, STENCIL_WEIGHTS)]
                blocks = [place((z.width[level], LANES), (0, self.lane[level], block)) for block in blocks]
                return np.concatenate(blocks, axis=1)

            pieces = [place((tall, cols), (0, 0, mixed(b)))]
            layers = FACE if level == 1 else 13
            for step in (0, 1):
                side, target = self.near_z(b, step)
                if target is None:
                    pieces.append(np.zeros((16, cols)))
                else:
                    block = mixed(target)
                    pieces.append(place((16, cols), (0, 0, block[:layers] if side > 0 else block[-layers:])))
            whole = np.concatenate(pieces, axis=0)
            tables.append(left3t(place((up(len(whole), 16), cols), (0, 0, whole))))
        return np.stack(tables)

    def top_z(self):
        z, tall, tables = self.z, self.tall[3], []
        for b in range(z.count):
            pieces = []
            for s, (sigma, w) in enumerate(zip(TOP_SIGMAS, TOP_WEIGHTS)):
                for m in range(z.count):
                    pieces.append((tall * s, tall * m, w * z.mix(3, sigma, b, b ^ m)))
            tables.append(left3(place((2 * tall, z.count * tall), *pieces)))
        self.top_cols = tables[0].shape[1]
        widen = up(self.top_cols, LANES) - self.top_cols
        return np.pad(np.stack(tables), ((0, 0), (0, 0), (0, widen)))

    def top_select(self):
        matrix = place((up(self.tall[3], 16), LANES), (0, self.lane[3], np.eye(self.z.width[3])))
        return np.concatenate([matrix, matrix], axis=1).astype(jnp.bfloat16)

    def finish(self):
        x, y, z = self.x, self.y, self.z
        rows = (y.length, self.rows1, self.rows2, self.rows3)
        exact = lambda m: np.asarray(m, dtype=jnp.bfloat16)
        tall = []
        for b in range(z.count):
            ends = (0, z.length - 8) if b % 2 else (z.length - 8, 0)
            one = z.prolong(1, b)
            two = one @ z.prolong(2, b)
            three = two @ z.prolong(3, b)
            deep = [place((up(self.tall[l], 16), LANES), (0, 0, m.T)) for l, m in ((1, one), (2, two), (3, three))]
            ends = place((16, LANES), *[(8 * k, 0, np.eye(8, LANES, end)) for k, end in enumerate(ends)])
            parts = [exact(deep[0]), exact(deep[0]), exact(ends), exact(ends), right3(deep[1]), right3(deep[2])]
            tall.append(np.concatenate(parts))
        self.tall_rows = np.cumsum([0] + [2 * up(self.tall[1], 16), 32, 3 * up(self.tall[2], 16), 3 * up(self.tall[3], 16)])

        flat = []
        for level in (3, 2, 1):
            p, q = (Axis(5, axis.length).prolong(level, 2) for axis in (x, y))
            matrix = np.kron(p, place((rows[level - 1], rows[level]), (0, 0, q)))
            if level == 1:
                matrix = matrix[[x_ * y.length + 8 * t + k for x_, t in self.tiles() for k in range(8)]]
            flat.append(matrix)
        self.flat_rows = np.cumsum([0] + [up(len(m), 16) for m in flat])
        cols = up(max(self.flat), LANES)
        joined = np.concatenate([np.pad(m, ((0, -len(m) % 16), (0, cols - m.shape[1]))) for m in flat])
        return exact(joined), np.stack(tall)


def plane(ref, base, rows, index):
    return ref[pl.ds(base // 8 + rows // 8 * index, rows // 8)].reshape(rows, LANES)


def put_plane(ref, row, value):
    ref[row // 8 : (row + value.shape[0]) // 8] = value.reshape(value.shape[0] // 8, 8, LANES)


def put_flat(ref, row, value):
    for c in range(value.shape[1] // LANES):
        put_plane(ref, row + c * value.shape[0], value[:, c * LANES : (c + 1) * LANES])


def get_flat(ref, row, shape):
    parts = [plane(ref, row, shape[0], c) for c in range(shape[1] // LANES)]
    return jnp.concatenate(parts, axis=1)


def restrict_kernel(plan, q_hbm, table_hbm, own_ref, top_ref, y_table_ref, z_table_ref, *rest):
    targets, (mixed, top, q_ref, table_ref, sems) = rest[: plan.kinds], rest[plan.kinds :]
    nx, ny, nz = plan.x.length, plan.y.length, plan.z.length
    by, bz = lax.axis_index("gy"), lax.axis_index("gz")
    copies, starts, source, at = [pltpu.make_async_copy(q_hbm, q_ref, sems.at[0])], [], 0, 0
    bricks = ((plan.z.count, bz), (plan.y.count, by), (plan.y.count, by), (plan.z.count, bz), (1, 0))
    for n, (blocks, (count, brick)) in enumerate(zip(plan.blocks, bricks)):
        part = table_hbm.at[pl.ds(source + blocks * brick, blocks)]
        copies.append(pltpu.make_async_copy(part, table_ref.at[pl.ds(at, blocks)], sems.at[n + 1]))
        starts.append(at)
        source, at = source + count * blocks, at + blocks
    for copy in copies:
        copy.start()
    for copy in copies:
        copy.wait()
    blocks_z, blocks_y = plan.blocks[:2]
    matrix_z = table_ref[:blocks_z].reshape(3 * nz, LANES)
    matrix_y = table_ref[blocks_z : blocks_z + blocks_y].reshape(16 * blocks_y, LANES)
    matrix_y = matrix_y[:, : 3 * ny]
    at_select = starts[4]
    for ref, at in ((y_table_ref, starts[2]), (z_table_ref, starts[3])):
        rows = ref.shape[0]
        for c in range(ref.shape[1] // LANES):
            first = at + rows // 16 * c
            ref[:, c * LANES : (c + 1) * LANES] = table_ref[first : first + rows // 16].reshape(rows, LANES)
    for i in range(nx):
        faces = [q_ref[i, ny - REACH :, :], q_ref[i, :REACH, :]]
        if plan.kinds == 1:
            faces = [jnp.where(by == 0, *faces)]
        for face, ref in zip(faces, targets):
            ref[i] = face
    high, low = split(q_ref[...].reshape(nx * ny, nz))
    along_z = dot(jnp.concatenate([high, low, high], axis=1), matrix_z)
    high, low = split(along_z)
    high, low = high.reshape(nx, ny, LANES), low.reshape(nx, ny, LANES)
    for i in range(0, nx, 2):
        pair = [jnp.concatenate([high[j], high[j], low[j]], axis=0) for j in (i, i + 1)]
        both = dot(matrix_y, jnp.concatenate(pair, axis=1))[: plan.rows_restricted]
        mixed[i] = both[:, :LANES]
        mixed[i + 1] = both[:, LANES:]

    brick = lax.axis_index("gx")
    keep_low = jnp.where(brick > 0, 1.0, 0.0).astype(F32)
    keep_high = jnp.where(brick < plan.x.count - 1, 1.0, 0.0).astype(F32)

    def coarsen(planes, level):
        size = nx >> level
        result = {}
        for i in range(LOW[level], LOW[level] + plan.x.width[level]):
            get = lambda j: planes.get(2 * i + j)
            total = None
            for offsets, weight in (((-3, 3), -0.0625), ((-1, 1), 0.5625), ((0,), 1.0)):
                terms = [get(j) for j in offsets if get(j) is not None]
                if terms:
                    term = functools.reduce(jnp.add, terms)
                    term = term * weight if weight != 1.0 else term
                    total = term if total is None else total + term
            if i < 0:
                total = total * keep_low
            elif i >= size:
                total = total * keep_high
            result[i] = total
        return result

    lanes = lax.broadcasted_iota(jnp.int32, (8, LANES), 1)
    in1, in2 = lanes < plan.lane[2], lanes < plan.lane[3]

    def rows_of(start, count, depth):
        levels = [{i: mixed[i, start : start + count, :] for i in range(nx)}]
        for level in range(1, depth + 1):
            levels.append(coarsen(levels[-1], level))
        return levels[-1]

    zero = jnp.zeros((8, LANES), F32)
    first = {r: rows_of(r, 8, 1) for r in range(0, plan.rows1, 8)}
    second = {r: rows_of(plan.row[2] + r, 8, 2) for r in (0, 8)}
    face = [{r: rows_of(plan.row_face + 16 * f + r, 8, 1) for r in (0, 8)} for f in range(plan.kinds)]
    for r in range(0, plan.whole3, 8):
        third = rows_of(plan.row[3] + r, 8, 3)
        for k in range(plan.x.width[3]):
            top[k, r : r + 8, :] = third[LOW[3] + k]
    high, low = split(top[...].reshape(plan.x.width[3] * plan.whole3, LANES))
    select = table_ref[at_select:].reshape(2, -1, LANES)
    select = jnp.concatenate([select[0], select[1]], axis=1)
    flat = dot(select, jnp.concatenate([high, low], axis=1), ((1,), (1,)))[: plan.tall[3]]
    flat = jnp.concatenate([flat, jnp.zeros((plan.tall[3], plan.flat_top - flat.shape[1]), F32)], axis=1)
    start = ((plan.x.length >> 3) * brick + LOW[3]) * plan.whole3
    top_ref[...] = pltpu.roll(flat, lax.rem(start + plan.flat_top, plan.flat_top), 1)
    for k in range(plan.x.width[1]):
        for r in range(0, plan.rows1, 8):
            one = first[r][LOW[1] + k]
            two = second[r][LOW[2] + k] if r < 16 and k < plan.x.width[2] else zero
            rest_ = jnp.where(in2, two, 0.0)
            own_ref[k, r : r + 8, :] = jnp.where(in1, one, rest_)
            if r < 16:
                for f in range(plan.kinds):
                    targets[f][nx + 2 * k + r // 8] = jnp.where(in1, face[f][r][LOW[1] + k], rest_)


def mask(condition):
    return jnp.where(condition, 1.0, 0.0).astype(F32)


def top_z_kernel(plan, own_ref, *refs):
    others, (table_ref, out_ref) = refs[: plan.z.count - 1], refs[plan.z.count - 1 :]
    value = jnp.concatenate([ref[...] for ref in (own_ref, *others)], axis=0)
    high, low = split(value)
    stacked = jnp.concatenate([high, high, low], axis=0)
    out_ref[...] = dot(table_ref[...][:, : plan.top_cols], stacked)


def roll_lanes(value, amount):
    return pltpu.roll(value, amount % LANES, 1)


def pack_faces(plan, faces):
    lanes = lax.broadcasted_iota(jnp.int32, (1, LANES), 1)
    groups = []
    for g in range(plan.face_groups):
        value = faces[g]
        if g + plan.face_groups < FACE:
            value = jnp.where(lanes < plan.half, value, roll_lanes(faces[g + plan.face_groups], plan.half))
        groups.append(value)
    rest = jnp.zeros(faces[0].shape, F32)
    for p, face in enumerate(faces):
        start = plan.left * p
        inside = (lanes >= start) & (lanes < start + plan.left)
        rest = jnp.where(inside, roll_lanes(face, start - plan.half), rest)
    return groups + [rest]


def unpack_face(plan, groups, p):
    lanes = lax.broadcasted_iota(jnp.int32, (1, LANES), 1)
    value = groups[p] if p < plan.face_groups else roll_lanes(groups[p - plan.face_groups], plan.half)
    return jnp.where(lanes < plan.half, value, roll_lanes(groups[-1], plan.half - plan.left * p))


def extend_kernel(plan, q_ref, own_ref, top_ref, *refs):
    count = plan.y.count - 1
    halos, (ext_ref, partner_ref, side_ref) = refs[:count], refs[count:]
    x, y = plan.x, plan.y
    odd = lax.axis_index("gx") % 2
    end = x.length - REACH
    near = plan.near_y(halos)
    put_flat(partner_ref, plan.top_row, top_ref[...])
    for start, ref in ((end * odd, side_ref), (end * (1 - odd), partner_ref)):
        for i in range(REACH):
            row = plan.fine_rows * i
            put_plane(ref, row, q_ref[start + i])
            for h, halo in enumerate(near):
                ref[(row + y.length) // 8 + h] = halo[start + i]

    base = [8 * halo.shape[0] - 16 * x.width[1] for halo in halos]
    for i in range(x.width[1]):
        own = own_ref[i]
        parts = [plane(halo, at, 16, i) for halo, at in zip(halos, base)]
        if plan.overlay:
            halo = parts[0]
            parts = [own[:16], own[16:] + halo[8:], halo[:8]]
        else:
            pad = plan.coarse_rows - 24 - 16 * count
            parts = [own] + parts + ([jnp.zeros((pad, LANES), F32)] if pad else [])
        ext_ref[i] = jnp.concatenate(parts, axis=0)
    lanes = lax.broadcasted_iota(jnp.int32, (1, LANES), 1)
    start = (x.width[1] - FACE) * (1 - odd)
    for p in range(plan.planes):
        row = plan.fine_rows * REACH + plan.coarse_rows * p
        value = jnp.where(lanes < plan.lane[2], ext_ref[start + min(p, FACE - 1)], ext_ref[p])
        put_plane(partner_ref, row, value)
    start = (x.width[1] - FACE) * odd
    for g, value in enumerate(pack_faces(plan, [ext_ref[start + p] for p in range(FACE)])):
        put_plane(side_ref, plan.fine_rows * REACH + plan.coarse_rows * g, value)


def chip_kernel(plan, ext_ref, pair_ref, top_ref, top_out, *targets):
    x, gx = plan.x, lax.axis_index("gx")
    odd, chip = gx % 2, gx // 2
    lanes = lax.broadcasted_iota(jnp.int32, (1, LANES), 1)
    keep_even, keep_odd = mask(odd == 0), mask(odd == 1)
    top = top_ref[...] + get_flat(pair_ref, plan.top_row, plan.top_shape)
    top_out[...] = top

    def merged(level, cell):
        size, total = x.length >> level, None
        for where_own, where_partner, at in ((keep_even, keep_odd, cell), (keep_odd, keep_even, cell - size)):
            if 0 <= at < x.width[level]:
                value = ext_ref[at] * where_own + plan.pair_plane(pair_ref, at) * where_partner
                total = value if total is None else total + value
        return total

    second = [merged(2, c) for c in range(plan.pair_width[2])]
    chips = x.count // 2
    high = x.length >> 2
    for k, ref in zip(range(1, chips), targets):
        for g in range(plan.pair_groups):
            total = None
            for slot, p in enumerate(range(3 * g, min(3 * g + 3, plan.planes))):
                if chips == 2:
                    two = jnp.where(chip == 0, second[high + p], second[p])
                else:
                    two = second[high + p] if k == 1 else second[p]
                two = roll_lanes(two, SLOT * slot - plan.lane[2])
                total = two if slot == 0 else jnp.where(lanes < SLOT * slot, total, two)
            put_plane(ref, plan.coarse_rows * g, total)
        put_flat(ref, plan.coarse_rows * plan.pair_groups, top)


def mix_planes(get, put, count, matrix):
    for i in range(0, count, 2):
        pair = [i, min(i + 1, count - 1)]
        stacked = []
        for j in pair:
            high, low = split(get(j))
            stacked.append(jnp.concatenate([high, high, low], axis=0))
        both = dot(matrix, jnp.concatenate(stacked, axis=1))
        put(i, both[:, :LANES])
        if pair[1] != i:
            put(pair[1], both[:, LANES:])


def stencil(cells, wanted, sigma, reach=REACH):
    result = []
    for i in wanted:
        total = cells.get(i)
        for k in range(1, reach + 1):
            terms = [cells[j] for j in (i - k, i + k) if j in cells]
            if terms:
                term = functools.reduce(jnp.add, terms) * float(np.exp(-((k / sigma) ** 2)))
                total = term if total is None else total + term
        result.append(total)
    return result


def put_ready(ready, sigmas, s, row, value):
    high, low = split(value)
    rows = slice(row, row + value.shape[0])
    step = LANES * sigmas
    ready[rows, s * LANES : (s + 1) * LANES] = high
    ready[rows, step + s * LANES : step + (s + 1) * LANES] = low
    ready[rows, 2 * step + s * LANES : 2 * step + (s + 1) * LANES] = high


def fine_padding(plan):
    pad = up(plan.fine_rows, 16) - plan.fine_rows
    return [jnp.zeros((pad, LANES), F32)] if pad else []


def fine_inner_kernel(plan, q_ref, y_table, inner_ref, edge_ref, q_out, mixed):
    x, y = plan.x, plan.y
    q_out[...] = q_ref[...]
    halo = jnp.zeros((up(plan.fine_rows, 16) - y.length, LANES), F32)

    def put(i, value):
        mixed[i] = value

    mix_planes(lambda i: jnp.concatenate([q_ref[i], halo], axis=0), put, x.length, plan.fine_matrix(y_table))
    inner = range(REACH, x.length - REACH)
    edge = [*range(REACH), *range(x.length - REACH, x.length)]
    half = len(inner) * (y.length - 16)
    for s, sigma in enumerate(STENCIL_SIGMAS):
        row, end = s * y.length, (s + 1) * y.length
        planes = {i: mixed[i, row + 8 : end - 8, :] for i in range(x.length)}
        step = y.length - 16
        for i, value in enumerate(stencil(planes, inner, sigma)):
            inner_ref[s, i * step : (i + 1) * step, :] = value
        for i, value in enumerate(stencil(planes, edge, sigma)):
            edge_ref[i, row + 8 : end - 8, :] = value
        ends = lambda i: jnp.concatenate([mixed[i, row : row + 8, :], mixed[i, end - 8 : end, :]], axis=0)
        planes = {i: ends(i) for i in range(x.length)}
        for i, value in enumerate(stencil(planes, inner, sigma)):
            inner_ref[s, half + i * 16 : half + i * 16 + 16, :] = value
        for i, value in enumerate(stencil(planes, edge, sigma)):
            edge_ref[i, row : row + 8, :] = value[:8]
            edge_ref[i, end - 8 : end, :] = value[8:]


def fine_halo_kernel(plan, inner_ref, edge_ref, y_table, z_table, *refs):
    halos, (main_ref, push_ref, out_ref, mixed, ready) = refs[: plan.y.count - 1], refs[plan.y.count - 1 :]
    x, y = plan.x, plan.y
    near = plan.near_y(halos)
    padding = [jnp.zeros((8, LANES), F32)] * (plan.halo_cols // 24 - len(near))

    def get(i):
        return jnp.concatenate([plane(h, 0, 8, i) for h in near] + padding, axis=0)

    def put(i, value):
        mixed[i] = value

    mix_planes(get, put, x.length, plan.halo_matrix(y_table))
    inner = range(REACH, x.length - REACH)
    edge = [*range(REACH), *range(x.length - REACH, x.length)]
    out_ref[...] = edge_ref[...]
    half = len(inner) * (y.length - 16)
    for s, sigma in enumerate(STENCIL_SIGMAS):
        row, end = s * y.length, (s + 1) * y.length
        planes = {i: mixed[i, 16 * s : 16 * s + 16, :] for i in range(x.length)}
        for start in range(0, half, 64):
            put_ready(ready, 3, s, start, inner_ref[s, start : start + 64, :])
        for i, value in enumerate(stencil(planes, inner, sigma)):
            start = half + 16 * i
            put_ready(ready, 3, s, start, inner_ref[s, start : start + 16, :] + value)
        for i, value in enumerate(stencil(planes, edge, sigma)):
            out_ref[i, row : row + 8, :] += value[:8]
            out_ref[i, end - 8 : end, :] += value[8:]
    main_ref[...] = dot(ready[...], plan.z_matrix(z_table, 0), ((1,), (1,)))
    push_ref[...] = dot(plan.z_matrix(z_table, 1), ready[...], ((1,), (1,)))


def fine_edge_kernel(plan, halo_ref, edge_ref, y_table, z_table, push_ref, ready_ref, mixed, *, partner):
    x, y = plan.x, plan.y
    gx = lax.axis_index("gx")
    odd = gx % 2
    high = 1 - odd if partner else odd
    keep = mask(True) if partner else mask(jnp.where(high == 1, gx < x.count - 1, gx > 0))
    padding = fine_padding(plan)
    away = lambda k: jnp.where(high == 1, k, REACH - 1 - k)

    def get(k):
        return jnp.concatenate([plane(halo_ref, 0, plan.fine_rows, away(k)) * keep] + padding, axis=0)

    def put(k, value):
        mixed[k] = value

    mix_planes(get, put, REACH, plan.fine_matrix(y_table))
    for s, sigma in enumerate(STENCIL_SIGMAS):
        for r in range(0, y.length, 16):
            row = s * y.length + r
            after = {REACH + k: mixed[k, row : row + 16, :] for k in range(REACH)}
            for i, added in enumerate(stencil(after, range(REACH), sigma)):
                value = edge_ref[away(i) + REACH * high, row : row + 16, :] + added
                top, low = split(value)
                at = away(i) * (y.length // 16) + r // 16
                for c, part in enumerate((top, low, top)):
                    start = (3 * c + s) * LANES
                    ready_ref[at, :, start : start + LANES] = part
    whole = ready_ref[...].reshape(REACH * y.length, 9 * LANES)
    push_ref[...] = dot(plan.z_matrix(z_table, 1), whole, ((1,), (1,)))


def fine_main_kernel(plan, partner_ref, side_ref, z_table, out_ref):
    odd = lax.axis_index("gx") % 2
    for ref, at in ((partner_ref, 1 - odd), (side_ref, odd)):
        whole = ref[...].reshape(REACH * plan.y.length, 9 * LANES)
        out_ref[at] = dot(whole, plan.z_matrix(z_table, 0), ((1,), (1,)))


def coarse_inner_kernel(plan, ext_ref, pair_ref, y_table, *refs):
    *parts, mixed = refs
    own = plan.x.width[1]

    def put(i, value):
        mixed[i] = value

    get = lambda i: ext_ref[i] if i < own else plan.pair_plane(pair_ref, i - own)
    mix_planes(get, put, own + plan.planes, plan.coarse_matrix(y_table))
    for level, part in zip((1, 2), parts):
        rows, width = (plan.rows1, plan.rows2)[level - 1], plan.x.width[level]
        wanted = range(LOW[level], LOW[level] + width)
        for s, sigma in enumerate(STENCIL_SIGMAS):
            for r in range(0, rows, 8):
                cells = collect_inner(plan, level, mixed, plan.group[level] + s * rows + r, 8)
                for i, value in enumerate(stencil(cells, wanted, sigma)):
                    part[s * width + i, r : r + 8, :] = value


def adder(plan, level, cells):
    start, width = LOW[level], plan.x.width[level]

    def add(cell, value, keep):
        if start - REACH <= cell < start + width + REACH:
            value = value * keep
            cells[cell] = cells[cell] + value if cell in cells else value

    return add


def collect_inner(plan, level, inner, row, rows):
    x, odd = plan.x, lax.axis_index("gx") % 2
    size, width, start, own = x.length >> level, x.width[level], LOW[level], x.width[1]
    cells = {start + k: inner[k, row : row + rows, :] for k in range(width)}
    add = adder(plan, level, cells)
    layers = FACE if level == 1 else width
    for k in range(layers):
        value = inner[own + k, row : row + rows, :]
        add(size + start + k, value, mask(odd == 0))
        add(-size + start + width - layers + k, value, mask(odd == 1))
    return cells


def collect_outer(plan, level, outer, row, rows):
    x, gx = plan.x, lax.axis_index("gx")
    odd, chip, chips = gx % 2, gx // 2, plan.x.count // 2
    size, width, start = x.length >> level, x.width[level], LOW[level]
    cells = {}
    add = adder(plan, level, cells)
    if level == 1:
        for k in range(FACE):
            value = outer[k, row : row + rows, :]
            add(-size + start + width - FACE + k, value, mask((chip > 0) & (odd == 0)))
            add(size + start + k, value, mask((chip < chips - 1) & (odd == 1)))
        return cells
    for n, offset in enumerate(plan.near_chips):
        for shift, here in ((-offset, chip >= offset), (chips - offset, chip < offset)):
            if abs(shift) != 1:
                continue
            for core in (0, 1):
                keep = mask(here & (odd == core))
                first = 2 * size * shift - size * core + start + (size if shift < 0 else 0)
                for k in range(plan.planes):
                    add(first + k, outer[plan.planes * n + k, row : row + rows, :], keep)
    return cells


def coarse_kernel(plan, part1, part2, *refs):
    chips = plan.x.count // 2 - 1
    others, refs = refs[:chips], refs[chips:]
    side_in, *pushes = refs[:4]
    y_table, z_table, partner_ref, side_ref, e1_ref, e2_ref, outer, *ready = refs[4:]

    def put(i, value):
        outer[i] = value

    lanes = lax.broadcasted_iota(jnp.int32, (1, LANES), 1)
    groups = [plane(side_in, plan.fine_rows * REACH, plan.coarse_rows, g) for g in range(plan.face_groups + 1)]

    def get(i):
        n, p = i // plan.planes, i % plan.planes
        two = plane(others[plan.near_chips[n] - 1], 0, plan.coarse_rows, p // 3)
        value = roll_lanes(two, plan.lane[2] - SLOT * (p % 3))
        if n == 0 and p < FACE:
            value = jnp.where(lanes < plan.lane[2], unpack_face(plan, groups, p), value)
        return value

    mix_planes(get, put, plan.planes * len(plan.near_chips), plan.coarse_matrix(y_table))
    x = plan.x
    results = []
    for level in (1, 2):
        rows = plan.rows1 if level == 1 else plan.rows2
        wanted = range(LOW[level], LOW[level] + x.width[level])
        for s, sigma in enumerate(STENCIL_SIGMAS):
            for r in range(0, rows, 8):
                cells = collect_outer(plan, level, outer, plan.group[level] + s * rows + r, 8)
                for i, added in enumerate(stencil(cells, wanted, sigma)):
                    value = (part1, part2)[level - 1][s * x.width[level] + i, r : r + 8, :]
                    put_ready(ready[level - 1], 3, s, i * rows + r, value if added is None else value + added)
        results.append(dot(plan.z_matrix(z_table, level + 1), ready[level - 1][...], ((1,), (1,))))
    one, two = results
    e1_ref[...] = one[: plan.tall[1]]
    e2_ref[...] = two[: plan.tall[2]]
    inner, partner, side = (p[...] for p in pushes)
    odd = lax.axis_index("gx") % 2 == 1
    pushed = jnp.concatenate([inner, jnp.where(odd, partner, side), jnp.where(odd, side, partner)], axis=1)
    for n, ref in enumerate((partner_ref, side_ref)):
        ref[:8, :] = pushed[8 * n : 8 * n + 8, :]
        ref[8:, :] = jnp.zeros((16, ref.shape[1]), F32)
        start = plan.tall[1] + 16 * n
        ref[8:, : plan.flat[1]] = one[start : start + 16]
        start = plan.tall[2] + 16 * n
        ref[8:, 512 : 512 + plan.flat[2]] = two[start : start + 16]


def top_chips_kernel(plan, top_ref, *refs):
    *others, out_ref = refs
    total = top_ref[...]
    for ref in others:
        total = total + get_flat(ref, plan.coarse_rows * plan.pair_groups, plan.top_shape)
    out_ref[...] = total


def top_kernel(plan, *refs):
    *values, out_ref = refs
    total = functools.reduce(jnp.add, [v[...] for v in values])
    shape = (plan.flat_top, plan.flat[3])
    source, target = (lax.broadcasted_iota(jnp.int32, shape, d) for d in (0, 1))
    first_x = (plan.x.length >> 3) * lax.axis_index("gx") + LOW[3]
    first_y = (plan.y.length >> 3) * lax.axis_index("gy") + LOW[3]
    apart_x = source // plan.whole3 - target // plan.rows3 - first_x
    apart_y = source % plan.whole3 - target % plan.rows3 - first_y
    square = (apart_x * apart_x + apart_y * apart_y).astype(F32)
    result, tall = None, plan.tall[3]
    for s, sigma in enumerate(TOP_SIGMAS):
        matrix = jnp.exp(square * (-1.0 / sigma**2))
        matrix_high, matrix_low = split(matrix)
        high, low = split(total[s * tall : (s + 1) * tall])
        left = jnp.concatenate([high, low, high], axis=1)
        term = dot(left, jnp.concatenate([matrix_high, matrix_high, matrix_low], axis=0))
        result = term if result is None else result + term
    out_ref[...] = result


def finish_kernel(plan, inner_ref, edge_ref, e1_ref, e2_ref, partner_ref, side_ref, e3_ref, flat, tall, out_hbm, e1, e2, out_ref, sems):
    x, y, z = plan.x, plan.y, plan.z
    gx, gy, gz = (lax.axis_index(name) for name in ("gx", "gy", "gz"))
    odd = gz % 2
    for window, own, tall_ in ((e1, e1_ref, plan.tall[1]), (e2, e2_ref, plan.tall[2])):
        window[:tall_, :] = own[...]
        if window.shape[0] > tall_:
            window[tall_:, :] = jnp.zeros((window.shape[0] - tall_, window.shape[1]), F32)
    kept = lax.broadcasted_iota(jnp.int32, (16, 1), 0) < FACE
    for ref, high in ((partner_ref, odd == 0), (side_ref, odd == 1)):
        one = jnp.where(kept, ref[8:, : plan.flat[1]], 0.0)
        two = ref[8:, 512 : 512 + plan.flat[2]]
        for window, value, tall_ in ((e1, one, plan.tall[1]), (e2, two, plan.tall[2])):
            window[:16, :] += value * mask(~high)
            window[tall_ - 16 : tall_, :] += value * mask(high)

    bounds = [int(r) for r in plan.tall_rows]

    def along_z(value, number, parts):
        high, low = split(value)
        stacked = jnp.concatenate([high, low, high][:parts], axis=0)
        return dot(stacked, tall[gz, bounds[number] : bounds[number + 1], :], ((0,), (0,)))

    def inside(level):
        rows = (0, plan.rows1, plan.rows2, plan.rows3)[level]
        index = lax.broadcasted_iota(jnp.int32, (plan.flat[level], LANES), 0)
        cell_x = index // rows + ((x.length >> level) * gx + LOW[level])
        cell_y = index % rows + ((y.length >> level) * gy + LOW[level])
        in_x = (cell_x >= 0) & (cell_x < (x.count * x.length) >> level)
        return in_x & (cell_y >= 0) & (cell_y < (y.count * y.length) >> level)

    flat_bounds = [int(r) for r in plan.flat_rows]

    def finer(value, number):
        high, low = split(value)
        matrix = flat[flat_bounds[number] : flat_bounds[number + 1], :][:, : value.shape[0]]
        both = dot(matrix, jnp.concatenate([high, low], axis=1))
        return both[:, :LANES] + both[:, LANES:]

    pad = up(plan.tall[3], 16) - plan.tall[3]
    e3 = jnp.concatenate([e3_ref[...]] + ([jnp.zeros((pad, e3_ref.shape[1]), F32)] if pad else []), axis=0)
    ends = along_z(jnp.concatenate([partner_ref[:8], side_ref[:8]], axis=0), 1, 2)
    one, two, three = along_z(e1[...], 0, 2), along_z(e2[...], 2, 3), along_z(e3, 3, 3)
    three = jnp.where(inside(3), three, 0.0)
    two = jnp.where(inside(2), two + finer(three, 0)[: plan.flat[2]], 0.0)
    one = jnp.where(inside(1), one + finer(two, 1)[: plan.flat[1]], 0.0)
    high, low = split(one)
    stacked = jnp.concatenate([high, low], axis=1)
    inner = inner_ref.shape[0]
    edge, tiles, order = edge_ref.shape[1], y.length // 8, plan.tiles()
    copies = []
    for first, last, to in ((inner, inner + edge, 0), (inner + edge, inner + 2 * edge, inner + edge), (0, inner, edge)):
        matrix = flat[flat_bounds[2] + first : flat_bounds[2] + last, :][:, : plan.flat[1]]
        both = dot(matrix, stacked)
        coarse = both[:, :LANES] + both[:, LANES:] + ends[first:last]
        for row in range(first, last, 8):
            x_, t = order[row // 8]
            value = coarse[row - first : row - first + 8]
            if row < inner:
                value = value + inner_ref[row : row + 8]
            else:
                end, at = divmod(row - inner, edge)
                value = value + edge_ref[end, at : at + 8]
            out_ref[8 * (tiles * x_ + t) : 8 * (tiles * x_ + t) + 8] = value
        rows = pl.ds(to, last - first)
        copies.append(pltpu.make_async_copy(out_ref.at[rows], out_hbm.at[rows], sems.at[len(copies)]))
        copies[-1].start()
    for copy in copies:
        copy.wait()


def call(kernel, plan, operands, outs, scratch=(), hbm=(), vmem=32, out=None):
    whole, left = pl.BlockSpec(memory_space=pltpu.VMEM), pl.BlockSpec(memory_space=pl.ANY)
    return pl.pallas_call(
        functools.partial(kernel, plan),
        in_specs=[left if i in hbm else whole for i in range(len(operands))],
        out_specs=[out or whole] * len(outs),
        scratch_shapes=list(scratch),
        out_shape=list(outs),
        compiler_params=pltpu.CompilerParams(vmem_limit_bytes=int(vmem * 2**20)),
    )(*[jnp.asarray(o) for o in operands])


def shift(value, axis, offset):
    count = lax.axis_size(axis)
    return lax.ppermute(value, axis, [(i, (i + offset) % count) for i in range(count)])


def swap(value, axes, partner):
    first, second = (lax.axis_size(a) for a in axes)
    pairs = []
    for i in range(first):
        for j in range(second):
            k, m = partner(i, j)
            pairs.append((i * second + j, k * second + m))
    return lax.ppermute(value, axes, pairs)


def side_of(count):
    return lambda i: None if i in (0, count - 1) else i + (1 if i % 2 else -1)


def shards(plan, charges):
    x, y, z = plan.x, plan.y, plan.z
    array = lambda *shape: jax.ShapeDtypeStruct(shape, F32)
    vmem = lambda *shape: pltpu.VMEM(shape, F32)
    ready = lambda rows, sigmas: pltpu.VMEM((rows, 3 * sigmas * LANES), BF)
    side_x, side_z = side_of(x.count), side_of(z.count)
    partner_x = lambda v: swap(v, ("gx", "gy"), lambda i, j: (i ^ 1, j))
    across_x = lambda v: swap(v, ("gx", "gy"), lambda i, j: (i, j ^ 1) if side_x(i) is None else (side_x(i), j))
    partner_z = lambda v: swap(v, ("gx", "gz"), lambda i, j: (i, j ^ 1))
    across_z = lambda v: swap(v, ("gx", "gz"), lambda i, j: (i ^ 1, j) if side_z(j) is None else (i, side_z(j)))

    rows_y = 8 * x.length + 16 * x.width[1]
    table = plan.restrict_tables()
    own, top, y_table, top_table, *to_y = call(
        restrict_kernel,
        plan,
        [charges, table],
        [
            array(x.width[1], plan.rows1, LANES),
            array(plan.tall[3], plan.flat_top),
            jax.ShapeDtypeStruct((3 * y.length + plan.rows_mixed + plan.halo_rows, plan.y_cols), BF),
            jax.ShapeDtypeStruct((2 * plan.tall[3], up(plan.top_cols, LANES)), BF),
        ]
        + [array(rows_y // 8, 8, LANES)] * plan.kinds,
        [
            vmem(x.length, plan.rows_restricted, LANES),
            vmem(x.width[3], plan.whole3, LANES),
            vmem(*charges.shape),
            pltpu.VMEM((sum(plan.blocks), 16, LANES), BF),
            pltpu.SemaphoreType.DMA((6,)),
        ],
        hbm=(0, 1),
        vmem=53,
    )
    from_y = []
    for offset in range(1, y.count):
        value = to_y[0 if offset == 1 else -1]
        value = value if offset in (1, y.count - 1) else value[x.length :]
        from_y.append(shift(value, "gy", offset))

    tops = [swap(top, ("gx", "gz"), lambda i, j, m=m: (i, j ^ m)) for m in range(1, z.count)]
    (top,) = call(top_z_kernel, plan, [top, *tops, top_table], [array(*plan.top_shape)])

    z_table = plan.z_tables()
    inner_cells = (x.length - 2 * REACH) * y.length
    inner, edge, held = call(
        fine_inner_kernel,
        plan,
        [charges, y_table],
        [array(3, inner_cells, LANES), array(2 * REACH, 3 * y.length, LANES), array(*charges.shape)],
        [vmem(x.length, 3 * y.length, LANES)],
    )
    edge, *from_y = lax.optimization_barrier((edge, *from_y))

    ext, to_partner, to_side = call(
        extend_kernel,
        plan,
        [held, own, top, *from_y],
        [
            array(x.width[1], plan.coarse_rows, LANES),
            array((plan.top_row + plan.top_rows) // 8, 8, LANES),
            array(plan.side_rows // 8, 8, LANES),
        ],
    )
    from_side, pair = across_x(to_side), partner_x(to_partner)

    main_inner, push_inner, edge = call(
        fine_halo_kernel,
        plan,
        [inner, edge, y_table, z_table, *from_y],
        [array(inner_cells, z.length), array(16, inner_cells), array(2 * REACH, 3 * y.length, LANES)],
        [vmem(x.length, plan.halo_rows, LANES), ready(inner_cells, 3)],
    )

    chips = x.count // 2
    rows_x = plan.pair_groups * plan.coarse_rows + plan.top_rows
    top, *to_chips = call(
        chip_kernel,
        plan,
        [ext, pair, top],
        [array(*plan.top_shape)] + [array(rows_x // 8, 8, LANES)] * (chips - 1),
    )
    from_chips = [
        swap(v, ("gx", "gy"), lambda i, j, k=k: ((i + 2 * k) % x.count ^ 1, j))
        for k, v in zip(range(1, chips), to_chips)
    ]
    parts = call(
        coarse_inner_kernel,
        plan,
        [ext, pair, y_table],
        [array(3 * x.width[1], plan.rows1, LANES), array(3 * x.width[2], plan.rows2, LANES)],
        [vmem(x.width[1] + plan.planes, plan.rows_mixed, LANES)],
    )

    def fine_end(halo, is_partner):
        return call(
            functools.partial(fine_edge_kernel, partner=is_partner),
            plan,
            [halo, edge, y_table, z_table],
            [array(16, REACH * y.length), jax.ShapeDtypeStruct((REACH * y.length // 16, 16, 9 * LANES), BF)],
            [vmem(REACH, 3 * y.length, LANES)],
        )

    push_partner, ready_partner = fine_end(pair, True)
    from_side, push_partner, *parts = lax.optimization_barrier((from_side, push_partner, *parts))
    push_side, ready_side = fine_end(from_side, False)
    pushes = [push_inner, push_partner, push_side]
    window = lambda level: array(plan.tall[level], plan.flat[level])
    to_partner, to_side, e1, e2 = call(
        coarse_kernel,
        plan,
        [*parts, *from_chips, from_side, *pushes, y_table, z_table],
        [array(24, 1024), array(24, 1024), window(1), window(2)],
        [vmem(plan.planes * len(plan.near_chips), plan.rows_mixed, LANES), ready(plan.flat[1], 3), ready(plan.flat[2], 3)],
    )
    from_near = [partner_z(to_partner), across_z(to_side)]

    (top,) = call(top_chips_kernel, plan, [top, *from_chips], [array(*top.shape)])
    tops = [top] + [shift(top, "gy", offset) for offset in range(1, y.count)]
    (e3,) = call(top_kernel, plan, tops, [window(3)])

    (main_edge,) = call(
        fine_main_kernel, plan, [ready_partner, ready_side, z_table], [array(2, REACH * y.length, z.length)]
    )
    (potential,) = call(
        finish_kernel,
        plan,
        [main_inner, main_edge, e1, e2, *from_near, e3, *plan.finish()],
        [array(x.length * y.length, z.length)],
        [vmem(up(plan.tall[level], 16), plan.flat[level]) for level in (1, 2)]
        + [vmem(x.length * y.length, z.length), pltpu.SemaphoreType.DMA((3,))],
        out=pl.BlockSpec(memory_space=pl.ANY),
    )
    return potential.reshape(charges.shape)


def solution(mesh):
    counts = [mesh.shape[name] for name in ("gx", "gy", "gz")]

    def run(charges):
        plan = Plan(counts, [size // n for size, n in zip(charges.shape, counts)])
        placed = P("gx", "gy", "gz")
        return jax.shard_map(
            functools.partial(shards, plan), mesh=mesh, in_specs=(placed,), out_specs=placed, check_vma=False
        )(charges)

    return run
```

```python
import functools

import jax
import jax.numpy as jnp
import numpy as np
from jax import lax
from jax.experimental import pallas as pl
from jax.experimental.pallas import tpu as pltpu
from jax.sharding import PartitionSpec as P

REACH = 8
STENCIL_SIGMAS = (1.0, 2.0, 3.5)
STENCIL_WEIGHTS = (0.4, 0.1, 0.03)
TOP_SIGMAS = (1.5, 4.0)
TOP_WEIGHTS = (0.03, 0.006)
SPLINE_TAPS = np.array((-1.0, 0.0, 9.0, 16.0, 9.0, 0.0, -1.0)) / 16.0

LOW = (0, -1, -2, -2)
EXTRA = (0, 3, 5, 5)
SLOT = 40
FACE = 11
LANES = 128
BF = jnp.bfloat16
F32 = jnp.float32


def up(value, unit):
    return -(-value // unit) * unit


def band(rows, cols, sigma, reach):
    distance = cols[None, :] - rows[:, None]
    return np.where(abs(distance) <= reach, np.exp(-((distance / sigma) ** 2)), 0.0)


def restriction(size):
    position = np.arange(size)[None, :] - 2 * np.arange(size // 2)[:, None] + 3
    inside = (position >= 0) & (position <= 6)
    return np.where(inside, SPLINE_TAPS[np.clip(position, 0, 6)], 0.0)


class Axis:
    def __init__(self, count, length):
        self.count, self.length = count, length
        self.width = [(length >> level) + EXTRA[level] for level in range(4)]

    def window(self, level, brick):
        size = self.length >> level
        cells = brick * size + LOW[level] + np.arange(self.width[level])
        return cells, ((cells >= 0) & (cells < self.count * size)).astype(float)

    def partial(self, level, brick):
        matrix = np.eye(self.count * self.length)
        for _ in range(level):
            matrix = restriction(matrix.shape[0]) @ matrix
        cells, inside = self.window(level, brick)
        rows = matrix[np.clip(cells, 0, len(matrix) - 1)] * inside[:, None]
        return rows[:, brick * self.length : (brick + 1) * self.length]

    def prolong(self, level, brick):
        matrix = restriction((self.count * self.length) >> (level - 1)).T
        rows, row_inside = self.window(level - 1, brick)
        cols, col_inside = self.window(level, brick)
        taken = matrix[np.clip(rows, 0, len(matrix) - 1)][:, np.clip(cols, 0, matrix.shape[1] - 1)]
        return taken * row_inside[:, None] * col_inside[None, :]

    def mix(self, level, sigma, target, source):
        rows, row_inside = self.window(level, target)
        cols, col_inside = self.window(level, source)
        reach = REACH if level < 3 else self.count * self.length
        return band(rows, cols, sigma, reach) * row_inside[:, None] * col_inside[None, :]


def place(shape, *pieces):
    whole = np.zeros(shape)
    for row, col, block in pieces:
        whole[row : row + block.shape[0], col : col + block.shape[1]] += block
    return whole


def halves(matrix):
    high = matrix.astype(jnp.bfloat16)
    low = (matrix - high.astype(np.float64)).astype(jnp.bfloat16)
    return high, low


def left3(matrix):
    high, low = halves(matrix)
    return np.concatenate([high, low, high], axis=-1)


def left3t(matrix):
    high, low = halves(matrix)
    return np.concatenate([high, high, low], axis=-1)


def right3(matrix):
    high, low = halves(matrix)
    return np.concatenate([high, high, low], axis=-2)


def split(value):
    high = value.astype(BF)
    return high, (value - high.astype(F32)).astype(BF)


def dot(left, right, dims=((1,), (0,))):
    return lax.dot_general(left, right, (dims, ((), ())), preferred_element_type=F32)


class Plan:
    def __init__(self, counts, lengths):
        self.x, self.y, self.z = (Axis(n, length) for n, length in zip(counts, lengths))
        x, y, z = self.x, self.y, self.z
        assert x.count % 2 == 0 and x.count >= 4 and y.count % 2 == 0
        assert z.count >= 4 and z.count & (z.count - 1) == 0
        self.lane = [0, 0, z.width[1], z.width[1] + z.width[2]]
        self.lane_end = self.lane[3] + z.width[3]
        assert self.lane_end <= LANES and z.length == LANES
        self.rows1, self.rows2 = up(y.width[1], 8), up(y.width[2], 16)
        self.rows3, self.whole3 = up(y.width[3], 16), up(y.count * y.length >> 3, 8)
        assert self.rows2 <= 16 and self.rows3 <= 16 and FACE <= 14 and self.rows1 == 24
        self.row = [0, 0, self.rows1, self.rows1 + self.rows2]
        self.row_face = self.rows1 + self.rows2 + self.whole3
        self.kinds = 1 if y.count == 2 else 2
        self.rows_restricted = self.row_face + 16 * self.kinds
        self.overlay = y.count == 2 and y.width[1] + 3 <= self.rows1
        self.coarse_rows = up(24 + 16 * (y.count - 1), 16) if not self.overlay else 32
        self.fine_halos = 1 if y.count == 2 else 2
        self.fine_rows = y.length + 8 * self.fine_halos
        self.pair_width = [w + (x.length >> l) for l, w in enumerate(x.width)]
        self.planes = max(FACE, x.width[2])
        self.half, self.left = LANES // 2, z.width[1] - LANES // 2
        self.face_groups = up(FACE, 2) // 2
        assert 0 < self.left and self.left * FACE <= LANES and z.width[2] <= SLOT
        chips = x.count // 2
        self.near_chips = [1] if chips == 2 else [1, chips - 1]
        self.pair_groups = up(self.planes, 3) // 3
        self.side_rows = REACH * self.fine_rows + (self.face_groups + 1) * self.coarse_rows
        self.flat_top = up((x.count * x.length >> 3) * self.whole3, LANES)
        self.top_shape = 2 * up(z.width[3], 8), self.flat_top
        self.top_rows = self.top_shape[0] * self.flat_top // LANES
        self.top_row = REACH * self.fine_rows + self.planes * self.coarse_rows
        assert self.planes <= x.width[1]
        self.group = [0, 0, 3 * self.rows1]
        self.rows_mixed = up(3 * self.rows1 + 3 * self.rows2, 16)
        self.tall = [0, up(z.width[1], 8), up(z.width[2], 8), up(z.width[3], 8)]
        assert self.tall[1] - 16 == z.width[1] - FACE and self.tall[2] - 16 == z.width[2] - 13
        self.flat = [0, x.width[1] * self.rows1, x.width[2] * self.rows2, x.width[3] * self.rows3]
        assert self.flat[1] <= 512 and self.flat[2] <= 256 and self.flat[3] <= 256

    def face_kind(self, axis, offset, source):
        if axis.count == 2:
            return 1 - source
        return 1 if offset == 1 else 0

    def near_y(self, halos):
        return [halos[0]] if self.y.count == 2 else [halos[0], halos[-1]]

    def tiles(self):
        nx, nt = self.x.length, self.y.length // 8
        inner = range(REACH, nx - REACH)
        edge = [*range(REACH), *range(nx - REACH, nx)]
        order = [(x, t) for x in inner for t in range(1, nt - 1)]
        order += [(x, t) for x in inner for t in (0, nt - 1)]
        return order + [(x, t) for x in edge for t in range(nt)]

    def pair_plane(self, ref, index):
        return plane(ref, self.fine_rows * REACH, self.coarse_rows, index)

    def face_row(self, j):
        return j if j < 8 or not self.overlay else j + 3

    def restrict_tables(self):
        rows = up(self.rows_restricted, 16)
        along_y = np.stack([place((rows, LANES), (0, 0, m)) for m in self.restrict_y().astype(np.float32)])
        parts = [self.restrict_z(), along_y, self.y_tables(), self.top_z()]
        parts = [p.astype(np.float32) for p in parts]
        blocks = []
        for p in parts:
            columns = [p[:, :, c : c + LANES] for c in range(0, p.shape[2], LANES)]
            blocks.append(np.concatenate(columns, axis=1).reshape(len(p), -1, 16, LANES))
        self.blocks = [b.shape[1] for b in blocks]
        self.blocks.append(2 * up(self.tall[3], 16) // 16)
        table = np.concatenate([b.reshape(-1, 16, LANES) for b in blocks] + [self.top_select().reshape(-1, 2, LANES)
            .transpose(1, 0, 2).reshape(-1, 16, LANES).astype(np.float32)])
        return table.astype(jnp.bfloat16)

    def y_tables(self):
        fine, halo, coarse = self.fine_y(), self.halo_y(), self.coarse_y()
        cols = up(max(fine.shape[2], coarse.shape[2]), LANES)
        self.halo_rows, self.halo_cols = halo.shape[1:]
        widen = lambda t: np.pad(t, ((0, 0), (0, 0), (0, cols - t.shape[2])))
        self.fine_cols, self.coarse_cols = fine.shape[2], coarse.shape[2]
        self.y_cols = cols
        return np.concatenate([widen(fine), widen(coarse), widen(halo)], axis=1)

    def z_tables(self):
        tables = [*self.fine_z(), *[self.coarse_z(level) for level in (1, 2)]]
        cols = 9 * LANES
        self.z_rows = np.cumsum([0] + [t.shape[1] for t in tables])
        return np.concatenate([np.pad(t, ((0, 0), (0, 0), (0, cols - t.shape[2]))) for t in tables], axis=1)

    def fine_matrix(self, ref):
        return ref[: 3 * self.y.length, :][:, : self.fine_cols]

    def coarse_matrix(self, ref):
        start = 3 * self.y.length
        return ref[start : start + self.rows_mixed, :][:, : self.coarse_cols]

    def halo_matrix(self, ref):
        return ref[3 * self.y.length + self.rows_mixed :, :][:, : self.halo_cols]

    def z_matrix(self, ref, number):
        return ref[lax.axis_index("gz"), int(self.z_rows[number]) : int(self.z_rows[number + 1]), :]

    def restrict_z(self):
        z = self.z
        return np.stack(
            [
                right3(place((z.length, LANES), *[(0, self.lane[l], z.partial(l, b).T) for l in (1, 2, 3)]))
                for b in range(z.count)
            ]
        )

    def restrict_y(self):
        y, tables = self.y, []
        for b in range(y.count):
            pieces = [(self.row[l], 0, y.partial(l, b)) for l in (1, 2)]
            cells, inside = y.window(3, b)
            for cell, line in zip(cells[inside > 0], y.partial(3, b)[inside > 0]):
                pieces.append((self.row[3] + cell, 0, line[None]))
            first = y.partial(1, b)
            for k in range(self.kinds):
                kind = self.face_kind(y, 1, b) if self.kinds == 1 else 1 - k
                start = (y.width[1] - FACE) * kind
                for j in range(FACE):
                    pieces.append((self.row_face + 16 * k + self.face_row(j), 0, first[start + j][None]))
            tables.append(left3(place((self.rows_restricted, y.length), *pieces)))
        return np.stack(tables)

    def fine_y(self):
        y, tables = self.y, []
        for b in range(y.count):
            pieces = []
            for s, sigma in enumerate(STENCIL_SIGMAS):
                row = s * y.length
                pieces.append((row, 0, y.mix(0, sigma, b, b)))
                for h in range(self.fine_halos):
                    offset = 1 if h == 0 else y.count - 1
                    source = (b - offset) % y.count
                    start = (y.length - REACH) * self.face_kind(y, offset, source)
                    block = y.mix(0, sigma, b, source)[:, start : start + REACH]
                    pieces.append((row, y.length + 8 * h, block))
            tables.append(left3(place((3 * y.length, up(self.fine_rows, 16)), *pieces)))
        return np.stack(tables)

    def halo_y(self):
        n, cols = self.y.length, up(self.fine_rows, 16)
        rows = [s * n + r for s in range(3) for r in (*range(8), *range(n - 8, n))]
        columns = [c * cols + n + k for c in range(3) for k in range(cols - n)]
        return self.fine_y()[:, rows][:, :, columns]

    def coarse_y(self):
        y, tables = self.y, []
        for b in range(y.count):
            whole = np.zeros((self.rows_mixed, self.coarse_rows))
            for level in (1, 2):
                rows = self.rows1 if level == 1 else self.rows2
                for s, sigma in enumerate(STENCIL_SIGMAS):
                    top = self.group[level] + s * rows
                    for offset in range(y.count):
                        source = (b - offset) % y.count
                        block = y.mix(level, sigma, b, source)
                        if level == 1 and offset:
                            start = (y.width[1] - FACE) * self.face_kind(y, offset, source)
                            block = block[:, start : start + FACE]
                        for j in range(block.shape[1]):
                            slot = self.face_row(j) if level == 1 and offset else j
                            if self.overlay and offset:
                                slot = 24 + slot if slot < 8 else 8 + slot
                            elif offset:
                                slot = 24 + 16 * (offset - 1) + slot
                            whole[top : top + y.width[level], slot] += block[:, j]
            tables.append(left3(whole))
        return np.stack(tables)

    def near_z(self, b, step):
        side = 1 if (b % 2 == 0) == (step == 0) else -1
        return side, b + side if 0 <= b + side < self.z.count else None

    def fine_z(self):
        z, own, pushed = self.z, [], []
        for b in range(z.count):
            mixes = lambda target: [
                w * z.mix(0, sigma, target, b) for sigma, w in zip(STENCIL_SIGMAS, STENCIL_WEIGHTS)
            ]
            own.append(left3t(np.concatenate(mixes(b), axis=1)))
            rows = []
            for step in (0, 1):
                side, target = self.near_z(b, step)
                if target is None:
                    rows.append(np.zeros((8, 3 * z.length)))
                else:
                    rows.append(np.concatenate([m[:8] if side > 0 else m[-8:] for m in mixes(target)], axis=1))
            pushed.append(left3t(np.concatenate(rows, axis=0)))
        return np.stack(own), np.stack(pushed)

    def coarse_z(self, level):
        z, tables = self.z, []
        cols, tall = LANES * len(STENCIL_SIGMAS), self.tall[level]
        for b in range(z.count):

            def mixed(target):
                blocks = [z.mix(level, sigma, target, b) * w * 0.5**level for sigma, w in zip(STENCIL_SIGMAS, STENCIL_WEIGHTS)]
                blocks = [place((z.width[level], LANES), (0, self.lane[level], block)) for block in blocks]
                return np.concatenate(blocks, axis=1)

            pieces = [place((tall, cols), (0, 0, mixed(b)))]
            layers = FACE if level == 1 else 13
            for step in (0, 1):
                side, target = self.near_z(b, step)
                if target is None:
                    pieces.append(np.zeros((16, cols)))
                else:
                    block = mixed(target)
                    pieces.append(place((16, cols), (0, 0, block[:layers] if side > 0 else block[-layers:])))
            whole = np.concatenate(pieces, axis=0)
            tables.append(left3t(place((up(len(whole), 16), cols), (0, 0, whole))))
        return np.stack(tables)

    def top_z(self):
        z, tall, tables = self.z, self.tall[3], []
        for b in range(z.count):
            pieces = []
            for s, (sigma, w) in enumerate(zip(TOP_SIGMAS, TOP_WEIGHTS)):
                for m in range(z.count):
                    pieces.append((tall * s, tall * m, w * z.mix(3, sigma, b, b ^ m)))
            tables.append(left3(place((2 * tall, z.count * tall), *pieces)))
        self.top_cols = tables[0].shape[1]
        widen = up(self.top_cols, LANES) - self.top_cols
        return np.pad(np.stack(tables), ((0, 0), (0, 0), (0, widen)))

    def top_select(self):
        matrix = place((up(self.tall[3], 16), LANES), (0, self.lane[3], np.eye(self.z.width[3])))
        return np.concatenate([matrix, matrix], axis=1).astype(jnp.bfloat16)

    def finish(self):
        x, y, z = self.x, self.y, self.z
        rows = (y.length, self.rows1, self.rows2, self.rows3)
        exact = lambda m: np.asarray(m, dtype=jnp.bfloat16)
        tall = []
        for b in range(z.count):
            ends = (0, z.length - 8) if b % 2 else (z.length - 8, 0)
            one = z.prolong(1, b)
            two = one @ z.prolong(2, b)
            three = two @ z.prolong(3, b)
            deep = [place((up(self.tall[l], 16), LANES), (0, 0, m.T)) for l, m in ((1, one), (2, two), (3, three))]
            ends = place((16, LANES), *[(8 * k, 0, np.eye(8, LANES, end)) for k, end in enumerate(ends)])
            parts = [exact(deep[0]), exact(deep[0]), exact(ends), exact(ends), right3(deep[1]), right3(deep[2])]
            tall.append(np.concatenate(parts))
        self.tall_rows = np.cumsum([0] + [2 * up(self.tall[1], 16), 32, 3 * up(self.tall[2], 16), 3 * up(self.tall[3], 16)])

        flat = []
        for level in (3, 2, 1):
            p, q = (Axis(5, axis.length).prolong(level, 2) for axis in (x, y))
            matrix = np.kron(p, place((rows[level - 1], rows[level]), (0, 0, q)))
            if level == 1:
                matrix = matrix[[x_ * y.length + 8 * t + k for x_, t in self.tiles() for k in range(8)]]
            flat.append(matrix)
        self.flat_rows = np.cumsum([0] + [up(len(m), 16) for m in flat])
        cols = up(max(self.flat), LANES)
        joined = np.concatenate([np.pad(m, ((0, -len(m) % 16), (0, cols - m.shape[1]))) for m in flat])
        return exact(joined), np.stack(tall)


def plane(ref, base, rows, index):
    return ref[pl.ds(base // 8 + rows // 8 * index, rows // 8)].reshape(rows, LANES)


def put_plane(ref, row, value):
    ref[row // 8 : (row + value.shape[0]) // 8] = value.reshape(value.shape[0] // 8, 8, LANES)


def put_flat(ref, row, value):
    for c in range(value.shape[1] // LANES):
        put_plane(ref, row + c * value.shape[0], value[:, c * LANES : (c + 1) * LANES])


def get_flat(ref, row, shape):
    parts = [plane(ref, row, shape[0], c) for c in range(shape[1] // LANES)]
    return jnp.concatenate(parts, axis=1)


def restrict_kernel(plan, q_hbm, table_hbm, own_ref, top_ref, y_table_ref, z_table_ref, *rest):
    targets, (mixed, top, q_ref, table_ref, sems) = rest[: plan.kinds], rest[plan.kinds :]
    nx, ny, nz = plan.x.length, plan.y.length, plan.z.length
    by, bz = lax.axis_index("gy"), lax.axis_index("gz")
    copies, starts, source, at = [pltpu.make_async_copy(q_hbm, q_ref, sems.at[0])], [], 0, 0
    bricks = ((plan.z.count, bz), (plan.y.count, by), (plan.y.count, by), (plan.z.count, bz), (1, 0))
    for n, (blocks, (count, brick)) in enumerate(zip(plan.blocks, bricks)):
        part = table_hbm.at[pl.ds(source + blocks * brick, blocks)]
        copies.append(pltpu.make_async_copy(part, table_ref.at[pl.ds(at, blocks)], sems.at[n + 1]))
        starts.append(at)
        source, at = source + count * blocks, at + blocks
    for copy in copies:
        copy.start()
    for copy in copies:
        copy.wait()
    blocks_z, blocks_y = plan.blocks[:2]
    matrix_z = table_ref[:blocks_z].reshape(3 * nz, LANES)
    matrix_y = table_ref[blocks_z : blocks_z + blocks_y].reshape(16 * blocks_y, LANES)
    matrix_y = matrix_y[:, : 3 * ny]
    at_select = starts[4]
    for ref, at in ((y_table_ref, starts[2]), (z_table_ref, starts[3])):
        rows = ref.shape[0]
        for c in range(ref.shape[1] // LANES):
            first = at + rows // 16 * c
            ref[:, c * LANES : (c + 1) * LANES] = table_ref[first : first + rows // 16].reshape(rows, LANES)
    for i in range(nx):
        faces = [q_ref[i, ny - REACH :, :], q_ref[i, :REACH, :]]
        if plan.kinds == 1:
            faces = [jnp.where(by == 0, *faces)]
        for face, ref in zip(faces, targets):
            ref[i] = face
    high, low = split(q_ref[...].reshape(nx * ny, nz))
    along_z = dot(jnp.concatenate([high, low, high], axis=1), matrix_z)
    high, low = split(along_z)
    high, low = high.reshape(nx, ny, LANES), low.reshape(nx, ny, LANES)
    for i in range(0, nx, 2):
        pair = [jnp.concatenate([high[j], high[j], low[j]], axis=0) for j in (i, i + 1)]
        both = dot(matrix_y, jnp.concatenate(pair, axis=1))[: plan.rows_restricted]
        mixed[i] = both[:, :LANES]
        mixed[i + 1] = both[:, LANES:]

    brick = lax.axis_index("gx")
    keep_low = jnp.where(brick > 0, 1.0, 0.0).astype(F32)
    keep_high = jnp.where(brick < plan.x.count - 1, 1.0, 0.0).astype(F32)

    def coarsen(planes, level):
        size = nx >> level
        result = {}
        for i in range(LOW[level], LOW[level] + plan.x.width[level]):
            get = lambda j: planes.get(2 * i + j)
            total = None
            for offsets, weight in (((-3, 3), -0.0625), ((-1, 1), 0.5625), ((0,), 1.0)):
                terms = [get(j) for j in offsets if get(j) is not None]
                if terms:
                    term = functools.reduce(jnp.add, terms)
                    term = term * weight if weight != 1.0 else term
                    total = term if total is None else total + term
            if i < 0:
                total = total * keep_low
            elif i >= size:
                total = total * keep_high
            result[i] = total
        return result

    lanes = lax.broadcasted_iota(jnp.int32, (8, LANES), 1)
    in1, in2 = lanes < plan.lane[2], lanes < plan.lane[3]

    def rows_of(start, count, depth):
        levels = [{i: mixed[i, start : start + count, :] for i in range(nx)}]
        for level in range(1, depth + 1):
            levels.append(coarsen(levels[-1], level))
        return levels[-1]

    zero = jnp.zeros((8, LANES), F32)
    first = {r: rows_of(r, 8, 1) for r in range(0, plan.rows1, 8)}
    second = {r: rows_of(plan.row[2] + r, 8, 2) for r in (0, 8)}
    face = [{r: rows_of(plan.row_face + 16 * f + r, 8, 1) for r in (0, 8)} for f in range(plan.kinds)]
    for r in range(0, plan.whole3, 8):
        third = rows_of(plan.row[3] + r, 8, 3)
        for k in range(plan.x.width[3]):
            top[k, r : r + 8, :] = third[LOW[3] + k]
    high, low = split(top[...].reshape(plan.x.width[3] * plan.whole3, LANES))
    select = table_ref[at_select:].reshape(2, -1, LANES)
    select = jnp.concatenate([select[0], select[1]], axis=1)
    flat = dot(select, jnp.concatenate([high, low], axis=1), ((1,), (1,)))[: plan.tall[3]]
    flat = jnp.concatenate([flat, jnp.zeros((plan.tall[3], plan.flat_top - flat.shape[1]), F32)], axis=1)
    start = ((plan.x.length >> 3) * brick + LOW[3]) * plan.whole3
    top_ref[...] = pltpu.roll(flat, lax.rem(start + plan.flat_top, plan.flat_top), 1)
    for k in range(plan.x.width[1]):
        for r in range(0, plan.rows1, 8):
            one = first[r][LOW[1] + k]
            two = second[r][LOW[2] + k] if r < 16 and k < plan.x.width[2] else zero
            rest_ = jnp.where(in2, two, 0.0)
            own_ref[k, r : r + 8, :] = jnp.where(in1, one, rest_)
            if r < 16:
                for f in range(plan.kinds):
                    targets[f][nx + 2 * k + r // 8] = jnp.where(in1, face[f][r][LOW[1] + k], rest_)


def mask(condition):
    return jnp.where(condition, 1.0, 0.0).astype(F32)


def top_z_kernel(plan, own_ref, *refs):
    others, (table_ref, out_ref) = refs[: plan.z.count - 1], refs[plan.z.count - 1 :]
    value = jnp.concatenate([ref[...] for ref in (own_ref, *others)], axis=0)
    high, low = split(value)
    stacked = jnp.concatenate([high, high, low], axis=0)
    out_ref[...] = dot(table_ref[...][:, : plan.top_cols], stacked)


def roll_lanes(value, amount):
    return pltpu.roll(value, amount % LANES, 1)


def pack_faces(plan, faces):
    lanes = lax.broadcasted_iota(jnp.int32, (1, LANES), 1)
    groups = []
    for g in range(plan.face_groups):
        value = faces[g]
        if g + plan.face_groups < FACE:
            value = jnp.where(lanes < plan.half, value, roll_lanes(faces[g + plan.face_groups], plan.half))
        groups.append(value)
    rest = jnp.zeros(faces[0].shape, F32)
    for p, face in enumerate(faces):
        start = plan.left * p
        inside = (lanes >= start) & (lanes < start + plan.left)
        rest = jnp.where(inside, roll_lanes(face, start - plan.half), rest)
    return groups + [rest]


def unpack_face(plan, groups, p):
    lanes = lax.broadcasted_iota(jnp.int32, (1, LANES), 1)
    value = groups[p] if p < plan.face_groups else roll_lanes(groups[p - plan.face_groups], plan.half)
    return jnp.where(lanes < plan.half, value, roll_lanes(groups[-1], plan.half - plan.left * p))


def extend_kernel(plan, q_ref, own_ref, top_ref, *refs):
    count = plan.y.count - 1
    halos, (ext_ref, partner_ref, side_ref) = refs[:count], refs[count:]
    x, y = plan.x, plan.y
    odd = lax.axis_index("gx") % 2
    end = x.length - REACH
    near = plan.near_y(halos)
    put_flat(partner_ref, plan.top_row, top_ref[...])
    for start, ref in ((end * odd, side_ref), (end * (1 - odd), partner_ref)):
        for i in range(REACH):
            row = plan.fine_rows * i
            put_plane(ref, row, q_ref[start + i])
            for h, halo in enumerate(near):
                ref[(row + y.length) // 8 + h] = halo[start + i]

    base = [8 * halo.shape[0] - 16 * x.width[1] for halo in halos]
    for i in range(x.width[1]):
        own = own_ref[i]
        parts = [plane(halo, at, 16, i) for halo, at in zip(halos, base)]
        if plan.overlay:
            halo = parts[0]
            parts = [own[:16], own[16:] + halo[8:], halo[:8]]
        else:
            pad = plan.coarse_rows - 24 - 16 * count
            parts = [own] + parts + ([jnp.zeros((pad, LANES), F32)] if pad else [])
        ext_ref[i] = jnp.concatenate(parts, axis=0)
    lanes = lax.broadcasted_iota(jnp.int32, (1, LANES), 1)
    start = (x.width[1] - FACE) * (1 - odd)
    for p in range(plan.planes):
        row = plan.fine_rows * REACH + plan.coarse_rows * p
        value = jnp.where(lanes < plan.lane[2], ext_ref[start + min(p, FACE - 1)], ext_ref[p])
        put_plane(partner_ref, row, value)
    start = (x.width[1] - FACE) * odd
    for g, value in enumerate(pack_faces(plan, [ext_ref[start + p] for p in range(FACE)])):
        put_plane(side_ref, plan.fine_rows * REACH + plan.coarse_rows * g, value)


def chip_kernel(plan, ext_ref, pair_ref, top_ref, top_out, *targets):
    x, gx = plan.x, lax.axis_index("gx")
    odd, chip = gx % 2, gx // 2
    lanes = lax.broadcasted_iota(jnp.int32, (1, LANES), 1)
    keep_even, keep_odd = mask(odd == 0), mask(odd == 1)
    top = top_ref[...] + get_flat(pair_ref, plan.top_row, plan.top_shape)
    top_out[...] = top

    def merged(level, cell):
        size, total = x.length >> level, None
        for where_own, where_partner, at in ((keep_even, keep_odd, cell), (keep_odd, keep_even, cell - size)):
            if 0 <= at < x.width[level]:
                value = ext_ref[at] * where_own + plan.pair_plane(pair_ref, at) * where_partner
                total = value if total is None else total + value
        return total

    second = [merged(2, c) for c in range(plan.pair_width[2])]
    chips = x.count // 2
    high = x.length >> 2
    for k, ref in zip(range(1, chips), targets):
        for g in range(plan.pair_groups):
            total = None
            for slot, p in enumerate(range(3 * g, min(3 * g + 3, plan.planes))):
                if chips == 2:
                    two = jnp.where(chip == 0, second[high + p], second[p])
                else:
                    two = second[high + p] if k == 1 else second[p]
                two = roll_lanes(two, SLOT * slot - plan.lane[2])
                total = two if slot == 0 else jnp.where(lanes < SLOT * slot, total, two)
            put_plane(ref, plan.coarse_rows * g, total)
        put_flat(ref, plan.coarse_rows * plan.pair_groups, top)


def mix_planes(get, put, count, matrix):
    for i in range(0, count, 2):
        pair = [i, min(i + 1, count - 1)]
        stacked = []
        for j in pair:
            high, low = split(get(j))
            stacked.append(jnp.concatenate([high, high, low], axis=0))
        both = dot(matrix, jnp.concatenate(stacked, axis=1))
        put(i, both[:, :LANES])
        if pair[1] != i:
            put(pair[1], both[:, LANES:])


def stencil(cells, wanted, sigma, reach=REACH):
    result = []
    for i in wanted:
        total = cells.get(i)
        for k in range(1, reach + 1):
            terms = [cells[j] for j in (i - k, i + k) if j in cells]
            if terms:
                term = functools.reduce(jnp.add, terms) * float(np.exp(-((k / sigma) ** 2)))
                total = term if total is None else total + term
        result.append(total)
    return result


def put_ready(ready, sigmas, s, row, value):
    high, low = split(value)
    rows = slice(row, row + value.shape[0])
    step = LANES * sigmas
    ready[rows, s * LANES : (s + 1) * LANES] = high
    ready[rows, step + s * LANES : step + (s + 1) * LANES] = low
    ready[rows, 2 * step + s * LANES : 2 * step + (s + 1) * LANES] = high


def fine_padding(plan):
    pad = up(plan.fine_rows, 16) - plan.fine_rows
    return [jnp.zeros((pad, LANES), F32)] if pad else []


def fine_inner_kernel(plan, q_ref, y_table, inner_ref, edge_ref, q_out, mixed):
    x, y = plan.x, plan.y
    q_out[...] = q_ref[...]
    halo = jnp.zeros((up(plan.fine_rows, 16) - y.length, LANES), F32)

    def put(i, value):
        mixed[i] = value

    mix_planes(lambda i: jnp.concatenate([q_ref[i], halo], axis=0), put, x.length, plan.fine_matrix(y_table))
    inner = range(REACH, x.length - REACH)
    edge = [*range(REACH), *range(x.length - REACH, x.length)]
    half = len(inner) * (y.length - 16)
    for s, sigma in enumerate(STENCIL_SIGMAS):
        row, end = s * y.length, (s + 1) * y.length
        planes = {i: mixed[i, row + 8 : end - 8, :] for i in range(x.length)}
        step = y.length - 16
        for i, value in enumerate(stencil(planes, inner, sigma)):
            inner_ref[s, i * step : (i + 1) * step, :] = value
        for i, value in enumerate(stencil(planes, edge, sigma)):
            edge_ref[i, row + 8 : end - 8, :] = value
        ends = lambda i: jnp.concatenate([mixed[i, row : row + 8, :], mixed[i, end - 8 : end, :]], axis=0)
        planes = {i: ends(i) for i in range(x.length)}
        for i, value in enumerate(stencil(planes, inner, sigma)):
            inner_ref[s, half + i * 16 : half + i * 16 + 16, :] = value
        for i, value in enumerate(stencil(planes, edge, sigma)):
            edge_ref[i, row : row + 8, :] = value[:8]
            edge_ref[i, end - 8 : end, :] = value[8:]


def fine_halo_kernel(plan, inner_ref, edge_ref, y_table, z_table, *refs):
    halos, (main_ref, push_ref, out_ref, mixed, ready) = refs[: plan.y.count - 1], refs[plan.y.count - 1 :]
    x, y = plan.x, plan.y
    near = plan.near_y(halos)
    padding = [jnp.zeros((8, LANES), F32)] * (plan.halo_cols // 24 - len(near))

    def get(i):
        return jnp.concatenate([plane(h, 0, 8, i) for h in near] + padding, axis=0)

    def put(i, value):
        mixed[i] = value

    mix_planes(get, put, x.length, plan.halo_matrix(y_table))
    inner = range(REACH, x.length - REACH)
    edge = [*range(REACH), *range(x.length - REACH, x.length)]
    out_ref[...] = edge_ref[...]
    half = len(inner) * (y.length - 16)
    for s, sigma in enumerate(STENCIL_SIGMAS):
        row, end = s * y.length, (s + 1) * y.length
        planes = {i: mixed[i, 16 * s : 16 * s + 16, :] for i in range(x.length)}
        for start in range(0, half, 64):
            put_ready(ready, 3, s, start, inner_ref[s, start : start + 64, :])
        for i, value in enumerate(stencil(planes, inner, sigma)):
            start = half + 16 * i
            put_ready(ready, 3, s, start, inner_ref[s, start : start + 16, :] + value)
        for i, value in enumerate(stencil(planes, edge, sigma)):
            out_ref[i, row : row + 8, :] += value[:8]
            out_ref[i, end - 8 : end, :] += value[8:]
    main_ref[...] = dot(ready[...], plan.z_matrix(z_table, 0), ((1,), (1,)))
    push_ref[...] = dot(plan.z_matrix(z_table, 1), ready[...], ((1,), (1,)))


def fine_edge_kernel(plan, halo_ref, edge_ref, y_table, z_table, push_ref, ready_ref, mixed, *, partner):
    x, y = plan.x, plan.y
    gx = lax.axis_index("gx")
    odd = gx % 2
    high = 1 - odd if partner else odd
    keep = mask(True) if partner else mask(jnp.where(high == 1, gx < x.count - 1, gx > 0))
    padding = fine_padding(plan)
    away = lambda k: jnp.where(high == 1, k, REACH - 1 - k)

    def get(k):
        return jnp.concatenate([plane(halo_ref, 0, plan.fine_rows, away(k)) * keep] + padding, axis=0)

    def put(k, value):
        mixed[k] = value

    mix_planes(get, put, REACH, plan.fine_matrix(y_table))
    for s, sigma in enumerate(STENCIL_SIGMAS):
        for r in range(0, y.length, 16):
            row = s * y.length + r
            after = {REACH + k: mixed[k, row : row + 16, :] for k in range(REACH)}
            for i, added in enumerate(stencil(after, range(REACH), sigma)):
                value = edge_ref[away(i) + REACH * high, row : row + 16, :] + added
                top, low = split(value)
                at = away(i) * (y.length // 16) + r // 16
                for c, part in enumerate((top, low, top)):
                    start = (3 * c + s) * LANES
                    ready_ref[at, :, start : start + LANES] = part
    whole = ready_ref[...].reshape(REACH * y.length, 9 * LANES)
    push_ref[...] = dot(plan.z_matrix(z_table, 1), whole, ((1,), (1,)))


def fine_main_kernel(plan, partner_ref, side_ref, z_table, out_ref):
    odd = lax.axis_index("gx") % 2
    for ref, at in ((partner_ref, 1 - odd), (side_ref, odd)):
        whole = ref[...].reshape(REACH * plan.y.length, 9 * LANES)
        out_ref[at] = dot(whole, plan.z_matrix(z_table, 0), ((1,), (1,)))


def coarse_inner_kernel(plan, ext_ref, pair_ref, y_table, *refs):
    *parts, mixed = refs
    own = plan.x.width[1]

    def put(i, value):
        mixed[i] = value

    get = lambda i: ext_ref[i] if i < own else plan.pair_plane(pair_ref, i - own)
    mix_planes(get, put, own + plan.planes, plan.coarse_matrix(y_table))
    for level, part in zip((1, 2), parts):
        rows, width = (plan.rows1, plan.rows2)[level - 1], plan.x.width[level]
        wanted = range(LOW[level], LOW[level] + width)
        for s, sigma in enumerate(STENCIL_SIGMAS):
            for r in range(0, rows, 8):
                cells = collect_inner(plan, level, mixed, plan.group[level] + s * rows + r, 8)
                for i, value in enumerate(stencil(cells, wanted, sigma)):
                    part[s * width + i, r : r + 8, :] = value


def adder(plan, level, cells):
    start, width = LOW[level], plan.x.width[level]

    def add(cell, value, keep):
        if start - REACH <= cell < start + width + REACH:
            value = value * keep
            cells[cell] = cells[cell] + value if cell in cells else value

    return add


def collect_inner(plan, level, inner, row, rows):
    x, odd = plan.x, lax.axis_index("gx") % 2
    size, width, start, own = x.length >> level, x.width[level], LOW[level], x.width[1]
    cells = {start + k: inner[k, row : row + rows, :] for k in range(width)}
    add = adder(plan, level, cells)
    layers = FACE if level == 1 else width
    for k in range(layers):
        value = inner[own + k, row : row + rows, :]
        add(size + start + k, value, mask(odd == 0))
        add(-size + start + width - layers + k, value, mask(odd == 1))
    return cells


def collect_outer(plan, level, outer, row, rows):
    x, gx = plan.x, lax.axis_index("gx")
    odd, chip, chips = gx % 2, gx // 2, plan.x.count // 2
    size, width, start = x.length >> level, x.width[level], LOW[level]
    cells = {}
    add = adder(plan, level, cells)
    if level == 1:
        for k in range(FACE):
            value = outer[k, row : row + rows, :]
            add(-size + start + width - FACE + k, value, mask((chip > 0) & (odd == 0)))
            add(size + start + k, value, mask((chip < chips - 1) & (odd == 1)))
        return cells
    for n, offset in enumerate(plan.near_chips):
        for shift, here in ((-offset, chip >= offset), (chips - offset, chip < offset)):
            if abs(shift) != 1:
                continue
            for core in (0, 1):
                keep = mask(here & (odd == core))
                first = 2 * size * shift - size * core + start + (size if shift < 0 else 0)
                for k in range(plan.planes):
                    add(first + k, outer[plan.planes * n + k, row : row + rows, :], keep)
    return cells


def coarse_kernel(plan, part1, part2, *refs):
    chips = plan.x.count // 2 - 1
    others, refs = refs[:chips], refs[chips:]
    side_in, *pushes = refs[:4]
    y_table, z_table, partner_ref, side_ref, e1_ref, e2_ref, outer, *ready = refs[4:]

    def put(i, value):
        outer[i] = value

    lanes = lax.broadcasted_iota(jnp.int32, (1, LANES), 1)
    groups = [plane(side_in, plan.fine_rows * REACH, plan.coarse_rows, g) for g in range(plan.face_groups + 1)]

    def get(i):
        n, p = i // plan.planes, i % plan.planes
        two = plane(others[plan.near_chips[n] - 1], 0, plan.coarse_rows, p // 3)
        value = roll_lanes(two, plan.lane[2] - SLOT * (p % 3))
        if n == 0 and p < FACE:
            value = jnp.where(lanes < plan.lane[2], unpack_face(plan, groups, p), value)
        return value

    mix_planes(get, put, plan.planes * len(plan.near_chips), plan.coarse_matrix(y_table))
    x = plan.x
    results = []
    for level in (1, 2):
        rows = plan.rows1 if level == 1 else plan.rows2
        wanted = range(LOW[level], LOW[level] + x.width[level])
        for s, sigma in enumerate(STENCIL_SIGMAS):
            for r in range(0, rows, 8):
                cells = collect_outer(plan, level, outer, plan.group[level] + s * rows + r, 8)
                for i, added in enumerate(stencil(cells, wanted, sigma)):
                    value = (part1, part2)[level - 1][s * x.width[level] + i, r : r + 8, :]
                    put_ready(ready[level - 1], 3, s, i * rows + r, value if added is None else value + added)
        results.append(dot(plan.z_matrix(z_table, level + 1), ready[level - 1][...], ((1,), (1,))))
    one, two = results
    e1_ref[...] = one[: plan.tall[1]]
    e2_ref[...] = two[: plan.tall[2]]
    inner, partner, side = (p[...] for p in pushes)
    odd = lax.axis_index("gx") % 2 == 1
    pushed = jnp.concatenate([inner, jnp.where(odd, partner, side), jnp.where(odd, side, partner)], axis=1)
    for n, ref in enumerate((partner_ref, side_ref)):
        ref[:8, :] = pushed[8 * n : 8 * n + 8, :]
        ref[8:, :] = jnp.zeros((16, ref.shape[1]), F32)
        start = plan.tall[1] + 16 * n
        ref[8:, : plan.flat[1]] = one[start : start + 16]
        start = plan.tall[2] + 16 * n
        ref[8:, 512 : 512 + plan.flat[2]] = two[start : start + 16]


def top_chips_kernel(plan, top_ref, *refs):
    *others, out_ref = refs
    total = top_ref[...]
    for ref in others:
        total = total + get_flat(ref, plan.coarse_rows * plan.pair_groups, plan.top_shape)
    out_ref[...] = total


def top_kernel(plan, *refs):
    *values, out_ref = refs
    total = functools.reduce(jnp.add, [v[...] for v in values])
    shape = (plan.flat_top, plan.flat[3])
    source, target = (lax.broadcasted_iota(jnp.int32, shape, d) for d in (0, 1))
    first_x = (plan.x.length >> 3) * lax.axis_index("gx") + LOW[3]
    first_y = (plan.y.length >> 3) * lax.axis_index("gy") + LOW[3]
    apart_x = source // plan.whole3 - target // plan.rows3 - first_x
    apart_y = source % plan.whole3 - target % plan.rows3 - first_y
    square = (apart_x * apart_x + apart_y * apart_y).astype(F32)
    result, tall = None, plan.tall[3]
    for s, sigma in enumerate(TOP_SIGMAS):
        matrix = jnp.exp(square * (-1.0 / sigma**2))
        matrix_high, matrix_low = split(matrix)
        high, low = split(total[s * tall : (s + 1) * tall])
        left = jnp.concatenate([high, low, high], axis=1)
        term = dot(left, jnp.concatenate([matrix_high, matrix_high, matrix_low], axis=0))
        result = term if result is None else result + term
    out_ref[...] = result


def finish_kernel(plan, inner_ref, edge_ref, e1_ref, e2_ref, partner_ref, side_ref, e3_ref, flat, tall, out_ref, e1, e2):
    x, y, z = plan.x, plan.y, plan.z
    gx, gy, gz = (lax.axis_index(name) for name in ("gx", "gy", "gz"))
    odd = gz % 2
    for window, own, tall_ in ((e1, e1_ref, plan.tall[1]), (e2, e2_ref, plan.tall[2])):
        window[:tall_, :] = own[...]
        if window.shape[0] > tall_:
            window[tall_:, :] = jnp.zeros((window.shape[0] - tall_, window.shape[1]), F32)
    kept = lax.broadcasted_iota(jnp.int32, (16, 1), 0) < FACE
    for ref, high in ((partner_ref, odd == 0), (side_ref, odd == 1)):
        one = jnp.where(kept, ref[8:, : plan.flat[1]], 0.0)
        two = ref[8:, 512 : 512 + plan.flat[2]]
        for window, value, tall_ in ((e1, one, plan.tall[1]), (e2, two, plan.tall[2])):
            window[:16, :] += value * mask(~high)
            window[tall_ - 16 : tall_, :] += value * mask(high)

    bounds = [int(r) for r in plan.tall_rows]

    def along_z(value, number, parts):
        high, low = split(value)
        stacked = jnp.concatenate([high, low, high][:parts], axis=0)
        return dot(stacked, tall[gz, bounds[number] : bounds[number + 1], :], ((0,), (0,)))

    def inside(level):
        rows = (0, plan.rows1, plan.rows2, plan.rows3)[level]
        index = lax.broadcasted_iota(jnp.int32, (plan.flat[level], LANES), 0)
        cell_x = index // rows + ((x.length >> level) * gx + LOW[level])
        cell_y = index % rows + ((y.length >> level) * gy + LOW[level])
        in_x = (cell_x >= 0) & (cell_x < (x.count * x.length) >> level)
        return in_x & (cell_y >= 0) & (cell_y < (y.count * y.length) >> level)

    flat_bounds = [int(r) for r in plan.flat_rows]

    def finer(value, number):
        high, low = split(value)
        matrix = flat[flat_bounds[number] : flat_bounds[number + 1], :][:, : value.shape[0]]
        both = dot(matrix, jnp.concatenate([high, low], axis=1))
        return both[:, :LANES] + both[:, LANES:]

    pad = up(plan.tall[3], 16) - plan.tall[3]
    e3 = jnp.concatenate([e3_ref[...]] + ([jnp.zeros((pad, e3_ref.shape[1]), F32)] if pad else []), axis=0)
    ends = along_z(jnp.concatenate([partner_ref[:8], side_ref[:8]], axis=0), 1, 2)
    one, two, three = along_z(e1[...], 0, 2), along_z(e2[...], 2, 3), along_z(e3, 3, 3)
    three = jnp.where(inside(3), three, 0.0)
    two = jnp.where(inside(2), two + finer(three, 0)[: plan.flat[2]], 0.0)
    one = jnp.where(inside(1), one + finer(two, 1)[: plan.flat[1]], 0.0)
    coarse = finer(one, 2) + ends
    inner = inner_ref.shape[0]
    tiles = y.length // 8
    for k, (x_, t) in enumerate(plan.tiles()):
        row = 8 * k
        value = coarse[row : row + 8]
        if row < inner:
            value = value + inner_ref[row : row + 8]
        else:
            end, row = divmod(row - inner, edge_ref.shape[1])
            value = value + edge_ref[end, row : row + 8]
        out_ref[8 * (tiles * x_ + t) : 8 * (tiles * x_ + t) + 8] = value


def call(kernel, plan, operands, outs, scratch=(), hbm=(), vmem=32):
    whole, left = pl.BlockSpec(memory_space=pltpu.VMEM), pl.BlockSpec(memory_space=pl.ANY)
    return pl.pallas_call(
        functools.partial(kernel, plan),
        in_specs=[left if i in hbm else whole for i in range(len(operands))],
        out_specs=[whole] * len(outs),
        scratch_shapes=list(scratch),
        out_shape=list(outs),
        compiler_params=pltpu.CompilerParams(vmem_limit_bytes=int(vmem * 2**20)),
    )(*[jnp.asarray(o) for o in operands])


def shift(value, axis, offset):
    count = lax.axis_size(axis)
    return lax.ppermute(value, axis, [(i, (i + offset) % count) for i in range(count)])


def swap(value, axes, partner):
    first, second = (lax.axis_size(a) for a in axes)
    pairs = []
    for i in range(first):
        for j in range(second):
            k, m = partner(i, j)
            pairs.append((i * second + j, k * second + m))
    return lax.ppermute(value, axes, pairs)


def side_of(count):
    return lambda i: None if i in (0, count - 1) else i + (1 if i % 2 else -1)


def shards(plan, charges):
    x, y, z = plan.x, plan.y, plan.z
    array = lambda *shape: jax.ShapeDtypeStruct(shape, F32)
    vmem = lambda *shape: pltpu.VMEM(shape, F32)
    ready = lambda rows, sigmas: pltpu.VMEM((rows, 3 * sigmas * LANES), BF)
    side_x, side_z = side_of(x.count), side_of(z.count)
    partner_x = lambda v: swap(v, ("gx", "gy"), lambda i, j: (i ^ 1, j))
    across_x = lambda v: swap(v, ("gx", "gy"), lambda i, j: (i, j ^ 1) if side_x(i) is None else (side_x(i), j))
    partner_z = lambda v: swap(v, ("gx", "gz"), lambda i, j: (i, j ^ 1))
    across_z = lambda v: swap(v, ("gx", "gz"), lambda i, j: (i ^ 1, j) if side_z(j) is None else (i, side_z(j)))

    rows_y = 8 * x.length + 16 * x.width[1]
    table = plan.restrict_tables()
    own, top, y_table, top_table, *to_y = call(
        restrict_kernel,
        plan,
        [charges, table],
        [
            array(x.width[1], plan.rows1, LANES),
            array(plan.tall[3], plan.flat_top),
            jax.ShapeDtypeStruct((3 * y.length + plan.rows_mixed + plan.halo_rows, plan.y_cols), BF),
            jax.ShapeDtypeStruct((2 * plan.tall[3], up(plan.top_cols, LANES)), BF),
        ]
        + [array(rows_y // 8, 8, LANES)] * plan.kinds,
        [
            vmem(x.length, plan.rows_restricted, LANES),
            vmem(x.width[3], plan.whole3, LANES),
            vmem(*charges.shape),
            pltpu.VMEM((sum(plan.blocks), 16, LANES), BF),
            pltpu.SemaphoreType.DMA((6,)),
        ],
        hbm=(0, 1),
        vmem=53,
    )
    from_y = []
    for offset in range(1, y.count):
        value = to_y[0 if offset == 1 else -1]
        value = value if offset in (1, y.count - 1) else value[x.length :]
        from_y.append(shift(value, "gy", offset))

    tops = {m: swap(top, ("gx", "gz"), lambda i, j, m=m: (i, j ^ m)) for m in sorted(range(1, z.count), key=lambda m: (m == 2, m))}
    tops = [tops[m] for m in range(1, z.count)]
    (top,) = call(top_z_kernel, plan, [top, *tops, top_table], [array(*plan.top_shape)])

    z_table = plan.z_tables()
    inner_cells = (x.length - 2 * REACH) * y.length
    inner, edge, held = call(
        fine_inner_kernel,
        plan,
        [charges, y_table],
        [array(3, inner_cells, LANES), array(2 * REACH, 3 * y.length, LANES), array(*charges.shape)],
        [vmem(x.length, 3 * y.length, LANES)],
    )
    edge, *from_y = lax.optimization_barrier((edge, *from_y))

    ext, to_partner, to_side = call(
        extend_kernel,
        plan,
        [held, own, top, *from_y],
        [
            array(x.width[1], plan.coarse_rows, LANES),
            array((plan.top_row + plan.top_rows) // 8, 8, LANES),
            array(plan.side_rows // 8, 8, LANES),
        ],
    )
    from_side, pair = across_x(to_side), partner_x(to_partner)

    main_inner, push_inner, edge = call(
        fine_halo_kernel,
        plan,
        [inner, edge, y_table, z_table, *from_y],
        [array(inner_cells, z.length), array(16, inner_cells), array(2 * REACH, 3 * y.length, LANES)],
        [vmem(x.length, plan.halo_rows, LANES), ready(inner_cells, 3)],
    )

    chips = x.count // 2
    rows_x = plan.pair_groups * plan.coarse_rows + plan.top_rows
    top, *to_chips = call(
        chip_kernel,
        plan,
        [ext, pair, top],
        [array(*plan.top_shape)] + [array(rows_x // 8, 8, LANES)] * (chips - 1),
    )
    from_chips = [
        swap(v, ("gx", "gy"), lambda i, j, k=k: ((i + 2 * k) % x.count ^ 1, j))
        for k, v in zip(range(1, chips), to_chips)
    ]
    parts = call(
        coarse_inner_kernel,
        plan,
        [ext, pair, y_table],
        [array(3 * x.width[1], plan.rows1, LANES), array(3 * x.width[2], plan.rows2, LANES)],
        [vmem(x.width[1] + plan.planes, plan.rows_mixed, LANES)],
    )

    def fine_end(halo, is_partner):
        return call(
            functools.partial(fine_edge_kernel, partner=is_partner),
            plan,
            [halo, edge, y_table, z_table],
            [array(16, REACH * y.length), jax.ShapeDtypeStruct((REACH * y.length // 16, 16, 9 * LANES), BF)],
            [vmem(REACH, 3 * y.length, LANES)],
        )

    push_partner, ready_partner = fine_end(pair, True)
    from_side, push_partner, *parts = lax.optimization_barrier((from_side, push_partner, *parts))
    push_side, ready_side = fine_end(from_side, False)
    pushes = [push_inner, push_partner, push_side]
    window = lambda level: array(plan.tall[level], plan.flat[level])
    to_partner, to_side, e1, e2 = call(
        coarse_kernel,
        plan,
        [*parts, *from_chips, from_side, *pushes, y_table, z_table],
        [array(24, 1024), array(24, 1024), window(1), window(2)],
        [vmem(plan.planes * len(plan.near_chips), plan.rows_mixed, LANES), ready(plan.flat[1], 3), ready(plan.flat[2], 3)],
    )
    from_near = [partner_z(to_partner), across_z(to_side)]

    (top,) = call(top_chips_kernel, plan, [top, *from_chips], [array(*top.shape)])
    tops = [top] + [shift(top, "gy", offset) for offset in range(1, y.count)]
    (e3,) = call(top_kernel, plan, tops, [window(3)])

    (main_edge,) = call(
        fine_main_kernel, plan, [ready_partner, ready_side, z_table], [array(2, REACH * y.length, z.length)]
    )
    (potential,) = call(
        finish_kernel,
        plan,
        [main_inner, main_edge, e1, e2, *from_near, e3, *plan.finish()],
        [array(x.length * y.length, z.length)],
        [vmem(up(plan.tall[level], 16), plan.flat[level]) for level in (1, 2)],
    )
    return potential.reshape(charges.shape)


def solution(mesh):
    counts = [mesh.shape[name] for name in ("gx", "gy", "gz")]

    def run(charges):
        plan = Plan(counts, [size // n for size, n in zip(charges.shape, counts)])
        placed = P("gx", "gy", "gz")
        return jax.shard_map(
            functools.partial(shards, plan), mesh=mesh, in_specs=(placed,), out_specs=placed, check_vma=False
        )(charges)

    return run
```
